32 devices in a mesh: gz: 8 (over y, x, core), gy: 4 (over z).
Axes of the slice: x: 2, y: 2, z: 4, core: 2. Of those that a mesh axis runs over, the one named last changes fastest.
Arguments:
- velocity: float32 [3, 128, 128, 512], P(None, 'gz', 'gy'), may hold values from -5 to 8
- diffusion: float32 [128, 512], P('gy'), may hold values from 0.5 to 1000
- wall_types: int32 [128, 512], P('gy'), may hold values from 0 to 3
- stretch_index: int32 [128], replicated, may hold values from 0 to 6
- bulk_target: float32 [1], replicated, may hold values from 0.5 to 1.5
Outputs:
- velocity_out: float32 [3, 128, 128, 512], P(None, 'gz', 'gy')
The draws below stay inside these ranges and needn't reach their ends.
All inputs are finite; a program needn't handle non-finite values.
Results may differ from the reference program's by a relative error of at most 0.0028.
Values sent between devices are 32-bit elements; how exact they have to be, the bound alone decides.
No kernel may reach another device: no remote copies, remote signals or barrier semaphores. Data moves between devices by JAX's collectives and lax.ppermute only.
A program may use at most 192 MiB of HBM per device.

```python
import math
import jax
import jax.numpy as jnp
from jax import lax

NX = 512
NZ = 128
NY = 128


def draw_velocity(key, part):
    z_position = jnp.arange(NZ, dtype=jnp.float32) / NZ
    noise = jnp.clip(jax.random.normal(key, (3, NZ, NY, NX), jnp.float32), -5.0, 5.0)
    mean_part = 1.0 + 2.0 * z_position
    component_scale = jnp.array([1.0, 0.3, 0.0], jnp.float32)
    return noise + component_scale[:, None, None, None] * mean_part[None, :, None, None]


def with_ends(entries, key, least, largest):
    shape = entries.shape
    place = [jax.random.randint(jax.random.fold_in(key, axis), (), 0, shape[axis]) for axis in range(len(shape))]
    entries = entries.at[tuple(place)].set(least)
    longest = shape.index(max(shape))
    place[longest] = (place[longest] + 1) % shape[longest]
    return entries.at[tuple(place)].set(largest)


def block_scale(rng, dims, cuts, smallest, largest):
    def one(axis_at, blocks):
        steps = jax.random.uniform(jax.random.fold_in(jax.random.fold_in(rng, 6), axis_at), (blocks,), jnp.float32, smallest / len(cuts), largest / len(cuts))
        return jnp.repeat(jnp.exp(steps), dims[axis_at] // blocks).reshape((-1,) + (1,) * (len(dims) - axis_at - 1))

    gain = one(*cuts[0])
    for cut in cuts[1:]:
        gain = gain * one(*cut)
    return gain


def setup_inputs(seed: int = 0) -> dict:
    seeds = jax.random.split(jax.random.key(seed), 6)
    return {
        "velocity": draw_velocity(jax.random.fold_in(seeds[5], 71), 0),
        "diffusion": jnp.clip(jnp.exp(math.log(1000.0) - 7.6009025 * jax.random.uniform(seeds[1], (NY, NX), jnp.float32) ** block_scale(seeds[1], (NY, NX), ((0, 4),), -0.2, 0.2)), 0.5, 1000.0),
        "wall_types": with_ends(jax.random.randint(seeds[2], (NY, NX), 0, 4), jax.random.fold_in(seeds[2], 1), 0, 3).astype(jnp.int32),
        "stretch_index": with_ends(jax.random.randint(seeds[3], (NZ,), 0, 7), jax.random.fold_in(seeds[3], 1), 0, 6).astype(jnp.int32),
        "bulk_target": jnp.clip(jax.random.uniform(seeds[4], (1,), jnp.float32, 0.5, 1.5), 0.5, 1.5),
    }


def spacing(stretch_index):
    return 0.5 + 0.25 * stretch_index.astype(jnp.float32)


def face_tables(heights):
    faces = 2.0 / (heights[:-1] + heights[1:])
    padding = jnp.zeros((1,), jnp.float32)
    return jnp.concatenate([padding, faces]), jnp.concatenate([faces, padding])


def cell_rows(heights, face_left, face_right, is_first, is_last, diffusion, lower_wall, upper_wall):
    left_sum = face_left + is_first * lower_wall
    right_sum = face_right + is_last * upper_wall
    diagonal = heights + diffusion * (left_sum + right_sum)
    return -diffusion * face_left, diagonal, -diffusion * face_right


def reference(velocity, diffusion, wall_types, stretch_index, bulk_target):
    heights = spacing(stretch_index)
    face_left, face_right = face_tables(heights)
    cell_ids = jnp.arange(NZ, dtype=jnp.int32)
    is_first = (cell_ids == 0).astype(jnp.float32)
    is_last = (cell_ids == NZ - 1).astype(jnp.float32)
    lower_wall = (wall_types % 2).astype(jnp.float32) * (2.0 / heights[0])
    upper_wall = (wall_types // 2).astype(jnp.float32) * (2.0 / heights[NZ - 1])
    unit_field = jnp.ones((1, NY, NX), jnp.float32)

    def forward(carry, cell_index):
        ratio_prev, value_prev = carry
        lower_band, diagonal, upper_band = cell_rows(heights[cell_index], face_left[cell_index], face_right[cell_index], is_first[cell_index], is_last[cell_index], diffusion, lower_wall, upper_wall)
        column = lax.dynamic_index_in_dim(velocity, cell_index, axis=1, keepdims=False)
        rhs_row = jnp.concatenate([heights[cell_index] * column, heights[cell_index] * unit_field], axis=0)
        divisor = diagonal - lower_band * ratio_prev
        factor = upper_band / divisor
        solved_row = (rhs_row - lower_band[None] * value_prev) / divisor[None]
        return (factor, solved_row), (factor, solved_row)

    zero_state = (jnp.zeros((NY, NX), jnp.float32), jnp.zeros((4, NY, NX), jnp.float32))
    _, (factors, values) = lax.scan(forward, zero_state, cell_ids)

    def backward(following, row_data):
        factor, solved_row = row_data
        current = solved_row - factor[None] * following
        return current, current

    _, solved = lax.scan(backward, jnp.zeros((4, NY, NX), jnp.float32), (factors, values), reverse=True)
    flow_total = jnp.sum(heights[:, None, None] * solved[:, 0])
    weight_total = jnp.sum(heights[:, None, None] * solved[:, 3])
    volume = jnp.sum(heights) * NY * NX
    streamwise = solved[:, 0] + ((bulk_target[0] * volume - flow_total) / weight_total) * solved[:, 3]
    return jnp.stack([streamwise, solved[:, 1], solved[:, 2]], axis=0)
```

```python
import functools

import jax
import jax.numpy as jnp
from jax import lax
from jax.experimental import pallas as pl
from jax.experimental.pallas import tpu as pltpu
from jax.sharding import PartitionSpec as P

SUB = 8
LANES = 128
MIB = 1024 * 1024


def height(index_ref, k):
    return 0.5 + 0.25 * index_ref[k].astype(jnp.float32)


def half_sum(index_ref, k):
    return 0.5 * (height(index_ref, k) + height(index_ref, k + 1))


def ladder_kernel(
    cells, blocks, chips,
    index_ref, diffusion_ref, walls_ref, velocity_hbm,
    sums_ref, pair_ref, chip_ref, left_ref, right_ref, ends_ref, tile_ref,
    velocity_ref, through_ref, inverse_ref, sems,
):
    total = cells * blocks
    components = velocity_ref.shape[0]
    copies = [
        pltpu.make_async_copy(velocity_hbm.at[c], velocity_ref.at[c], sems.at[c])
        for c in range(components)
    ]
    for copy in copies:
        copy.start()
    me = lax.axis_index("gz")
    chip = me // 2
    first = chip * 2
    diffusion = diffusion_ref[...]
    inverse_ref[...] = 1.0 / diffusion
    walls = walls_ref[...]
    lower = diffusion * (walls % 2).astype(jnp.float32) * 2.0 / height(index_ref, 0)
    upper = diffusion * (walls // 2).astype(jnp.float32) * 2.0 / height(index_ref, total - 1)

    def forward(block, kappa, keep=None):
        start = block * cells
        inverse = inverse_ref[...]
        flux = height(index_ref, start) + kappa
        value = jnp.ones_like(flux)
        for j in range(cells):
            if keep is not None:
                keep(j, flux, value)
            k = start + j
            if j < cells - 1:
                value = value + (half_sum(index_ref, k) * inverse) * flux
                flux = flux + height(index_ref, k + 1) * value
        k = jnp.minimum(start + cells - 1, total - 2)
        after = 1.0 / (value + (half_sum(index_ref, k) * inverse) * flux)
        return flux * after, after

    def backward(block, kappa, scale=None, keep=None):
        start = block * cells
        inverse = inverse_ref[...]
        flux = height(index_ref, start + cells - 1) + kappa
        value = jnp.ones_like(flux)
        if scale is not None:
            flux, value = flux * scale, scale
        for j in reversed(range(cells)):
            if keep is not None:
                keep(j, flux, value)
            k = start + j
            if j > 0:
                value = value + (half_sum(index_ref, k - 1) * inverse) * flux
                flux = flux + height(index_ref, k - 1) * value
        k = jnp.maximum(start - 1, 0)
        after = 1.0 / (value + (half_sum(index_ref, k) * inverse) * flux)
        return flux * after, after

    def sweep_forward(block, state):
        kappa, product = state
        kappa, after = forward(block, kappa)
        through_ref[block] = after
        return kappa, product * after

    def sweep_backward(step, state):
        block = blocks - 1 - step
        kappa, product = state
        kappa, after = backward(block, kappa)
        through_ref[block] = after
        return kappa, product * after

    ones = jnp.ones_like(diffusion)
    kappa_left, product_left = lax.fori_loop(0, me, sweep_forward, (lower, ones))
    ends = {}

    def keep_left(j, flux, value):
        left_ref[j] = value
        ends["flux"], ends["value"] = flux, value

    kappa, own_forward = forward(me, kappa_left, keep_left)
    ends_ref[0] = kappa
    ends_ref[1] = lower * product_left

    @pl.when(me == first)
    def _():
        _, after = forward(me + 1, kappa)
        pair_ref[0] = after

    @pl.when(me != first)
    def _():
        pair_ref[0] = own_forward
        pair_ref[2] = through_ref[first]

    kappa_right, product_right = lax.fori_loop(
        0, blocks - 1 - me, sweep_backward, (upper, ones)
    )
    scale = 1.0 / (ends["flux"] + kappa_right * ends["value"])

    def keep_right(j, flux, value):
        right_ref[j] = value

    kappa, own_backward = backward(me, kappa_right, scale, keep_right)

    @pl.when(me == first)
    def _():
        pair_ref[1] = own_backward * scale
        pair_ref[2] = through_ref[first + 1]

    @pl.when(me != first)
    def _():
        _, after = backward(me - 1, kappa)
        pair_ref[1] = after

    ends_ref[0] = lower * product_left
    ends_ref[1] = upper * product_right
    for m in range(1, chips):
        other = chip ^ m
        low = jnp.minimum(chip, other)
        high = jnp.maximum(chip, other)
        chip_ref[m - 1] = lax.fori_loop(
            low + 1,
            high,
            lambda r, product: product * (through_ref[2 * r] * through_ref[2 * r + 1]),
            ones,
        )
    for copy in copies:
        copy.wait()
    flow = jnp.zeros((SUB, LANES), jnp.float32)
    weight = jnp.zeros((SUB, LANES), jnp.float32)

    def fold(array):
        parts = [array[:, i * LANES:(i + 1) * LANES] for i in range(array.shape[1] // LANES)]
        return functools.reduce(jnp.add, parts)

    for t in range(diffusion.shape[0] // SUB):
        rows = pl.ds(t * SUB, SUB)
        from_left = [0.0] * components
        from_right = [0.0] * components
        plain = 0.0
        left_total = 0.0
        right_total = 0.0
        extent = 0.0
        for j in range(cells):
            h = height(index_ref, me * cells + j)
            left = h * left_ref[j, rows]
            right = h * right_ref[j, rows]
            extent = extent + h
            left_total = left_total + left
            right_total = right_total + right
            for c in range(components):
                v = velocity_ref[c, j, rows]
                from_left[c] = from_left[c] + left * v
                from_right[c] = from_right[c] + right * v
                if c == 0:
                    plain = plain + h * v
        block_scale = scale[t * SUB:(t + 1) * SUB]
        low_part = ends_ref[0, rows]
        high_part = ends_ref[1, rows] * block_scale
        for c in range(components):
            sums_ref[t, c] = from_left[c] * own_forward[t * SUB:(t + 1) * SUB]
            sums_ref[t, components + c] = from_right[c] * own_backward[t * SUB:(t + 1) * SUB]
        flow = flow + fold(plain - low_part * from_right[0] - high_part * from_left[0])
        weight = weight + fold(extent - low_part * right_total - high_part * left_total)
    tile_ref[0] = flow
    tile_ref[1] = weight


def merge_kernel(chips, components, tiles_count, sums_ref, mate_ref, pair_ref, *rest):
    tile_refs = rest[:tiles_count]
    send_refs = rest[tiles_count:tiles_count + chips - 1]
    column_ref = rest[-1]
    me = lax.axis_index("gz")
    chip = me // 2
    is_first = me == chip * 2
    row_tiles = sums_ref.shape[0]
    column = functools.reduce(jnp.add, [ref[...] for ref in tile_refs])
    column_ref[...] = column
    for ref in send_refs:
        ref[components * row_tiles] = jnp.zeros(ref.shape[1:], jnp.float32)
        ref[components * row_tiles, :, 0:LANES] = column[0]
        ref[components * row_tiles, :, LANES:2 * LANES] = column[1]
    for t in range(row_tiles):
        for c in range(components):
            mine, mate = sums_ref[t, c], mate_ref[t, c]
            first = jnp.where(is_first, mine, mate)
            second = jnp.where(is_first, mate, mine)
            to_right = second + pair_ref[0, t * SUB:(t + 1) * SUB] * first
            mine, mate = sums_ref[t, components + c], mate_ref[t, components + c]
            first = jnp.where(is_first, mine, mate)
            second = jnp.where(is_first, mate, mine)
            to_left = first + pair_ref[1, t * SUB:(t + 1) * SUB] * second
            for m in range(1, chips):
                goes_right = (chip ^ m) > chip
                send_refs[m - 1][t * components + c] = jnp.where(goes_right, to_right, to_left)


def inner_kernel(cells, index_ref, velocity_ref, left_ref, right_ref, base_ref):
    me = lax.axis_index("gz")
    components = velocity_ref.shape[0]
    heights = [height(index_ref, me * cells + j) for j in range(cells)]
    gathered = [jnp.zeros(left_ref.shape[1:], jnp.float32)] * components
    for j in reversed(range(cells)):
        left = left_ref[j]
        right = heights[j] * right_ref[j]
        for c in range(components):
            base_ref[c, j] = left * gathered[c]
            if j > 0:
                gathered[c] = gathered[c] + right * velocity_ref[c, j]
    gathered = [jnp.zeros(left_ref.shape[1:], jnp.float32)] * components
    for j in range(cells):
        left = heights[j] * left_ref[j]
        right = right_ref[j]
        for c in range(components):
            gathered[c] = gathered[c] + left * velocity_ref[c, j]
            base_ref[c, j] = base_ref[c, j] + right * gathered[c]


def finish_kernel(
    cells, blocks, chips, lines,
    index_ref, target_ref, column_ref, base_ref, left_ref, right_ref,
    mate_ref, pair_ref, chip_ref, ends_ref, *rest,
):
    recv_refs = rest[:chips - 1]
    scalar_refs = rest[chips - 1:2 * (chips - 1)]
    out_ref, alpha_ref = rest[-2:]
    me = lax.axis_index("gz")
    chip = me // 2
    is_first = me == chip * 2
    components = base_ref.shape[0]

    @pl.when(pl.program_id(0) == 0)
    def _():
        extent = lax.fori_loop(
            0, cells * blocks, lambda k, total: total + height(index_ref, k), jnp.float32(0.0)
        )
        flow = column_ref[0]
        weight = column_ref[1]
        for ref in scalar_refs:
            flow = flow + ref[0, :, 0:LANES]
            weight = weight + ref[0, :, LANES:2 * LANES]
        flow = jnp.sum(flow, keepdims=True)
        weight = jnp.sum(weight, keepdims=True)
        alpha = (target_ref[0] * (extent * lines) - flow) / weight
        alpha_ref[...] = jnp.broadcast_to(alpha, alpha_ref.shape)

    alpha = alpha_ref[0:1, 0:1]
    scale = right_ref[cells - 1]
    lefts, rights = [], []
    for c in range(components):
        left_in = jnp.zeros(scale.shape, jnp.float32)
        right_in = jnp.zeros(scale.shape, jnp.float32)
        for m in range(1, chips):
            term = chip_ref[m - 1] * recv_refs[m - 1][c]
            from_left = (chip ^ m) < chip
            left_in = left_in + jnp.where(from_left, term, 0.0)
            right_in = right_in + jnp.where(from_left, 0.0, term)
        near = pair_ref[0]
        left_in = jnp.where(is_first, left_in, mate_ref[0, c] + near * left_in)
        right_in = jnp.where(is_first, mate_ref[0, components + c] + near * right_in, right_in)
        if c == 0:
            left_in = left_in - alpha * ends_ref[0]
            right_in = right_in - alpha * ends_ref[1]
        lefts.append(left_in)
        rights.append(right_in * scale)
    for j in range(cells):
        left = left_ref[j]
        right = right_ref[j]
        for c in range(components):
            value = base_ref[c, j] + (right * lefts[c] + left * rights[c])
            out_ref[c, j] = value + alpha if c == 0 else value


def shards(velocity, diffusion, wall_types, stretch_index, bulk_target):
    blocks = lax.axis_size("gz")
    columns = lax.axis_size("gy")
    components, cells, lines_y, lines_x = velocity.shape
    chips = blocks // 2
    row_tiles = lines_y // SUB
    f32 = jnp.float32
    vmem = pl.BlockSpec(memory_space=pltpu.VMEM)
    smem = pl.BlockSpec(memory_space=pltpu.SMEM)
    plane = (lines_y, lines_x)
    sums, pair, chip_coefs, left, right, ends, tile = pl.pallas_call(
        functools.partial(ladder_kernel, cells, blocks, chips),
        out_shape=[
            jax.ShapeDtypeStruct((row_tiles, 2 * components, SUB, lines_x), f32),
            jax.ShapeDtypeStruct((3,) + plane, f32),
            jax.ShapeDtypeStruct((chips - 1,) + plane, f32),
            jax.ShapeDtypeStruct((cells,) + plane, f32),
            jax.ShapeDtypeStruct((cells,) + plane, f32),
            jax.ShapeDtypeStruct((2,) + plane, f32),
            jax.ShapeDtypeStruct((2, SUB, LANES), f32),
        ],
        in_specs=[smem, vmem, vmem, pl.BlockSpec(memory_space=pl.ANY)],
        out_specs=[vmem] * 7,
        scratch_shapes=[
            pltpu.VMEM(velocity.shape, f32),
            pltpu.VMEM((blocks,) + plane, f32),
            pltpu.VMEM(plane, f32),
            pltpu.SemaphoreType.DMA((components,)),
        ],
        compiler_params=pltpu.CompilerParams(vmem_limit_bytes=24 * MIB),
        cost_estimate=pl.CostEstimate(flops=40_000_000, bytes_accessed=6_000_000, transcendentals=0),
        name="ladder",
    )(stretch_index, diffusion, wall_types, velocity)

    def route(partner):
        return [
            (z * columns + y, partner(z, y)[0] * columns + partner(z, y)[1])
            for z in range(blocks)
            for y in range(columns)
        ]

    def send(array, partner):
        return lax.ppermute(array, ("gz", "gy"), route(partner))

    mate = send(sums, lambda z, y: (z ^ 1, y))
    tiles = [tile] + [
        send(tile, lambda z, y: (z ^ flip, (y + shift) % columns))
        for flip in range(2)
        for shift in range(columns)
        if (flip, shift) != (0, 0)
    ]
    outgoing = pl.pallas_call(
        functools.partial(merge_kernel, chips, components, len(tiles)),
        out_shape=[
            jax.ShapeDtypeStruct((components * row_tiles + 1, SUB, lines_x), f32)
            for _ in range(chips - 1)
        ] + [jax.ShapeDtypeStruct((2, SUB, LANES), f32)],
        in_specs=[vmem] * (3 + len(tiles)),
        out_specs=[vmem] * chips,
        compiler_params=pltpu.CompilerParams(vmem_limit_bytes=16 * MIB),
        cost_estimate=pl.CostEstimate(flops=500_000, bytes_accessed=1_600_000, transcendentals=0),
        name="merge",
    )(sums, mate, pair, *tiles)
    column = outgoing[-1]
    incoming = [
        send(outgoing[m - 1], lambda z, y: (z ^ (2 * m), y)) for m in range(1, chips)
    ]

    state = pl.BlockSpec((components, cells, SUB, lines_x), lambda t: (0, 0, t, 0))
    profile = pl.BlockSpec((cells, SUB, lines_x), lambda t: (0, t, 0))
    base = pl.pallas_call(
        functools.partial(inner_kernel, cells),
        grid=(row_tiles,),
        out_shape=jax.ShapeDtypeStruct(velocity.shape, f32),
        in_specs=[smem, state, profile, profile],
        out_specs=state,
        compiler_params=pltpu.CompilerParams(vmem_limit_bytes=16 * MIB),
        cost_estimate=pl.CostEstimate(flops=8_000_000, bytes_accessed=8_000_000, transcendentals=0),
        name="inner",
    )(stretch_index, velocity, left, right)
    one = pl.BlockSpec((1, SUB, lines_x), lambda t: (2, t, 0))
    received = pl.BlockSpec((components, SUB, lines_x), lambda t: (t, 0, 0))
    scalars = pl.BlockSpec((1, SUB, lines_x), lambda t: (components * row_tiles, 0, 0))
    return pl.pallas_call(
        functools.partial(finish_kernel, cells, blocks, chips, float(lines_y * columns * lines_x)),
        grid=(row_tiles,),
        out_shape=jax.ShapeDtypeStruct(velocity.shape, f32),
        in_specs=[
            smem,
            smem,
            vmem,
            state,
            profile,
            profile,
            pl.BlockSpec((1, 2 * components, SUB, lines_x), lambda t: (t, 0, 0, 0)),
            one,
            pl.BlockSpec((chips - 1, SUB, lines_x), lambda t: (0, t, 0)),
            pl.BlockSpec((2, SUB, lines_x), lambda t: (0, t, 0)),
        ] + [received] * (chips - 1) + [scalars] * (chips - 1),
        out_specs=state,
        scratch_shapes=[pltpu.VMEM((SUB, LANES), f32)],
        compiler_params=pltpu.CompilerParams(vmem_limit_bytes=16 * MIB),
        cost_estimate=pl.CostEstimate(flops=4_000_000, bytes_accessed=9_000_000, transcendentals=0),
        name="finish",
    )(stretch_index, bulk_target, column, base, left, right, mate, pair, chip_coefs, ends,
      *incoming, *incoming)


def solution(mesh):
    return jax.shard_map(
        shards,
        mesh=mesh,
        in_specs=(P(None, "gz", "gy", None), P("gy", None), P("gy", None), P(), P()),
        out_specs=P(None, "gz", "gy", None),
        check_vma=False,
    )
```

```python
import functools

import jax
import jax.numpy as jnp
from jax import lax
from jax.experimental import pallas as pl
from jax.experimental.pallas import tpu as pltpu
from jax.sharding import PartitionSpec as P

SUB = 8
LANES = 128
MIB = 1024 * 1024


def row_tile(t):
    return pl.ds(pl.multiple_of(t * SUB, SUB), SUB)


def height(index_ref, k):
    return 0.5 + 0.25 * index_ref[k].astype(jnp.float32)


def half_sum(index_ref, k):
    return 0.5 * (height(index_ref, k) + height(index_ref, k + 1))


def ladder_kernel(
    cells, blocks, chips,
    index_hbm, diffusion_hbm, walls_hbm, velocity_hbm,
    mine_ref, away_ref, pair_ref, chip_ref, left_ref, right_ref, ends_ref,
    index_ref, diffusion_ref, walls_ref, velocity_ref, through_ref, inverse_ref, scale_ref, sems,
):
    total = cells * blocks
    components = velocity_ref.shape[0]
    small = [
        pltpu.make_async_copy(index_hbm, index_ref, sems.at[0]),
        pltpu.make_async_copy(diffusion_hbm, diffusion_ref, sems.at[1]),
        pltpu.make_async_copy(walls_hbm, walls_ref, sems.at[2]),
    ]
    large = [
        pltpu.make_async_copy(velocity_hbm.at[c], velocity_ref.at[c], sems.at[3 + c])
        for c in range(components)
    ]
    for copy in small + large:
        copy.start()
    me = lax.axis_index("gz")
    chip = me // 2
    first = chip * 2
    for copy in small:
        copy.wait()
    diffusion = diffusion_ref[...]
    inverse_ref[...] = 1.0 / diffusion
    walls = walls_ref[...]
    lower = diffusion * (walls % 2).astype(jnp.float32) * 2.0 / height(index_ref, 0)
    upper = diffusion * (walls // 2).astype(jnp.float32) * 2.0 / height(index_ref, total - 1)

    def forward(block, kappa, keep=None):
        start = block * cells
        inverse = inverse_ref[...]
        flux = height(index_ref, start) + kappa
        value = jnp.ones_like(flux)
        for j in range(cells):
            if keep is not None:
                keep(j, flux, value)
            k = start + j
            if j < cells - 1:
                value = value + (half_sum(index_ref, k) * inverse) * flux
                flux = flux + height(index_ref, k + 1) * value
        k = jnp.minimum(start + cells - 1, total - 2)
        after = 1.0 / (value + (half_sum(index_ref, k) * inverse) * flux)
        return flux * after, after

    def backward(block, kappa, scale=None, keep=None):
        start = block * cells
        inverse = inverse_ref[...]
        flux = height(index_ref, start + cells - 1) + kappa
        value = jnp.ones_like(flux)
        if scale is not None:
            flux, value = flux * scale, scale
        for j in reversed(range(cells)):
            if keep is not None:
                keep(j, flux, value)
            k = start + j
            if j > 0:
                value = value + (half_sum(index_ref, k - 1) * inverse) * flux
                flux = flux + height(index_ref, k - 1) * value
        k = jnp.maximum(start - 1, 0)
        after = 1.0 / (value + (half_sum(index_ref, k) * inverse) * flux)
        return flux * after, after

    def sweep_forward(block, state):
        kappa, product = state
        kappa, after = forward(block, kappa)
        through_ref[block] = after
        return kappa, product * after

    def sweep_backward(step, state):
        block = blocks - 1 - step
        kappa, product = state
        kappa, after = backward(block, kappa)
        through_ref[block] = after
        return kappa, product * after

    ones = jnp.ones_like(diffusion)
    kappa_left, product_left = lax.fori_loop(0, me, sweep_forward, (lower, ones))
    ends_ref[0] = lower * product_left
    state = {}

    def keep_left(j, flux, value):
        left_ref[j] = value
        state["flux"], state["value"] = flux, value

    kappa, own_forward = forward(me, kappa_left, keep_left)

    @pl.when(me == first)
    def _():
        pair_ref[2] = own_forward
        _, after = forward(me + 1, kappa)
        pair_ref[0] = after

    @pl.when(me != first)
    def _():
        pair_ref[2] = through_ref[first]
        pair_ref[0] = own_forward

    kappa_right, product_right = lax.fori_loop(
        0, blocks - 1 - me, sweep_backward, (upper, ones)
    )
    ends_ref[1] = upper * product_right
    scale = 1.0 / (state["flux"] + kappa_right * state["value"])
    scale_ref[0] = scale

    def keep_right(j, flux, value):
        right_ref[j] = value

    kappa, own_backward = backward(me, kappa_right, scale, keep_right)
    scale_ref[1] = own_forward
    scale_ref[2] = own_backward

    @pl.when(me == first)
    def _():
        pair_ref[1] = own_backward * scale
        pair_ref[3] = through_ref[first + 1]

    @pl.when(me != first)
    def _():
        pair_ref[3] = own_backward * scale
        _, after = backward(me - 1, kappa)
        pair_ref[1] = after

    for m in range(1, chips):
        other = chip ^ m
        low = jnp.minimum(chip, other)
        high = jnp.maximum(chip, other)
        chip_ref[m - 1] = lax.fori_loop(
            low + 1,
            high,
            lambda r, product: product * (through_ref[2 * r] * through_ref[2 * r + 1]),
            ones,
        )
    for copy in large:
        copy.wait()
    flow = jnp.zeros((SUB, LANES), jnp.float32)
    weight = jnp.zeros((SUB, LANES), jnp.float32)

    def fold(array):
        parts = [array[:, i * LANES:(i + 1) * LANES] for i in range(array.shape[1] // LANES)]
        return functools.reduce(jnp.add, parts)

    half = diffusion.shape[0] // SUB // 2
    heights = [height(index_ref, me * cells + j) for j in range(cells)]
    for ref, whose in ((away_ref, 1 - (me - first)), (mine_ref, me - first)):
        for i in range(half):
            rows = row_tile(whose * half + i)
            from_left = [0.0] * components
            from_right = [0.0] * components
            plain = 0.0
            left_total = 0.0
            right_total = 0.0
            extent = 0.0
            for j in range(cells):
                h = heights[j]
                left = h * left_ref[j, rows]
                right = h * right_ref[j, rows]
                extent = extent + h
                left_total = left_total + left
                right_total = right_total + right
                for c in range(components):
                    v = velocity_ref[c, j, rows]
                    from_left[c] = from_left[c] + left * v
                    from_right[c] = from_right[c] + right * v
                    if c == 0:
                        plain = plain + h * v
            low_part = ends_ref[0, rows]
            high_part = ends_ref[1, rows] * scale_ref[0, rows]
            for c in range(components):
                ref[i * 2 * components + c] = from_left[c] * scale_ref[1, rows]
                ref[i * 2 * components + components + c] = from_right[c] * scale_ref[2, rows]
            flow = flow + fold(plain - low_part * from_right[0] - high_part * from_left[0])
            weight = weight + fold(extent - low_part * right_total - high_part * left_total)
    away_ref[half * 2 * components] = jnp.zeros(away_ref.shape[1:], jnp.float32)
    away_ref[half * 2 * components, :, 0:LANES] = flow
    away_ref[half * 2 * components, :, LANES:2 * LANES] = weight


def merge_kernel(chips, components, mine_ref, away_ref, mate_ref, pair_ref, _, *rest):
    send_refs, tile_ref = rest[:-1], rest[-1]
    me = lax.axis_index("gz")
    chip = me // 2
    is_first = me == chip * 2
    half = mine_ref.shape[0] // (2 * components)
    slot = half * 2 * components
    for i in range(2):
        lanes = slice(i * LANES, (i + 1) * LANES)
        tile_ref[i] = away_ref[slot, :, lanes] + mate_ref[slot, :, lanes]
    for i in range(half):
        rows = row_tile((me - chip * 2) * half + i)
        for c in range(components):
            at = i * 2 * components + c
            mine, mate = mine_ref[at], mate_ref[at]
            first = jnp.where(is_first, mine, mate)
            second = jnp.where(is_first, mate, mine)
            to_right = second + pair_ref[0, rows] * first
            at = at + components
            mine, mate = mine_ref[at], mate_ref[at]
            first = jnp.where(is_first, mine, mate)
            second = jnp.where(is_first, mate, mine)
            to_left = first + pair_ref[1, rows] * second
            for m in range(1, chips):
                goes_right = (chip ^ m) > chip
                send_refs[m - 1][i * components + c] = jnp.where(goes_right, to_right, to_left)


def spread_kernel(chips, components, mine_ref, mate_ref, pair_ref, chip_ref, _, *rest):
    recv_refs, (own_ref, other_ref) = rest[:chips - 1], rest[chips - 1:]
    me = lax.axis_index("gz")
    chip = me // 2
    is_first = me == chip * 2
    half = mine_ref.shape[0] // (2 * components)
    for i in range(half):
        rows = row_tile((me - chip * 2) * half + i)
        coefs = [chip_ref[m, rows] for m in range(chips - 1)]
        for c in range(components):
            left_in = jnp.zeros(mine_ref.shape[1:], jnp.float32)
            right_in = jnp.zeros(mine_ref.shape[1:], jnp.float32)
            for m in range(1, chips):
                term = coefs[m - 1] * recv_refs[m - 1][i * components + c]
                from_left = (chip ^ m) < chip
                left_in = left_in + jnp.where(from_left, term, 0.0)
                right_in = right_in + jnp.where(from_left, 0.0, term)
            at = i * 2 * components + c
            first_out = jnp.where(is_first, mine_ref[at], mate_ref[at])
            left_second = first_out + pair_ref[2, rows] * left_in
            at = at + components
            second_out = jnp.where(is_first, mate_ref[at], mine_ref[at])
            right_first = second_out + pair_ref[3, rows] * right_in
            at = i * 2 * components + c
            own_ref[at] = jnp.where(is_first, left_in, left_second)
            other_ref[at] = jnp.where(is_first, left_second, left_in)
            at = at + components
            own_ref[at] = jnp.where(is_first, right_first, right_in)
            other_ref[at] = jnp.where(is_first, right_in, right_first)


def add_kernel(*refs):
    refs[-1][...] = functools.reduce(jnp.add, [ref[...] for ref in refs[:-1]])


def inner_kernel(cells, index_ref, velocity_ref, left_ref, right_ref, base_ref):
    me = lax.axis_index("gz")
    components = velocity_ref.shape[0]
    heights = [height(index_ref, me * cells + j) for j in range(cells)]
    gathered = [jnp.zeros(left_ref.shape[1:], jnp.float32)] * components
    for j in reversed(range(cells)):
        left = left_ref[j]
        right = heights[j] * right_ref[j]
        for c in range(components):
            base_ref[c, j] = left * gathered[c]
            if j > 0:
                gathered[c] = gathered[c] + right * velocity_ref[c, j]
    gathered = [jnp.zeros(left_ref.shape[1:], jnp.float32)] * components
    for j in range(cells):
        left = heights[j] * left_ref[j]
        right = right_ref[j]
        for c in range(components):
            gathered[c] = gathered[c] + left * velocity_ref[c, j]
            base_ref[c, j] = base_ref[c, j] + right * gathered[c]


def emit(parts, rows, alpha, ends_ref, incoming_ref, at, base_ref, left_ref, right_ref, result_ref):
    cells = left_ref.shape[0]
    components = base_ref.shape[0]
    scale = right_ref[cells - 1, rows]
    lefts, rights = {}, {}
    for c in parts:
        left_in = incoming_ref[at + c]
        right_in = incoming_ref[at + components + c]
        if c == 0:
            left_in = left_in - alpha * ends_ref[0, rows]
            right_in = right_in - alpha * ends_ref[1, rows]
        lefts[c] = left_in
        rights[c] = right_in * scale
    for j in range(cells):
        left = left_ref[j, rows]
        right = right_ref[j, rows]
        for c in parts:
            value = base_ref[c, j, rows] + (right * lefts[c] + left * rights[c])
            result_ref[c, j, rows] = value + alpha if c == 0 else value


def early_kernel(own_ref, base_ref, left_ref, right_ref, out_hbm, result_ref, sems):
    components = base_ref.shape[0]
    half = own_ref.shape[0] // (2 * components)
    me = lax.axis_index("gz")
    copies = []
    for i in range(half):
        rows = row_tile(lax.rem(me, 2) * half + i)
        emit(range(1, components), rows, None, None, own_ref, i * 2 * components,
             base_ref, left_ref, right_ref, result_ref)
        for c in range(1, components):
            copies.append(pltpu.make_async_copy(
                result_ref.at[c, :, rows], out_hbm.at[c, :, rows], sems.at[len(copies)]))
            copies[-1].start()
    for copy in copies:
        copy.wait()


def late_kernel(
    lines, index_ref, target_ref, ends_ref, own_ref, other_ref, base_ref, left_ref, right_ref,
    *rest,
):
    tile_refs, (_, out_hbm, result_ref, sems) = rest[:-4], rest[-4:]
    components = base_ref.shape[0]
    half = own_ref.shape[0] // (2 * components)
    me = lax.axis_index("gz")
    copies = []

    def leave(c, rows):
        copies.append(pltpu.make_async_copy(
            result_ref.at[c, :, rows], out_hbm.at[c, :, rows], sems.at[len(copies)]))
        copies[-1].start()

    for i in range(half):
        rows = row_tile((1 - lax.rem(me, 2)) * half + i)
        emit(range(1, components), rows, None, None, other_ref, i * 2 * components,
             base_ref, left_ref, right_ref, result_ref)
        for c in range(1, components):
            leave(c, rows)
    extent = 0.0
    for k in range(index_ref.shape[0]):
        extent = extent + height(index_ref, k)
    totals = functools.reduce(jnp.add, [ref[...] for ref in tile_refs])
    flow = jnp.sum(totals[0], keepdims=True)
    weight = jnp.sum(totals[1], keepdims=True)
    alpha = (target_ref[0] * (extent * lines) - flow) / weight
    for ref, whose in ((own_ref, lax.rem(me, 2)), (other_ref, 1 - lax.rem(me, 2))):
        for i in range(half):
            rows = row_tile(whose * half + i)
            emit((0,), rows, alpha, ends_ref, ref, i * 2 * components,
                 base_ref, left_ref, right_ref, result_ref)
            leave(0, rows)
    for copy in copies:
        copy.wait()


def shards(velocity, diffusion, wall_types, stretch_index, bulk_target):
    blocks = lax.axis_size("gz")
    columns = lax.axis_size("gy")
    components, cells, lines_y, lines_x = velocity.shape
    chips = blocks // 2
    row_tiles = lines_y // SUB
    half = row_tiles // 2
    f32 = jnp.float32
    vmem = pl.BlockSpec(memory_space=pltpu.VMEM)
    smem = pl.BlockSpec(memory_space=pltpu.SMEM)
    anywhere = pl.BlockSpec(memory_space=pl.ANY)
    plane = (lines_y, lines_x)
    sheet = (SUB, lines_x)
    tile = jax.ShapeDtypeStruct((2, SUB, LANES), f32)

    def shape(*dims):
        return jax.ShapeDtypeStruct(dims, f32)

    def in_hbm(array):
        return pltpu.with_memory_space_constraint(array, pltpu.HBM)

    def options(mib):
        return pltpu.CompilerParams(vmem_limit_bytes=mib * MIB)

    def cost(flops, transferred):
        return pl.CostEstimate(flops=flops, bytes_accessed=transferred, transcendentals=0)

    mine, away, pair, chip_coefs, left, right, ends = pl.pallas_call(
        functools.partial(ladder_kernel, cells, blocks, chips),
        out_shape=[
            shape(half * 2 * components, *sheet),
            shape(half * 2 * components + 1, *sheet),
            shape(4, *plane),
            shape(chips - 1, *plane),
            shape(cells, *plane),
            shape(cells, *plane),
            shape(2, *plane),
        ],
        in_specs=[anywhere] * 4,
        out_specs=[vmem] * 7,
        scratch_shapes=[
            pltpu.SMEM(stretch_index.shape, jnp.int32),
            pltpu.VMEM(plane, f32),
            pltpu.VMEM(plane, jnp.int32),
            pltpu.VMEM(velocity.shape, f32),
            pltpu.VMEM((blocks,) + plane, f32),
            pltpu.VMEM(plane, f32),
            pltpu.VMEM((3,) + plane, f32),
            pltpu.SemaphoreType.DMA((3 + components,)),
        ],
        compiler_params=options(24),
        cost_estimate=cost(40_000_000, 6_000_000),
        name="ladder",
    )(in_hbm(stretch_index), in_hbm(diffusion), in_hbm(wall_types), in_hbm(velocity))

    def send(array, partner):
        pairs = [((z, y), partner(z, y)) for z in range(blocks) for y in range(columns)]
        route = [(a * columns + b, c * columns + d) for (a, b), (c, d) in pairs]
        return lax.ppermute(array, ("gz", "gy"), route)

    def to_mate(array):
        return send(array, lambda z, y: (z ^ 1, y))

    def to_chips(array):
        return [send(array, lambda z, y: (z ^ (2 * m), y)) for m in range(1, chips)]

    mate = to_mate(away)
    state = pl.BlockSpec((components, cells, SUB, lines_x), lambda t: (0, 0, t, 0))
    profile = pl.BlockSpec((cells, SUB, lines_x), lambda t: (0, t, 0))
    base = pl.pallas_call(
        functools.partial(inner_kernel, cells),
        grid=(row_tiles,),
        out_shape=shape(*velocity.shape),
        in_specs=[smem, state, profile, profile],
        out_specs=state,
        compiler_params=options(16),
        cost_estimate=cost(8_000_000, 8_000_000),
        name="inner",
    )(stretch_index, in_hbm(velocity), left, right)
    *outgoing, chip_tile = pl.pallas_call(
        functools.partial(merge_kernel, chips, components),
        out_shape=[shape(half * components, *sheet)] * (chips - 1) + [tile],
        in_specs=[vmem] * 4 + [anywhere],
        out_specs=[vmem] * chips,
        compiler_params=options(16),
        cost_estimate=cost(500_000, 1_600_000),
        name="merge",
    )(mine, away, mate, pair, base)
    incoming = [
        send(outgoing[m - 1], lambda z, y: (z ^ (2 * m), y)) for m in range(1, chips)
    ]
    tiles = [chip_tile] + [
        send(chip_tile, lambda z, y: (z, (y + shift) % columns)) for shift in range(1, columns)
    ]
    column_tile = pl.pallas_call(
        add_kernel,
        out_shape=tile,
        in_specs=[vmem] * len(tiles),
        out_specs=vmem,
        compiler_params=options(16),
        cost_estimate=cost(10_000, 40_000),
        name="column_sum",
    )(*tiles)

    own_in, other_out = pl.pallas_call(
        functools.partial(spread_kernel, chips, components),
        out_shape=[shape(half * 2 * components, *sheet)] * 2,
        in_specs=[vmem] * 4 + [anywhere] + [vmem] * (chips - 1),
        out_specs=[vmem] * 2,
        compiler_params=options(16),
        cost_estimate=cost(500_000, 1_600_000),
        name="spread",
    )(mine, mate, pair, chip_coefs, column_tile, *incoming)
    other_in = to_mate(other_out)
    plane_tiles = [column_tile] + to_chips(column_tile)
    early = pl.pallas_call(
        early_kernel,
        out_shape=shape(*velocity.shape),
        in_specs=[vmem] * 4,
        out_specs=anywhere,
        scratch_shapes=[
            pltpu.VMEM(velocity.shape, f32),
            pltpu.SemaphoreType.DMA(((components - 1) * half,)),
        ],
        compiler_params=options(16),
        cost_estimate=cost(2_000_000, 4_000_000),
        name="early",
    )(own_in, base, left, right)
    return pl.pallas_call(
        functools.partial(late_kernel, float(lines_y * columns * lines_x)),
        out_shape=shape(*velocity.shape),
        in_specs=[smem, smem] + [vmem] * (6 + chips) + [anywhere],
        out_specs=anywhere,
        scratch_shapes=[
            pltpu.VMEM(velocity.shape, f32),
            pltpu.SemaphoreType.DMA(((components + 1) * half,)),
        ],
        input_output_aliases={8 + chips: 0},
        compiler_params=options(16),
        cost_estimate=cost(3_000_000, 6_000_000),
        name="late",
    )(stretch_index, bulk_target, ends, own_in, other_in, base, left, right, *plane_tiles, early)


def solution(mesh):
    return jax.shard_map(
        shards,
        mesh=mesh,
        in_specs=(P(None, "gz", "gy", None), P("gy", None), P("gy", None), P(), P()),
        out_specs=P(None, "gz", "gy", None),
        check_vma=False,
    )
```

```python
import functools

import jax
import jax.numpy as jnp
from jax import lax
from jax.experimental import pallas as pl
from jax.experimental.pallas import tpu as pltpu
from jax.sharding import PartitionSpec as P

SUB = 8
LANES = 128
MIB = 1024 * 1024


def row_tile(t):
    return pl.ds(pl.multiple_of(t * SUB, SUB), SUB)


def height(index_ref, k):
    return 0.5 + 0.25 * index_ref[k].astype(jnp.float32)


def half_sum(index_ref, k):
    return 0.5 * (height(index_ref, k) + height(index_ref, k + 1))


def ladder_kernel(
    cells, blocks, chips,
    index_hbm, diffusion_hbm, walls_hbm, velocity_hbm,
    mine_ref, away_ref, pair_ref, chip_ref, left_ref, right_ref, ends_ref, tile_ref,
    index_ref, diffusion_ref, walls_ref, velocity_ref, through_ref, inverse_ref, scale_ref, sems,
):
    total = cells * blocks
    components = velocity_ref.shape[0]
    small = [
        pltpu.make_async_copy(index_hbm, index_ref, sems.at[0]),
        pltpu.make_async_copy(diffusion_hbm, diffusion_ref, sems.at[1]),
        pltpu.make_async_copy(walls_hbm, walls_ref, sems.at[2]),
    ]
    large = [
        pltpu.make_async_copy(velocity_hbm.at[c], velocity_ref.at[c], sems.at[3 + c])
        for c in range(components)
    ]
    for copy in small + large:
        copy.start()
    me = lax.axis_index("gz")
    chip = me // 2
    first = chip * 2
    for copy in small:
        copy.wait()
    diffusion = diffusion_ref[...]
    inverse_ref[...] = 1.0 / diffusion
    walls = walls_ref[...]
    lower = diffusion * (walls & 1).astype(jnp.float32) * 2.0 / height(index_ref, 0)
    upper = diffusion * (walls >> 1).astype(jnp.float32) * 2.0 / height(index_ref, total - 1)

    def forward(block, kappa, keep=None):
        start = block * cells
        inverse = inverse_ref[...]
        flux = height(index_ref, start) + kappa
        value = jnp.ones_like(flux)
        for j in range(cells):
            if keep is not None:
                keep(j, flux, value)
            k = start + j
            if j < cells - 1:
                value = value + (half_sum(index_ref, k) * inverse) * flux
                flux = flux + height(index_ref, k + 1) * value
        k = jnp.minimum(start + cells - 1, total - 2)
        after = 1.0 / (value + (half_sum(index_ref, k) * inverse) * flux)
        return flux * after, after

    def backward(block, kappa, scale=None, keep=None):
        start = block * cells
        inverse = inverse_ref[...]
        flux = height(index_ref, start + cells - 1) + kappa
        value = jnp.ones_like(flux)
        if scale is not None:
            flux, value = flux * scale, scale
        for j in reversed(range(cells)):
            if keep is not None:
                keep(j, flux, value)
            k = start + j
            if j > 0:
                value = value + (half_sum(index_ref, k - 1) * inverse) * flux
                flux = flux + height(index_ref, k - 1) * value
        k = jnp.maximum(start - 1, 0)
        after = 1.0 / (value + (half_sum(index_ref, k) * inverse) * flux)
        return flux * after, after

    def sweep_forward(block, state):
        kappa, product = state
        kappa, after = forward(block, kappa)
        through_ref[block] = after
        return kappa, product * after

    def sweep_backward(step, state):
        block = blocks - 1 - step
        kappa, product = state
        kappa, after = backward(block, kappa)
        through_ref[block] = after
        return kappa, product * after

    ones = jnp.ones_like(diffusion)
    kappa_left, product_left = lax.fori_loop(0, me, sweep_forward, (lower, ones))
    ends_ref[0] = lower * product_left
    state = {}

    def keep_left(j, flux, value):
        left_ref[j] = value
        state["flux"], state["value"] = flux, value

    kappa, own_forward = forward(me, kappa_left, keep_left)

    @pl.when(me == first)
    def _():
        pair_ref[2] = own_forward
        _, after = forward(me + 1, kappa)
        pair_ref[0] = after

    @pl.when(me != first)
    def _():
        pair_ref[2] = through_ref[first]
        pair_ref[0] = own_forward

    kappa_right, product_right = lax.fori_loop(
        0, blocks - 1 - me, sweep_backward, (upper, ones)
    )
    ends_ref[1] = upper * product_right
    scale = 1.0 / (state["flux"] + kappa_right * state["value"])
    scale_ref[0] = scale

    def keep_right(j, flux, value):
        right_ref[j] = value

    kappa, own_backward = backward(me, kappa_right, scale, keep_right)
    scale_ref[1] = own_forward
    scale_ref[2] = own_backward

    @pl.when(me == first)
    def _():
        pair_ref[1] = own_backward * scale
        pair_ref[3] = through_ref[first + 1]

    @pl.when(me != first)
    def _():
        pair_ref[3] = own_backward * scale
        _, after = backward(me - 1, kappa)
        pair_ref[1] = after

    for m in range(1, chips):
        other = chip ^ m
        low = jnp.minimum(chip, other)
        high = jnp.maximum(chip, other)
        chip_ref[m - 1] = lax.fori_loop(
            low + 1,
            high,
            lambda r, product: product * (through_ref[2 * r] * through_ref[2 * r + 1]),
            ones,
        )
    for copy in large:
        copy.wait()
    flow = [jnp.zeros((SUB, LANES), jnp.float32)] * 2
    weight = [jnp.zeros((SUB, LANES), jnp.float32)] * 2

    def fold(sums, array):
        for i in range(array.shape[1] // LANES):
            sums[i % 2] = sums[i % 2] + array[:, i * LANES:(i + 1) * LANES]

    half = diffusion.shape[0] // SUB // 2
    heights = [height(index_ref, me * cells + j) for j in range(cells)]
    for ref, whose in ((away_ref, 1 - (me - first)), (mine_ref, me - first)):
        for i in range(half):
            rows = row_tile(whose * half + i)
            from_left = [0.0] * components
            from_right = [0.0] * components
            plain = 0.0
            left_total = 0.0
            right_total = 0.0
            extent = 0.0
            for j in range(cells):
                h = heights[j]
                left = h * left_ref[j, rows]
                right = h * right_ref[j, rows]
                extent = extent + h
                left_total = left_total + left
                right_total = right_total + right
                for c in range(components):
                    v = velocity_ref[c, j, rows]
                    from_left[c] = from_left[c] + left * v
                    from_right[c] = from_right[c] + right * v
                    if c == 0:
                        plain = plain + h * v
            low_part = ends_ref[0, rows]
            high_part = ends_ref[1, rows] * scale_ref[0, rows]
            for c in range(components):
                ref[i * 2 * components + c] = from_left[c] * scale_ref[1, rows]
                ref[i * 2 * components + components + c] = from_right[c] * scale_ref[2, rows]
            fold(flow, plain - low_part * from_right[0] - high_part * from_left[0])
            fold(weight, extent - low_part * right_total - high_part * left_total)
    for i, part in enumerate(flow + weight):
        tile_ref[i * SUB:(i + 1) * SUB] = part


def merge_kernel(chips, components, mine_ref, mate_ref, pair_ref, *send_refs):
    me = lax.axis_index("gz")
    chip = me // 2
    is_first = me == chip * 2
    half = mine_ref.shape[0] // (2 * components)
    for i in range(half):
        rows = row_tile((me - chip * 2) * half + i)
        for c in range(components):
            at = i * 2 * components + c
            mine, mate = mine_ref[at], mate_ref[at]
            first = jnp.where(is_first, mine, mate)
            second = jnp.where(is_first, mate, mine)
            to_right = second + pair_ref[0, rows] * first
            at = at + components
            mine, mate = mine_ref[at], mate_ref[at]
            first = jnp.where(is_first, mine, mate)
            second = jnp.where(is_first, mate, mine)
            to_left = first + pair_ref[1, rows] * second
            for m in range(1, chips):
                goes_right = (chip ^ m) > chip
                send_refs[m - 1][i * components + c] = jnp.where(goes_right, to_right, to_left)


def spread_kernel(chips, components, mine_ref, mate_ref, pair_ref, chip_ref, _, *rest):
    recv_refs, (own_ref, other_ref) = rest[:chips - 1], rest[chips - 1:]
    me = lax.axis_index("gz")
    chip = me // 2
    is_first = me == chip * 2
    half = mine_ref.shape[0] // (2 * components)
    for i in range(half):
        rows = row_tile((me - chip * 2) * half + i)
        coefs = [chip_ref[m, rows] for m in range(chips - 1)]
        for c in range(components):
            left_in = jnp.zeros(mine_ref.shape[1:], jnp.float32)
            right_in = jnp.zeros(mine_ref.shape[1:], jnp.float32)
            for m in range(1, chips):
                term = coefs[m - 1] * recv_refs[m - 1][i * components + c]
                from_left = (chip ^ m) < chip
                left_in = left_in + jnp.where(from_left, term, 0.0)
                right_in = right_in + jnp.where(from_left, 0.0, term)
            at = i * 2 * components + c
            first_out = jnp.where(is_first, mine_ref[at], mate_ref[at])
            left_second = first_out + pair_ref[2, rows] * left_in
            at = at + components
            second_out = jnp.where(is_first, mate_ref[at], mine_ref[at])
            right_first = second_out + pair_ref[3, rows] * right_in
            at = i * 2 * components + c
            own_ref[at] = jnp.where(is_first, left_in, left_second)
            other_ref[at] = jnp.where(is_first, left_second, left_in)
            at = at + components
            own_ref[at] = jnp.where(is_first, right_first, right_in)
            other_ref[at] = jnp.where(is_first, right_in, right_first)


def inner_kernel(cells, index_ref, velocity_ref, left_ref, right_ref, _, base_ref):
    me = lax.axis_index("gz")
    components = velocity_ref.shape[0]
    heights = [height(index_ref, me * cells + j) for j in range(cells)]
    gathered = [jnp.zeros(left_ref.shape[1:], jnp.float32)] * components
    for j in reversed(range(cells)):
        left = left_ref[j]
        right = heights[j] * right_ref[j]
        for c in range(components):
            base_ref[c, j] = left * gathered[c]
            if j > 0:
                gathered[c] = gathered[c] + right * velocity_ref[c, j]
    gathered = [jnp.zeros(left_ref.shape[1:], jnp.float32)] * components
    for j in range(cells):
        left = heights[j] * left_ref[j]
        right = right_ref[j]
        for c in range(components):
            gathered[c] = gathered[c] + left * velocity_ref[c, j]
            base_ref[c, j] = base_ref[c, j] + right * gathered[c]


def emit(parts, rows, alpha, ends_ref, incoming_ref, at, base_ref, left_ref, right_ref, result_ref):
    cells = left_ref.shape[0]
    components = base_ref.shape[0]
    scale = right_ref[cells - 1, rows]
    lefts, rights = {}, {}
    for c in parts:
        left_in = incoming_ref[at + c]
        right_in = incoming_ref[at + components + c]
        if c == 0:
            left_in = left_in - alpha * ends_ref[0, rows]
            right_in = right_in - alpha * ends_ref[1, rows]
        lefts[c] = left_in
        rights[c] = right_in * scale
    for j in range(cells):
        left = left_ref[j, rows]
        right = right_ref[j, rows]
        for c in parts:
            value = base_ref[c, j, rows] + (right * lefts[c] + left * rights[c])
            result_ref[c, j, rows] = value + alpha if c == 0 else value


def early_kernel(own_ref, base_ref, left_ref, right_ref, out_hbm, result_ref, sems):
    components = base_ref.shape[0]
    half = own_ref.shape[0] // (2 * components)
    me = lax.axis_index("gz")
    copies = []
    for i in range(half):
        rows = row_tile(lax.rem(me, 2) * half + i)
        emit(range(1, components), rows, None, None, own_ref, i * 2 * components,
             base_ref, left_ref, right_ref, result_ref)
        for c in range(1, components):
            copies.append(pltpu.make_async_copy(
                result_ref.at[c, :, rows], out_hbm.at[c, :, rows], sems.at[len(copies)]))
            copies[-1].start()
    for copy in copies:
        copy.wait()


def late_kernel(
    lines, index_ref, target_ref, ends_ref, own_ref, other_ref, base_ref, left_ref, right_ref,
    *rest,
):
    tiles_hbm, _, out_hbm, result_ref, tiles_ref, sems = rest
    components = base_ref.shape[0]
    half = own_ref.shape[0] // (2 * components)
    me = lax.axis_index("gz")
    arrival = pltpu.make_async_copy(tiles_hbm, tiles_ref, sems.at[sems.shape[0] - 1])
    arrival.start()
    copies = []

    def leave(c, rows):
        copies.append(pltpu.make_async_copy(
            result_ref.at[c, :, rows], out_hbm.at[c, :, rows], sems.at[len(copies)]))
        copies[-1].start()

    for i in range(half):
        rows = row_tile((1 - lax.rem(me, 2)) * half + i)
        emit(range(1, components), rows, None, None, other_ref, i * 2 * components,
             base_ref, left_ref, right_ref, result_ref)
        for c in range(1, components):
            leave(c, rows)
    extent = 0.0
    for k in range(index_ref.shape[0]):
        extent = extent + height(index_ref, k)
    arrival.wait()
    tiles = [tiles_ref[i * SUB:(i + 1) * SUB] for i in range(tiles_ref.shape[0] // SUB)]
    flow = functools.reduce(jnp.add, tiles[0::4] + tiles[1::4])
    weight = functools.reduce(jnp.add, tiles[2::4] + tiles[3::4])
    flow = jnp.sum(flow, keepdims=True)
    weight = jnp.sum(weight, keepdims=True)
    alpha = (target_ref[0] * (extent * lines) - flow) / weight
    for ref, whose in ((own_ref, lax.rem(me, 2)), (other_ref, 1 - lax.rem(me, 2))):
        for i in range(half):
            rows = row_tile(whose * half + i)
            emit((0,), rows, alpha, ends_ref, ref, i * 2 * components,
                 base_ref, left_ref, right_ref, result_ref)
            leave(0, rows)
    for copy in copies:
        copy.wait()


def shards(velocity, diffusion, wall_types, stretch_index, bulk_target):
    blocks = lax.axis_size("gz")
    columns = lax.axis_size("gy")
    components, cells, lines_y, lines_x = velocity.shape
    chips = blocks // 2
    row_tiles = lines_y // SUB
    half = row_tiles // 2
    f32 = jnp.float32
    vmem = pl.BlockSpec(memory_space=pltpu.VMEM)
    smem = pl.BlockSpec(memory_space=pltpu.SMEM)
    anywhere = pl.BlockSpec(memory_space=pl.ANY)
    plane = (lines_y, lines_x)
    sheet = (SUB, lines_x)

    def shape(*dims):
        return jax.ShapeDtypeStruct(dims, f32)

    def in_hbm(array):
        return pltpu.with_memory_space_constraint(array, pltpu.HBM)

    def options(mib):
        return pltpu.CompilerParams(vmem_limit_bytes=mib * MIB)

    def cost(flops, transferred):
        return pl.CostEstimate(flops=flops, bytes_accessed=transferred, transcendentals=0)

    mine, away, pair, chip_coefs, left, right, ends, tile = pl.pallas_call(
        functools.partial(ladder_kernel, cells, blocks, chips),
        out_shape=[
            shape(half * 2 * components, *sheet),
            shape(half * 2 * components, *sheet),
            shape(4, *plane),
            shape(chips - 1, *plane),
            shape(cells, *plane),
            shape(cells, *plane),
            shape(2, *plane),
            shape(4 * SUB, LANES),
        ],
        in_specs=[anywhere] * 4,
        out_specs=[vmem] * 8,
        scratch_shapes=[
            pltpu.SMEM(stretch_index.shape, jnp.int32),
            pltpu.VMEM(plane, f32),
            pltpu.VMEM(plane, jnp.int32),
            pltpu.VMEM(velocity.shape, f32),
            pltpu.VMEM((blocks,) + plane, f32),
            pltpu.VMEM(plane, f32),
            pltpu.VMEM((3,) + plane, f32),
            pltpu.SemaphoreType.DMA((3 + components,)),
        ],
        compiler_params=options(24),
        cost_estimate=cost(40_000_000, 6_000_000),
        name="ladder",
    )(in_hbm(stretch_index), in_hbm(diffusion), in_hbm(wall_types), in_hbm(velocity))

    def send(array, partner):
        pairs = [((z, y), partner(z, y)) for z in range(blocks) for y in range(columns)]
        route = [(a * columns + b, c * columns + d) for (a, b), (c, d) in pairs]
        return lax.ppermute(array, ("gz", "gy"), route)

    def to_mate(array):
        return send(array, lambda z, y: (z ^ 1, y))

    mate = to_mate(away)
    outgoing = pl.pallas_call(
        functools.partial(merge_kernel, chips, components),
        out_shape=[shape(half * components, *sheet)] * (chips - 1),
        in_specs=[vmem] * 3,
        out_specs=[vmem] * (chips - 1),
        compiler_params=options(16),
        cost_estimate=cost(500, 1_600),
        name="merge",
    )(mine, mate, pair)
    incoming = [
        send(outgoing[m - 1], lambda z, y: (z ^ (2 * m), y)) for m in range(1, chips)
    ]
    tiles = lax.all_gather(tile, ("gz", "gy"), axis=0, tiled=True)
    state = pl.BlockSpec((components, cells, SUB, lines_x), lambda t: (0, 0, t, 0))
    profile = pl.BlockSpec((cells, SUB, lines_x), lambda t: (0, t, 0))
    base = pl.pallas_call(
        functools.partial(inner_kernel, cells),
        grid=(row_tiles,),
        out_shape=shape(*velocity.shape),
        in_specs=[smem, state, profile, profile, anywhere],
        out_specs=state,
        compiler_params=options(16),
        cost_estimate=cost(800, 800),
        name="inner",
    )(stretch_index, in_hbm(velocity), left, right, outgoing[0])
    own_in, other_out = pl.pallas_call(
        functools.partial(spread_kernel, chips, components),
        out_shape=[shape(half * 2 * components, *sheet)] * 2,
        in_specs=[vmem] * 4 + [anywhere] + [vmem] * (chips - 1),
        out_specs=[vmem] * 2,
        compiler_params=options(16),
        cost_estimate=cost(500, 1_600),
        name="spread",
    )(mine, mate, pair, chip_coefs, base, *incoming)
    other_in = to_mate(other_out)
    early = pl.pallas_call(
        early_kernel,
        out_shape=shape(*velocity.shape),
        in_specs=[vmem] * 4,
        out_specs=anywhere,
        scratch_shapes=[
            pltpu.VMEM(velocity.shape, f32),
            pltpu.SemaphoreType.DMA(((components - 1) * half,)),
        ],
        compiler_params=options(16),
        cost_estimate=cost(500, 500),
        name="early",
    )(own_in, base, left, right)
    return pl.pallas_call(
        functools.partial(late_kernel, float(lines_y * columns * lines_x)),
        out_shape=shape(*velocity.shape),
        in_specs=[smem, smem] + [vmem] * 6 + [anywhere] * 2,
        out_specs=anywhere,
        scratch_shapes=[
            pltpu.VMEM(velocity.shape, f32),
            pltpu.VMEM(tiles.shape, f32),
            pltpu.SemaphoreType.DMA(((2 * components) * half + 1,)),
        ],
        input_output_aliases={9: 0},
        compiler_params=options(16),
        cost_estimate=cost(500, 500),
        name="late",
    )(stretch_index, bulk_target, ends, own_in, other_in, base, left, right, in_hbm(tiles), early)


def solution(mesh):
    return jax.shard_map(
        shards,
        mesh=mesh,
        in_specs=(P(None, "gz", "gy", None), P("gy", None), P("gy", None), P(), P()),
        out_specs=P(None, "gz", "gy", None),
        check_vma=False,
    )
```

```python
import functools

import jax
import jax.numpy as jnp
from jax import lax
from jax.experimental import pallas as pl
from jax.experimental.pallas import tpu as pltpu
from jax.sharding import PartitionSpec as P

SUB = 8
STRETCHES = 7
LANES = 128
MIB = 1024 * 1024


def row_tile(t):
    return pl.ds(pl.multiple_of(t * SUB, SUB), SUB)


def height(index_ref, k):
    return 0.5 + 0.25 * index_ref[k].astype(jnp.float32)


def half_sum(index_ref, k):
    return 0.5 * (height(index_ref, k) + height(index_ref, k + 1))


def ladder_kernel(
    cells, blocks, chips, lines,
    index_hbm, diffusion_hbm, walls_hbm, velocity_hbm,
    mine_ref, away_ref, pair_ref, chip_ref, left_ref, right_ref, left_h_ref, right_h_ref,
    ends_ref, tile_ref, volume_ref, velocity_ref,
    index_ref, diffusion_ref, walls_ref, through_ref, table_ref, held_ref, sems,
):
    total = cells * blocks
    components = velocity_ref.shape[0]
    row_tiles = diffusion_ref.shape[0] // SUB
    small = [
        pltpu.make_async_copy(index_hbm, index_ref, sems.at[0]),
        pltpu.make_async_copy(diffusion_hbm, diffusion_ref, sems.at[1]),
        pltpu.make_async_copy(walls_hbm, walls_ref, sems.at[2]),
    ]
    large = [
        pltpu.make_async_copy(velocity_hbm.at[c], velocity_ref.at[c], sems.at[3 + c])
        for c in range(components)
    ]
    for copy in small + large:
        copy.start()
    me = lax.axis_index("gz")
    chip = me // 2
    first = chip * 2
    for copy in small:
        copy.wait()
    diffusion = diffusion_ref[...]
    inverse = 1.0 / diffusion
    for i in range(STRETCHES):
        table_ref[i] = (0.5 + 0.25 * i) * inverse
    walls = walls_ref[...]

    def wall(bits, k):
        face = 1.0 / jnp.full((SUB, diffusion.shape[1]), 0.5 * height(index_ref, k))
        return bits.astype(jnp.float32) * jnp.concatenate([face] * row_tiles, axis=0)

    lower = wall(walls & 1, 0)
    upper = wall(walls >> 1, total - 1)

    def forward(block, kappa, keep=None):
        start = block * cells
        flux = table_ref[index_ref[start]] + kappa
        value = jnp.ones_like(flux)
        for j in range(cells):
            if keep is not None:
                keep(j, flux, value)
            k = start + j
            if j < cells - 1:
                value = value + half_sum(index_ref, k) * flux
                flux = flux + table_ref[index_ref[k + 1]] * value
        k = jnp.minimum(start + cells - 1, total - 2)
        after = 1.0 / (value + half_sum(index_ref, k) * flux)
        return flux * after, after

    def backward(block, kappa, scale=None, keep=None):
        start = block * cells
        flux = table_ref[index_ref[start + cells - 1]] + kappa
        value = jnp.ones_like(flux)
        if scale is not None:
            flux, value = flux * scale, scale
        for j in reversed(range(cells)):
            if keep is not None:
                keep(j, flux, value)
            k = start + j
            if j > 0:
                value = value + half_sum(index_ref, k - 1) * flux
                flux = flux + table_ref[index_ref[k - 1]] * value
        k = jnp.maximum(start - 1, 0)
        after = 1.0 / (value + half_sum(index_ref, k) * flux)
        return flux * after, after

    def thickness(block):
        parts = [height(index_ref, block * cells + j) for j in range(cells)]
        return functools.reduce(jnp.add, parts)

    def sweep_forward(block, state):
        kappa, product, extent = state
        kappa, after = forward(block, kappa)
        through_ref[block] = after
        return kappa, product * after, extent + thickness(block)

    def sweep_backward(step, state):
        block = blocks - 1 - step
        kappa, product, extent = state
        kappa, after = backward(block, kappa)
        through_ref[block] = after
        return kappa, product * after, extent + thickness(block)

    ones = jnp.ones_like(diffusion)
    kappa_left, product, extent = lax.fori_loop(
        0, me, sweep_forward, (lower, ones, thickness(me))
    )
    ends_ref[0] = diffusion * lower * product
    state = {}

    def keep_left(j, flux, value):
        left_ref[j] = value
        left_h_ref[j] = height(index_ref, me * cells + j) * value
        state["flux"], state["value"] = flux, value

    kappa, own_forward = forward(me, kappa_left, keep_left)
    held_ref[1] = own_forward
    held_ref[3] = state["flux"]
    held_ref[4] = state["value"]
    held_ref[5] = state["flux"] - kappa_left

    @pl.when(me == first)
    def _():
        pair_ref[2] = own_forward
        _, after = forward(me + 1, kappa)
        pair_ref[0] = after

    @pl.when(me != first)
    def _():
        pair_ref[2] = through_ref[first]
        pair_ref[0] = own_forward

    kappa_right, product, extent = lax.fori_loop(
        0, blocks - 1 - me, sweep_backward, (upper, ones, extent)
    )
    ends_ref[1] = diffusion_ref[...] * upper * product
    scale = 1.0 / (diffusion_ref[...] * (held_ref[3] + kappa_right * held_ref[4]))
    held_ref[0] = scale

    def keep_right(j, flux, value):
        right_ref[j] = value
        right_h_ref[j] = height(index_ref, me * cells + j) * value
        state["flux"] = flux

    kappa, own_backward = backward(me, kappa_right, scale, keep_right)
    held_ref[2] = own_backward
    held_ref[6] = state["flux"] - kappa_right * scale

    @pl.when(me == first)
    def _():
        pair_ref[1] = own_backward * held_ref[0]
        pair_ref[3] = through_ref[first + 1]

    @pl.when(me != first)
    def _():
        pair_ref[3] = own_backward * held_ref[0]
        _, after = backward(me - 1, kappa)
        pair_ref[1] = after

    for m in range(1, chips):
        other = chip ^ m
        low = jnp.minimum(chip, other)
        high = jnp.maximum(chip, other)
        chip_ref[m - 1] = lax.fori_loop(
            low + 1,
            high,
            lambda r, product: product * (through_ref[2 * r] * through_ref[2 * r + 1]),
            ones,
        )
    flow = jnp.zeros((SUB, LANES), jnp.float32)
    weight = jnp.zeros((SUB, LANES), jnp.float32)

    def fold(array):
        parts = [array[:, i * LANES:(i + 1) * LANES] for i in range(array.shape[1] // LANES)]
        return functools.reduce(jnp.add, parts)

    for copy in large:
        copy.wait()
    volume_ref[...] = jnp.full(volume_ref.shape, extent * lines)
    half = row_tiles // 2
    own_extent = thickness(me)
    heights = [height(index_ref, me * cells + j) for j in range(cells)]
    for ref, whose in ((away_ref, 1 - (me - first)), (mine_ref, me - first)):
        for i in range(half):
            rows = row_tile(whose * half + i)
            from_left = [0.0] * components
            from_right = [0.0] * components
            plain = 0.0
            for j in range(cells):
                left = left_h_ref[j, rows]
                right = right_h_ref[j, rows]
                for c in range(components):
                    v = velocity_ref[c, j, rows]
                    from_left[c] = from_left[c] + left * v
                    from_right[c] = from_right[c] + right * v
                    if c == 0:
                        plain = plain + heights[j] * v
            for c in range(components):
                ref[i * 2 * components + c] = from_left[c] * held_ref[1, rows]
                ref[i * 2 * components + components + c] = from_right[c] * held_ref[2, rows]
            low_part = ends_ref[0, rows]
            high_part = ends_ref[1, rows] * held_ref[0, rows]
            flow = flow + fold(plain - low_part * from_right[0] - high_part * from_left[0])
            totals = low_part * held_ref[6, rows] + high_part * held_ref[5, rows]
            weight = weight + fold(own_extent - diffusion_ref[rows] * totals)
    middle = SUB // 2
    for i in range(tile_ref.shape[0]):
        tile_ref[i, 0:middle] = flow[0:middle] + flow[middle:]
        tile_ref[i, middle:] = weight[0:middle] + weight[middle:]


def merge_kernel(chips, components, mine_ref, mate_ref, pair_ref, *send_refs):
    me = lax.axis_index("gz")
    chip = me // 2
    is_first = me == chip * 2
    half = mine_ref.shape[0] // (2 * components)
    for i in range(half):
        rows = row_tile((me - chip * 2) * half + i)
        for c in range(components):
            at = i * 2 * components + c
            mine, mate = mine_ref[at], mate_ref[at]
            first = jnp.where(is_first, mine, mate)
            second = jnp.where(is_first, mate, mine)
            to_right = second + pair_ref[0, rows] * first
            at = at + components
            mine, mate = mine_ref[at], mate_ref[at]
            first = jnp.where(is_first, mine, mate)
            second = jnp.where(is_first, mate, mine)
            to_left = first + pair_ref[1, rows] * second
            for m in range(1, chips):
                goes_right = (chip ^ m) > chip
                send_refs[m - 1][i * components + c] = jnp.where(goes_right, to_right, to_left)


def spread_kernel(chips, components, mine_ref, mate_ref, pair_ref, chip_ref, _, *rest):
    recv_refs, (own_ref, other_ref) = rest[:chips - 1], rest[chips - 1:]
    me = lax.axis_index("gz")
    chip = me // 2
    is_first = me == chip * 2
    half = mine_ref.shape[0] // (2 * components)
    for i in range(half):
        rows = row_tile((me - chip * 2) * half + i)
        coefs = [chip_ref[m, rows] for m in range(chips - 1)]
        for c in range(components):
            left_in = jnp.zeros(mine_ref.shape[1:], jnp.float32)
            right_in = jnp.zeros(mine_ref.shape[1:], jnp.float32)
            for m in range(1, chips):
                term = coefs[m - 1] * recv_refs[m - 1][i * components + c]
                from_left = (chip ^ m) < chip
                left_in = left_in + jnp.where(from_left, term, 0.0)
                right_in = right_in + jnp.where(from_left, 0.0, term)
            at = i * 2 * components + c
            first_out = jnp.where(is_first, mine_ref[at], mate_ref[at])
            left_second = first_out + pair_ref[2, rows] * left_in
            at = at + components
            second_out = jnp.where(is_first, mate_ref[at], mine_ref[at])
            right_first = second_out + pair_ref[3, rows] * right_in
            at = i * 2 * components + c
            own_ref[at] = jnp.where(is_first, left_in, left_second)
            other_ref[at] = jnp.where(is_first, left_second, left_in)
            at = at + components
            own_ref[at] = jnp.where(is_first, right_first, right_in)
            other_ref[at] = jnp.where(is_first, right_in, right_first)


def inner_kernel(velocity_ref, left_ref, right_ref, left_h_ref, right_h_ref, *rest):
    base_ref = rest[-1]
    components, cells, lines_y, lines_x = velocity_ref.shape
    for t in range(lines_y // SUB):
        rows = row_tile(t)
        gathered = [jnp.zeros((SUB, lines_x), jnp.float32)] * components
        for j in reversed(range(cells)):
            left = left_ref[j, rows]
            right = right_h_ref[j, rows]
            for c in range(components):
                base_ref[c, j, rows] = left * gathered[c]
                if j > 0:
                    gathered[c] = gathered[c] + right * velocity_ref[c, j, rows]
        gathered = [jnp.zeros((SUB, lines_x), jnp.float32)] * components
        for j in range(cells):
            left = left_h_ref[j, rows]
            right = right_ref[j, rows]
            for c in range(components):
                gathered[c] = gathered[c] + left * velocity_ref[c, j, rows]
                base_ref[c, j, rows] = base_ref[c, j, rows] + right * gathered[c]


def emit(parts, rows, alpha, ends_ref, incoming_ref, at, base_ref, left_ref, right_ref, result_ref):
    cells = left_ref.shape[0]
    components = base_ref.shape[0]
    scale = right_ref[cells - 1, rows]
    lefts, rights = {}, {}
    for c in parts:
        left_in = incoming_ref[at + c]
        right_in = incoming_ref[at + components + c]
        if c == 0:
            left_in = left_in - alpha * ends_ref[0, rows]
            right_in = right_in - alpha * ends_ref[1, rows]
        lefts[c] = left_in
        rights[c] = right_in * scale
    for j in range(cells):
        left = left_ref[j, rows]
        right = right_ref[j, rows]
        for c in parts:
            value = base_ref[c, j, rows] + (right * lefts[c] + left * rights[c])
            result_ref[c, j, rows] = value + alpha if c == 0 else value


def early_kernel(own_ref, base_ref, left_ref, right_ref, out_hbm, result_ref, sems):
    components = base_ref.shape[0]
    half = own_ref.shape[0] // (2 * components)
    me = lax.axis_index("gz")
    copies = []
    for i in range(half):
        rows = row_tile(lax.rem(me, 2) * half + i)
        emit(range(1, components), rows, None, None, own_ref, i * 2 * components,
             base_ref, left_ref, right_ref, result_ref)
        for c in range(1, components):
            copies.append(pltpu.make_async_copy(
                result_ref.at[c, :, rows], out_hbm.at[c, :, rows], sems.at[len(copies)]))
            copies[-1].start()
    for copy in copies:
        copy.wait()


def late_kernel(
    target_ref, volume_ref, ends_ref, own_ref, other_ref, base_ref, left_ref, right_ref, *rest
):
    tiles_ref, _, out_hbm, result_ref, sems = rest
    components = base_ref.shape[0]
    half = own_ref.shape[0] // (2 * components)
    me = lax.axis_index("gz")
    copies = []

    def leave(c, rows):
        copies.append(pltpu.make_async_copy(
            result_ref.at[c, :, rows], out_hbm.at[c, :, rows], sems.at[len(copies)]))
        copies[-1].start()

    for i in range(half):
        rows = row_tile((1 - lax.rem(me, 2)) * half + i)
        emit(range(1, components), rows, None, None, other_ref, i * 2 * components,
             base_ref, left_ref, right_ref, result_ref)
        for c in range(1, components):
            leave(c, rows)
    totals = functools.reduce(jnp.add, [tiles_ref[i] for i in range(tiles_ref.shape[0])])
    flow = jnp.sum(totals[0:SUB // 2], keepdims=True)
    weight = jnp.sum(totals[SUB // 2:], keepdims=True)
    alpha = (target_ref[...] * volume_ref[0:1, 0:1] - flow) / weight
    for ref, whose in ((own_ref, lax.rem(me, 2)), (other_ref, 1 - lax.rem(me, 2))):
        for i in range(half):
            rows = row_tile(whose * half + i)
            emit((0,), rows, alpha, ends_ref, ref, i * 2 * components,
                 base_ref, left_ref, right_ref, result_ref)
            leave(0, rows)
    for copy in copies:
        copy.wait()


def shards(velocity, diffusion, wall_types, stretch_index, bulk_target):
    blocks = lax.axis_size("gz")
    columns = lax.axis_size("gy")
    components, cells, lines_y, lines_x = velocity.shape
    chips = blocks // 2
    row_tiles = lines_y // SUB
    half = row_tiles // 2
    f32 = jnp.float32
    vmem = pl.BlockSpec(memory_space=pltpu.VMEM)
    anywhere = pl.BlockSpec(memory_space=pl.ANY)
    plane = (lines_y, lines_x)
    sheet = (SUB, lines_x)

    def shape(*dims):
        return jax.ShapeDtypeStruct(dims, f32)

    def in_hbm(array):
        return pltpu.with_memory_space_constraint(array, pltpu.HBM)

    def options(mib):
        return pltpu.CompilerParams(vmem_limit_bytes=mib * MIB)

    def cost(flops, transferred):
        return pl.CostEstimate(flops=flops, bytes_accessed=transferred, transcendentals=0)

    def send(array, partner):
        pairs = [((z, y), partner(z, y)) for z in range(blocks) for y in range(columns)]
        route = [(a * columns + b, c * columns + d) for (a, b), (c, d) in pairs]
        return lax.ppermute(array, ("gz", "gy"), route)

    def to_mate(array):
        return send(array, lambda z, y: (z ^ 1, y))

    def to_chip(array, m):
        return send(array, lambda z, y: (z ^ (2 * m), y))

    lines = float(lines_y * columns * lines_x)
    (mine, away, pair, chip_coefs, left, right, left_h, right_h, ends, tile, volume,
     near_velocity) = pl.pallas_call(
        functools.partial(ladder_kernel, cells, blocks, chips, lines),
        out_shape=[
            shape(half * 2 * components, *sheet),
            shape(half * 2 * components, *sheet),
            shape(4, *plane),
            shape(chips - 1, *plane),
            shape(cells, *plane),
            shape(cells, *plane),
            shape(cells, *plane),
            shape(cells, *plane),
            shape(2, *plane),
            shape(blocks * columns, SUB, LANES),
            shape(SUB, LANES),
            shape(*velocity.shape),
        ],
        in_specs=[anywhere] * 4,
        out_specs=[vmem] * 12,
        scratch_shapes=[
            pltpu.SMEM(stretch_index.shape, jnp.int32),
            pltpu.VMEM(plane, f32),
            pltpu.VMEM(plane, jnp.int32),
            pltpu.VMEM((blocks,) + plane, f32),
            pltpu.VMEM((STRETCHES,) + plane, f32),
            pltpu.VMEM((7,) + plane, f32),
            pltpu.SemaphoreType.DMA((3 + components,)),
        ],
        compiler_params=options(24),
        cost_estimate=cost(40_000_000, 6_000_000),
        name="ladder",
    )(in_hbm(stretch_index), in_hbm(diffusion), in_hbm(wall_types), in_hbm(velocity))

    mate = to_mate(away)
    tiles = lax.all_to_all(tile, ("gz", "gy"), 0, 0, tiled=True)
    outgoing = pl.pallas_call(
        functools.partial(merge_kernel, chips, components),
        out_shape=[shape(half * components, *sheet)] * (chips - 1),
        in_specs=[vmem] * 3,
        out_specs=[vmem] * (chips - 1),
        compiler_params=options(16),
        cost_estimate=cost(500_000, 1_600_000),
        name="merge",
    )(mine, mate, pair)
    incoming = [to_chip(outgoing[m - 1], m) for m in range(1, chips)]
    base = pl.pallas_call(
        inner_kernel,
        out_shape=shape(*velocity.shape),
        in_specs=[vmem] * 5 + [anywhere],
        out_specs=vmem,
        compiler_params=options(16),
        cost_estimate=cost(8_000_000, 8_000_000),
        name="inner",
    )(near_velocity, left, right, left_h, right_h, outgoing[0])
    own_in, other_out = pl.pallas_call(
        functools.partial(spread_kernel, chips, components),
        out_shape=[shape(half * 2 * components, *sheet)] * 2,
        in_specs=[vmem] * 4 + [anywhere] + [vmem] * (chips - 1),
        out_specs=[vmem] * 2,
        compiler_params=options(16),
        cost_estimate=cost(500_000, 1_600_000),
        name="spread",
    )(mine, mate, pair, chip_coefs, base, *incoming)
    other_in = to_mate(other_out)
    early = pl.pallas_call(
        early_kernel,
        out_shape=shape(*velocity.shape),
        in_specs=[vmem] * 4,
        out_specs=anywhere,
        scratch_shapes=[
            pltpu.VMEM(velocity.shape, f32),
            pltpu.SemaphoreType.DMA(((components - 1) * half,)),
        ],
        compiler_params=options(16),
        cost_estimate=cost(2_000_000, 4_000_000),
        name="early",
    )(own_in, base, left, right)
    return pl.pallas_call(
        late_kernel,
        out_shape=shape(*velocity.shape),
        in_specs=[vmem] * 9 + [anywhere],
        out_specs=anywhere,
        scratch_shapes=[
            pltpu.VMEM(velocity.shape, f32),
            pltpu.SemaphoreType.DMA(((components + 1) * half,)),
        ],
        input_output_aliases={9: 0},
        compiler_params=options(16),
        cost_estimate=cost(3_000_000, 6_000_000),
        name="late",
    )(bulk_target.reshape(1, 1), volume, ends, own_in, other_in, base, left, right, tiles, early)


def solution(mesh):
    return jax.shard_map(
        shards,
        mesh=mesh,
        in_specs=(P(None, "gz", "gy", None), P("gy", None), P("gy", None), P(), P()),
        out_specs=P(None, "gz", "gy", None),
        check_vma=False,
    )
```

```python
import functools

import jax
import jax.numpy as jnp
from jax import lax
from jax.experimental import pallas as pl
from jax.experimental.pallas import tpu as pltpu
from jax.sharding import PartitionSpec as P

SUB = 8
STRETCHES = 7
LANES = 128
MIB = 1024 * 1024


def row_tile(t):
    return pl.ds(pl.multiple_of(t * SUB, SUB), SUB)


def height(index_ref, k):
    return 0.5 + 0.25 * index_ref[k].astype(jnp.float32)


def half_sum(index_ref, k):
    return 0.5 * (height(index_ref, k) + height(index_ref, k + 1))


def ladder_kernel(
    cells, blocks, chips, lines,
    index_hbm, diffusion_hbm, walls_hbm, velocity_hbm,
    mine_ref, away_ref, pair_ref, chip_ref, ends_ref, state_ref, volume_ref,
    left_h_ref, right_h_ref, velocity_ref,
    index_ref, diffusion_ref, walls_ref, through_ref, table_ref, held_ref, sems,
):
    total = cells * blocks
    components = velocity_ref.shape[0]
    row_tiles = diffusion_ref.shape[0] // SUB
    small = [
        pltpu.make_async_copy(index_hbm, index_ref, sems.at[0]),
        pltpu.make_async_copy(diffusion_hbm, diffusion_ref, sems.at[1]),
        pltpu.make_async_copy(walls_hbm, walls_ref, sems.at[2]),
    ]
    large = [
        pltpu.make_async_copy(velocity_hbm.at[c], velocity_ref.at[c], sems.at[3 + c])
        for c in range(components)
    ]
    for copy in small + large:
        copy.start()
    me = lax.axis_index("gz")
    chip = me // 2
    first = chip * 2
    for copy in small:
        copy.wait()
    diffusion = diffusion_ref[...]
    inverse = 1.0 / diffusion
    for i in range(STRETCHES):
        table_ref[i] = (0.5 + 0.25 * i) * inverse
    walls = walls_ref[...]

    def wall(bits, k):
        face = 1.0 / jnp.full((SUB, diffusion.shape[1]), 0.5 * height(index_ref, k))
        return bits.astype(jnp.float32) * jnp.concatenate([face] * row_tiles, axis=0)

    lower = wall(walls & 1, 0)
    upper = wall(walls >> 1, total - 1)

    def forward(block, kappa, keep=None):
        start = block * cells
        flux = table_ref[index_ref[start]] + kappa
        value = jnp.ones_like(flux)
        for j in range(cells):
            if keep is not None:
                keep(j, flux, value)
            k = start + j
            if j < cells - 1:
                value = value + half_sum(index_ref, k) * flux
                flux = flux + table_ref[index_ref[k + 1]] * value
        k = jnp.minimum(start + cells - 1, total - 2)
        after = 1.0 / (value + half_sum(index_ref, k) * flux)
        return flux * after, after

    def backward(block, kappa, scale=None, keep=None):
        start = block * cells
        flux = table_ref[index_ref[start + cells - 1]] + kappa
        value = jnp.ones_like(flux)
        if scale is not None:
            flux, value = flux * scale, scale
        for j in reversed(range(cells)):
            if keep is not None:
                keep(j, flux, value)
            k = start + j
            if j > 0:
                value = value + half_sum(index_ref, k - 1) * flux
                flux = flux + table_ref[index_ref[k - 1]] * value
        k = jnp.maximum(start - 1, 0)
        after = 1.0 / (value + half_sum(index_ref, k) * flux)
        return flux * after, after

    def thickness(block):
        parts = [height(index_ref, block * cells + j) for j in range(cells)]
        return functools.reduce(jnp.add, parts)

    def sweep_forward(block, state):
        kappa, product, extent = state
        kappa, after = forward(block, kappa)
        through_ref[block] = after
        return kappa, product * after, extent + thickness(block)

    def sweep_backward(step, state):
        block = blocks - 1 - step
        kappa, product, extent = state
        kappa, after = backward(block, kappa)
        through_ref[block] = after
        return kappa, product * after, extent + thickness(block)

    ones = jnp.ones_like(diffusion)
    kappa_left, product, extent = lax.fori_loop(
        0, me, sweep_forward, (lower, ones, thickness(me))
    )
    ends_ref[0] = diffusion * lower * product
    state_ref[0] = kappa_left
    state = {}

    def keep_left(j, flux, value):
        left_h_ref[j] = height(index_ref, me * cells + j) * value
        state["flux"], state["value"] = flux, value

    kappa, own_forward = forward(me, kappa_left, keep_left)
    held_ref[1] = own_forward
    held_ref[3] = state["flux"]
    held_ref[4] = state["value"]
    held_ref[5] = state["flux"] - kappa_left

    @pl.when(me == first)
    def _():
        pair_ref[2] = own_forward
        _, after = forward(me + 1, kappa)
        pair_ref[0] = after

    @pl.when(me != first)
    def _():
        pair_ref[2] = through_ref[first]
        pair_ref[0] = own_forward

    kappa_right, product, extent = lax.fori_loop(
        0, blocks - 1 - me, sweep_backward, (upper, ones, extent)
    )
    ends_ref[1] = diffusion_ref[...] * upper * product
    scale = 1.0 / (diffusion_ref[...] * (held_ref[3] + kappa_right * held_ref[4]))
    held_ref[0] = scale

    state_ref[1] = kappa_right
    state_ref[2] = scale

    def keep_right(j, flux, value):
        right_h_ref[j] = height(index_ref, me * cells + j) * value
        state["flux"] = flux

    kappa, own_backward = backward(me, kappa_right, scale, keep_right)
    held_ref[2] = own_backward
    held_ref[6] = state["flux"] - kappa_right * scale

    @pl.when(me == first)
    def _():
        pair_ref[1] = own_backward * held_ref[0]
        pair_ref[3] = through_ref[first + 1]

    @pl.when(me != first)
    def _():
        pair_ref[3] = own_backward * held_ref[0]
        _, after = backward(me - 1, kappa)
        pair_ref[1] = after

    for other in range(chips):
        low = jnp.minimum(chip, other)
        high = jnp.maximum(chip, other)
        chip_ref[other] = lax.fori_loop(
            low + 1,
            high,
            lambda r, product: product * (through_ref[2 * r] * through_ref[2 * r + 1]),
            jnp.where(chip == other, 0.0, ones),
        )
    flow = jnp.zeros((SUB, LANES), jnp.float32)
    weight = jnp.zeros((SUB, LANES), jnp.float32)

    def fold(array):
        parts = [array[:, i * LANES:(i + 1) * LANES] for i in range(array.shape[1] // LANES)]
        return functools.reduce(jnp.add, parts)

    for copy in large:
        copy.wait()
    volume_ref[...] = jnp.full(volume_ref.shape, extent * lines)
    half = row_tiles // 2
    own_extent = thickness(me)
    heights = [height(index_ref, me * cells + j) for j in range(cells)]
    for ref, whose in ((away_ref, 1 - (me - first)), (mine_ref, me - first)):
        for i in range(half):
            rows = row_tile(whose * half + i)
            from_left = [0.0] * components
            from_right = [0.0] * components
            plain = 0.0
            for j in range(cells):
                left = left_h_ref[j, rows]
                right = right_h_ref[j, rows]
                for c in range(components):
                    v = velocity_ref[c, j, rows]
                    from_left[c] = from_left[c] + left * v
                    from_right[c] = from_right[c] + right * v
                    if c == 0:
                        plain = plain + heights[j] * v
            for c in range(components):
                ref[i * 2 * components + c] = from_left[c] * held_ref[1, rows]
                ref[i * 2 * components + components + c] = from_right[c] * held_ref[2, rows]
            low_part = ends_ref[0, rows]
            high_part = ends_ref[1, rows] * held_ref[0, rows]
            flow = flow + fold(plain - low_part * from_right[0] - high_part * from_left[0])
            totals = low_part * held_ref[6, rows] + high_part * held_ref[5, rows]
            weight = weight + fold(own_extent - diffusion_ref[rows] * totals)
    slot = half * 2 * components
    away_ref[slot] = jnp.zeros(away_ref.shape[1:], jnp.float32)
    away_ref[slot, :, 0:LANES] = flow
    away_ref[slot, :, LANES:2 * LANES] = weight


def merge_kernel(chips, components, mine_ref, away_ref, mate_ref, pair_ref, send_ref):
    me = lax.axis_index("gz")
    chip = me // 2
    is_first = me == chip * 2
    half = mine_ref.shape[0] // (2 * components)
    tile = away_ref[half * 2 * components] + mate_ref[half * 2 * components]
    for other in range(chips):
        send_ref[other, half * components] = tile
    for i in range(half):
        rows = row_tile((me - chip * 2) * half + i)
        for c in range(components):
            at = i * 2 * components + c
            mine, mate = mine_ref[at], mate_ref[at]
            first = jnp.where(is_first, mine, mate)
            second = jnp.where(is_first, mate, mine)
            to_right = second + pair_ref[0, rows] * first
            at = at + components
            mine, mate = mine_ref[at], mate_ref[at]
            first = jnp.where(is_first, mine, mate)
            second = jnp.where(is_first, mate, mine)
            to_left = first + pair_ref[1, rows] * second
            for other in range(chips):
                send_ref[other, i * components + c] = jnp.where(other > chip, to_right, to_left)


def spread_kernel(
    chips, components, mine_ref, mate_ref, pair_ref, chip_ref, recv_ref, own_ref, other_ref, tile_ref
):
    me = lax.axis_index("gz")
    chip = me // 2
    is_first = me == chip * 2
    half = mine_ref.shape[0] // (2 * components)
    slot = half * components
    tile = functools.reduce(jnp.add, [recv_ref[k, slot, :, 0:2 * LANES] for k in range(chips)])
    for y in range(tile_ref.shape[0]):
        tile_ref[y, 0] = tile[:, 0:LANES]
        tile_ref[y, 1] = tile[:, LANES:]
    for i in range(half):
        rows = row_tile((me - chip * 2) * half + i)
        coefs = [chip_ref[k, rows] for k in range(chips)]
        for c in range(components):
            left_in = jnp.zeros(mine_ref.shape[1:], jnp.float32)
            right_in = jnp.zeros(mine_ref.shape[1:], jnp.float32)
            for k in range(chips):
                term = coefs[k] * recv_ref[k, i * components + c]
                left_in = left_in + jnp.where(k < chip, term, 0.0)
                right_in = right_in + jnp.where(k < chip, 0.0, term)
            at = i * 2 * components + c
            first_out = jnp.where(is_first, mine_ref[at], mate_ref[at])
            left_second = first_out + pair_ref[2, rows] * left_in
            at = at + components
            second_out = jnp.where(is_first, mate_ref[at], mine_ref[at])
            right_first = second_out + pair_ref[3, rows] * right_in
            at = i * 2 * components + c
            own_ref[at] = jnp.where(is_first, left_in, left_second)
            other_ref[at] = jnp.where(is_first, left_second, left_in)
            at = at + components
            own_ref[at] = jnp.where(is_first, right_first, right_in)
            other_ref[at] = jnp.where(is_first, right_in, right_first)


def leave(copies, source, target, sems):
    copies.append(pltpu.make_async_copy(source, target, sems.at[len(copies)]))
    copies[-1].start()


def early_kernel(
    index_hbm, diffusion_hbm, velocity_hbm, state_ref, ends_ref, own_ref,
    out_hbm, plain_ref, unit_ref, base_ref, left_ref, right_ref,
    index_ref, diffusion_ref, velocity_ref, near_ref, far_ref, result_ref, in_sems, out_sems,
):
    components, cells, lines_y, lines_x = velocity_ref.shape
    half = lines_y // SUB // 2
    middle = half * SUB
    me = lax.axis_index("gz")
    starts = [lax.rem(me, 2) * middle, (1 - lax.rem(me, 2)) * middle]
    parts = [pl.ds(pl.multiple_of(start, SUB), middle) for start in starts]
    small = [
        pltpu.make_async_copy(index_hbm, index_ref, in_sems.at[0]),
        pltpu.make_async_copy(diffusion_hbm, diffusion_ref, in_sems.at[1]),
    ]
    large = [
        pltpu.make_async_copy(
            velocity_hbm.at[:, :, part], velocity_ref.at[:, :, part], in_sems.at[2 + i])
        for i, part in enumerate(parts)
    ]
    for copy in small + large:
        copy.start()
    for copy in small:
        copy.wait()
    heights = [height(index_ref, me * cells + j) for j in range(cells)]
    for part, low_ref, high_ref in ((parts[0], near_ref, far_ref), (parts[1], left_ref, right_ref)):
        inverse = 1.0 / diffusion_ref[part]
        flux = heights[0] * inverse + state_ref[0, part]
        value = jnp.ones_like(flux)
        for j in range(cells):
            low_ref[j] = value
            if j < cells - 1:
                value = value + (0.5 * (heights[j] + heights[j + 1])) * flux
                flux = flux + (heights[j + 1] * inverse) * value
        scale = state_ref[2, part]
        flux = (heights[cells - 1] * inverse + state_ref[1, part]) * scale
        value = scale
        for j in reversed(range(cells)):
            high_ref[j] = value
            if j > 0:
                value = value + (0.5 * (heights[j] + heights[j - 1])) * flux
                flux = flux + (heights[j - 1] * inverse) * value
    copies = []
    for side, (low_ref, high_ref) in enumerate(((near_ref, far_ref), (left_ref, right_ref))):
        large[side].wait()
        for i in range(half):
            rows = row_tile(starts[side] // SUB + i)
            near = slice(i * SUB, (i + 1) * SUB)
            scale = high_ref[cells - 1, near]
            below, above = [], []
            for c in range(components):
                if side == 0:
                    below.append(own_ref[i * 2 * components + c])
                    above.append(own_ref[i * 2 * components + components + c] * scale)
                else:
                    below.append(jnp.zeros((SUB, lines_x), jnp.float32))
                    above.append(jnp.zeros((SUB, lines_x), jnp.float32))

            def place(c, j):
                if side == 1:
                    return base_ref, (c, j, near)
                if c == 0:
                    return plain_ref, (j, near)
                return result_ref, (c - 1, j, near)

            for j in reversed(range(cells)):
                low = low_ref[j, near]
                high = heights[j] * high_ref[j, near]
                for c in range(components):
                    ref, at = place(c, j)
                    ref[at] = low * above[c]
                    if j > 0:
                        above[c] = above[c] + high * velocity_ref[c, j, rows]
            for j in range(cells):
                low = heights[j] * low_ref[j, near]
                high = high_ref[j, near]
                for c in range(components):
                    below[c] = below[c] + low * velocity_ref[c, j, rows]
                    ref, at = place(c, j)
                    ref[at] = ref[at] + high * below[c]
            if side == 0:
                low_part = ends_ref[0, rows]
                high_part = ends_ref[1, rows] * scale
                for j in range(cells):
                    unit_ref[j, near] = 1.0 - (
                        low_part * high_ref[j, near] + high_part * low_ref[j, near])
                for c in range(1, components):
                    leave(copies, result_ref.at[c - 1, :, near], out_hbm.at[c, :, rows], out_sems)
    for copy in copies:
        copy.wait()


def late_kernel(
    ends_ref, other_ref, base_ref, left_ref, right_ref, _,
    out_hbm, plain_ref, unit_ref, result_ref, sems,
):
    components, cells, middle, _ = base_ref.shape
    half = middle // SUB
    me = lax.axis_index("gz")
    copies = []
    for i in range(half):
        rows = row_tile((1 - lax.rem(me, 2)) * half + i)
        near = slice(i * SUB, (i + 1) * SUB)
        scale = right_ref[cells - 1, near]
        lefts = [other_ref[i * 2 * components + c] for c in range(components)]
        rights = [other_ref[i * 2 * components + components + c] * scale for c in range(components)]
        low_part = ends_ref[0, rows]
        high_part = ends_ref[1, rows] * scale
        for j in range(cells):
            left = left_ref[j, near]
            right = right_ref[j, near]
            unit_ref[j, near] = 1.0 - (low_part * right + high_part * left)
            for c in range(components):
                value = base_ref[c, j, near] + (right * lefts[c] + left * rights[c])
                if c == 0:
                    plain_ref[j, near] = value
                else:
                    result_ref[c - 1, j, near] = value
        for c in range(1, components):
            leave(copies, result_ref.at[c - 1, :, near], out_hbm.at[c, :, rows], sems)
    for copy in copies:
        copy.wait()


def correct_kernel(
    target_ref, volume_ref, tiles_ref, own_plain_ref, own_unit_ref, other_plain_ref, other_unit_ref,
    _, out_hbm, result_ref, sems,
):
    totals = functools.reduce(jnp.add, [tiles_ref[y] for y in range(tiles_ref.shape[0])])
    flow = jnp.sum(totals[0], keepdims=True)
    weight = jnp.sum(totals[1], keepdims=True)
    alpha = (target_ref[...] * volume_ref[0:1, 0:1] - flow) / weight
    cells, middle, _ = own_plain_ref.shape
    half = middle // SUB
    me = lax.axis_index("gz")
    sides = (
        (lax.rem(me, 2), own_plain_ref, own_unit_ref),
        (1 - lax.rem(me, 2), other_plain_ref, other_unit_ref),
    )
    copies = []
    for whose, plain_ref, unit_ref in sides:
        for i in range(half):
            rows = row_tile(whose * half + i)
            near = slice(i * SUB, (i + 1) * SUB)
            for j in range(cells):
                result_ref[j, rows] = plain_ref[j, near] + alpha * unit_ref[j, near]
            leave(copies, result_ref.at[:, rows], out_hbm.at[0, :, rows], sems)
    for copy in copies:
        copy.wait()


def shards(velocity, diffusion, wall_types, stretch_index, bulk_target):
    blocks = lax.axis_size("gz")
    columns = lax.axis_size("gy")
    components, cells, lines_y, lines_x = velocity.shape
    chips = blocks // 2
    row_tiles = lines_y // SUB
    half = row_tiles // 2
    f32 = jnp.float32
    vmem = pl.BlockSpec(memory_space=pltpu.VMEM)
    anywhere = pl.BlockSpec(memory_space=pl.ANY)
    plane = (lines_y, lines_x)
    sheet = (SUB, lines_x)

    def shape(*dims):
        return jax.ShapeDtypeStruct(dims, f32)

    def in_hbm(array):
        return pltpu.with_memory_space_constraint(array, pltpu.HBM)

    def options(mib):
        return pltpu.CompilerParams(vmem_limit_bytes=mib * MIB)

    def cost(flops, transferred):
        return pl.CostEstimate(flops=flops, bytes_accessed=transferred, transcendentals=0)

    def send(array, partner):
        pairs = [((z, y), partner(z, y)) for z in range(blocks) for y in range(columns)]
        route = [(a * columns + b, c * columns + d) for (a, b), (c, d) in pairs]
        return lax.ppermute(array, ("gz", "gy"), route)

    def to_mate(array):
        return send(array, lambda z, y: (z ^ 1, y))

    middle = half * SUB
    lines = float(lines_y * columns * lines_x)
    mine, away, pair, chip_coefs, ends, state, volume = pl.pallas_call(
        functools.partial(ladder_kernel, cells, blocks, chips, lines),
        out_shape=[
            shape(half * 2 * components, *sheet),
            shape(half * 2 * components + 1, *sheet),
            shape(4, *plane),
            shape(chips, *plane),
            shape(2, *plane),
            shape(3, *plane),
            shape(SUB, LANES),
        ],
        in_specs=[anywhere] * 4,
        out_specs=[vmem] * 7,
        scratch_shapes=[
            pltpu.VMEM((cells,) + plane, f32),
            pltpu.VMEM((cells,) + plane, f32),
            pltpu.VMEM(velocity.shape, f32),
            pltpu.SMEM(stretch_index.shape, jnp.int32),
            pltpu.VMEM(plane, f32),
            pltpu.VMEM(plane, jnp.int32),
            pltpu.VMEM((blocks,) + plane, f32),
            pltpu.VMEM((STRETCHES,) + plane, f32),
            pltpu.VMEM((7,) + plane, f32),
            pltpu.SemaphoreType.DMA((3 + components,)),
        ],
        compiler_params=options(24),
        cost_estimate=cost(40_000_000, 6_000_000),
        name="ladder",
    )(in_hbm(stretch_index), in_hbm(diffusion), in_hbm(wall_types), in_hbm(velocity))

    mate = to_mate(away)
    outgoing = pl.pallas_call(
        functools.partial(merge_kernel, chips, components),
        out_shape=shape(chips, half * components + 1, *sheet),
        in_specs=[vmem] * 4,
        out_specs=vmem,
        compiler_params=options(16),
        cost_estimate=cost(500_000, 1_600_000),
        name="merge",
    )(mine, away, mate, pair)
    same_core = [[2 * k + core for k in range(chips)] for core in range(2)]
    incoming = lax.all_to_all(
        outgoing, "gz", 0, 0, axis_index_groups=same_core, tiled=True
    )
    own_in, other_out, tile = pl.pallas_call(
        functools.partial(spread_kernel, chips, components),
        out_shape=[shape(half * 2 * components, *sheet)] * 2 + [shape(columns, 2, SUB, LANES)],
        in_specs=[vmem] * 5,
        out_specs=[vmem] * 3,
        compiler_params=options(16),
        cost_estimate=cost(500_000, 1_600_000),
        name="spread",
    )(mine, mate, pair, chip_coefs, incoming)
    other_in = to_mate(other_out)
    tiles = lax.all_to_all(tile, "gy", 0, 0, tiled=True)
    partial, own_plain, own_unit, base, left, right = pl.pallas_call(
        early_kernel,
        out_shape=[
            shape(*velocity.shape),
            shape(cells, middle, lines_x),
            shape(cells, middle, lines_x),
            shape(components, cells, middle, lines_x),
            shape(cells, middle, lines_x),
            shape(cells, middle, lines_x),
        ],
        in_specs=[anywhere] * 3 + [vmem] * 3,
        out_specs=[anywhere] + [vmem] * 5,
        scratch_shapes=[
            pltpu.SMEM(stretch_index.shape, jnp.int32),
            pltpu.VMEM(plane, f32),
            pltpu.VMEM(velocity.shape, f32),
            pltpu.VMEM((cells, middle, lines_x), f32),
            pltpu.VMEM((cells, middle, lines_x), f32),
            pltpu.VMEM((components - 1, cells, middle, lines_x), f32),
            pltpu.SemaphoreType.DMA((4,)),
            pltpu.SemaphoreType.DMA(((components - 1) * half,)),
        ],
        compiler_params=options(24),
        cost_estimate=cost(8_000_000, 8_000_000),
        name="early",
    )(in_hbm(stretch_index), in_hbm(diffusion), in_hbm(velocity), state, ends, own_in)
    partial, other_plain, other_unit = pl.pallas_call(
        late_kernel,
        out_shape=[
            shape(*velocity.shape),
            shape(cells, middle, lines_x),
            shape(cells, middle, lines_x),
        ],
        in_specs=[vmem] * 5 + [anywhere],
        out_specs=[anywhere] + [vmem] * 2,
        scratch_shapes=[
            pltpu.VMEM((components - 1, cells, middle, lines_x), f32),
            pltpu.SemaphoreType.DMA(((components - 1) * half,)),
        ],
        input_output_aliases={5: 0},
        compiler_params=options(16),
        cost_estimate=cost(3_000_000, 6_000_000),
        name="late",
    )(ends, other_in, base, left, right, partial)
    return pl.pallas_call(
        correct_kernel,
        out_shape=shape(*velocity.shape),
        in_specs=[vmem] * 7 + [anywhere],
        out_specs=anywhere,
        scratch_shapes=[
            pltpu.VMEM((cells,) + plane, f32),
            pltpu.SemaphoreType.DMA((row_tiles,)),
        ],
        input_output_aliases={7: 0},
        compiler_params=options(16),
        cost_estimate=cost(500_000, 1_600_000),
        name="correct",
    )(bulk_target.reshape(1, 1), volume, tiles, own_plain, own_unit, other_plain, other_unit, partial)


def solution(mesh):
    return jax.shard_map(
        shards,
        mesh=mesh,
        in_specs=(P(None, "gz", "gy", None), P("gy", None), P("gy", None), P(), P()),
        out_specs=P(None, "gz", "gy", None),
        check_vma=False,
    )
```

```python
import functools

import jax
import jax.numpy as jnp
from jax import lax
from jax.experimental import pallas as pl
from jax.experimental.pallas import tpu as pltpu
from jax.sharding import PartitionSpec as P

SUB = 8
STRETCHES = 7
LANES = 128
MIB = 1024 * 1024


def row_tile(t):
    return pl.ds(pl.multiple_of(t * SUB, SUB), SUB)


def wide(tile, lines_x):
    return jnp.concatenate([tile] * (lines_x // LANES), axis=1)


def height(index_ref, k):
    return 0.5 + 0.25 * index_ref[k].astype(jnp.float32)


def half_sum(index_ref, k):
    return 0.5 * (height(index_ref, k) + height(index_ref, k + 1))


def ladder_kernel(
    cells, blocks, chips, lines,
    index_hbm, diffusion_hbm, walls_hbm, velocity_hbm,
    mine_ref, away_ref, pair_ref, chip_ref, ends_ref, state_ref, heights_ref, near_velocity_ref,
    tile_ref, volume_ref,
    left_h_ref, right_h_ref, far_velocity_ref,
    index_ref, diffusion_ref, walls_ref, through_ref, table_ref, held_ref, sems,
):
    total = cells * blocks
    components = near_velocity_ref.shape[0]
    row_tiles = diffusion_ref.shape[0] // SUB
    half = row_tiles // 2
    me = lax.axis_index("gz")
    chip = me // 2
    first = chip * 2
    sides = ((away_ref, far_velocity_ref, 1 - (me - first)), (mine_ref, near_velocity_ref, me - first))
    small = [
        pltpu.make_async_copy(index_hbm, index_ref, sems.at[0]),
        pltpu.make_async_copy(diffusion_hbm, diffusion_ref, sems.at[1]),
        pltpu.make_async_copy(walls_hbm, walls_ref, sems.at[2]),
    ]
    large = [
        pltpu.make_async_copy(
            velocity_hbm.at[:, :, pl.ds(pl.multiple_of(whose * half * SUB, SUB), half * SUB)],
            ref, sems.at[3 + i])
        for i, (_, ref, whose) in enumerate(sides)
    ]
    for copy in small + large:
        copy.start()
    for copy in small:
        copy.wait()
    diffusion = diffusion_ref[...]
    inverse = 1.0 / diffusion
    state_ref[3] = inverse
    for i in range(STRETCHES):
        table_ref[i] = (0.5 + 0.25 * i) * inverse
    walls = walls_ref[...]

    def wall(bits, k):
        face = 1.0 / jnp.full((SUB, diffusion.shape[1]), 0.5 * height(index_ref, k))
        return bits.astype(jnp.float32) * jnp.concatenate([face] * row_tiles, axis=0)

    lower = wall(walls & 1, 0)
    upper = wall(walls >> 1, total - 1)

    def forward(block, kappa, keep=None):
        start = block * cells
        flux = table_ref[index_ref[start]] + kappa
        value = jnp.ones_like(flux)
        for j in range(cells):
            if keep is not None:
                keep(j, flux, value)
            k = start + j
            if j < cells - 1:
                value = value + half_sum(index_ref, k) * flux
                flux = flux + table_ref[index_ref[k + 1]] * value
        k = jnp.minimum(start + cells - 1, total - 2)
        after = 1.0 / (value + half_sum(index_ref, k) * flux)
        return flux * after, after

    def backward(block, kappa, scale=None, keep=None):
        start = block * cells
        flux = table_ref[index_ref[start + cells - 1]] + kappa
        value = jnp.ones_like(flux)
        if scale is not None:
            flux, value = flux * scale, scale
        for j in reversed(range(cells)):
            if keep is not None:
                keep(j, flux, value)
            k = start + j
            if j > 0:
                value = value + half_sum(index_ref, k - 1) * flux
                flux = flux + table_ref[index_ref[k - 1]] * value
        k = jnp.maximum(start - 1, 0)
        after = 1.0 / (value + half_sum(index_ref, k) * flux)
        return flux * after, after

    def thickness(block):
        parts = [height(index_ref, block * cells + j) for j in range(cells)]
        return functools.reduce(jnp.add, parts)

    def sweep_forward(block, state):
        kappa, product, extent = state
        kappa, after = forward(block, kappa)
        through_ref[block] = after
        return kappa, product * after, extent + thickness(block)

    def sweep_backward(step, state):
        block = blocks - 1 - step
        kappa, product, extent = state
        kappa, after = backward(block, kappa)
        through_ref[block] = after
        return kappa, product * after, extent + thickness(block)

    ones = jnp.ones_like(diffusion)
    kappa_left, product, extent = lax.fori_loop(
        0, me, sweep_forward, (lower, ones, thickness(me))
    )
    ends_ref[0] = diffusion * lower * product
    state_ref[0] = kappa_left
    state = {}

    def keep_left(j, flux, value):
        left_h_ref[j] = height(index_ref, me * cells + j) * value
        state["flux"], state["value"] = flux, value

    kappa, own_forward = forward(me, kappa_left, keep_left)
    held_ref[1] = own_forward
    held_ref[3] = state["flux"]
    held_ref[4] = state["value"]
    held_ref[5] = state["flux"] - kappa_left

    @pl.when(me == first)
    def _():
        pair_ref[2] = own_forward
        _, after = forward(me + 1, kappa)
        pair_ref[0] = after

    @pl.when(me != first)
    def _():
        pair_ref[2] = through_ref[first]
        pair_ref[0] = own_forward

    kappa_right, product, extent = lax.fori_loop(
        0, blocks - 1 - me, sweep_backward, (upper, ones, extent)
    )
    ends_ref[1] = diffusion_ref[...] * upper * product
    scale = 1.0 / (diffusion_ref[...] * (held_ref[3] + kappa_right * held_ref[4]))
    held_ref[0] = scale

    state_ref[1] = kappa_right
    state_ref[2] = scale

    def keep_right(j, flux, value):
        right_h_ref[j] = height(index_ref, me * cells + j) * value
        state["flux"] = flux

    kappa, own_backward = backward(me, kappa_right, scale, keep_right)
    held_ref[2] = own_backward
    held_ref[6] = state["flux"] - kappa_right * scale

    @pl.when(me == first)
    def _():
        pair_ref[1] = own_backward * held_ref[0]
        pair_ref[3] = through_ref[first + 1]

    @pl.when(me != first)
    def _():
        pair_ref[3] = own_backward * held_ref[0]
        _, after = backward(me - 1, kappa)
        pair_ref[1] = after

    for m in range(1, chips):
        other = chip ^ m
        low = jnp.minimum(chip, other)
        high = jnp.maximum(chip, other)
        chip_ref[m - 1] = lax.fori_loop(
            low + 1,
            high,
            lambda r, product: product * (through_ref[2 * r] * through_ref[2 * r + 1]),
            ones,
        )
    flow = jnp.zeros((SUB, LANES), jnp.float32)
    weight = jnp.zeros((SUB, LANES), jnp.float32)

    def fold(array):
        parts = [array[:, i * LANES:(i + 1) * LANES] for i in range(array.shape[1] // LANES)]
        return functools.reduce(jnp.add, parts)

    for copy in large:
        copy.wait()
    volume_ref[...] = jnp.full(volume_ref.shape, extent * lines)
    own_extent = thickness(me)
    heights = [height(index_ref, me * cells + j) for j in range(cells)]
    for j in range(cells):
        heights_ref[j] = jnp.full((SUB, LANES), heights[j])
    for ref, velocity_ref, whose in sides:
        for i in range(half):
            rows = row_tile(whose * half + i)
            near = slice(i * SUB, (i + 1) * SUB)
            from_left = [0.0] * components
            from_right = [0.0] * components
            plain = 0.0
            for j in range(cells):
                left = left_h_ref[j, rows]
                right = right_h_ref[j, rows]
                for c in range(components):
                    v = velocity_ref[c, j, near]
                    from_left[c] = from_left[c] + left * v
                    from_right[c] = from_right[c] + right * v
                    if c == 0:
                        plain = plain + heights[j] * v
            for c in range(components):
                ref[i * 2 * components + c] = from_left[c] * held_ref[1, rows]
                ref[i * 2 * components + components + c] = from_right[c] * held_ref[2, rows]
            low_part = ends_ref[0, rows]
            high_part = ends_ref[1, rows] * held_ref[0, rows]
            flow = flow + fold(plain - low_part * from_right[0] - high_part * from_left[0])
            totals = low_part * held_ref[6, rows] + high_part * held_ref[5, rows]
            weight = weight + fold(own_extent - diffusion_ref[rows] * totals)
    middle = SUB // 2
    tile_ref[0:middle] = flow[0:middle] + flow[middle:]
    tile_ref[middle:] = weight[0:middle] + weight[middle:]


def copies_kernel(tile_ref, volume_ref, target_ref, tiles_ref, goal_ref):
    tile = tile_ref[...]
    for i in range(tiles_ref.shape[0]):
        tiles_ref[i] = tile
    goal_ref[...] = target_ref[...] * volume_ref[...]


def merge_kernel(chips, components, mine_ref, mate_ref, pair_ref, *rest):
    send_refs, near_ref = rest[1:-1], rest[-1]
    me = lax.axis_index("gz")
    chip = me // 2
    is_first = me == chip * 2
    half = mine_ref.shape[0] // (2 * components)
    for i in range(half):
        rows = row_tile((me - chip * 2) * half + i)
        for c in range(components):
            at = i * 2 * components + c
            mine, mate = mine_ref[at], mate_ref[at]
            first = jnp.where(is_first, mine, mate)
            second = jnp.where(is_first, mate, mine)
            near_ref[at] = first
            to_right = second + pair_ref[0, rows] * first
            at = at + components
            mine, mate = mine_ref[at], mate_ref[at]
            first = jnp.where(is_first, mine, mate)
            second = jnp.where(is_first, mate, mine)
            near_ref[at] = second
            to_left = first + pair_ref[1, rows] * second
            for m in range(1, chips):
                goes_right = (chip ^ m) > chip
                send_refs[m - 1][i * components + c] = jnp.where(goes_right, to_right, to_left)


def spread_kernel(chips, components, near_ref, pair_ref, chip_ref, *rest):
    recv_refs, (own_ref, other_ref) = rest[:chips - 1], rest[chips - 1:]
    me = lax.axis_index("gz")
    chip = me // 2
    is_first = me == chip * 2
    half = near_ref.shape[0] // (2 * components)
    for i in range(half):
        rows = row_tile((me - chip * 2) * half + i)
        coefs = [chip_ref[m, rows] for m in range(chips - 1)]
        for c in range(components):
            left_in = jnp.zeros(near_ref.shape[1:], jnp.float32)
            right_in = jnp.zeros(near_ref.shape[1:], jnp.float32)
            for m in range(1, chips):
                term = coefs[m - 1] * recv_refs[m - 1][i * components + c]
                from_left = (chip ^ m) < chip
                left_in = left_in + jnp.where(from_left, term, 0.0)
                right_in = right_in + jnp.where(from_left, 0.0, term)
            at = i * 2 * components + c
            left_second = near_ref[at] + pair_ref[2, rows] * left_in
            right_first = near_ref[at + components] + pair_ref[3, rows] * right_in
            own_ref[at] = jnp.where(is_first, left_in, left_second)
            other_ref[at] = jnp.where(is_first, left_second, left_in)
            at = at + components
            own_ref[at] = jnp.where(is_first, right_first, right_in)
            other_ref[at] = jnp.where(is_first, right_in, right_first)


def leave(copies, source, target, sems):
    copies.append(pltpu.make_async_copy(source, target, sems.at[len(copies)]))
    copies[-1].start()


def finish(i, rows, incoming_ref, ends_ref, heights_ref, velocity_ref, low_ref, high_ref,
           plain_ref, unit_ref, result_ref):
    components, cells, _, lines_x = velocity_ref.shape
    near = slice(i * SUB, (i + 1) * SUB)
    scale = high_ref[cells - 1, near]

    def place(c):
        return (plain_ref, ()) if c == 0 else (result_ref, (c - 1,))

    below = [incoming_ref[i * 2 * components + c] for c in range(components)]
    above = [
        incoming_ref[i * 2 * components + components + c] * scale for c in range(components)
    ]
    for j in reversed(range(cells)):
        low = low_ref[j, near]
        high = wide(heights_ref[j], lines_x) * high_ref[j, near]
        for c in range(components):
            ref, at = place(c)
            ref[at + (j, near)] = low * above[c]
            if j > 0:
                above[c] = above[c] + high * velocity_ref[c, j, near]
    low_part = ends_ref[0, rows]
    high_part = ends_ref[1, rows] * scale
    for j in range(cells):
        low = low_ref[j, near]
        high = high_ref[j, near]
        weighted = wide(heights_ref[j], lines_x) * low
        for c in range(components):
            below[c] = below[c] + weighted * velocity_ref[c, j, near]
            ref, at = place(c)
            ref[at + (j, near)] = ref[at + (j, near)] + high * below[c]
        unit_ref[j, near] = 1.0 - (low_part * high + high_part * low)


def profiles(part, heights_ref, state_ref, low_ref, high_ref):
    cells, middle, lines_x = low_ref.shape
    heights = [
        jnp.concatenate([wide(heights_ref[j], lines_x)] * (middle // SUB), axis=0)
        for j in range(cells)
    ]
    inverse = state_ref[3, part]
    flux = heights[0] * inverse + state_ref[0, part]
    value = jnp.ones_like(flux)
    for j in range(cells):
        low_ref[j] = value
        if j < cells - 1:
            value = value + (0.5 * (heights[j] + heights[j + 1])) * flux
            flux = flux + (heights[j + 1] * inverse) * value
    scale = state_ref[2, part]
    flux = (heights[cells - 1] * inverse + state_ref[1, part]) * scale
    value = scale
    for j in reversed(range(cells)):
        high_ref[j] = value
        if j > 0:
            value = value + (0.5 * (heights[j] + heights[j - 1])) * flux
            flux = flux + (heights[j - 1] * inverse) * value


def early_kernel(
    velocity_hbm, near_velocity_ref, heights_ref, state_ref, ends_ref, own_ref,
    out_hbm, plain_ref, unit_ref, far_velocity_ref, left_ref, right_ref,
    low_ref, high_ref, result_ref, arrival, sems,
):
    components, cells, middle, _ = near_velocity_ref.shape
    half = middle // SUB
    me = lax.axis_index("gz")
    starts = [lax.rem(me, 2) * middle, (1 - lax.rem(me, 2)) * middle]
    parts = [pl.ds(pl.multiple_of(start, SUB), middle) for start in starts]
    load = pltpu.make_async_copy(velocity_hbm.at[:, :, parts[1]], far_velocity_ref, arrival)
    load.start()
    copies = []
    profiles(parts[0], heights_ref, state_ref, low_ref, high_ref)
    for i in range(half):
        rows = row_tile(lax.rem(me, 2) * half + i)
        finish(i, rows, own_ref, ends_ref, heights_ref, near_velocity_ref, low_ref, high_ref,
               plain_ref, unit_ref, result_ref)
        for c in range(1, components):
            leave(copies, result_ref.at[c - 1, :, i * SUB:(i + 1) * SUB],
                  out_hbm.at[c, :, rows], sems)
    profiles(parts[1], heights_ref, state_ref, left_ref, right_ref)
    load.wait()
    for copy in copies:
        copy.wait()


def late_kernel(
    heights_ref, ends_ref, other_ref, far_velocity_ref, left_ref, right_ref, _,
    out_hbm, plain_ref, unit_ref, result_ref, sems,
):
    components, cells, middle, _ = far_velocity_ref.shape
    half = middle // SUB
    me = lax.axis_index("gz")
    copies = []
    for i in range(half):
        rows = row_tile((1 - lax.rem(me, 2)) * half + i)
        finish(i, rows, other_ref, ends_ref, heights_ref, far_velocity_ref, left_ref, right_ref,
               plain_ref, unit_ref, result_ref)
        for c in range(1, components):
            leave(copies, result_ref.at[c - 1, :, i * SUB:(i + 1) * SUB],
                  out_hbm.at[c, :, rows], sems)
    for copy in copies:
        copy.wait()


def correct_kernel(
    goal_ref, tiles_ref, own_plain_ref, own_unit_ref, other_plain_ref, other_unit_ref,
    _, out_hbm, result_ref, sems,
):
    totals = functools.reduce(jnp.add, [tiles_ref[i] for i in range(tiles_ref.shape[0])])
    flow = jnp.sum(totals[0:SUB // 2], keepdims=True)
    weight = jnp.sum(totals[SUB // 2:], keepdims=True)
    alpha = (goal_ref[0:1, 0:1] - flow) / weight
    cells, middle, _ = own_plain_ref.shape
    half = middle // SUB
    me = lax.axis_index("gz")
    sides = (
        (lax.rem(me, 2), own_plain_ref, own_unit_ref),
        (1 - lax.rem(me, 2), other_plain_ref, other_unit_ref),
    )
    copies = []
    for whose, plain_ref, unit_ref in sides:
        for i in range(half):
            rows = row_tile(whose * half + i)
            near = slice(i * SUB, (i + 1) * SUB)
            for j in range(cells):
                result_ref[j, rows] = plain_ref[j, near] + alpha * unit_ref[j, near]
            leave(copies, result_ref.at[:, rows], out_hbm.at[0, :, rows], sems)
    for copy in copies:
        copy.wait()


def shards(velocity, diffusion, wall_types, stretch_index, bulk_target):
    blocks = lax.axis_size("gz")
    columns = lax.axis_size("gy")
    components, cells, lines_y, lines_x = velocity.shape
    chips = blocks // 2
    row_tiles = lines_y // SUB
    half = row_tiles // 2
    f32 = jnp.float32
    vmem = pl.BlockSpec(memory_space=pltpu.VMEM)
    anywhere = pl.BlockSpec(memory_space=pl.ANY)
    plane = (lines_y, lines_x)
    sheet = (SUB, lines_x)

    def shape(*dims):
        return jax.ShapeDtypeStruct(dims, f32)

    def in_hbm(array):
        return pltpu.with_memory_space_constraint(array, pltpu.HBM)

    def options(mib):
        return pltpu.CompilerParams(vmem_limit_bytes=mib * MIB)

    def cost(flops, transferred):
        return pl.CostEstimate(flops=flops, bytes_accessed=transferred, transcendentals=0)

    def send(array, partner):
        pairs = [((z, y), partner(z, y)) for z in range(blocks) for y in range(columns)]
        route = [(a * columns + b, c * columns + d) for (a, b), (c, d) in pairs]
        return lax.ppermute(array, ("gz", "gy"), route)

    def to_mate(array):
        return send(array, lambda z, y: (z ^ 1, y))

    middle = half * SUB
    lines = float(lines_y * columns * lines_x)
    (mine, away, pair, chip_coefs, ends, state, heights, near_velocity, tile,
     volume) = pl.pallas_call(
        functools.partial(ladder_kernel, cells, blocks, chips, lines),
        out_shape=[
            shape(half * 2 * components, *sheet),
            shape(half * 2 * components, *sheet),
            shape(4, *plane),
            shape(chips - 1, *plane),
            shape(2, *plane),
            shape(4, *plane),
            shape(cells, SUB, LANES),
            shape(components, cells, middle, lines_x),
            shape(SUB, LANES),
            shape(SUB, LANES),
        ],
        in_specs=[anywhere] * 4,
        out_specs=[vmem] * 10,
        scratch_shapes=[
            pltpu.VMEM((cells,) + plane, f32),
            pltpu.VMEM((cells,) + plane, f32),
            pltpu.VMEM((components, cells, middle, lines_x), f32),
            pltpu.SMEM(stretch_index.shape, jnp.int32),
            pltpu.VMEM(plane, f32),
            pltpu.VMEM(plane, jnp.int32),
            pltpu.VMEM((blocks,) + plane, f32),
            pltpu.VMEM((STRETCHES,) + plane, f32),
            pltpu.VMEM((7,) + plane, f32),
            pltpu.SemaphoreType.DMA((5,)),
        ],
        compiler_params=options(24),
        cost_estimate=cost(40_000_000, 6_000_000),
        name="ladder",
    )(in_hbm(stretch_index), in_hbm(diffusion), in_hbm(wall_types), in_hbm(velocity))

    mate = to_mate(away)
    tile_copies, goal = pl.pallas_call(
        copies_kernel,
        out_shape=[shape(blocks * columns, SUB, LANES), shape(SUB, LANES)],
        in_specs=[vmem] * 3,
        out_specs=[vmem] * 2,
        compiler_params=options(16),
        cost_estimate=cost(10_000, 200_000),
        name="copies",
    )(tile, volume, bulk_target.reshape(1, 1))
    tiles = lax.all_to_all(tile_copies, ("gz", "gy"), 0, 0, tiled=True)
    *outgoing, near = pl.pallas_call(
        functools.partial(merge_kernel, chips, components),
        out_shape=[shape(half * components, *sheet)] * (chips - 1)
        + [shape(half * 2 * components, *sheet)],
        in_specs=[vmem] * 3 + [anywhere],
        out_specs=[vmem] * chips,
        compiler_params=options(16),
        cost_estimate=cost(500_000, 1_600_000),
        name="merge",
    )(mine, mate, pair, goal)
    incoming = [
        send(outgoing[m - 1], lambda z, y: (z ^ (2 * m), y)) for m in range(1, chips)
    ]
    own_in, other_out = pl.pallas_call(
        functools.partial(spread_kernel, chips, components),
        out_shape=[shape(half * 2 * components, *sheet)] * 2,
        in_specs=[vmem] * (3 + chips - 1),
        out_specs=[vmem] * 2,
        compiler_params=options(16),
        cost_estimate=cost(500_000, 1_600_000),
        name="spread",
    )(near, pair, chip_coefs, *incoming)
    other_in = to_mate(other_out)
    part = (components, cells, middle, lines_x)
    profile = shape(cells, middle, lines_x)
    partial, own_plain, own_unit, far_velocity, left, right = pl.pallas_call(
        early_kernel,
        out_shape=[shape(*velocity.shape), profile, profile, shape(*part), profile, profile],
        in_specs=[anywhere] + [vmem] * 5,
        out_specs=[anywhere] + [vmem] * 5,
        scratch_shapes=[
            pltpu.VMEM((cells, middle, lines_x), f32),
            pltpu.VMEM((cells, middle, lines_x), f32),
            pltpu.VMEM((components - 1, cells, middle, lines_x), f32),
            pltpu.SemaphoreType.DMA,
            pltpu.SemaphoreType.DMA(((components - 1) * half,)),
        ],
        compiler_params=options(24),
        cost_estimate=cost(8_000_000, 8_000_000),
        name="early",
    )(in_hbm(velocity), near_velocity, heights, state, ends, own_in)
    partial, other_plain, other_unit = pl.pallas_call(
        late_kernel,
        out_shape=[shape(*velocity.shape), profile, profile],
        in_specs=[vmem] * 6 + [anywhere],
        out_specs=[anywhere] + [vmem] * 2,
        scratch_shapes=[
            pltpu.VMEM((components - 1, cells, middle, lines_x), f32),
            pltpu.SemaphoreType.DMA(((components - 1) * half,)),
        ],
        input_output_aliases={6: 0},
        compiler_params=options(16),
        cost_estimate=cost(3_000_000, 6_000_000),
        name="late",
    )(heights, ends, other_in, far_velocity, left, right, partial)
    return pl.pallas_call(
        correct_kernel,
        out_shape=shape(*velocity.shape),
        in_specs=[vmem] * 6 + [anywhere],
        out_specs=anywhere,
        scratch_shapes=[
            pltpu.VMEM((cells,) + plane, f32),
            pltpu.SemaphoreType.DMA((row_tiles,)),
        ],
        input_output_aliases={6: 0},
        compiler_params=options(16),
        cost_estimate=cost(500_000, 1_600_000),
        name="correct",
    )(goal, tiles, own_plain, own_unit, other_plain, other_unit, partial)


def solution(mesh):
    return jax.shard_map(
        shards,
        mesh=mesh,
        in_specs=(P(None, "gz", "gy", None), P("gy", None), P("gy", None), P(), P()),
        out_specs=P(None, "gz", "gy", None),
        check_vma=False,
    )
```

```python
import functools

import jax
import jax.numpy as jnp
from jax import lax
from jax.experimental import pallas as pl
from jax.experimental.pallas import tpu as pltpu
from jax.sharding import PartitionSpec as P

SUB = 8
STRETCHES = 7
LANES = 128
MIB = 1024 * 1024


def row_tile(t):
    return pl.ds(pl.multiple_of(t * SUB, SUB), SUB)


def height(index_ref, k):
    return 0.5 + 0.25 * index_ref[k].astype(jnp.float32)


def half_sum(index_ref, k):
    return 0.5 * (height(index_ref, k) + height(index_ref, k + 1))


def ladder_kernel(
    cells, blocks, chips, lines,
    index_hbm, diffusion_hbm, walls_hbm, velocity_hbm,
    mine_ref, away_ref, pair_ref, chip_ref, left_ref, right_ref, left_h_ref, right_h_ref,
    ends_ref, volume_ref, velocity_ref,
    index_ref, diffusion_ref, walls_ref, through_ref, table_ref, held_ref, sems,
):
    total = cells * blocks
    components = velocity_ref.shape[0]
    row_tiles = diffusion_ref.shape[0] // SUB
    small = [
        pltpu.make_async_copy(index_hbm, index_ref, sems.at[0]),
        pltpu.make_async_copy(diffusion_hbm, diffusion_ref, sems.at[1]),
        pltpu.make_async_copy(walls_hbm, walls_ref, sems.at[2]),
    ]
    large = [
        pltpu.make_async_copy(velocity_hbm.at[c], velocity_ref.at[c], sems.at[3 + c])
        for c in range(components)
    ]
    for copy in small + large:
        copy.start()
    me = lax.axis_index("gz")
    chip = me // 2
    first = chip * 2
    for copy in small:
        copy.wait()
    diffusion = diffusion_ref[...]
    inverse = 1.0 / diffusion
    for i in range(STRETCHES):
        table_ref[i] = (0.5 + 0.25 * i) * inverse
    walls = walls_ref[...]

    def wall(bits, k):
        face = 1.0 / jnp.full((SUB, diffusion.shape[1]), 0.5 * height(index_ref, k))
        return bits.astype(jnp.float32) * jnp.concatenate([face] * row_tiles, axis=0)

    lower = wall(walls & 1, 0)
    upper = wall(walls >> 1, total - 1)

    def forward(block, kappa, keep=None):
        start = block * cells
        flux = table_ref[index_ref[start]] + kappa
        value = jnp.ones_like(flux)
        for j in range(cells):
            if keep is not None:
                keep(j, flux, value)
            k = start + j
            if j < cells - 1:
                value = value + half_sum(index_ref, k) * flux
                flux = flux + table_ref[index_ref[k + 1]] * value
        k = jnp.minimum(start + cells - 1, total - 2)
        after = 1.0 / (value + half_sum(index_ref, k) * flux)
        return flux * after, after

    def backward(block, kappa, scale=None, keep=None):
        start = block * cells
        flux = table_ref[index_ref[start + cells - 1]] + kappa
        value = jnp.ones_like(flux)
        if scale is not None:
            flux, value = flux * scale, scale
        for j in reversed(range(cells)):
            if keep is not None:
                keep(j, flux, value)
            k = start + j
            if j > 0:
                value = value + half_sum(index_ref, k - 1) * flux
                flux = flux + table_ref[index_ref[k - 1]] * value
        k = jnp.maximum(start - 1, 0)
        after = 1.0 / (value + half_sum(index_ref, k) * flux)
        return flux * after, after

    def thickness(block):
        parts = [height(index_ref, block * cells + j) for j in range(cells)]
        return functools.reduce(jnp.add, parts)

    def sweep_forward(block, state):
        kappa, product, extent = state
        kappa, after = forward(block, kappa)
        through_ref[block] = after
        return kappa, product * after, extent + thickness(block)

    def sweep_backward(step, state):
        block = blocks - 1 - step
        kappa, product, extent = state
        kappa, after = backward(block, kappa)
        through_ref[block] = after
        return kappa, product * after, extent + thickness(block)

    ones = jnp.ones_like(diffusion)
    kappa_left, product, extent = lax.fori_loop(
        0, me, sweep_forward, (lower, ones, thickness(me))
    )
    ends_ref[0] = diffusion * lower * product
    state = {}

    def keep_left(j, flux, value):
        left_ref[j] = value
        left_h_ref[j] = height(index_ref, me * cells + j) * value
        state["flux"], state["value"] = flux, value

    kappa, own_forward = forward(me, kappa_left, keep_left)
    held_ref[1] = own_forward
    held_ref[3] = state["flux"]
    held_ref[4] = state["value"]
    held_ref[5] = state["flux"] - kappa_left

    @pl.when(me == first)
    def _():
        pair_ref[2] = own_forward
        _, after = forward(me + 1, kappa)
        pair_ref[0] = after

    @pl.when(me != first)
    def _():
        pair_ref[2] = through_ref[first]
        pair_ref[0] = own_forward

    kappa_right, product, extent = lax.fori_loop(
        0, blocks - 1 - me, sweep_backward, (upper, ones, extent)
    )
    ends_ref[1] = diffusion_ref[...] * upper * product
    scale = 1.0 / (diffusion_ref[...] * (held_ref[3] + kappa_right * held_ref[4]))
    held_ref[0] = scale

    def keep_right(j, flux, value):
        right_ref[j] = value
        right_h_ref[j] = height(index_ref, me * cells + j) * value
        state["flux"] = flux

    kappa, own_backward = backward(me, kappa_right, scale, keep_right)
    held_ref[2] = own_backward
    held_ref[6] = state["flux"] - kappa_right * scale

    @pl.when(me == first)
    def _():
        pair_ref[1] = own_backward * held_ref[0]
        pair_ref[3] = through_ref[first + 1]

    @pl.when(me != first)
    def _():
        pair_ref[3] = own_backward * held_ref[0]
        _, after = backward(me - 1, kappa)
        pair_ref[1] = after

    for m in range(1, chips):
        other = chip ^ m
        low = jnp.minimum(chip, other)
        high = jnp.maximum(chip, other)
        chip_ref[m - 1] = lax.fori_loop(
            low + 1,
            high,
            lambda r, product: product * (through_ref[2 * r] * through_ref[2 * r + 1]),
            ones,
        )
    flow = jnp.zeros((SUB, LANES), jnp.float32)
    weight = jnp.zeros((SUB, LANES), jnp.float32)

    def fold(array):
        parts = [array[:, i * LANES:(i + 1) * LANES] for i in range(array.shape[1] // LANES)]
        return functools.reduce(jnp.add, parts)

    for copy in large:
        copy.wait()
    volume_ref[...] = jnp.full(volume_ref.shape, extent * lines)
    half = row_tiles // 2
    own_extent = thickness(me)
    heights = [height(index_ref, me * cells + j) for j in range(cells)]
    for ref, whose in ((away_ref, 1 - (me - first)), (mine_ref, me - first)):
        for i in range(half):
            rows = row_tile(whose * half + i)
            from_left = [0.0] * components
            from_right = [0.0] * components
            plain = 0.0
            for j in range(cells):
                left = left_h_ref[j, rows]
                right = right_h_ref[j, rows]
                for c in range(components):
                    v = velocity_ref[c, j, rows]
                    from_left[c] = from_left[c] + left * v
                    from_right[c] = from_right[c] + right * v
                    if c == 0:
                        plain = plain + heights[j] * v
            for c in range(components):
                ref[i * 2 * components + c] = from_left[c] * held_ref[1, rows]
                ref[i * 2 * components + components + c] = from_right[c] * held_ref[2, rows]
            low_part = ends_ref[0, rows]
            high_part = ends_ref[1, rows] * held_ref[0, rows]
            flow = flow + fold(plain - low_part * from_right[0] - high_part * from_left[0])
            totals = low_part * held_ref[6, rows] + high_part * held_ref[5, rows]
            weight = weight + fold(own_extent - diffusion_ref[rows] * totals)
    slot = half * 2 * components
    away_ref[slot] = jnp.zeros(away_ref.shape[1:], jnp.float32)
    away_ref[slot, :, 0:LANES] = flow
    away_ref[slot, :, LANES:2 * LANES] = weight


def merge_kernel(chips, components, mine_ref, away_ref, mate_ref, pair_ref, *rest):
    send_refs, near_ref = rest[:-1], rest[-1]
    me = lax.axis_index("gz")
    chip = me // 2
    is_first = me == chip * 2
    half = mine_ref.shape[0] // (2 * components)
    slot = half * 2 * components
    tile = away_ref[slot] + mate_ref[slot]
    near_ref[slot] = tile
    for ref in send_refs:
        ref[half * components] = tile
    for i in range(half):
        rows = row_tile((me - chip * 2) * half + i)
        for c in range(components):
            at = i * 2 * components + c
            mine, mate = mine_ref[at], mate_ref[at]
            first = jnp.where(is_first, mine, mate)
            second = jnp.where(is_first, mate, mine)
            near_ref[at] = first
            to_right = second + pair_ref[0, rows] * first
            at = at + components
            mine, mate = mine_ref[at], mate_ref[at]
            first = jnp.where(is_first, mine, mate)
            second = jnp.where(is_first, mate, mine)
            near_ref[at] = second
            to_left = first + pair_ref[1, rows] * second
            for m in range(1, chips):
                goes_right = (chip ^ m) > chip
                send_refs[m - 1][i * components + c] = jnp.where(goes_right, to_right, to_left)


def spread_kernel(chips, components, near_ref, pair_ref, chip_ref, *rest):
    recv_refs, (own_ref, other_ref, tile_ref) = rest[1:chips], rest[chips:]
    me = lax.axis_index("gz")
    chip = me // 2
    is_first = me == chip * 2
    half = near_ref.shape[0] // (2 * components)
    tile = near_ref[half * 2 * components]
    for ref in recv_refs:
        tile = tile + ref[half * components]
    tile_ref[0] = tile[:, 0:LANES]
    tile_ref[1] = tile[:, LANES:2 * LANES]
    for i in range(half):
        rows = row_tile((me - chip * 2) * half + i)
        coefs = [chip_ref[m, rows] for m in range(chips - 1)]
        for c in range(components):
            left_in = jnp.zeros(near_ref.shape[1:], jnp.float32)
            right_in = jnp.zeros(near_ref.shape[1:], jnp.float32)
            for m in range(1, chips):
                term = coefs[m - 1] * recv_refs[m - 1][i * components + c]
                from_left = (chip ^ m) < chip
                left_in = left_in + jnp.where(from_left, term, 0.0)
                right_in = right_in + jnp.where(from_left, 0.0, term)
            at = i * 2 * components + c
            left_second = near_ref[at] + pair_ref[2, rows] * left_in
            right_first = near_ref[at + components] + pair_ref[3, rows] * right_in
            own_ref[at] = jnp.where(is_first, left_in, left_second)
            other_ref[at] = jnp.where(is_first, left_second, left_in)
            at = at + components
            own_ref[at] = jnp.where(is_first, right_first, right_in)
            other_ref[at] = jnp.where(is_first, right_in, right_first)


def leave(copies, source, target, sems):
    copies.append(pltpu.make_async_copy(source, target, sems.at[len(copies)]))
    copies[-1].start()


def inner_kernel(
    velocity_ref, left_ref, right_ref, left_h_ref, right_h_ref, ends_ref, volume_ref, target_ref,
    _, base_ref, unit_ref, goal_ref,
):
    components, cells, lines_y, lines_x = velocity_ref.shape
    goal_ref[...] = target_ref[...] * volume_ref[...]
    for t in range(lines_y // SUB):
        rows = row_tile(t)
        gathered = [jnp.zeros((SUB, lines_x), jnp.float32)] * components
        for j in reversed(range(cells)):
            left = left_ref[j, rows]
            right = right_h_ref[j, rows]
            for c in range(components):
                base_ref[c, j, rows] = left * gathered[c]
                if j > 0:
                    gathered[c] = gathered[c] + right * velocity_ref[c, j, rows]
        gathered = [jnp.zeros((SUB, lines_x), jnp.float32)] * components
        low_part = ends_ref[0, rows]
        high_part = ends_ref[1, rows] * right_ref[cells - 1, rows]
        for j in range(cells):
            left = left_h_ref[j, rows]
            right = right_ref[j, rows]
            unit_ref[j, rows] = 1.0 - (low_part * right + high_part * left_ref[j, rows])
            for c in range(components):
                gathered[c] = gathered[c] + left * velocity_ref[c, j, rows]
                base_ref[c, j, rows] = base_ref[c, j, rows] + right * gathered[c]


def finish_kernel(side, incoming_ref, base_ref, left_ref, right_ref, *rest):
    out_hbm, plain_ref, result_ref, sems = rest[-4:]
    components, cells, _, _ = base_ref.shape
    half = incoming_ref.shape[0] // (2 * components)
    me = lax.axis_index("gz")
    copies = []
    for i in range(half):
        rows = row_tile(lax.rem(me + side, 2) * half + i)
        near = slice(i * SUB, (i + 1) * SUB)
        scale = right_ref[cells - 1, rows]
        at = i * 2 * components
        lefts = [incoming_ref[at + c] for c in range(components)]
        rights = [incoming_ref[at + components + c] * scale for c in range(components)]
        for j in range(cells):
            left = left_ref[j, rows]
            right = right_ref[j, rows]
            for c in range(components):
                value = base_ref[c, j, rows] + (right * lefts[c] + left * rights[c])
                if c == 0:
                    plain_ref[j, near] = value
                else:
                    result_ref[c - 1, j, near] = value
        for c in range(1, components):
            leave(copies, result_ref.at[c - 1, :, near], out_hbm.at[c, :, rows], sems)
    for copy in copies:
        copy.wait()


def correct_kernel(columns, goal_ref, unit_ref, *rest):
    tile_refs, plain_refs = rest[:columns], rest[columns:columns + 2]
    out_hbm, result_ref, sems = rest[-3:]
    totals = functools.reduce(jnp.add, [ref[...] for ref in tile_refs])
    flow = jnp.sum(totals[0], keepdims=True)
    weight = jnp.sum(totals[1], keepdims=True)
    alpha = (goal_ref[0:1, 0:1] - flow) / weight
    cells, middle, _ = plain_refs[0].shape
    half = middle // SUB
    me = lax.axis_index("gz")
    copies = []
    for side, plain_ref in enumerate(plain_refs):
        for i in range(half):
            rows = row_tile(lax.rem(me + side, 2) * half + i)
            for j in range(cells):
                plain = plain_ref[j, i * SUB:(i + 1) * SUB]
                result_ref[j, rows] = plain + alpha * unit_ref[j, rows]
            leave(copies, result_ref.at[:, rows], out_hbm.at[0, :, rows], sems)
    for copy in copies:
        copy.wait()


def shards(velocity, diffusion, wall_types, stretch_index, bulk_target):
    blocks = lax.axis_size("gz")
    columns = lax.axis_size("gy")
    components, cells, lines_y, lines_x = velocity.shape
    chips = blocks // 2
    row_tiles = lines_y // SUB
    half = row_tiles // 2
    f32 = jnp.float32
    vmem = pl.BlockSpec(memory_space=pltpu.VMEM)
    anywhere = pl.BlockSpec(memory_space=pl.ANY)
    plane = (lines_y, lines_x)
    sheet = (SUB, lines_x)

    def shape(*dims):
        return jax.ShapeDtypeStruct(dims, f32)

    def in_hbm(array):
        return pltpu.with_memory_space_constraint(array, pltpu.HBM)

    def options(mib):
        return pltpu.CompilerParams(vmem_limit_bytes=mib * MIB)

    def cost(flops, transferred):
        return pl.CostEstimate(flops=flops, bytes_accessed=transferred, transcendentals=0)

    def send(array, partner):
        pairs = [((z, y), partner(z, y)) for z in range(blocks) for y in range(columns)]
        route = [(a * columns + b, c * columns + d) for (a, b), (c, d) in pairs]
        return lax.ppermute(array, ("gz", "gy"), route)

    def to_mate(array):
        return send(array, lambda z, y: (z ^ 1, y))

    middle = half * SUB
    lines = float(lines_y * columns * lines_x)
    (mine, away, pair, chip_coefs, left, right, left_h, right_h, ends, volume,
     near_velocity) = pl.pallas_call(
        functools.partial(ladder_kernel, cells, blocks, chips, lines),
        out_shape=[
            shape(half * 2 * components, *sheet),
            shape(half * 2 * components + 1, *sheet),
            shape(4, *plane),
            shape(chips - 1, *plane),
            shape(cells, *plane),
            shape(cells, *plane),
            shape(cells, *plane),
            shape(cells, *plane),
            shape(2, *plane),
            shape(SUB, LANES),
            shape(*velocity.shape),
        ],
        in_specs=[anywhere] * 4,
        out_specs=[vmem] * 11,
        scratch_shapes=[
            pltpu.SMEM(stretch_index.shape, jnp.int32),
            pltpu.VMEM(plane, f32),
            pltpu.VMEM(plane, jnp.int32),
            pltpu.VMEM((blocks,) + plane, f32),
            pltpu.VMEM((STRETCHES,) + plane, f32),
            pltpu.VMEM((7,) + plane, f32),
            pltpu.SemaphoreType.DMA((3 + components,)),
        ],
        compiler_params=options(24),
        cost_estimate=cost(40_000_000, 6_000_000),
        name="ladder",
    )(in_hbm(stretch_index), in_hbm(diffusion), in_hbm(wall_types), in_hbm(velocity))

    mate = to_mate(away)
    *outgoing, near = pl.pallas_call(
        functools.partial(merge_kernel, chips, components),
        out_shape=[shape(half * components + 1, *sheet)] * (chips - 1)
        + [shape(half * 2 * components + 1, *sheet)],
        in_specs=[vmem] * 4,
        out_specs=[vmem] * chips,
        compiler_params=options(16),
        cost_estimate=cost(500_000, 1_600_000),
        name="merge",
    )(mine, away, mate, pair)
    incoming = [
        send(outgoing[m - 1], lambda z, y: (z ^ (2 * m), y)) for m in range(1, chips)
    ]
    profile = shape(cells, *plane)
    base, unit, goal = pl.pallas_call(
        inner_kernel,
        out_shape=[shape(*velocity.shape), profile, shape(SUB, LANES)],
        in_specs=[vmem] * 8 + [anywhere],
        out_specs=[vmem] * 3,
        compiler_params=options(16),
        cost_estimate=cost(8_000_000, 8_000_000),
        name="inner",
    )(near_velocity, left, right, left_h, right_h, ends, volume, bulk_target.reshape(1, 1),
      outgoing[0])
    own_in, other_out, tile = pl.pallas_call(
        functools.partial(spread_kernel, chips, components),
        out_shape=[shape(half * 2 * components, *sheet)] * 2 + [shape(2, SUB, LANES)],
        in_specs=[vmem] * 3 + [anywhere] + [vmem] * (chips - 1),
        out_specs=[vmem] * 3,
        compiler_params=options(16),
        cost_estimate=cost(500_000, 1_600_000),
        name="spread",
    )(near, pair, chip_coefs, base, *incoming)
    other_in = to_mate(other_out)
    tiles = [tile] + [
        send(tile, lambda z, y: (z, (y + shift) % columns)) for shift in range(1, columns)
    ]

    def finish(side, arrived, *before):
        return pl.pallas_call(
            functools.partial(finish_kernel, side),
            out_shape=[shape(*velocity.shape), shape(cells, middle, lines_x)],
            in_specs=[vmem] * 4 + [anywhere] * len(before),
            out_specs=[anywhere, vmem],
            scratch_shapes=[
                pltpu.VMEM((components - 1, cells, middle, lines_x), f32),
                pltpu.SemaphoreType.DMA(((components - 1) * half,)),
            ],
            input_output_aliases={4: 0} if before else {},
            compiler_params=options(16),
            cost_estimate=cost(3_000_000, 6_000_000),
            name="finish" + str(side),
        )(arrived, base, left, right, *before)

    partial, own_plain = finish(0, own_in)
    partial, other_plain = finish(1, other_in, partial)
    return pl.pallas_call(
        functools.partial(correct_kernel, columns),
        out_shape=shape(*velocity.shape),
        in_specs=[vmem] * (4 + columns) + [anywhere],
        out_specs=anywhere,
        scratch_shapes=[
            pltpu.VMEM((cells,) + plane, f32),
            pltpu.SemaphoreType.DMA((row_tiles,)),
        ],
        input_output_aliases={4 + columns: 0},
        compiler_params=options(16),
        cost_estimate=cost(500_000, 1_600_000),
        name="correct",
    )(goal, unit, *tiles, own_plain, other_plain, partial)


def solution(mesh):
    return jax.shard_map(
        shards,
        mesh=mesh,
        in_specs=(P(None, "gz", "gy", None), P("gy", None), P("gy", None), P(), P()),
        out_specs=P(None, "gz", "gy", None),
        check_vma=False,
    )
```

```python
import functools

import jax
import jax.numpy as jnp
from jax import lax
from jax.experimental import pallas as pl
from jax.experimental.pallas import tpu as pltpu
from jax.sharding import PartitionSpec as P

SUB = 8
STRETCHES = 7
LANES = 128
MIB = 1024 * 1024


def row_tile(t):
    return pl.ds(pl.multiple_of(t * SUB, SUB), SUB)


def put(ref, at, sheet):
    count = sheet.shape[1] // LANES
    for i in range(count):
        ref[at * count + i] = sheet[:, i * LANES:(i + 1) * LANES]


def get(ref, at, count):
    return jnp.concatenate([ref[at * count + i] for i in range(count)], axis=1)


def height(index_ref, k):
    return 0.5 + 0.25 * index_ref[k].astype(jnp.float32)


def half_sum(index_ref, k):
    return 0.5 * (height(index_ref, k) + height(index_ref, k + 1))


def ladder_kernel(
    cells, blocks, chips, lines,
    index_hbm, diffusion_hbm, walls_hbm, velocity_hbm,
    mine_ref, away_ref, pair_ref, chip_ref, left_ref, right_ref, left_h_ref, right_h_ref,
    ends_ref, volume_ref, velocity_ref,
    index_ref, diffusion_ref, walls_ref, through_ref, table_ref, held_ref, sems,
):
    total = cells * blocks
    components = velocity_ref.shape[0]
    row_tiles = diffusion_ref.shape[0] // SUB
    small = [
        pltpu.make_async_copy(index_hbm, index_ref, sems.at[0]),
        pltpu.make_async_copy(diffusion_hbm, diffusion_ref, sems.at[1]),
        pltpu.make_async_copy(walls_hbm, walls_ref, sems.at[2]),
    ]
    large = [
        pltpu.make_async_copy(velocity_hbm.at[c], velocity_ref.at[c], sems.at[3 + c])
        for c in range(components)
    ]
    for copy in small + large:
        copy.start()
    me = lax.axis_index("gz")
    chip = me // 2
    first = chip * 2
    for copy in small:
        copy.wait()
    diffusion = diffusion_ref[...]
    inverse = 1.0 / diffusion
    for i in range(STRETCHES):
        table_ref[i] = (0.5 + 0.25 * i) * inverse
    walls = walls_ref[...]

    def wall(bits, k):
        face = 1.0 / jnp.full((SUB, diffusion.shape[1]), 0.5 * height(index_ref, k))
        return bits.astype(jnp.float32) * jnp.concatenate([face] * row_tiles, axis=0)

    lower = wall(walls & 1, 0)
    upper = wall(walls >> 1, total - 1)

    def forward(block, kappa, keep=None):
        start = block * cells
        flux = table_ref[index_ref[start]] + kappa
        value = jnp.ones_like(flux)
        for j in range(cells):
            if keep is not None:
                keep(j, flux, value)
            k = start + j
            if j < cells - 1:
                value = value + half_sum(index_ref, k) * flux
                flux = flux + table_ref[index_ref[k + 1]] * value
        k = jnp.minimum(start + cells - 1, total - 2)
        after = 1.0 / (value + half_sum(index_ref, k) * flux)
        return flux * after, after

    def backward(block, kappa, scale=None, keep=None):
        start = block * cells
        flux = table_ref[index_ref[start + cells - 1]] + kappa
        value = jnp.ones_like(flux)
        if scale is not None:
            flux, value = flux * scale, scale
        for j in reversed(range(cells)):
            if keep is not None:
                keep(j, flux, value)
            k = start + j
            if j > 0:
                value = value + half_sum(index_ref, k - 1) * flux
                flux = flux + table_ref[index_ref[k - 1]] * value
        k = jnp.maximum(start - 1, 0)
        after = 1.0 / (value + half_sum(index_ref, k) * flux)
        return flux * after, after

    def thickness(block):
        parts = [height(index_ref, block * cells + j) for j in range(cells)]
        return functools.reduce(jnp.add, parts)

    def sweep_forward(block, state):
        kappa, product, extent = state
        kappa, after = forward(block, kappa)
        through_ref[block] = after
        return kappa, product * after, extent + thickness(block)

    def sweep_backward(step, state):
        block = blocks - 1 - step
        kappa, product, extent = state
        kappa, after = backward(block, kappa)
        through_ref[block] = after
        return kappa, product * after, extent + thickness(block)

    ones = jnp.ones_like(diffusion)
    kappa_left, product, extent = lax.fori_loop(
        0, me, sweep_forward, (lower, ones, thickness(me))
    )
    ends_ref[0] = diffusion * lower * product
    state = {}

    def keep_left(j, flux, value):
        left_ref[j] = value
        left_h_ref[j] = height(index_ref, me * cells + j) * value
        state["flux"], state["value"] = flux, value

    kappa, own_forward = forward(me, kappa_left, keep_left)
    held_ref[1] = own_forward
    held_ref[3] = state["flux"]
    held_ref[4] = state["value"]
    held_ref[5] = state["flux"] - kappa_left

    @pl.when(me == first)
    def _():
        pair_ref[2] = own_forward
        _, after = forward(me + 1, kappa)
        pair_ref[0] = after

    @pl.when(me != first)
    def _():
        pair_ref[2] = through_ref[first]
        pair_ref[0] = own_forward

    kappa_right, product, extent = lax.fori_loop(
        0, blocks - 1 - me, sweep_backward, (upper, ones, extent)
    )
    ends_ref[1] = diffusion_ref[...] * upper * product
    scale = 1.0 / (diffusion_ref[...] * (held_ref[3] + kappa_right * held_ref[4]))
    held_ref[0] = scale

    def keep_right(j, flux, value):
        right_ref[j] = value
        right_h_ref[j] = height(index_ref, me * cells + j) * value
        state["flux"] = flux

    kappa, own_backward = backward(me, kappa_right, scale, keep_right)
    held_ref[2] = own_backward
    held_ref[6] = state["flux"] - kappa_right * scale

    @pl.when(me == first)
    def _():
        pair_ref[1] = own_backward * held_ref[0]
        pair_ref[3] = through_ref[first + 1]

    @pl.when(me != first)
    def _():
        pair_ref[3] = own_backward * held_ref[0]
        _, after = backward(me - 1, kappa)
        pair_ref[1] = after

    for m in range(1, chips):
        other = chip ^ m
        low = jnp.minimum(chip, other)
        high = jnp.maximum(chip, other)
        chip_ref[m - 1] = lax.fori_loop(
            low + 1,
            high,
            lambda r, product: product * (through_ref[2 * r] * through_ref[2 * r + 1]),
            ones,
        )
    flow = jnp.zeros((SUB, LANES), jnp.float32)
    weight = jnp.zeros((SUB, LANES), jnp.float32)

    def fold(array):
        parts = [array[:, i * LANES:(i + 1) * LANES] for i in range(array.shape[1] // LANES)]
        return functools.reduce(jnp.add, parts)

    for copy in large:
        copy.wait()
    volume_ref[...] = jnp.full(volume_ref.shape, extent * lines)
    half = row_tiles // 2
    own_extent = thickness(me)
    heights = [height(index_ref, me * cells + j) for j in range(cells)]
    for ref, whose in ((away_ref, 1 - (me - first)), (mine_ref, me - first)):
        for i in range(half):
            rows = row_tile(whose * half + i)
            from_left = [0.0] * components
            from_right = [0.0] * components
            plain = 0.0
            for j in range(cells):
                left = left_h_ref[j, rows]
                right = right_h_ref[j, rows]
                for c in range(components):
                    v = velocity_ref[c, j, rows]
                    from_left[c] = from_left[c] + left * v
                    from_right[c] = from_right[c] + right * v
                    if c == 0:
                        plain = plain + heights[j] * v
            for c in range(components):
                at = i * 2 * components + c
                put(ref, at, from_left[c] * held_ref[1, rows])
                put(ref, at + components, from_right[c] * held_ref[2, rows])
            low_part = ends_ref[0, rows]
            high_part = ends_ref[1, rows] * held_ref[0, rows]
            flow = flow + fold(plain - low_part * from_right[0] - high_part * from_left[0])
            totals = low_part * held_ref[6, rows] + high_part * held_ref[5, rows]
            weight = weight + fold(own_extent - diffusion_ref[rows] * totals)
    slot, middle = away_ref.shape[0] - 1, SUB // 2
    away_ref[slot, 0:middle] = flow[0:middle] + flow[middle:]
    away_ref[slot, middle:] = weight[0:middle] + weight[middle:]


def merge_kernel(chips, components, mine_ref, away_ref, mate_ref, pair_ref, *rest):
    send_refs, near_ref = rest[:-1], rest[-1]
    me = lax.axis_index("gz")
    chip = me // 2
    is_first = me == chip * 2
    count = pair_ref.shape[2] // LANES
    half = mine_ref.shape[0] // (2 * components * count)
    slot = away_ref.shape[0] - 1
    tile = away_ref[slot] + mate_ref[slot]
    near_ref[slot] = tile
    for ref in send_refs:
        ref[ref.shape[0] - 1] = tile
    for i in range(half):
        rows = row_tile((me - chip * 2) * half + i)
        for c in range(components):
            at = i * 2 * components + c
            mine, mate = get(mine_ref, at, count), get(mate_ref, at, count)
            first = jnp.where(is_first, mine, mate)
            second = jnp.where(is_first, mate, mine)
            put(near_ref, at, first)
            to_right = second + pair_ref[0, rows] * first
            at = at + components
            mine, mate = get(mine_ref, at, count), get(mate_ref, at, count)
            first = jnp.where(is_first, mine, mate)
            second = jnp.where(is_first, mate, mine)
            put(near_ref, at, second)
            to_left = first + pair_ref[1, rows] * second
            for m in range(1, chips):
                goes_right = (chip ^ m) > chip
                sheet = jnp.where(goes_right, to_right, to_left)
                put(send_refs[m - 1], i * components + c, sheet)


def spread_kernel(order, components, near_ref, pair_ref, chip_ref, *rest):
    recv_refs, (own_ref, other_ref, tile_ref) = rest[1:-3], rest[-3:]
    me = lax.axis_index("gz")
    chip = me // 2
    is_first = me == chip * 2
    count = pair_ref.shape[2] // LANES
    half = near_ref.shape[0] // (2 * components * count)
    tiles = [ref[ref.shape[0] - 1] for ref in (near_ref, *recv_refs)]
    tile_ref[...] = functools.reduce(jnp.add, tiles)
    for i in range(half):
        rows = row_tile((me - chip * 2) * half + i)
        coefs = [chip_ref[m - 1, rows] for m in order]
        for c in range(components):
            left_in = jnp.zeros(own_ref.shape[1:], jnp.float32)
            right_in = jnp.zeros(own_ref.shape[1:], jnp.float32)
            for m, coef, ref in zip(order, coefs, recv_refs):
                term = coef * get(ref, i * components + c, count)
                from_left = (chip ^ m) < chip
                left_in = left_in + jnp.where(from_left, term, 0.0)
                right_in = right_in + jnp.where(from_left, 0.0, term)
            at = i * 2 * components + c
            left_second = get(near_ref, at, count) + pair_ref[2, rows] * left_in
            right_first = get(near_ref, at + components, count) + pair_ref[3, rows] * right_in
            own_ref[at] = jnp.where(is_first, left_in, left_second)
            other_ref[at] = jnp.where(is_first, left_second, left_in)
            at = at + components
            own_ref[at] = jnp.where(is_first, right_first, right_in)
            other_ref[at] = jnp.where(is_first, right_in, right_first)


def leave(copies, source, target, sems):
    copies.append(pltpu.make_async_copy(source, target, sems.at[len(copies)]))
    copies[-1].start()


def inner_kernel(
    velocity_ref, left_ref, right_ref, left_h_ref, right_h_ref, ends_ref, volume_ref, target_ref,
    _, base_ref, unit_ref, goal_ref,
):
    components, cells, lines_y, lines_x = velocity_ref.shape
    goal_ref[...] = target_ref[...] * volume_ref[...]
    for t in range(lines_y // SUB):
        rows = row_tile(t)
        gathered = [jnp.zeros((SUB, lines_x), jnp.float32)] * components
        for j in reversed(range(cells)):
            left = left_ref[j, rows]
            right = right_h_ref[j, rows]
            for c in range(components):
                base_ref[c, j, rows] = left * gathered[c]
                if j > 0:
                    gathered[c] = gathered[c] + right * velocity_ref[c, j, rows]
        gathered = [jnp.zeros((SUB, lines_x), jnp.float32)] * components
        low_part = ends_ref[0, rows]
        high_part = ends_ref[1, rows] * right_ref[cells - 1, rows]
        for j in range(cells):
            left = left_h_ref[j, rows]
            right = right_ref[j, rows]
            unit_ref[j, rows] = 1.0 - (low_part * right + high_part * left_ref[j, rows])
            for c in range(components):
                gathered[c] = gathered[c] + left * velocity_ref[c, j, rows]
                base_ref[c, j, rows] = base_ref[c, j, rows] + right * gathered[c]


def finish_kernel(side, incoming_ref, base_ref, left_ref, right_ref, *rest):
    out_hbm, plain_ref, result_ref, sems = rest[-4:]
    components, cells, _, _ = base_ref.shape
    half = incoming_ref.shape[0] // (2 * components)
    me = lax.axis_index("gz")
    copies = []
    for i in range(half):
        rows = row_tile(lax.rem(me + side, 2) * half + i)
        near = slice(i * SUB, (i + 1) * SUB)
        scale = right_ref[cells - 1, rows]
        at = i * 2 * components
        lefts = [incoming_ref[at + c] for c in range(components)]
        rights = [incoming_ref[at + components + c] * scale for c in range(components)]
        for j in range(cells):
            left = left_ref[j, rows]
            right = right_ref[j, rows]
            for c in range(components):
                value = base_ref[c, j, rows] + (right * lefts[c] + left * rights[c])
                if c == 0:
                    plain_ref[j, near] = value
                else:
                    result_ref[c - 1, j, near] = value
        for c in range(1, components):
            leave(copies, result_ref.at[c - 1, :, near], out_hbm.at[c, :, rows], sems)
    for copy in copies:
        copy.wait()


def correct_kernel(columns, goal_ref, unit_ref, *rest):
    tile_refs, plain_refs = rest[:columns], rest[columns:columns + 2]
    out_hbm, result_ref, sems = rest[-3:]
    totals = functools.reduce(jnp.add, [ref[...] for ref in tile_refs])
    flow = jnp.sum(totals[0:SUB // 2], keepdims=True)
    weight = jnp.sum(totals[SUB // 2:], keepdims=True)
    alpha = (goal_ref[0:1, 0:1] - flow) / weight
    cells, middle, _ = plain_refs[0].shape
    half = middle // SUB
    me = lax.axis_index("gz")
    copies = []
    for side, plain_ref in enumerate(plain_refs):
        for i in range(half):
            rows = row_tile(lax.rem(me + side, 2) * half + i)
            for j in range(cells):
                plain = plain_ref[j, i * SUB:(i + 1) * SUB]
                result_ref[j, rows] = plain + alpha * unit_ref[j, rows]
            leave(copies, result_ref.at[:, rows], out_hbm.at[0, :, rows], sems)
    for copy in copies:
        copy.wait()


def shards(velocity, diffusion, wall_types, stretch_index, bulk_target):
    blocks = lax.axis_size("gz")
    columns = lax.axis_size("gy")
    components, cells, lines_y, lines_x = velocity.shape
    chips = blocks // 2
    row_tiles = lines_y // SUB
    half = row_tiles // 2
    f32 = jnp.float32
    vmem = pl.BlockSpec(memory_space=pltpu.VMEM)
    anywhere = pl.BlockSpec(memory_space=pl.ANY)
    plane = (lines_y, lines_x)
    sheet = (SUB, lines_x)

    def shape(*dims):
        return jax.ShapeDtypeStruct(dims, f32)

    def in_hbm(array):
        return pltpu.with_memory_space_constraint(array, pltpu.HBM)

    def options(mib):
        return pltpu.CompilerParams(vmem_limit_bytes=mib * MIB)

    def cost(flops, transferred):
        return pl.CostEstimate(flops=flops, bytes_accessed=transferred, transcendentals=0)

    def send(array, partner):
        pairs = [((z, y), partner(z, y)) for z in range(blocks) for y in range(columns)]
        route = [(a * columns + b, c * columns + d) for (a, b), (c, d) in pairs]
        return lax.ppermute(array, ("gz", "gy"), route)

    def to_mate(array):
        return send(array, lambda z, y: (z ^ 1, y))

    middle = half * SUB
    count = lines_x // LANES
    lines = float(lines_y * columns * lines_x)
    (mine, away, pair, chip_coefs, left, right, left_h, right_h, ends, volume,
     near_velocity) = pl.pallas_call(
        functools.partial(ladder_kernel, cells, blocks, chips, lines),
        out_shape=[
            shape(half * 2 * components * count, SUB, LANES),
            shape(half * 2 * components * count + 1, SUB, LANES),
            shape(4, *plane),
            shape(chips - 1, *plane),
            shape(cells, *plane),
            shape(cells, *plane),
            shape(cells, *plane),
            shape(cells, *plane),
            shape(2, *plane),
            shape(SUB, LANES),
            shape(*velocity.shape),
        ],
        in_specs=[anywhere] * 4,
        out_specs=[vmem] * 11,
        scratch_shapes=[
            pltpu.SMEM(stretch_index.shape, jnp.int32),
            pltpu.VMEM(plane, f32),
            pltpu.VMEM(plane, jnp.int32),
            pltpu.VMEM((blocks,) + plane, f32),
            pltpu.VMEM((STRETCHES,) + plane, f32),
            pltpu.VMEM((7,) + plane, f32),
            pltpu.SemaphoreType.DMA((3 + components,)),
        ],
        compiler_params=options(24),
        cost_estimate=cost(40_000_000, 6_000_000),
        name="ladder",
    )(in_hbm(stretch_index), in_hbm(diffusion), in_hbm(wall_types), in_hbm(velocity))

    mate = to_mate(away)
    *outgoing, near = pl.pallas_call(
        functools.partial(merge_kernel, chips, components),
        out_shape=[shape(half * components * count + 1, SUB, LANES)] * (chips - 1)
        + [shape(half * 2 * components * count + 1, SUB, LANES)],
        in_specs=[vmem] * 4,
        out_specs=[vmem] * chips,
        compiler_params=options(16),
        cost_estimate=cost(500_000, 1_600_000),
        name="merge",
    )(mine, away, mate, pair)
    order = sorted(range(1, chips), key=lambda m: -m.bit_count())
    incoming = [send(outgoing[m - 1], lambda z, y: (z ^ (2 * m), y)) for m in order]
    profile = shape(cells, *plane)
    base, unit, goal = pl.pallas_call(
        inner_kernel,
        out_shape=[shape(*velocity.shape), profile, shape(SUB, LANES)],
        in_specs=[vmem] * 8 + [anywhere],
        out_specs=[vmem] * 3,
        compiler_params=options(16),
        cost_estimate=cost(8_000_000, 8_000_000),
        name="inner",
    )(near_velocity, left, right, left_h, right_h, ends, volume, bulk_target.reshape(1, 1),
      outgoing[0])
    own_in, other_out, tile = pl.pallas_call(
        functools.partial(spread_kernel, order, components),
        out_shape=[shape(half * 2 * components, *sheet)] * 2 + [shape(SUB, LANES)],
        in_specs=[vmem] * 3 + [anywhere] + [vmem] * (chips - 1),
        out_specs=[vmem] * 3,
        compiler_params=options(16),
        cost_estimate=cost(500_000, 1_600_000),
        name="spread",
    )(near, pair, chip_coefs, base, *incoming)
    other_in = to_mate(other_out)
    tiles = [tile] + [
        send(tile, lambda z, y: (z, y ^ other)) for other in reversed(range(1, columns))
    ]

    def finish(side, arrived, *before):
        return pl.pallas_call(
            functools.partial(finish_kernel, side),
            out_shape=[shape(*velocity.shape), shape(cells, middle, lines_x)],
            in_specs=[vmem] * 4 + [anywhere] * len(before),
            out_specs=[anywhere, vmem],
            scratch_shapes=[
                pltpu.VMEM((components - 1, cells, middle, lines_x), f32),
                pltpu.SemaphoreType.DMA(((components - 1) * half,)),
            ],
            input_output_aliases={4: 0} if before else {},
            compiler_params=options(16),
            cost_estimate=cost(3_000_000, 6_000_000),
            name="finish" + str(side),
        )(arrived, base, left, right, *before)

    partial, own_plain = finish(0, own_in)
    partial, other_plain = finish(1, other_in, partial)
    return pl.pallas_call(
        functools.partial(correct_kernel, columns),
        out_shape=shape(*velocity.shape),
        in_specs=[vmem] * (4 + columns) + [anywhere],
        out_specs=anywhere,
        scratch_shapes=[
            pltpu.VMEM((cells,) + plane, f32),
            pltpu.SemaphoreType.DMA((row_tiles,)),
        ],
        input_output_aliases={4 + columns: 0},
        compiler_params=options(16),
        cost_estimate=cost(500_000, 1_600_000),
        name="correct",
    )(goal, unit, *tiles, own_plain, other_plain, partial)


def solution(mesh):
    return jax.shard_map(
        shards,
        mesh=mesh,
        in_specs=(P(None, "gz", "gy", None), P("gy", None), P("gy", None), P(), P()),
        out_specs=P(None, "gz", "gy", None),
        check_vma=False,
    )
```

```python
import functools

import jax
import jax.numpy as jnp
from jax import lax
from jax.experimental import pallas as pl
from jax.experimental.pallas import tpu as pltpu
from jax.sharding import PartitionSpec as P

SUB = 8
STRETCHES = 7
LANES = 128
MIB = 1024 * 1024


def row_tile(t):
    return pl.ds(pl.multiple_of(t * SUB, SUB), SUB)


def put(ref, at, sheet):
    count = sheet.shape[1] // LANES
    for i in range(count):
        ref[at * count + i] = sheet[:, i * LANES:(i + 1) * LANES]


def get(ref, at, count):
    return jnp.concatenate([ref[at * count + i] for i in range(count)], axis=1)


def height(index_ref, k):
    return 0.5 + 0.25 * index_ref[k].astype(jnp.float32)


def half_sum(index_ref, k):
    return 0.5 * (height(index_ref, k) + height(index_ref, k + 1))


def ladder_kernel(
    cells, blocks, chips, lines,
    index_hbm, diffusion_hbm, walls_hbm, velocity_hbm,
    mine_ref, away_ref, pair_ref, chip_ref, left_ref, right_ref, left_h_ref, right_h_ref,
    ends_ref, volume_ref, velocity_ref,
    index_ref, diffusion_ref, walls_ref, through_ref, table_ref, held_ref, sems,
):
    total = cells * blocks
    components = velocity_ref.shape[0]
    row_tiles = diffusion_ref.shape[0] // SUB
    small = [
        pltpu.make_async_copy(index_hbm, index_ref, sems.at[0]),
        pltpu.make_async_copy(diffusion_hbm, diffusion_ref, sems.at[1]),
        pltpu.make_async_copy(walls_hbm, walls_ref, sems.at[2]),
    ]
    large = [
        pltpu.make_async_copy(velocity_hbm.at[c], velocity_ref.at[c], sems.at[3 + c])
        for c in range(components)
    ]
    for copy in small + large:
        copy.start()
    me = lax.axis_index("gz")
    chip = me // 2
    first = chip * 2
    for copy in small:
        copy.wait()
    diffusion = diffusion_ref[...]
    inverse = 1.0 / diffusion
    for i in range(STRETCHES):
        table_ref[i] = (0.5 + 0.25 * i) * inverse
    walls = walls_ref[...]

    def wall(bits, k):
        face = 1.0 / jnp.full((SUB, diffusion.shape[1]), 0.5 * height(index_ref, k))
        return bits.astype(jnp.float32) * jnp.concatenate([face] * row_tiles, axis=0)

    lower = wall(walls & 1, 0)
    upper = wall(walls >> 1, total - 1)

    def forward(block, kappa, keep=None):
        start = block * cells
        flux = table_ref[index_ref[start]] + kappa
        value = jnp.ones_like(flux)
        for j in range(cells):
            if keep is not None:
                keep(j, flux, value)
            k = start + j
            if j < cells - 1:
                value = value + half_sum(index_ref, k) * flux
                flux = flux + table_ref[index_ref[k + 1]] * value
        k = jnp.minimum(start + cells - 1, total - 2)
        after = 1.0 / (value + half_sum(index_ref, k) * flux)
        return flux * after, after

    def backward(block, kappa, scale=None, keep=None):
        start = block * cells
        flux = table_ref[index_ref[start + cells - 1]] + kappa
        value = jnp.ones_like(flux)
        if scale is not None:
            flux, value = flux * scale, scale
        for j in reversed(range(cells)):
            if keep is not None:
                keep(j, flux, value)
            k = start + j
            if j > 0:
                value = value + half_sum(index_ref, k - 1) * flux
                flux = flux + table_ref[index_ref[k - 1]] * value
        k = jnp.maximum(start - 1, 0)
        after = 1.0 / (value + half_sum(index_ref, k) * flux)
        return flux * after, after

    def thickness(block):
        parts = [height(index_ref, block * cells + j) for j in range(cells)]
        return functools.reduce(jnp.add, parts)

    def sweep_forward(block, state):
        kappa, product, extent = state
        kappa, after = forward(block, kappa)
        through_ref[block] = after
        return kappa, product * after, extent + thickness(block)

    def sweep_backward(step, state):
        block = blocks - 1 - step
        kappa, product, extent = state
        kappa, after = backward(block, kappa)
        through_ref[block] = after
        return kappa, product * after, extent + thickness(block)

    ones = jnp.ones_like(diffusion)
    kappa_left, product, extent = lax.fori_loop(
        0, me, sweep_forward, (lower, ones, thickness(me))
    )
    ends_ref[0] = diffusion * lower * product
    state = {}

    def keep_left(j, flux, value):
        left_ref[j] = value
        left_h_ref[j] = height(index_ref, me * cells + j) * value
        state["flux"], state["value"] = flux, value

    kappa, own_forward = forward(me, kappa_left, keep_left)
    held_ref[1] = own_forward
    held_ref[3] = state["flux"]
    held_ref[4] = state["value"]
    held_ref[5] = state["flux"] - kappa_left

    @pl.when(me == first)
    def _():
        pair_ref[2] = own_forward
        _, after = forward(me + 1, kappa)
        pair_ref[0] = after

    @pl.when(me != first)
    def _():
        pair_ref[2] = through_ref[first]
        pair_ref[0] = own_forward

    kappa_right, product, extent = lax.fori_loop(
        0, blocks - 1 - me, sweep_backward, (upper, ones, extent)
    )
    ends_ref[1] = diffusion_ref[...] * upper * product
    scale = 1.0 / (diffusion_ref[...] * (held_ref[3] + kappa_right * held_ref[4]))
    held_ref[0] = scale

    def keep_right(j, flux, value):
        right_ref[j] = value
        right_h_ref[j] = height(index_ref, me * cells + j) * value
        state["flux"] = flux

    kappa, own_backward = backward(me, kappa_right, scale, keep_right)
    held_ref[2] = own_backward
    held_ref[6] = state["flux"] - kappa_right * scale

    @pl.when(me == first)
    def _():
        pair_ref[1] = own_backward * held_ref[0]
        pair_ref[3] = through_ref[first + 1]

    @pl.when(me != first)
    def _():
        pair_ref[3] = own_backward * held_ref[0]
        _, after = backward(me - 1, kappa)
        pair_ref[1] = after

    for m in range(1, chips):
        other = chip ^ m
        low = jnp.minimum(chip, other)
        high = jnp.maximum(chip, other)
        chip_ref[m - 1] = lax.fori_loop(
            low + 1,
            high,
            lambda r, product: product * (through_ref[2 * r] * through_ref[2 * r + 1]),
            ones,
        )
    flow = jnp.zeros((SUB, LANES), jnp.float32)
    weight = jnp.zeros((SUB, LANES), jnp.float32)

    def fold(array):
        parts = [array[:, i * LANES:(i + 1) * LANES] for i in range(array.shape[1] // LANES)]
        return functools.reduce(jnp.add, parts)

    for copy in large:
        copy.wait()
    volume_ref[...] = jnp.full(volume_ref.shape, extent * lines)
    half = row_tiles // 2
    own_extent = thickness(me)
    heights = [height(index_ref, me * cells + j) for j in range(cells)]
    for ref, whose in ((away_ref, 1 - (me - first)), (mine_ref, me - first)):
        for i in range(half):
            rows = row_tile(whose * half + i)
            from_left = [0.0] * components
            from_right = [0.0] * components
            plain = 0.0
            for j in range(cells):
                left = left_h_ref[j, rows]
                right = right_h_ref[j, rows]
                for c in range(components):
                    v = velocity_ref[c, j, rows]
                    from_left[c] = from_left[c] + left * v
                    from_right[c] = from_right[c] + right * v
                    if c == 0:
                        plain = plain + heights[j] * v
            for c in range(components):
                at = i * 2 * components + c
                put(ref, at, from_left[c] * held_ref[1, rows])
                put(ref, at + components, from_right[c] * held_ref[2, rows])
            low_part = ends_ref[0, rows]
            high_part = ends_ref[1, rows] * held_ref[0, rows]
            flow = flow + fold(plain - low_part * from_right[0] - high_part * from_left[0])
            totals = low_part * held_ref[6, rows] + high_part * held_ref[5, rows]
            weight = weight + fold(own_extent - diffusion_ref[rows] * totals)
    slot, middle = away_ref.shape[0] - 1, SUB // 2
    away_ref[slot, 0:middle] = flow[0:middle] + flow[middle:]
    away_ref[slot, middle:] = weight[0:middle] + weight[middle:]


def merge_kernel(chips, components, mine_ref, away_ref, mate_ref, pair_ref, *rest):
    send_refs, near_ref = rest[:-1], rest[-1]
    me = lax.axis_index("gz")
    chip = me // 2
    is_first = me == chip * 2
    count = pair_ref.shape[2] // LANES
    half = mine_ref.shape[0] // (2 * components * count)
    slot = away_ref.shape[0] - 1
    tile = away_ref[slot] + mate_ref[slot]
    near_ref[slot] = tile
    for ref in send_refs:
        for at in range(half * components * count, ref.shape[0]):
            ref[at] = tile
    for i in range(half):
        rows = row_tile((me - chip * 2) * half + i)
        for c in range(components):
            at = i * 2 * components + c
            mine, mate = get(mine_ref, at, count), get(mate_ref, at, count)
            first = jnp.where(is_first, mine, mate)
            second = jnp.where(is_first, mate, mine)
            put(near_ref, at, first)
            to_right = second + pair_ref[0, rows] * first
            at = at + components
            mine, mate = get(mine_ref, at, count), get(mate_ref, at, count)
            first = jnp.where(is_first, mine, mate)
            second = jnp.where(is_first, mate, mine)
            put(near_ref, at, second)
            to_left = first + pair_ref[1, rows] * second
            for m in range(1, chips):
                goes_right = (chip ^ m) > chip
                sheet = jnp.where(goes_right, to_right, to_left)
                put(send_refs[m - 1], i * components + c, sheet)


def spread_kernel(order, components, near_ref, pair_ref, chip_ref, *rest):
    recv_refs, (own_ref, other_ref, tile_ref) = rest[1:-3], rest[-3:]
    me = lax.axis_index("gz")
    chip = me // 2
    is_first = me == chip * 2
    count = pair_ref.shape[2] // LANES
    half = near_ref.shape[0] // (2 * components * count)
    tiles = [ref[ref.shape[0] - 1] for ref in (near_ref, *recv_refs)]
    tile_ref[...] = functools.reduce(jnp.add, tiles)
    for i in range(half):
        rows = row_tile((me - chip * 2) * half + i)
        coefs = [chip_ref[m - 1, rows] for m in order]
        for c in range(components):
            left_in = jnp.zeros(own_ref.shape[1:], jnp.float32)
            right_in = jnp.zeros(own_ref.shape[1:], jnp.float32)
            for m, coef, ref in zip(order, coefs, recv_refs):
                term = coef * get(ref, i * components + c, count)
                from_left = (chip ^ m) < chip
                left_in = left_in + jnp.where(from_left, term, 0.0)
                right_in = right_in + jnp.where(from_left, 0.0, term)
            at = i * 2 * components + c
            left_second = get(near_ref, at, count) + pair_ref[2, rows] * left_in
            right_first = get(near_ref, at + components, count) + pair_ref[3, rows] * right_in
            own_ref[at] = jnp.where(is_first, left_in, left_second)
            other_ref[at] = jnp.where(is_first, left_second, left_in)
            at = at + components
            own_ref[at] = jnp.where(is_first, right_first, right_in)
            other_ref[at] = jnp.where(is_first, right_in, right_first)


def leave(copies, source, target, sems):
    copies.append(pltpu.make_async_copy(source, target, sems.at[len(copies)]))
    copies[-1].start()


def inner_kernel(
    velocity_ref, left_ref, right_ref, left_h_ref, right_h_ref, ends_ref, volume_ref, target_ref,
    _, base_ref, unit_ref, goal_ref,
):
    components, cells, lines_y, lines_x = velocity_ref.shape
    goal_ref[...] = target_ref[...] * volume_ref[...]
    for t in range(lines_y // SUB):
        rows = row_tile(t)
        gathered = [jnp.zeros((SUB, lines_x), jnp.float32)] * components
        for j in reversed(range(cells)):
            left = left_ref[j, rows]
            right = right_h_ref[j, rows]
            for c in range(components):
                base_ref[c, j, rows] = left * gathered[c]
                if j > 0:
                    gathered[c] = gathered[c] + right * velocity_ref[c, j, rows]
        gathered = [jnp.zeros((SUB, lines_x), jnp.float32)] * components
        low_part = ends_ref[0, rows]
        high_part = ends_ref[1, rows] * right_ref[cells - 1, rows]
        for j in range(cells):
            left = left_h_ref[j, rows]
            right = right_ref[j, rows]
            unit_ref[j, rows] = 1.0 - (low_part * right + high_part * left_ref[j, rows])
            for c in range(components):
                gathered[c] = gathered[c] + left * velocity_ref[c, j, rows]
                base_ref[c, j, rows] = base_ref[c, j, rows] + right * gathered[c]


def finish_kernel(side, incoming_ref, base_ref, left_ref, right_ref, *rest):
    out_hbm, plain_ref, result_ref, sems = rest[-4:]
    components, cells, _, _ = base_ref.shape
    half = incoming_ref.shape[0] // (2 * components)
    me = lax.axis_index("gz")
    copies = []
    for i in range(half):
        rows = row_tile(lax.rem(me + side, 2) * half + i)
        near = slice(i * SUB, (i + 1) * SUB)
        scale = right_ref[cells - 1, rows]
        at = i * 2 * components
        lefts = [incoming_ref[at + c] for c in range(components)]
        rights = [incoming_ref[at + components + c] * scale for c in range(components)]
        for j in range(cells):
            left = left_ref[j, rows]
            right = right_ref[j, rows]
            for c in range(components):
                value = base_ref[c, j, rows] + (right * lefts[c] + left * rights[c])
                if c == 0:
                    plain_ref[j, near] = value
                else:
                    result_ref[c - 1, j, near] = value
        for c in range(1, components):
            leave(copies, result_ref.at[c - 1, :, near], out_hbm.at[c, :, rows], sems)
    for copy in copies:
        copy.wait()


def correct_kernel(columns, goal_ref, unit_ref, *rest):
    tile_refs, plain_refs = rest[:columns], rest[columns:columns + 2]
    out_hbm, result_ref, sems = rest[-3:]
    totals = functools.reduce(jnp.add, [ref[...] for ref in tile_refs])
    flow = jnp.sum(totals[0:SUB // 2], keepdims=True)
    weight = jnp.sum(totals[SUB // 2:], keepdims=True)
    alpha = (goal_ref[0:1, 0:1] - flow) / weight
    cells, middle, _ = plain_refs[0].shape
    half = middle // SUB
    me = lax.axis_index("gz")
    copies = []
    for side, plain_ref in enumerate(plain_refs):
        for i in range(half):
            rows = row_tile(lax.rem(me + side, 2) * half + i)
            for j in range(cells):
                plain = plain_ref[j, i * SUB:(i + 1) * SUB]
                result_ref[j, rows] = plain + alpha * unit_ref[j, rows]
            leave(copies, result_ref.at[:, rows], out_hbm.at[0, :, rows], sems)
    for copy in copies:
        copy.wait()


def shards(velocity, diffusion, wall_types, stretch_index, bulk_target):
    blocks = lax.axis_size("gz")
    columns = lax.axis_size("gy")
    components, cells, lines_y, lines_x = velocity.shape
    chips = blocks // 2
    row_tiles = lines_y // SUB
    half = row_tiles // 2
    f32 = jnp.float32
    vmem = pl.BlockSpec(memory_space=pltpu.VMEM)
    anywhere = pl.BlockSpec(memory_space=pl.ANY)
    plane = (lines_y, lines_x)
    sheet = (SUB, lines_x)

    def shape(*dims):
        return jax.ShapeDtypeStruct(dims, f32)

    def in_hbm(array):
        return pltpu.with_memory_space_constraint(array, pltpu.HBM)

    def options(mib):
        return pltpu.CompilerParams(vmem_limit_bytes=mib * MIB)

    def cost(flops, transferred):
        return pl.CostEstimate(flops=flops, bytes_accessed=transferred, transcendentals=0)

    def send(array, partner):
        pairs = [((z, y), partner(z, y)) for z in range(blocks) for y in range(columns)]
        route = [(a * columns + b, c * columns + d) for (a, b), (c, d) in pairs]
        return lax.ppermute(array, ("gz", "gy"), route)

    def to_mate(array):
        return send(array, lambda z, y: (z ^ 1, y))

    middle = half * SUB
    count = lines_x // LANES
    lines = float(lines_y * columns * lines_x)
    (mine, away, pair, chip_coefs, left, right, left_h, right_h, ends, volume,
     near_velocity) = pl.pallas_call(
        functools.partial(ladder_kernel, cells, blocks, chips, lines),
        out_shape=[
            shape(half * 2 * components * count, SUB, LANES),
            shape(half * 2 * components * count + 1, SUB, LANES),
            shape(4, *plane),
            shape(chips - 1, *plane),
            shape(cells, *plane),
            shape(cells, *plane),
            shape(cells, *plane),
            shape(cells, *plane),
            shape(2, *plane),
            shape(SUB, LANES),
            shape(*velocity.shape),
        ],
        in_specs=[anywhere] * 4,
        out_specs=[vmem] * 11,
        scratch_shapes=[
            pltpu.SMEM(stretch_index.shape, jnp.int32),
            pltpu.VMEM(plane, f32),
            pltpu.VMEM(plane, jnp.int32),
            pltpu.VMEM((blocks,) + plane, f32),
            pltpu.VMEM((STRETCHES,) + plane, f32),
            pltpu.VMEM((7,) + plane, f32),
            pltpu.SemaphoreType.DMA((3 + components,)),
        ],
        compiler_params=options(24),
        cost_estimate=cost(40_000_000, 6_000_000),
        name="ladder",
    )(in_hbm(stretch_index), in_hbm(diffusion), in_hbm(wall_types), in_hbm(velocity))

    mate = to_mate(away)
    *outgoing, near = pl.pallas_call(
        functools.partial(merge_kernel, chips, components),
        out_shape=[
            shape(half * components * count + m.bit_count(), SUB, LANES) for m in range(1, chips)
        ] + [shape(half * 2 * components * count + 1, SUB, LANES)],
        in_specs=[vmem] * 4,
        out_specs=[vmem] * chips,
        compiler_params=options(16),
        cost_estimate=cost(500_000, 1_600_000),
        name="merge",
    )(mine, away, mate, pair)
    order = sorted(range(1, chips), key=lambda m: -m.bit_count())
    incoming = [send(outgoing[m - 1], lambda z, y: (z ^ (2 * m), y)) for m in order]
    profile = shape(cells, *plane)
    base, unit, goal = pl.pallas_call(
        inner_kernel,
        out_shape=[shape(*velocity.shape), profile, shape(SUB, LANES)],
        in_specs=[vmem] * 8 + [anywhere],
        out_specs=[vmem] * 3,
        compiler_params=options(16),
        cost_estimate=cost(8_000_000, 8_000_000),
        name="inner",
    )(near_velocity, left, right, left_h, right_h, ends, volume, bulk_target.reshape(1, 1),
      outgoing[0])
    own_in, other_out, tile = pl.pallas_call(
        functools.partial(spread_kernel, order, components),
        out_shape=[shape(half * 2 * components, *sheet)] * 2 + [shape(SUB, LANES)],
        in_specs=[vmem] * 3 + [anywhere] + [vmem] * (chips - 1),
        out_specs=[vmem] * 3,
        compiler_params=options(16),
        cost_estimate=cost(500_000, 1_600_000),
        name="spread",
    )(near, pair, chip_coefs, base, *incoming)
    other_in = to_mate(other_out)
    tiles = [tile] + [
        send(tile, lambda z, y: (z, y ^ other)) for other in reversed(range(1, columns))
    ]

    def finish(side, arrived, *before):
        return pl.pallas_call(
            functools.partial(finish_kernel, side),
            out_shape=[shape(*velocity.shape), shape(cells, middle, lines_x)],
            in_specs=[vmem] * 4 + [anywhere] * len(before),
            out_specs=[anywhere, vmem],
            scratch_shapes=[
                pltpu.VMEM((components - 1, cells, middle, lines_x), f32),
                pltpu.SemaphoreType.DMA(((components - 1) * half,)),
            ],
            input_output_aliases={4: 0} if before else {},
            compiler_params=options(16),
            cost_estimate=cost(3_000_000, 6_000_000),
            name="finish" + str(side),
        )(arrived, base, left, right, *before)

    partial, own_plain = finish(0, own_in)
    partial, other_plain = finish(1, other_in, partial)
    return pl.pallas_call(
        functools.partial(correct_kernel, columns),
        out_shape=shape(*velocity.shape),
        in_specs=[vmem] * (4 + columns) + [anywhere],
        out_specs=anywhere,
        scratch_shapes=[
            pltpu.VMEM((cells,) + plane, f32),
            pltpu.SemaphoreType.DMA((row_tiles,)),
        ],
        input_output_aliases={4 + columns: 0},
        compiler_params=options(16),
        cost_estimate=cost(500_000, 1_600_000),
        name="correct",
    )(goal, unit, *tiles, own_plain, other_plain, partial)


def solution(mesh):
    return jax.shard_map(
        shards,
        mesh=mesh,
        in_specs=(P(None, "gz", "gy", None), P("gy", None), P("gy", None), P(), P()),
        out_specs=P(None, "gz", "gy", None),
        check_vma=False,
    )
```

```python
import functools

import jax
import jax.numpy as jnp
from jax import lax
from jax.experimental import pallas as pl
from jax.experimental.pallas import tpu as pltpu
from jax.sharding import PartitionSpec as P

SUB = 8
STRETCHES = 7
LANES = 128
MIB = 1024 * 1024


def row_tile(t):
    return pl.ds(pl.multiple_of(t * SUB, SUB), SUB)


def put(ref, at, sheet):
    count = sheet.shape[1] // LANES
    for i in range(count):
        ref[at * count + i] = sheet[:, i * LANES:(i + 1) * LANES]


def get(ref, at, count):
    return jnp.concatenate([ref[at * count + i] for i in range(count)], axis=1)


def height(index_ref, k):
    return 0.5 + 0.25 * index_ref[k].astype(jnp.float32)


def half_sum(index_ref, k):
    return 0.5 * (height(index_ref, k) + height(index_ref, k + 1))


def ladder_kernel(
    cells, blocks, chips, lines,
    index_hbm, diffusion_hbm, walls_hbm, velocity_hbm,
    mine_ref, away_ref, pair_ref, chip_ref, left_ref, right_ref, left_h_ref, right_h_ref,
    ends_ref, volume_ref, velocity_ref,
    index_ref, diffusion_ref, walls_ref, through_ref, table_ref, held_ref, sems,
):
    total = cells * blocks
    components = velocity_ref.shape[0]
    row_tiles = diffusion_ref.shape[0] // SUB
    small = [
        pltpu.make_async_copy(index_hbm, index_ref, sems.at[0]),
        pltpu.make_async_copy(diffusion_hbm, diffusion_ref, sems.at[1]),
        pltpu.make_async_copy(walls_hbm, walls_ref, sems.at[2]),
    ]
    large = [
        pltpu.make_async_copy(velocity_hbm.at[c], velocity_ref.at[c], sems.at[3 + c])
        for c in range(components)
    ]
    for copy in small + large:
        copy.start()
    me = lax.axis_index("gz")
    chip = me // 2
    first = chip * 2
    for copy in small:
        copy.wait()
    diffusion = diffusion_ref[...]
    inverse = 1.0 / diffusion
    for i in range(STRETCHES):
        table_ref[i] = (0.5 + 0.25 * i) * inverse
    walls = walls_ref[...]

    def wall(bits, k):
        face = 1.0 / jnp.full((SUB, diffusion.shape[1]), 0.5 * height(index_ref, k))
        return bits.astype(jnp.float32) * jnp.concatenate([face] * row_tiles, axis=0)

    lower = wall(walls & 1, 0)
    upper = wall(walls >> 1, total - 1)

    def forward(block, kappa, keep=None):
        start = block * cells
        flux = table_ref[index_ref[start]] + kappa
        value = jnp.ones_like(flux)
        for j in range(cells):
            if keep is not None:
                keep(j, flux, value)
            k = start + j
            if j < cells - 1:
                value = value + half_sum(index_ref, k) * flux
                flux = flux + table_ref[index_ref[k + 1]] * value
        k = jnp.minimum(start + cells - 1, total - 2)
        after = 1.0 / (value + half_sum(index_ref, k) * flux)
        return flux * after, after

    def backward(block, kappa, scale=None, keep=None):
        start = block * cells
        flux = table_ref[index_ref[start + cells - 1]] + kappa
        value = jnp.ones_like(flux)
        if scale is not None:
            flux, value = flux * scale, scale
        for j in reversed(range(cells)):
            if keep is not None:
                keep(j, flux, value)
            k = start + j
            if j > 0:
                value = value + half_sum(index_ref, k - 1) * flux
                flux = flux + table_ref[index_ref[k - 1]] * value
        k = jnp.maximum(start - 1, 0)
        after = 1.0 / (value + half_sum(index_ref, k) * flux)
        return flux * after, after

    def thickness(block):
        parts = [height(index_ref, block * cells + j) for j in range(cells)]
        return functools.reduce(jnp.add, parts)

    def sweep_forward(block, state):
        kappa, product, extent = state
        kappa, after = forward(block, kappa)
        through_ref[block] = after
        return kappa, product * after, extent + thickness(block)

    def sweep_backward(step, state):
        block = blocks - 1 - step
        kappa, product, extent = state
        kappa, after = backward(block, kappa)
        through_ref[block] = after
        return kappa, product * after, extent + thickness(block)

    ones = jnp.ones_like(diffusion)
    kappa_left, product, extent = lax.fori_loop(
        0, me, sweep_forward, (lower, ones, thickness(me))
    )
    ends_ref[0] = diffusion * lower * product
    state = {}

    def keep_left(j, flux, value):
        left_ref[j] = value
        left_h_ref[j] = height(index_ref, me * cells + j) * value
        state["flux"], state["value"] = flux, value

    kappa, own_forward = forward(me, kappa_left, keep_left)
    held_ref[1] = own_forward
    held_ref[3] = state["flux"]
    held_ref[4] = state["value"]
    held_ref[5] = state["flux"] - kappa_left

    @pl.when(me == first)
    def _():
        pair_ref[2] = own_forward
        _, after = forward(me + 1, kappa)
        pair_ref[0] = after

    @pl.when(me != first)
    def _():
        pair_ref[2] = through_ref[first]
        pair_ref[0] = own_forward

    kappa_right, product, extent = lax.fori_loop(
        0, blocks - 1 - me, sweep_backward, (upper, ones, extent)
    )
    ends_ref[1] = diffusion_ref[...] * upper * product
    scale = 1.0 / (diffusion_ref[...] * (held_ref[3] + kappa_right * held_ref[4]))
    held_ref[0] = scale

    def keep_right(j, flux, value):
        right_ref[j] = value
        right_h_ref[j] = height(index_ref, me * cells + j) * value
        state["flux"] = flux

    kappa, own_backward = backward(me, kappa_right, scale, keep_right)
    held_ref[2] = own_backward
    held_ref[6] = state["flux"] - kappa_right * scale

    @pl.when(me == first)
    def _():
        pair_ref[1] = own_backward * held_ref[0]
        pair_ref[3] = through_ref[first + 1]

    @pl.when(me != first)
    def _():
        pair_ref[3] = own_backward * held_ref[0]
        _, after = backward(me - 1, kappa)
        pair_ref[1] = after

    for m in range(1, chips):
        other = chip ^ m
        low = jnp.minimum(chip, other)
        high = jnp.maximum(chip, other)
        chip_ref[m - 1] = lax.fori_loop(
            low + 1,
            high,
            lambda r, product: product * (through_ref[2 * r] * through_ref[2 * r + 1]),
            ones,
        )
    flow = jnp.zeros((SUB, LANES), jnp.float32)
    weight = jnp.zeros((SUB, LANES), jnp.float32)

    def fold(array):
        parts = [array[:, i * LANES:(i + 1) * LANES] for i in range(array.shape[1] // LANES)]
        return functools.reduce(jnp.add, parts)

    for copy in large:
        copy.wait()
    volume_ref[...] = jnp.full(volume_ref.shape, extent * lines)
    half = row_tiles // 2
    own_extent = thickness(me)
    heights = [height(index_ref, me * cells + j) for j in range(cells)]
    for ref, whose in ((away_ref, 1 - (me - first)), (mine_ref, me - first)):
        for i in range(half):
            rows = row_tile(whose * half + i)
            from_left = [0.0] * components
            from_right = [0.0] * components
            plain = 0.0
            for j in range(cells):
                left = left_h_ref[j, rows]
                right = right_h_ref[j, rows]
                for c in range(components):
                    v = velocity_ref[c, j, rows]
                    from_left[c] = from_left[c] + left * v
                    from_right[c] = from_right[c] + right * v
                    if c == 0:
                        plain = plain + heights[j] * v
            for c in range(components):
                at = i * 2 * components + c
                put(ref, at, from_left[c] * held_ref[1, rows])
                put(ref, at + components, from_right[c] * held_ref[2, rows])
            low_part = ends_ref[0, rows]
            high_part = ends_ref[1, rows] * held_ref[0, rows]
            flow = flow + fold(plain - low_part * from_right[0] - high_part * from_left[0])
            totals = low_part * held_ref[6, rows] + high_part * held_ref[5, rows]
            weight = weight + fold(own_extent - diffusion_ref[rows] * totals)
    slot, middle = away_ref.shape[0] - 1, SUB // 2
    away_ref[slot, 0:middle] = flow[0:middle] + flow[middle:]
    away_ref[slot, middle:] = weight[0:middle] + weight[middle:]


def merge_kernel(chips, components, mine_ref, away_ref, mate_ref, pair_ref, *rest):
    send_refs, near_ref = rest[:-1], rest[-1]
    me = lax.axis_index("gz")
    chip = me // 2
    is_first = me == chip * 2
    count = pair_ref.shape[2] // LANES
    half = mine_ref.shape[0] // (2 * components * count)
    slot = away_ref.shape[0] - 1
    tile = away_ref[slot] + mate_ref[slot]
    near_ref[slot] = tile
    for ref in send_refs:
        for at in range(half * components * count, ref.shape[0]):
            ref[at] = tile
    for i in range(half):
        rows = row_tile((me - chip * 2) * half + i)
        for c in range(components):
            at = i * 2 * components + c
            mine, mate = get(mine_ref, at, count), get(mate_ref, at, count)
            first = jnp.where(is_first, mine, mate)
            second = jnp.where(is_first, mate, mine)
            put(near_ref, at, first)
            to_right = second + pair_ref[0, rows] * first
            at = at + components
            mine, mate = get(mine_ref, at, count), get(mate_ref, at, count)
            first = jnp.where(is_first, mine, mate)
            second = jnp.where(is_first, mate, mine)
            put(near_ref, at, second)
            to_left = first + pair_ref[1, rows] * second
            for m in range(1, chips):
                goes_right = (chip ^ m) > chip
                sheet = jnp.where(goes_right, to_right, to_left)
                put(send_refs[m - 1], i * components + c, sheet)


def spread_kernel(order, components, near_ref, pair_ref, chip_ref, *rest):
    recv_refs, (own_ref, other_ref, tile_ref) = rest[1:-3], rest[-3:]
    me = lax.axis_index("gz")
    chip = me // 2
    is_first = me == chip * 2
    count = pair_ref.shape[2] // LANES
    half = near_ref.shape[0] // (2 * components * count)
    tiles = [ref[ref.shape[0] - 1] for ref in (near_ref, *recv_refs)]
    tile_ref[...] = functools.reduce(jnp.add, tiles)
    for i in range(half):
        rows = row_tile((me - chip * 2) * half + i)
        coefs = [chip_ref[m - 1, rows] for m in order]
        for c in range(components):
            left_in = jnp.zeros(own_ref.shape[1:], jnp.float32)
            right_in = jnp.zeros(own_ref.shape[1:], jnp.float32)
            for m, coef, ref in zip(order, coefs, recv_refs):
                term = coef * get(ref, i * components + c, count)
                from_left = (chip ^ m) < chip
                left_in = left_in + jnp.where(from_left, term, 0.0)
                right_in = right_in + jnp.where(from_left, 0.0, term)
            at = i * 2 * components + c
            left_second = get(near_ref, at, count) + pair_ref[2, rows] * left_in
            right_first = get(near_ref, at + components, count) + pair_ref[3, rows] * right_in
            own_ref[at] = jnp.where(is_first, left_in, left_second)
            other_ref[at] = jnp.where(is_first, left_second, left_in)
            at = at + components
            own_ref[at] = jnp.where(is_first, right_first, right_in)
            other_ref[at] = jnp.where(is_first, right_in, right_first)


def leave(copies, source, target, sems):
    copies.append(pltpu.make_async_copy(source, target, sems.at[len(copies)]))
    copies[-1].start()


def inner_kernel(
    velocity_ref, left_ref, right_ref, left_h_ref, right_h_ref, ends_ref, volume_ref, target_ref,
    _, base_ref, unit_ref, goal_ref,
):
    components, cells, lines_y, lines_x = velocity_ref.shape
    goal_ref[...] = target_ref[...] * volume_ref[...]
    for t in range(lines_y // SUB):
        rows = row_tile(t)
        gathered = [jnp.zeros((SUB, lines_x), jnp.float32)] * components
        for j in reversed(range(cells)):
            left = left_ref[j, rows]
            right = right_h_ref[j, rows]
            for c in range(components):
                base_ref[c, j, rows] = left * gathered[c]
                if j > 0:
                    gathered[c] = gathered[c] + right * velocity_ref[c, j, rows]
        gathered = [jnp.zeros((SUB, lines_x), jnp.float32)] * components
        low_part = ends_ref[0, rows]
        high_part = ends_ref[1, rows] * right_ref[cells - 1, rows]
        for j in range(cells):
            left = left_h_ref[j, rows]
            right = right_ref[j, rows]
            unit_ref[j, rows] = 1.0 - (low_part * right + high_part * left_ref[j, rows])
            for c in range(components):
                gathered[c] = gathered[c] + left * velocity_ref[c, j, rows]
                base_ref[c, j, rows] = base_ref[c, j, rows] + right * gathered[c]


def finish_kernel(side, incoming_ref, base_ref, left_ref, right_ref, *rest):
    out_hbm, plain_ref, result_ref, sems = rest[-4:]
    components, cells, _, _ = base_ref.shape
    half = incoming_ref.shape[0] // (2 * components)
    me = lax.axis_index("gz")
    copies = []
    for i in range(half):
        rows = row_tile(lax.rem(me + side, 2) * half + i)
        near = slice(i * SUB, (i + 1) * SUB)
        scale = right_ref[cells - 1, rows]
        at = i * 2 * components
        lefts = [incoming_ref[at + c] for c in range(components)]
        rights = [incoming_ref[at + components + c] * scale for c in range(components)]
        for j in range(cells):
            left = left_ref[j, rows]
            right = right_ref[j, rows]
            for c in range(components):
                value = base_ref[c, j, rows] + (right * lefts[c] + left * rights[c])
                if c == 0:
                    plain_ref[j, near] = value
                else:
                    result_ref[c - 1, j, near] = value
        for c in range(1, components):
            leave(copies, result_ref.at[c - 1, :, near], out_hbm.at[c, :, rows], sems)
    for copy in copies:
        copy.wait()


def correct_kernel(columns, goal_ref, unit_ref, *rest):
    tile_refs, plain_refs = rest[:columns], rest[columns:columns + 2]
    out_hbm, result_ref, sems = rest[-3:]
    totals = functools.reduce(jnp.add, [ref[...] for ref in tile_refs])
    flow = jnp.sum(totals[0:SUB // 2], keepdims=True)
    weight = jnp.sum(totals[SUB // 2:], keepdims=True)
    alpha = (goal_ref[0:1, 0:1] - flow) / weight
    cells, middle, _ = plain_refs[0].shape
    half = middle // SUB
    me = lax.axis_index("gz")
    copies = []
    for side, plain_ref in enumerate(plain_refs):
        for i in range(half):
            rows = row_tile(lax.rem(me + side, 2) * half + i)
            for j in range(cells):
                plain = plain_ref[j, i * SUB:(i + 1) * SUB]
                result_ref[j, rows] = plain + alpha * unit_ref[j, rows]
            leave(copies, result_ref.at[:, rows], out_hbm.at[0, :, rows], sems)
    for copy in copies:
        copy.wait()


def shards(velocity, diffusion, wall_types, stretch_index, bulk_target):
    blocks = lax.axis_size("gz")
    columns = lax.axis_size("gy")
    components, cells, lines_y, lines_x = velocity.shape
    chips = blocks // 2
    row_tiles = lines_y // SUB
    half = row_tiles // 2
    f32 = jnp.float32
    vmem = pl.BlockSpec(memory_space=pltpu.VMEM)
    anywhere = pl.BlockSpec(memory_space=pl.ANY)
    plane = (lines_y, lines_x)
    sheet = (SUB, lines_x)

    def shape(*dims):
        return jax.ShapeDtypeStruct(dims, f32)

    def in_hbm(array):
        return pltpu.with_memory_space_constraint(array, pltpu.HBM)

    def options(mib):
        return pltpu.CompilerParams(vmem_limit_bytes=mib * MIB)

    def cost(flops, transferred):
        return pl.CostEstimate(flops=flops, bytes_accessed=transferred, transcendentals=0)

    def send(array, partner):
        pairs = [((z, y), partner(z, y)) for z in range(blocks) for y in range(columns)]
        route = [(a * columns + b, c * columns + d) for (a, b), (c, d) in pairs]
        return lax.ppermute(array, ("gz", "gy"), route)

    def to_mate(array):
        return send(array, lambda z, y: (z ^ 1, y))

    middle = half * SUB
    count = lines_x // LANES
    lines = float(lines_y * columns * lines_x)
    (mine, away, pair, chip_coefs, left, right, left_h, right_h, ends, volume,
     near_velocity) = pl.pallas_call(
        functools.partial(ladder_kernel, cells, blocks, chips, lines),
        out_shape=[
            shape(half * 2 * components * count, SUB, LANES),
            shape(half * 2 * components * count + 1, SUB, LANES),
            shape(4, *plane),
            shape(chips - 1, *plane),
            shape(cells, *plane),
            shape(cells, *plane),
            shape(cells, *plane),
            shape(cells, *plane),
            shape(2, *plane),
            shape(SUB, LANES),
            shape(*velocity.shape),
        ],
        in_specs=[anywhere] * 4,
        out_specs=[vmem] * 11,
        scratch_shapes=[
            pltpu.SMEM(stretch_index.shape, jnp.int32),
            pltpu.VMEM(plane, f32),
            pltpu.VMEM(plane, jnp.int32),
            pltpu.VMEM((blocks,) + plane, f32),
            pltpu.VMEM((STRETCHES,) + plane, f32),
            pltpu.VMEM((7,) + plane, f32),
            pltpu.SemaphoreType.DMA((3 + components,)),
        ],
        compiler_params=options(24),
        cost_estimate=cost(40_000_000, 6_000_000),
        name="ladder",
    )(in_hbm(stretch_index), in_hbm(diffusion), in_hbm(wall_types), in_hbm(velocity))

    mate = to_mate(away)
    *outgoing, near = pl.pallas_call(
        functools.partial(merge_kernel, chips, components),
        out_shape=[
            shape(half * components * count + m.bit_count(), SUB, LANES) for m in range(1, chips)
        ] + [shape(half * 2 * components * count + 1, SUB, LANES)],
        in_specs=[vmem] * 4,
        out_specs=[vmem] * chips,
        compiler_params=options(16),
        cost_estimate=cost(500_000, 1_600_000),
        name="merge",
    )(mine, away, mate, pair)
    order = sorted(range(1, chips), key=lambda m: -m.bit_count())
    incoming = [send(outgoing[m - 1], lambda z, y: (z ^ (2 * m), y)) for m in order]
    profile = shape(cells, *plane)
    base, unit, goal = pl.pallas_call(
        inner_kernel,
        out_shape=[shape(*velocity.shape), profile, shape(SUB, LANES)],
        in_specs=[vmem] * 8 + [anywhere],
        out_specs=[vmem] * 3,
        compiler_params=options(16),
        cost_estimate=cost(8_000_000, 8_000_000),
        name="inner",
    )(near_velocity, left, right, left_h, right_h, ends, volume, bulk_target.reshape(1, 1),
      outgoing[0])
    own_in, other_out, tile = pl.pallas_call(
        functools.partial(spread_kernel, order, components),
        out_shape=[shape(half * 2 * components, *sheet)] * 2 + [shape(SUB, LANES)],
        in_specs=[vmem] * 3 + [anywhere] + [vmem] * (chips - 1),
        out_specs=[vmem] * 3,
        compiler_params=options(16),
        cost_estimate=cost(500_000, 1_600_000),
        name="spread",
    )(near, pair, chip_coefs, base, *incoming)
    other_in = to_mate(other_out)
    tiles = [tile] + [
        send(tile, lambda z, y: (z, (y + shift) % columns)) for shift in range(1, columns)
    ]

    def finish(side, arrived, *before):
        return pl.pallas_call(
            functools.partial(finish_kernel, side),
            out_shape=[shape(*velocity.shape), shape(cells, middle, lines_x)],
            in_specs=[vmem] * 4 + [anywhere] * len(before),
            out_specs=[anywhere, vmem],
            scratch_shapes=[
                pltpu.VMEM((components - 1, cells, middle, lines_x), f32),
                pltpu.SemaphoreType.DMA(((components - 1) * half,)),
            ],
            input_output_aliases={4: 0} if before else {},
            compiler_params=options(16),
            cost_estimate=cost(3_000_000, 6_000_000),
            name="finish" + str(side),
        )(arrived, base, left, right, *before)

    partial, own_plain = finish(0, own_in)
    partial, other_plain = finish(1, other_in, partial)
    return pl.pallas_call(
        functools.partial(correct_kernel, columns),
        out_shape=shape(*velocity.shape),
        in_specs=[vmem] * (4 + columns) + [anywhere],
        out_specs=anywhere,
        scratch_shapes=[
            pltpu.VMEM((cells,) + plane, f32),
            pltpu.SemaphoreType.DMA((row_tiles,)),
        ],
        input_output_aliases={4 + columns: 0},
        compiler_params=options(16),
        cost_estimate=cost(500_000, 1_600_000),
        name="correct",
    )(goal, unit, *tiles, own_plain, other_plain, partial)


def solution(mesh):
    return jax.shard_map(
        shards,
        mesh=mesh,
        in_specs=(P(None, "gz", "gy", None), P("gy", None), P("gy", None), P(), P()),
        out_specs=P(None, "gz", "gy", None),
        check_vma=False,
    )
```

```python
import functools

import jax
import jax.numpy as jnp
from jax import lax
from jax.experimental import pallas as pl
from jax.experimental.pallas import tpu as pltpu
from jax.sharding import PartitionSpec as P

SUB = 8
STRETCHES = 7
TILES_TO_CHIPS = 3
TILES_TO_MATE = 22
TILES_ALONG_GY = 2
TILES_BACK = 47
LANES = 128
MIB = 1024 * 1024


def row_tile(t):
    return pl.ds(pl.multiple_of(t * SUB, SUB), SUB)


def put(ref, at, sheet):
    count = sheet.shape[1] // LANES
    for i in range(count):
        ref[at * count + i] = sheet[:, i * LANES:(i + 1) * LANES]


def get(ref, at, count):
    return jnp.concatenate([ref[at * count + i] for i in range(count)], axis=1)


def height(index_ref, k):
    return 0.5 + 0.25 * index_ref[k].astype(jnp.float32)


def half_sum(index_ref, k):
    return 0.5 * (height(index_ref, k) + height(index_ref, k + 1))


def ladder_kernel(
    cells, blocks, chips, lines,
    index_hbm, diffusion_hbm, walls_hbm, velocity_hbm,
    mine_ref, away_ref, pair_ref, chip_ref, left_ref, right_ref, left_h_ref, right_h_ref,
    ends_ref, volume_ref, velocity_ref, tile_ref,
    index_ref, diffusion_ref, walls_ref, through_ref, table_ref, held_ref, sems,
):
    total = cells * blocks
    components = velocity_ref.shape[0]
    row_tiles = diffusion_ref.shape[0] // SUB
    small = [
        pltpu.make_async_copy(index_hbm, index_ref, sems.at[0]),
        pltpu.make_async_copy(diffusion_hbm, diffusion_ref, sems.at[1]),
        pltpu.make_async_copy(walls_hbm, walls_ref, sems.at[2]),
    ]
    large = [
        pltpu.make_async_copy(velocity_hbm.at[c], velocity_ref.at[c], sems.at[3 + c])
        for c in range(components)
    ]
    for copy in small + large:
        copy.start()
    me = lax.axis_index("gz")
    chip = me // 2
    first = chip * 2
    for copy in small:
        copy.wait()
    diffusion = diffusion_ref[...]
    inverse = 1.0 / diffusion
    for i in range(STRETCHES):
        table_ref[i] = (0.5 + 0.25 * i) * inverse
    walls = walls_ref[...]

    def wall(bits, k):
        face = 1.0 / jnp.full((SUB, diffusion.shape[1]), 0.5 * height(index_ref, k))
        return bits.astype(jnp.float32) * jnp.concatenate([face] * row_tiles, axis=0)

    lower = wall(walls & 1, 0)
    upper = wall(walls >> 1, total - 1)

    def forward(block, kappa, keep=None):
        start = block * cells
        flux = table_ref[index_ref[start]] + kappa
        value = jnp.ones_like(flux)
        for j in range(cells):
            if keep is not None:
                keep(j, flux, value)
            k = start + j
            if j < cells - 1:
                value = value + half_sum(index_ref, k) * flux
                flux = flux + table_ref[index_ref[k + 1]] * value
        k = jnp.minimum(start + cells - 1, total - 2)
        after = 1.0 / (value + half_sum(index_ref, k) * flux)
        return flux * after, after

    def backward(block, kappa, scale=None, keep=None):
        start = block * cells
        flux = table_ref[index_ref[start + cells - 1]] + kappa
        value = jnp.ones_like(flux)
        if scale is not None:
            flux, value = flux * scale, scale
        for j in reversed(range(cells)):
            if keep is not None:
                keep(j, flux, value)
            k = start + j
            if j > 0:
                value = value + half_sum(index_ref, k - 1) * flux
                flux = flux + table_ref[index_ref[k - 1]] * value
        k = jnp.maximum(start - 1, 0)
        after = 1.0 / (value + half_sum(index_ref, k) * flux)
        return flux * after, after

    def thickness(block):
        parts = [height(index_ref, block * cells + j) for j in range(cells)]
        return functools.reduce(jnp.add, parts)

    def sweep_forward(block, state):
        kappa, product, extent = state
        kappa, after = forward(block, kappa)
        through_ref[block] = after
        return kappa, product * after, extent + thickness(block)

    def sweep_backward(step, state):
        block = blocks - 1 - step
        kappa, product, extent = state
        kappa, after = backward(block, kappa)
        through_ref[block] = after
        return kappa, product * after, extent + thickness(block)

    ones = jnp.ones_like(diffusion)
    kappa_left, product, extent = lax.fori_loop(
        0, me, sweep_forward, (lower, ones, thickness(me))
    )
    ends_ref[0] = diffusion * lower * product
    state = {}

    def keep_left(j, flux, value):
        left_ref[j] = value
        left_h_ref[j] = height(index_ref, me * cells + j) * value
        state["flux"], state["value"] = flux, value

    kappa, own_forward = forward(me, kappa_left, keep_left)
    held_ref[1] = own_forward
    held_ref[3] = state["flux"]
    held_ref[4] = state["value"]
    held_ref[5] = state["flux"] - kappa_left

    @pl.when(me == first)
    def _():
        pair_ref[2] = own_forward
        _, after = forward(me + 1, kappa)
        pair_ref[0] = after

    @pl.when(me != first)
    def _():
        pair_ref[2] = through_ref[first]
        pair_ref[0] = own_forward

    kappa_right, product, extent = lax.fori_loop(
        0, blocks - 1 - me, sweep_backward, (upper, ones, extent)
    )
    ends_ref[1] = diffusion_ref[...] * upper * product
    scale = 1.0 / (diffusion_ref[...] * (held_ref[3] + kappa_right * held_ref[4]))
    held_ref[0] = scale

    def keep_right(j, flux, value):
        right_ref[j] = value
        right_h_ref[j] = height(index_ref, me * cells + j) * value
        state["flux"] = flux

    kappa, own_backward = backward(me, kappa_right, scale, keep_right)
    held_ref[2] = own_backward
    held_ref[6] = state["flux"] - kappa_right * scale

    @pl.when(me == first)
    def _():
        pair_ref[1] = own_backward * held_ref[0]
        pair_ref[3] = through_ref[first + 1]

    @pl.when(me != first)
    def _():
        pair_ref[3] = own_backward * held_ref[0]
        _, after = backward(me - 1, kappa)
        pair_ref[1] = after

    for m in range(1, chips):
        other = chip ^ m
        low = jnp.minimum(chip, other)
        high = jnp.maximum(chip, other)
        chip_ref[m - 1] = lax.fori_loop(
            low + 1,
            high,
            lambda r, product: product * (through_ref[2 * r] * through_ref[2 * r + 1]),
            ones,
        )
    flow = jnp.zeros((SUB, LANES), jnp.float32)
    weight = jnp.zeros((SUB, LANES), jnp.float32)

    def fold(array):
        parts = [array[:, i * LANES:(i + 1) * LANES] for i in range(array.shape[1] // LANES)]
        return functools.reduce(jnp.add, parts)

    for copy in large:
        copy.wait()
    volume_ref[...] = jnp.full(volume_ref.shape, extent * lines)
    half = row_tiles // 2
    own_extent = thickness(me)
    heights = [height(index_ref, me * cells + j) for j in range(cells)]
    for ref, whose in ((away_ref, 1 - (me - first)), (mine_ref, me - first)):
        for i in range(half):
            rows = row_tile(whose * half + i)
            from_left = [0.0] * components
            from_right = [0.0] * components
            plain = 0.0
            for j in range(cells):
                left = left_h_ref[j, rows]
                right = right_h_ref[j, rows]
                for c in range(components):
                    v = velocity_ref[c, j, rows]
                    from_left[c] = from_left[c] + left * v
                    from_right[c] = from_right[c] + right * v
                    if c == 0:
                        plain = plain + heights[j] * v
            for c in range(components):
                at = i * 2 * components + c
                put(ref, at, from_left[c] * held_ref[1, rows])
                put(ref, at + components, from_right[c] * held_ref[2, rows])
            low_part = ends_ref[0, rows]
            high_part = ends_ref[1, rows] * held_ref[0, rows]
            flow = flow + fold(plain - low_part * from_right[0] - high_part * from_left[0])
            totals = low_part * held_ref[6, rows] + high_part * held_ref[5, rows]
            weight = weight + fold(own_extent - diffusion_ref[rows] * totals)
    middle = SUB // 2
    for i in range(tile_ref.shape[0]):
        tile_ref[i, 0:middle] = flow[0:middle] + flow[middle:]
        tile_ref[i, middle:] = weight[0:middle] + weight[middle:]


def merge_kernel(chips, components, mine_ref, mate_ref, pair_ref, *rest):
    send_refs, near_ref = rest[:-1], rest[-1]
    me = lax.axis_index("gz")
    chip = me // 2
    is_first = me == chip * 2
    count = pair_ref.shape[2] // LANES
    half = mine_ref.shape[0] // (2 * components * count)
    for ref in send_refs:
        for at in range(half * components * count, ref.shape[0]):
            ref[at] = jnp.zeros((SUB, LANES), jnp.float32)
    for i in range(half):
        rows = row_tile((me - chip * 2) * half + i)
        for c in range(components):
            at = i * 2 * components + c
            mine, mate = get(mine_ref, at, count), get(mate_ref, at, count)
            first = jnp.where(is_first, mine, mate)
            second = jnp.where(is_first, mate, mine)
            put(near_ref, at, first)
            to_right = second + pair_ref[0, rows] * first
            at = at + components
            mine, mate = get(mine_ref, at, count), get(mate_ref, at, count)
            first = jnp.where(is_first, mine, mate)
            second = jnp.where(is_first, mate, mine)
            put(near_ref, at, second)
            to_left = first + pair_ref[1, rows] * second
            for m in range(1, chips):
                goes_right = (chip ^ m) > chip
                sheet = jnp.where(goes_right, to_right, to_left)
                put(send_refs[m - 1], i * components + c, sheet)


def spread_kernel(order, components, near_ref, pair_ref, chip_ref, *rest):
    recv_refs, (own_ref, other_ref) = rest[1:-2], rest[-2:]
    me = lax.axis_index("gz")
    chip = me // 2
    is_first = me == chip * 2
    count = pair_ref.shape[2] // LANES
    half = near_ref.shape[0] // (2 * components * count)
    for i in range(half):
        rows = row_tile((me - chip * 2) * half + i)
        coefs = [chip_ref[m - 1, rows] for m in order]
        for c in range(components):
            left_in = jnp.zeros(own_ref.shape[1:], jnp.float32)
            right_in = jnp.zeros(own_ref.shape[1:], jnp.float32)
            for m, coef, ref in zip(order, coefs, recv_refs):
                term = coef * get(ref, i * components + c, count)
                from_left = (chip ^ m) < chip
                left_in = left_in + jnp.where(from_left, term, 0.0)
                right_in = right_in + jnp.where(from_left, 0.0, term)
            at = i * 2 * components + c
            left_second = get(near_ref, at, count) + pair_ref[2, rows] * left_in
            right_first = get(near_ref, at + components, count) + pair_ref[3, rows] * right_in
            own_ref[at] = jnp.where(is_first, left_in, left_second)
            other_ref[at] = jnp.where(is_first, left_second, left_in)
            at = at + components
            own_ref[at] = jnp.where(is_first, right_first, right_in)
            other_ref[at] = jnp.where(is_first, right_in, right_first)


def leave(copies, source, target, sems):
    copies.append(pltpu.make_async_copy(source, target, sems.at[len(copies)]))
    copies[-1].start()


def add_kernel(*refs):
    total = functools.reduce(jnp.add, [ref[0] for ref in refs[:-1]])
    for i in range(refs[-1].shape[0]):
        refs[-1][i] = total


def inner_kernel(
    velocity_ref, left_ref, right_ref, left_h_ref, right_h_ref, ends_ref, volume_ref, target_ref,
    _, base_ref, unit_ref, goal_ref,
):
    components, cells, lines_y, lines_x = velocity_ref.shape
    goal_ref[...] = target_ref[...] * volume_ref[...]
    for t in range(lines_y // SUB):
        rows = row_tile(t)
        gathered = [jnp.zeros((SUB, lines_x), jnp.float32)] * components
        for j in reversed(range(cells)):
            left = left_ref[j, rows]
            right = right_h_ref[j, rows]
            for c in range(components):
                base_ref[c, j, rows] = left * gathered[c]
                if j > 0:
                    gathered[c] = gathered[c] + right * velocity_ref[c, j, rows]
        gathered = [jnp.zeros((SUB, lines_x), jnp.float32)] * components
        low_part = ends_ref[0, rows]
        high_part = ends_ref[1, rows] * right_ref[cells - 1, rows]
        for j in range(cells):
            left = left_h_ref[j, rows]
            right = right_ref[j, rows]
            unit_ref[j, rows] = 1.0 - (low_part * right + high_part * left_ref[j, rows])
            for c in range(components):
                gathered[c] = gathered[c] + left * velocity_ref[c, j, rows]
                base_ref[c, j, rows] = base_ref[c, j, rows] + right * gathered[c]


def finish_kernel(
    own_ref, other_ref, base_ref, left_ref, right_ref, out_hbm, plain_ref, result_ref, sems
):
    components, cells, _, _ = base_ref.shape
    half = own_ref.shape[0] // (2 * components)
    me = lax.axis_index("gz")
    copies = []
    for side, incoming_ref in enumerate((own_ref, other_ref)):
        for i in range(half):
            rows = row_tile(lax.rem(me + side, 2) * half + i)
            scale = right_ref[cells - 1, rows]
            at = i * 2 * components
            lefts = [incoming_ref[at + c] for c in range(components)]
            rights = [incoming_ref[at + components + c] * scale for c in range(components)]
            for j in range(cells):
                left = left_ref[j, rows]
                right = right_ref[j, rows]
                for c in range(components):
                    value = base_ref[c, j, rows] + (right * lefts[c] + left * rights[c])
                    if c == 0:
                        plain_ref[j, rows] = value
                    else:
                        result_ref[c - 1, j, rows] = value
            for c in range(1, components):
                leave(copies, result_ref.at[c - 1, :, rows], out_hbm.at[c, :, rows], sems)
    for copy in copies:
        copy.wait()


def correct_kernel(
    goal_ref, unit_ref, tile_ref, plain_ref, _, out_hbm, result_ref, sems
):
    totals = tile_ref[0]
    flow = jnp.sum(totals[0:SUB // 2], keepdims=True)
    weight = jnp.sum(totals[SUB // 2:], keepdims=True)
    alpha = (goal_ref[0:1, 0:1] - flow) / weight
    cells, lines_y, _ = plain_ref.shape
    copies = []
    for t in range(lines_y // SUB):
        rows = row_tile(t)
        for j in range(cells):
            result_ref[j, rows] = plain_ref[j, rows] + alpha * unit_ref[j, rows]
        leave(copies, result_ref.at[:, rows], out_hbm.at[0, :, rows], sems)
    for copy in copies:
        copy.wait()


def shards(velocity, diffusion, wall_types, stretch_index, bulk_target):
    blocks = lax.axis_size("gz")
    columns = lax.axis_size("gy")
    components, cells, lines_y, lines_x = velocity.shape
    chips = blocks // 2
    row_tiles = lines_y // SUB
    half = row_tiles // 2
    f32 = jnp.float32
    vmem = pl.BlockSpec(memory_space=pltpu.VMEM)
    anywhere = pl.BlockSpec(memory_space=pl.ANY)
    plane = (lines_y, lines_x)
    sheet = (SUB, lines_x)

    def shape(*dims):
        return jax.ShapeDtypeStruct(dims, f32)

    def in_hbm(array):
        return pltpu.with_memory_space_constraint(array, pltpu.HBM)

    def options(mib):
        return pltpu.CompilerParams(vmem_limit_bytes=mib * MIB)

    def cost(flops, transferred):
        return pl.CostEstimate(flops=flops, bytes_accessed=transferred, transcendentals=0)

    def send(array, partner):
        pairs = [((z, y), partner(z, y)) for z in range(blocks) for y in range(columns)]
        route = [(a * columns + b, c * columns + d) for (a, b), (c, d) in pairs]
        return lax.ppermute(array, ("gz", "gy"), route)

    def to_mate(array):
        return send(array, lambda z, y: (z ^ 1, y))

    def to_chip(array, m):
        return send(array, lambda z, y: (z ^ (2 * m), y))

    def add(tiles, *arrays):
        return pl.pallas_call(
            add_kernel,
            out_shape=shape(tiles, SUB, LANES),
            in_specs=[vmem] * len(arrays),
            out_specs=vmem,
            compiler_params=options(16),
            cost_estimate=cost(10_000, 40_000),
            name="add",
        )(*arrays)

    count = lines_x // LANES
    lines = float(lines_y * columns * lines_x)
    (mine, away, pair, chip_coefs, left, right, left_h, right_h, ends, volume,
     near_velocity, tile) = pl.pallas_call(
        functools.partial(ladder_kernel, cells, blocks, chips, lines),
        out_shape=[
            shape(half * 2 * components * count, SUB, LANES),
            shape(half * 2 * components * count, SUB, LANES),
            shape(4, *plane),
            shape(chips - 1, *plane),
            shape(cells, *plane),
            shape(cells, *plane),
            shape(cells, *plane),
            shape(cells, *plane),
            shape(2, *plane),
            shape(SUB, LANES),
            shape(*velocity.shape),
            shape(TILES_TO_CHIPS, SUB, LANES),
        ],
        in_specs=[anywhere] * 4,
        out_specs=[vmem] * 12,
        scratch_shapes=[
            pltpu.SMEM(stretch_index.shape, jnp.int32),
            pltpu.VMEM(plane, f32),
            pltpu.VMEM(plane, jnp.int32),
            pltpu.VMEM((blocks,) + plane, f32),
            pltpu.VMEM((STRETCHES,) + plane, f32),
            pltpu.VMEM((7,) + plane, f32),
            pltpu.SemaphoreType.DMA((3 + components,)),
        ],
        compiler_params=options(24),
        cost_estimate=cost(40_000_000, 6_000_000),
        name="ladder",
    )(in_hbm(stretch_index), in_hbm(diffusion), in_hbm(wall_types), in_hbm(velocity))

    mate = to_mate(away)
    order = sorted(range(1, chips), key=lambda m: -m.bit_count())
    core_tile = add(TILES_TO_MATE, tile, *[to_chip(tile, m) for m in order])
    plane_tile = add(TILES_ALONG_GY, core_tile, to_mate(core_tile))
    gathered = [
        send(plane_tile, lambda z, y: (z, (y + shift) % columns)) for shift in range(1, columns)
    ]
    whole_tile = to_mate(add(TILES_BACK, plane_tile, *gathered))
    *outgoing, near = pl.pallas_call(
        functools.partial(merge_kernel, chips, components),
        out_shape=[
            shape(half * components * count + m.bit_count() - 1, SUB, LANES) for m in range(1, chips)
        ] + [shape(half * 2 * components * count, SUB, LANES)],
        in_specs=[vmem] * 3,
        out_specs=[vmem] * chips,
        compiler_params=options(16),
        cost_estimate=cost(500_000, 1_600_000),
        name="merge",
    )(mine, mate, pair)
    incoming = [to_chip(outgoing[m - 1], m) for m in order]
    profile = shape(cells, *plane)
    base, unit, goal = pl.pallas_call(
        inner_kernel,
        out_shape=[shape(*velocity.shape), profile, shape(SUB, LANES)],
        in_specs=[vmem] * 8 + [anywhere],
        out_specs=[vmem] * 3,
        compiler_params=options(16),
        cost_estimate=cost(8_000_000, 8_000_000),
        name="inner",
    )(near_velocity, left, right, left_h, right_h, ends, volume, bulk_target.reshape(1, 1),
      outgoing[0])
    own_in, other_out = pl.pallas_call(
        functools.partial(spread_kernel, order, components),
        out_shape=[shape(half * 2 * components, *sheet)] * 2,
        in_specs=[vmem] * 3 + [anywhere] + [vmem] * (chips - 1),
        out_specs=[vmem] * 2,
        compiler_params=options(16),
        cost_estimate=cost(500_000, 1_600_000),
        name="spread",
    )(near, pair, chip_coefs, base, *incoming)
    other_in = to_mate(other_out)
    partial, plain = pl.pallas_call(
        finish_kernel,
        out_shape=[shape(*velocity.shape), profile],
        in_specs=[vmem] * 5,
        out_specs=[anywhere, vmem],
        scratch_shapes=[
            pltpu.VMEM((components - 1, cells) + plane, f32),
            pltpu.SemaphoreType.DMA(((components - 1) * row_tiles,)),
        ],
        compiler_params=options(16),
        cost_estimate=cost(3_000_000, 6_000_000),
        name="finish",
    )(own_in, other_in, base, left, right)
    return pl.pallas_call(
        correct_kernel,
        out_shape=shape(*velocity.shape),
        in_specs=[vmem] * 4 + [anywhere],
        out_specs=anywhere,
        scratch_shapes=[
            pltpu.VMEM((cells,) + plane, f32),
            pltpu.SemaphoreType.DMA((row_tiles,)),
        ],
        input_output_aliases={4: 0},
        compiler_params=options(16),
        cost_estimate=cost(500_000, 1_600_000),
        name="correct",
    )(goal, unit, whole_tile, plain, partial)


def solution(mesh):
    return jax.shard_map(
        shards,
        mesh=mesh,
        in_specs=(P(None, "gz", "gy", None), P("gy", None), P("gy", None), P(), P()),
        out_specs=P(None, "gz", "gy", None),
        check_vma=False,
    )
```

```python
import functools

import jax
import jax.numpy as jnp
from jax import lax
from jax.experimental import pallas as pl
from jax.experimental.pallas import tpu as pltpu
from jax.sharding import PartitionSpec as P

SUB = 8
STRETCHES = 7
LANES = 128
MIB = 1024 * 1024


def row_tile(t):
    return pl.ds(pl.multiple_of(t * SUB, SUB), SUB)


def put(ref, at, sheet):
    count = sheet.shape[1] // LANES
    for i in range(count):
        ref[at * count + i] = sheet[:, i * LANES:(i + 1) * LANES]


def get(ref, at, count):
    return jnp.concatenate([ref[at * count + i] for i in range(count)], axis=1)


def height(index_ref, k):
    return 0.5 + 0.25 * index_ref[k].astype(jnp.float32)


def half_sum(index_ref, k):
    return 0.5 * (height(index_ref, k) + height(index_ref, k + 1))


def ladder_kernel(
    cells, blocks, chips, lines,
    index_hbm, diffusion_hbm, walls_hbm, velocity_hbm,
    mine_ref, away_ref, pair_ref, chip_ref, left_ref, right_ref, left_h_ref, right_h_ref,
    ends_ref, volume_ref, velocity_ref,
    index_ref, diffusion_ref, walls_ref, through_ref, table_ref, held_ref, sems,
):
    total = cells * blocks
    components = velocity_ref.shape[0]
    row_tiles = diffusion_ref.shape[0] // SUB
    small = [
        pltpu.make_async_copy(index_hbm, index_ref, sems.at[0]),
        pltpu.make_async_copy(diffusion_hbm, diffusion_ref, sems.at[1]),
        pltpu.make_async_copy(walls_hbm, walls_ref, sems.at[2]),
    ]
    large = [
        pltpu.make_async_copy(velocity_hbm.at[c], velocity_ref.at[c], sems.at[3 + c])
        for c in range(components)
    ]
    for copy in small + large:
        copy.start()
    me = lax.axis_index("gz")
    chip = me // 2
    first = chip * 2
    for copy in small:
        copy.wait()
    diffusion = diffusion_ref[...]
    inverse = 1.0 / diffusion
    for i in range(STRETCHES):
        table_ref[i] = (0.5 + 0.25 * i) * inverse
    walls = walls_ref[...]

    def wall(bits, k):
        face = 1.0 / jnp.full((SUB, diffusion.shape[1]), 0.5 * height(index_ref, k))
        return bits.astype(jnp.float32) * jnp.concatenate([face] * row_tiles, axis=0)

    lower = wall(walls & 1, 0)
    upper = wall(walls >> 1, total - 1)

    def forward(block, kappa, keep=None):
        start = block * cells
        flux = table_ref[index_ref[start]] + kappa
        value = jnp.ones_like(flux)
        for j in range(cells):
            if keep is not None:
                keep(j, flux, value)
            k = start + j
            if j < cells - 1:
                value = value + half_sum(index_ref, k) * flux
                flux = flux + table_ref[index_ref[k + 1]] * value
        k = jnp.minimum(start + cells - 1, total - 2)
        after = 1.0 / (value + half_sum(index_ref, k) * flux)
        return flux * after, after

    def backward(block, kappa, scale=None, keep=None):
        start = block * cells
        flux = table_ref[index_ref[start + cells - 1]] + kappa
        value = jnp.ones_like(flux)
        if scale is not None:
            flux, value = flux * scale, scale
        for j in reversed(range(cells)):
            if keep is not None:
                keep(j, flux, value)
            k = start + j
            if j > 0:
                value = value + half_sum(index_ref, k - 1) * flux
                flux = flux + table_ref[index_ref[k - 1]] * value
        k = jnp.maximum(start - 1, 0)
        after = 1.0 / (value + half_sum(index_ref, k) * flux)
        return flux * after, after

    def thickness(block):
        parts = [height(index_ref, block * cells + j) for j in range(cells)]
        return functools.reduce(jnp.add, parts)

    def sweep_forward(block, state):
        kappa, product, extent = state
        kappa, after = forward(block, kappa)
        through_ref[block] = after
        return kappa, product * after, extent + thickness(block)

    def sweep_backward(step, state):
        block = blocks - 1 - step
        kappa, product, extent = state
        kappa, after = backward(block, kappa)
        through_ref[block] = after
        return kappa, product * after, extent + thickness(block)

    ones = jnp.ones_like(diffusion)
    kappa_left, product, extent = lax.fori_loop(
        0, me, sweep_forward, (lower, ones, thickness(me))
    )
    ends_ref[0] = diffusion * lower * product
    state = {}

    def keep_left(j, flux, value):
        left_ref[j] = value
        left_h_ref[j] = height(index_ref, me * cells + j) * value
        state["flux"], state["value"] = flux, value

    _, own_forward = forward(me, kappa_left, keep_left)
    held_ref[1] = own_forward
    held_ref[3] = state["flux"]
    held_ref[4] = state["value"]
    held_ref[5] = state["flux"] - kappa_left

    kappa_right, product, extent = lax.fori_loop(
        0, blocks - 1 - me, sweep_backward, (upper, ones, extent)
    )
    ends_ref[1] = diffusion_ref[...] * upper * product
    scale = 1.0 / (diffusion_ref[...] * (held_ref[3] + kappa_right * held_ref[4]))
    held_ref[0] = scale

    def keep_right(j, flux, value):
        right_ref[j] = value
        right_h_ref[j] = height(index_ref, me * cells + j) * value
        state["flux"] = flux

    _, own_backward = backward(me, kappa_right, scale, keep_right)
    held_ref[2] = own_backward
    held_ref[6] = state["flux"] - kappa_right * scale

    is_first = me == first
    forth, back = held_ref[1], own_backward * held_ref[0]
    pair_ref[0] = jnp.where(is_first, back, forth)
    pair_ref[1] = jnp.where(is_first, forth, through_ref[first])
    pair_ref[2] = jnp.where(is_first, through_ref[first + 1], back)
    for m in range(1, chips):
        other = chip ^ m
        low = jnp.minimum(chip, other)
        high = jnp.maximum(chip, other)
        chip_ref[m - 1] = lax.fori_loop(
            low + 1,
            high,
            lambda r, product: product * (through_ref[2 * r] * through_ref[2 * r + 1]),
            ones,
        )

    def fold(array):
        parts = [array[:, i * LANES:(i + 1) * LANES] for i in range(array.shape[1] // LANES)]
        return functools.reduce(jnp.add, parts)

    for copy in large:
        copy.wait()
    volume_ref[...] = jnp.full(volume_ref.shape, extent * lines)
    half = row_tiles // 2
    own_extent = thickness(me)
    heights = [height(index_ref, me * cells + j) for j in range(cells)]

    def sums(ref, whose):
        def of_tile(i, state):
            flow, weight = state
            rows = row_tile(whose * half + i)
            from_left = [0.0] * components
            from_right = [0.0] * components
            plain = 0.0
            for j in range(cells):
                left = left_h_ref[j, rows]
                right = right_h_ref[j, rows]
                for c in range(components):
                    v = velocity_ref[c, j, rows]
                    from_left[c] = from_left[c] + left * v
                    from_right[c] = from_right[c] + right * v
                    if c == 0:
                        plain = plain + heights[j] * v
            for c in range(components):
                at = i * 2 * components + c
                put(ref, at, from_left[c] * held_ref[1, rows])
                put(ref, at + components, from_right[c] * held_ref[2, rows])
            low_part = ends_ref[0, rows]
            high_part = ends_ref[1, rows] * held_ref[0, rows]
            totals = low_part * held_ref[6, rows] + high_part * held_ref[5, rows]
            return (
                flow + fold(plain - low_part * from_right[0] - high_part * from_left[0]),
                weight + fold(own_extent - diffusion_ref[rows] * totals),
            )

        return of_tile

    state = (jnp.zeros((SUB, LANES), jnp.float32),) * 2
    mates = 1 - (me - first)
    state = lax.fori_loop(0, half, sums(away_ref, mates), state)
    flow, weight = lax.fori_loop(0, half, sums(mine_ref, me - first), state)
    for i in range(half):
        put(away_ref, half * 2 * components + i, pair_ref[0, row_tile(mates * half + i)])
    slot, middle = away_ref.shape[0] - 1, SUB // 2
    away_ref[slot, 0:middle] = flow[0:middle] + flow[middle:]
    away_ref[slot, middle:] = weight[0:middle] + weight[middle:]


def merge_kernel(chips, components, mine_ref, away_ref, mate_ref, pair_ref, *rest):
    send_refs, near_ref = rest[:-1], rest[-1]
    me = lax.axis_index("gz")
    chip = me // 2
    is_first = me == chip * 2
    count = pair_ref.shape[2] // LANES
    half = mine_ref.shape[0] // (2 * components * count)
    slot = away_ref.shape[0] - 1
    tile = away_ref[slot] + mate_ref[slot]
    near_ref[near_ref.shape[0] - 1] = tile
    for ref in send_refs:
        for at in range(half * components * count, ref.shape[0]):
            ref[at] = tile
    for i in range(half):
        rows = row_tile((me - chip * 2) * half + i)
        mine, mate = pair_ref[0, rows], get(mate_ref, half * 2 * components + i, count)
        forth = jnp.where(is_first, mate, mine)
        back = jnp.where(is_first, mine, mate)
        for c in range(components):
            at = i * 2 * components + c
            mine, mate = get(mine_ref, at, count), get(mate_ref, at, count)
            first = jnp.where(is_first, mine, mate)
            second = jnp.where(is_first, mate, mine)
            put(near_ref, at, first)
            to_right = second + forth * first
            at = at + components
            mine, mate = get(mine_ref, at, count), get(mate_ref, at, count)
            first = jnp.where(is_first, mine, mate)
            second = jnp.where(is_first, mate, mine)
            put(near_ref, at, second)
            to_left = first + back * second
            for m in range(1, chips):
                goes_right = (chip ^ m) > chip
                sheet = jnp.where(goes_right, to_right, to_left)
                put(send_refs[m - 1], i * components + c, sheet)


def spread_kernel(order, components, near_ref, pair_ref, chip_ref, *rest):
    recv_refs = rest[1:len(order) + 1]
    own_ref, other_ref, *tile_refs = rest[len(order) + 1:]
    me = lax.axis_index("gz")
    chip = me // 2
    is_first = me == chip * 2
    count = pair_ref.shape[2] // LANES
    half = near_ref.shape[0] // (2 * components * count)
    tiles = [ref[ref.shape[0] - 1] for ref in (near_ref, *recv_refs)]
    tile = functools.reduce(jnp.add, tiles)
    for ref in tile_refs:
        for i in range(ref.shape[0]):
            ref[i] = tile
    for i in range(half):
        rows = row_tile((me - chip * 2) * half + i)
        coefs = [chip_ref[m - 1, rows] for m in order]
        for c in range(components):
            left_in = jnp.zeros(own_ref.shape[1:], jnp.float32)
            right_in = jnp.zeros(own_ref.shape[1:], jnp.float32)
            for m, coef, ref in zip(order, coefs, recv_refs):
                term = coef * get(ref, i * components + c, count)
                from_left = (chip ^ m) < chip
                left_in = left_in + jnp.where(from_left, term, 0.0)
                right_in = right_in + jnp.where(from_left, 0.0, term)
            at = i * 2 * components + c
            left_second = get(near_ref, at, count) + pair_ref[1, rows] * left_in
            right_first = get(near_ref, at + components, count) + pair_ref[2, rows] * right_in
            own_ref[at] = jnp.where(is_first, left_in, left_second)
            other_ref[at] = jnp.where(is_first, left_second, left_in)
            at = at + components
            own_ref[at] = jnp.where(is_first, right_first, right_in)
            other_ref[at] = jnp.where(is_first, right_in, right_first)


def inner_kernel(
    velocity_ref, left_ref, right_ref, left_h_ref, right_h_ref, ends_ref, volume_ref, target_ref,
    _, base_ref, unit_ref, goal_ref,
):
    components, cells, lines_y, lines_x = velocity_ref.shape
    goal_ref[...] = target_ref[...] * volume_ref[...]

    def of_tile(t, _):
        rows = row_tile(t)
        gathered = [jnp.zeros((SUB, lines_x), jnp.float32)] * components
        for j in reversed(range(cells)):
            left = left_ref[j, rows]
            right = right_h_ref[j, rows]
            for c in range(components):
                base_ref[c, j, rows] = left * gathered[c]
                if j > 0:
                    gathered[c] = gathered[c] + right * velocity_ref[c, j, rows]
        gathered = [jnp.zeros((SUB, lines_x), jnp.float32)] * components
        low_part = ends_ref[0, rows]
        high_part = ends_ref[1, rows] * right_ref[cells - 1, rows]
        for j in range(cells):
            left = left_h_ref[j, rows]
            right = right_ref[j, rows]
            unit_ref[j, rows] = 1.0 - (low_part * right + high_part * left_ref[j, rows])
            for c in range(components):
                gathered[c] = gathered[c] + left * velocity_ref[c, j, rows]
                base_ref[c, j, rows] = base_ref[c, j, rows] + right * gathered[c]
        return 0

    lax.fori_loop(0, lines_y // SUB, of_tile, 0)


def finish_kernel(
    own_ref, other_ref, base_ref, left_ref, right_ref, out_hbm, plain_ref, result_ref, sems
):
    components, cells, lines_y, _ = base_ref.shape
    half = own_ref.shape[0] // (2 * components)
    me = lax.axis_index("gz")

    def copies(t):
        rows = row_tile(t)
        return [
            pltpu.make_async_copy(
                result_ref.at[c - 1, :, rows], out_hbm.at[c, :, rows], sems.at[t, c - 1])
            for c in range(1, components)
        ]

    def half_of(incoming_ref, side):
        def of_tile(i, _):
            t = lax.rem(me + side, 2) * half + i
            rows = row_tile(t)
            scale = right_ref[cells - 1, rows]
            at = i * 2 * components
            lefts = [incoming_ref[at + c] for c in range(components)]
            rights = [incoming_ref[at + components + c] * scale for c in range(components)]
            for j in range(cells):
                left = left_ref[j, rows]
                right = right_ref[j, rows]
                for c in range(components):
                    value = base_ref[c, j, rows] + (right * lefts[c] + left * rights[c])
                    if c == 0:
                        plain_ref[j, rows] = value
                    else:
                        result_ref[c - 1, j, rows] = value
            for copy in copies(t):
                copy.start()
            return 0

        lax.fori_loop(0, half, of_tile, 0)

    half_of(own_ref, 0)
    half_of(other_ref, 1)
    for t in range(lines_y // SUB):
        for copy in copies(t):
            copy.wait()


def correct_kernel(columns, goal_ref, unit_ref, *rest):
    tile_refs = rest[:columns]
    plain_ref, _, out_hbm, result_ref, sems = rest[columns:]
    totals = functools.reduce(jnp.add, [ref[0] for ref in tile_refs])
    flow = jnp.sum(totals[0:SUB // 2], keepdims=True)
    weight = jnp.sum(totals[SUB // 2:], keepdims=True)
    alpha = (goal_ref[0:1, 0:1] - flow) / weight
    cells, lines_y, _ = plain_ref.shape

    def copy(t):
        rows = row_tile(t)
        return pltpu.make_async_copy(result_ref.at[:, rows], out_hbm.at[0, :, rows], sems.at[t])

    def of_tile(t, _):
        rows = row_tile(t)
        for j in range(cells):
            result_ref[j, rows] = plain_ref[j, rows] + alpha * unit_ref[j, rows]
        copy(t).start()
        return 0

    lax.fori_loop(0, lines_y // SUB, of_tile, 0)
    for t in range(lines_y // SUB):
        copy(t).wait()


def shards(velocity, diffusion, wall_types, stretch_index, bulk_target):
    blocks = lax.axis_size("gz")
    columns = lax.axis_size("gy")
    components, cells, lines_y, lines_x = velocity.shape
    chips = blocks // 2
    row_tiles = lines_y // SUB
    half = row_tiles // 2
    f32 = jnp.float32
    vmem = pl.BlockSpec(memory_space=pltpu.VMEM)
    anywhere = pl.BlockSpec(memory_space=pl.ANY)
    plane = (lines_y, lines_x)
    sheet = (SUB, lines_x)

    def shape(*dims):
        return jax.ShapeDtypeStruct(dims, f32)

    def in_hbm(array):
        return pltpu.with_memory_space_constraint(array, pltpu.HBM)

    def options(mib):
        return pltpu.CompilerParams(vmem_limit_bytes=mib * MIB)

    def cost(flops, transferred):
        return pl.CostEstimate(flops=flops, bytes_accessed=transferred, transcendentals=0)

    def send(array, partner):
        pairs = [((z, y), partner(z, y)) for z in range(blocks) for y in range(columns)]
        route = [(a * columns + b, c * columns + d) for (a, b), (c, d) in pairs]
        return lax.ppermute(array, ("gz", "gy"), route)

    def to_mate(array):
        return send(array, lambda z, y: (z ^ 1, y))

    count = lines_x // LANES
    lines = float(lines_y * columns * lines_x)
    (mine, away, pair, chip_coefs, left, right, left_h, right_h, ends, volume,
     near_velocity) = pl.pallas_call(
        functools.partial(ladder_kernel, cells, blocks, chips, lines),
        out_shape=[
            shape(half * 2 * components * count, SUB, LANES),
            shape(half * (2 * components + 1) * count + 1, SUB, LANES),
            shape(3, *plane),
            shape(chips - 1, *plane),
            shape(cells, *plane),
            shape(cells, *plane),
            shape(cells, *plane),
            shape(cells, *plane),
            shape(2, *plane),
            shape(SUB, LANES),
            shape(*velocity.shape),
        ],
        in_specs=[anywhere] * 4,
        out_specs=[vmem] * 11,
        scratch_shapes=[
            pltpu.SMEM(stretch_index.shape, jnp.int32),
            pltpu.VMEM(plane, f32),
            pltpu.VMEM(plane, jnp.int32),
            pltpu.VMEM((blocks,) + plane, f32),
            pltpu.VMEM((STRETCHES,) + plane, f32),
            pltpu.VMEM((7,) + plane, f32),
            pltpu.SemaphoreType.DMA((3 + components,)),
        ],
        compiler_params=options(24),
        cost_estimate=cost(40_000_000, 6_000_000),
        name="ladder",
    )(in_hbm(stretch_index), in_hbm(diffusion), in_hbm(wall_types), in_hbm(velocity))

    mate = to_mate(away)
    *outgoing, near = pl.pallas_call(
        functools.partial(merge_kernel, chips, components),
        out_shape=[
            shape(half * components * count + m.bit_count(), SUB, LANES) for m in range(1, chips)
        ] + [shape(half * 2 * components * count + 1, SUB, LANES)],
        in_specs=[vmem] * 4,
        out_specs=[vmem] * chips,
        compiler_params=options(16),
        cost_estimate=cost(500_000, 1_600_000),
        name="merge",
    )(mine, away, mate, pair)
    order = sorted(range(1, chips), key=lambda m: -m.bit_count())
    incoming = [send(outgoing[m - 1], lambda z, y: (z ^ (2 * m), y)) for m in order]
    profile = shape(cells, *plane)
    base, unit, goal = pl.pallas_call(
        inner_kernel,
        out_shape=[shape(*velocity.shape), profile, shape(SUB, LANES)],
        in_specs=[vmem] * 8 + [anywhere],
        out_specs=[vmem] * 3,
        compiler_params=options(16),
        cost_estimate=cost(8_000_000, 8_000_000),
        name="inner",
    )(near_velocity, left, right, left_h, right_h, ends, volume, bulk_target.reshape(1, 1),
      outgoing[0])
    own_in, other_out, *tile = pl.pallas_call(
        functools.partial(spread_kernel, order, components),
        out_shape=[shape(half * 2 * components, *sheet)] * 2
        + [shape(columns - shift, SUB, LANES) for shift in range(1, columns)],
        in_specs=[vmem] * 3 + [anywhere] + [vmem] * (chips - 1),
        out_specs=[vmem] * (1 + columns),
        compiler_params=options(16),
        cost_estimate=cost(500_000, 1_600_000),
        name="spread",
    )(near, pair, chip_coefs, base, *incoming)
    other_in = to_mate(other_out)
    tiles = [tile[0]] + [
        send(tile[shift - 1], lambda z, y: (z, (y + shift) % columns))
        for shift in range(1, columns)
    ]
    partial, plain = pl.pallas_call(
        finish_kernel,
        out_shape=[shape(*velocity.shape), profile],
        in_specs=[vmem] * 5,
        out_specs=[anywhere, vmem],
        scratch_shapes=[
            pltpu.VMEM((components - 1, cells) + plane, f32),
            pltpu.SemaphoreType.DMA((row_tiles, components - 1)),
        ],
        compiler_params=options(16),
        cost_estimate=cost(3_000_000, 6_000_000),
        name="finish",
    )(own_in, other_in, base, left, right)
    return pl.pallas_call(
        functools.partial(correct_kernel, columns),
        out_shape=shape(*velocity.shape),
        in_specs=[vmem] * (3 + columns) + [anywhere],
        out_specs=anywhere,
        scratch_shapes=[
            pltpu.VMEM((cells,) + plane, f32),
            pltpu.SemaphoreType.DMA((row_tiles,)),
        ],
        input_output_aliases={3 + columns: 0},
        compiler_params=options(16),
        cost_estimate=cost(500_000, 1_600_000),
        name="correct",
    )(goal, unit, *tiles, plain, partial)


def solution(mesh):
    return jax.shard_map(
        shards,
        mesh=mesh,
        in_specs=(P(None, "gz", "gy", None), P("gy", None), P("gy", None), P(), P()),
        out_specs=P(None, "gz", "gy", None),
        check_vma=False,
    )
```

```python
import functools

import jax
import jax.numpy as jnp
from jax import lax
from jax.experimental import pallas as pl
from jax.experimental.pallas import tpu as pltpu
from jax.sharding import PartitionSpec as P

SUB = 8
STRETCHES = 7
LANES = 128
MIB = 1024 * 1024


def plane_rounds(columns):
    shifts = [[(y, (y + shift) % columns) for y in range(columns)] for shift in range(1, columns)]
    if columns != 4:
        return shifts
    return [shifts[0], [(2, 0)], shifts[2], [(0, 2), (1, 3), (3, 1)]]


def row_tile(t):
    return pl.ds(pl.multiple_of(t * SUB, SUB), SUB)


def put(ref, at, sheet):
    count = sheet.shape[1] // LANES
    for i in range(count):
        ref[at * count + i] = sheet[:, i * LANES:(i + 1) * LANES]


def get(ref, at, count):
    return jnp.concatenate([ref[at * count + i] for i in range(count)], axis=1)


def height(index_ref, k):
    return 0.5 + 0.25 * index_ref[k].astype(jnp.float32)


def half_sum(index_ref, k):
    return 0.5 * (height(index_ref, k) + height(index_ref, k + 1))


def ladder_kernel(
    cells, blocks, chips, lines,
    index_hbm, diffusion_hbm, walls_hbm, velocity_hbm,
    mine_ref, away_ref, pair_ref, chip_ref, left_ref, right_ref, left_h_ref, right_h_ref,
    ends_ref, volume_ref, velocity_ref,
    index_ref, diffusion_ref, walls_ref, through_ref, table_ref, held_ref, sems,
):
    total = cells * blocks
    components = velocity_ref.shape[0]
    row_tiles = diffusion_ref.shape[0] // SUB
    small = [
        pltpu.make_async_copy(index_hbm, index_ref, sems.at[0]),
        pltpu.make_async_copy(diffusion_hbm, diffusion_ref, sems.at[1]),
        pltpu.make_async_copy(walls_hbm, walls_ref, sems.at[2]),
    ]
    large = [
        pltpu.make_async_copy(velocity_hbm.at[c], velocity_ref.at[c], sems.at[3 + c])
        for c in range(components)
    ]
    for copy in small + large:
        copy.start()
    me = lax.axis_index("gz")
    chip = me // 2
    first = chip * 2
    for copy in small:
        copy.wait()
    diffusion = diffusion_ref[...]
    inverse = 1.0 / diffusion
    for i in range(STRETCHES):
        table_ref[i] = (0.5 + 0.25 * i) * inverse
    walls = walls_ref[...]

    def wall(bits, k):
        face = 1.0 / jnp.full((SUB, diffusion.shape[1]), 0.5 * height(index_ref, k))
        return bits.astype(jnp.float32) * jnp.concatenate([face] * row_tiles, axis=0)

    lower = wall(walls & 1, 0)
    upper = wall(walls >> 1, total - 1)

    def forward(block, kappa, keep=None):
        start = block * cells
        flux = table_ref[index_ref[start]] + kappa
        value = jnp.ones_like(flux)
        for j in range(cells):
            if keep is not None:
                keep(j, flux, value)
            k = start + j
            if j < cells - 1:
                value = value + half_sum(index_ref, k) * flux
                flux = flux + table_ref[index_ref[k + 1]] * value
        k = jnp.minimum(start + cells - 1, total - 2)
        after = 1.0 / (value + half_sum(index_ref, k) * flux)
        return flux * after, after

    def backward(block, kappa, scale=None, keep=None):
        start = block * cells
        flux = table_ref[index_ref[start + cells - 1]] + kappa
        value = jnp.ones_like(flux)
        if scale is not None:
            flux, value = flux * scale, scale
        for j in reversed(range(cells)):
            if keep is not None:
                keep(j, flux, value)
            k = start + j
            if j > 0:
                value = value + half_sum(index_ref, k - 1) * flux
                flux = flux + table_ref[index_ref[k - 1]] * value
        k = jnp.maximum(start - 1, 0)
        after = 1.0 / (value + half_sum(index_ref, k) * flux)
        return flux * after, after

    def thickness(block):
        parts = [height(index_ref, block * cells + j) for j in range(cells)]
        return functools.reduce(jnp.add, parts)

    def sweep_forward(block, state):
        kappa, product, extent = state
        kappa, after = forward(block, kappa)
        through_ref[block] = after
        return kappa, product * after, extent + thickness(block)

    def sweep_backward(step, state):
        block = blocks - 1 - step
        kappa, product, extent = state
        kappa, after = backward(block, kappa)
        through_ref[block] = after
        return kappa, product * after, extent + thickness(block)

    ones = jnp.ones_like(diffusion)
    kappa_left, product, extent = lax.fori_loop(
        0, me, sweep_forward, (lower, ones, thickness(me))
    )
    ends_ref[0] = diffusion * lower * product
    state = {}

    def keep_left(j, flux, value):
        left_ref[j] = value
        left_h_ref[j] = height(index_ref, me * cells + j) * value
        state["flux"], state["value"] = flux, value

    _, own_forward = forward(me, kappa_left, keep_left)
    held_ref[1] = own_forward
    held_ref[3] = state["flux"]
    held_ref[4] = state["value"]
    held_ref[5] = state["flux"] - kappa_left

    kappa_right, product, extent = lax.fori_loop(
        0, blocks - 1 - me, sweep_backward, (upper, ones, extent)
    )
    ends_ref[1] = diffusion_ref[...] * upper * product
    scale = 1.0 / (diffusion_ref[...] * (held_ref[3] + kappa_right * held_ref[4]))
    held_ref[0] = scale

    def keep_right(j, flux, value):
        right_ref[j] = value
        right_h_ref[j] = height(index_ref, me * cells + j) * value
        state["flux"] = flux

    _, own_backward = backward(me, kappa_right, scale, keep_right)
    held_ref[2] = own_backward
    held_ref[6] = state["flux"] - kappa_right * scale

    is_first = me == first
    forth, back = held_ref[1], own_backward * held_ref[0]
    pair_ref[0] = jnp.where(is_first, back, forth)
    pair_ref[1] = jnp.where(is_first, forth, through_ref[first])
    pair_ref[2] = jnp.where(is_first, through_ref[first + 1], back)
    for m in range(1, chips):
        other = chip ^ m
        low = jnp.minimum(chip, other)
        high = jnp.maximum(chip, other)
        chip_ref[m - 1] = lax.fori_loop(
            low + 1,
            high,
            lambda r, product: product * (through_ref[2 * r] * through_ref[2 * r + 1]),
            ones,
        )

    def fold(array):
        parts = [array[:, i * LANES:(i + 1) * LANES] for i in range(array.shape[1] // LANES)]
        return functools.reduce(jnp.add, parts)

    for copy in large:
        copy.wait()
    volume_ref[...] = jnp.full(volume_ref.shape, extent * lines)
    half = row_tiles // 2
    own_extent = thickness(me)
    heights = [height(index_ref, me * cells + j) for j in range(cells)]

    def sums(ref, whose):
        def of_tile(i, state):
            flow, weight = state
            rows = row_tile(whose * half + i)
            from_left = [0.0] * components
            from_right = [0.0] * components
            plain = 0.0
            for j in range(cells):
                left = left_h_ref[j, rows]
                right = right_h_ref[j, rows]
                for c in range(components):
                    v = velocity_ref[c, j, rows]
                    from_left[c] = from_left[c] + left * v
                    from_right[c] = from_right[c] + right * v
                    if c == 0:
                        plain = plain + heights[j] * v
            for c in range(components):
                at = i * 2 * components + c
                put(ref, at, from_left[c] * held_ref[1, rows])
                put(ref, at + components, from_right[c] * held_ref[2, rows])
            low_part = ends_ref[0, rows]
            high_part = ends_ref[1, rows] * held_ref[0, rows]
            totals = low_part * held_ref[6, rows] + high_part * held_ref[5, rows]
            return (
                flow + fold(plain - low_part * from_right[0] - high_part * from_left[0]),
                weight + fold(own_extent - diffusion_ref[rows] * totals),
            )

        return of_tile

    state = (jnp.zeros((SUB, LANES), jnp.float32),) * 2
    mates = 1 - (me - first)
    state = lax.fori_loop(0, half, sums(away_ref, mates), state)
    flow, weight = lax.fori_loop(0, half, sums(mine_ref, me - first), state)
    for i in range(half):
        put(away_ref, half * 2 * components + i, pair_ref[0, row_tile(mates * half + i)])
    slot, middle = away_ref.shape[0] - 1, SUB // 2
    away_ref[slot, 0:middle] = flow[0:middle] + flow[middle:]
    away_ref[slot, middle:] = weight[0:middle] + weight[middle:]


def merge_kernel(chips, components, mine_ref, away_ref, mate_ref, pair_ref, *rest):
    send_refs, near_ref = rest[:-1], rest[-1]
    me = lax.axis_index("gz")
    chip = me // 2
    is_first = me == chip * 2
    count = pair_ref.shape[2] // LANES
    half = mine_ref.shape[0] // (2 * components * count)
    slot = away_ref.shape[0] - 1
    tile = away_ref[slot] + mate_ref[slot]
    near_ref[near_ref.shape[0] - 1] = tile
    for ref in send_refs:
        for at in range(half * components * count, ref.shape[0]):
            ref[at] = tile
    for i in range(half):
        rows = row_tile((me - chip * 2) * half + i)
        mine, mate = pair_ref[0, rows], get(mate_ref, half * 2 * components + i, count)
        forth = jnp.where(is_first, mate, mine)
        back = jnp.where(is_first, mine, mate)
        for c in range(components):
            at = i * 2 * components + c
            mine, mate = get(mine_ref, at, count), get(mate_ref, at, count)
            first = jnp.where(is_first, mine, mate)
            second = jnp.where(is_first, mate, mine)
            put(near_ref, at, first)
            to_right = second + forth * first
            at = at + components
            mine, mate = get(mine_ref, at, count), get(mate_ref, at, count)
            first = jnp.where(is_first, mine, mate)
            second = jnp.where(is_first, mate, mine)
            put(near_ref, at, second)
            to_left = first + back * second
            for m in range(1, chips):
                goes_right = (chip ^ m) > chip
                sheet = jnp.where(goes_right, to_right, to_left)
                put(send_refs[m - 1], i * components + c, sheet)


def spread_kernel(order, components, near_ref, pair_ref, chip_ref, *rest):
    recv_refs = rest[1:len(order) + 1]
    own_ref, other_ref, *tile_refs = rest[len(order) + 1:]
    me = lax.axis_index("gz")
    chip = me // 2
    is_first = me == chip * 2
    count = pair_ref.shape[2] // LANES
    half = near_ref.shape[0] // (2 * components * count)
    tiles = [ref[ref.shape[0] - 1] for ref in (near_ref, *recv_refs)]
    tile = functools.reduce(jnp.add, tiles)
    for ref in tile_refs:
        for i in range(ref.shape[0]):
            ref[i] = tile
    for i in range(half):
        rows = row_tile((me - chip * 2) * half + i)
        coefs = [chip_ref[m - 1, rows] for m in order]
        for c in range(components):
            left_in = jnp.zeros(own_ref.shape[1:], jnp.float32)
            right_in = jnp.zeros(own_ref.shape[1:], jnp.float32)
            for m, coef, ref in zip(order, coefs, recv_refs):
                term = coef * get(ref, i * components + c, count)
                from_left = (chip ^ m) < chip
                left_in = left_in + jnp.where(from_left, term, 0.0)
                right_in = right_in + jnp.where(from_left, 0.0, term)
            at = i * 2 * components + c
            left_second = get(near_ref, at, count) + pair_ref[1, rows] * left_in
            right_first = get(near_ref, at + components, count) + pair_ref[2, rows] * right_in
            own_ref[at] = jnp.where(is_first, left_in, left_second)
            other_ref[at] = jnp.where(is_first, left_second, left_in)
            at = at + components
            own_ref[at] = jnp.where(is_first, right_first, right_in)
            other_ref[at] = jnp.where(is_first, right_in, right_first)


def inner_kernel(
    velocity_ref, left_ref, right_ref, left_h_ref, right_h_ref, ends_ref, volume_ref, target_ref,
    _, base_ref, unit_ref, goal_ref,
):
    components, cells, lines_y, lines_x = velocity_ref.shape
    goal_ref[...] = target_ref[...] * volume_ref[...]

    def of_tile(t, _):
        rows = row_tile(t)
        gathered = [jnp.zeros((SUB, lines_x), jnp.float32)] * components
        for j in reversed(range(cells)):
            left = left_ref[j, rows]
            right = right_h_ref[j, rows]
            for c in range(components):
                base_ref[c, j, rows] = left * gathered[c]
                if j > 0:
                    gathered[c] = gathered[c] + right * velocity_ref[c, j, rows]
        gathered = [jnp.zeros((SUB, lines_x), jnp.float32)] * components
        low_part = ends_ref[0, rows]
        high_part = ends_ref[1, rows] * right_ref[cells - 1, rows]
        for j in range(cells):
            left = left_h_ref[j, rows]
            right = right_ref[j, rows]
            unit_ref[j, rows] = 1.0 - (low_part * right + high_part * left_ref[j, rows])
            for c in range(components):
                gathered[c] = gathered[c] + left * velocity_ref[c, j, rows]
                base_ref[c, j, rows] = base_ref[c, j, rows] + right * gathered[c]
        return 0

    lax.fori_loop(0, lines_y // SUB, of_tile, 0)


def finish_kernel(
    own_ref, other_ref, base_ref, left_ref, right_ref, out_hbm, plain_ref, result_ref, sems
):
    components, cells, lines_y, _ = base_ref.shape
    half = own_ref.shape[0] // (2 * components)
    me = lax.axis_index("gz")

    def copies(t):
        rows = row_tile(t)
        return [
            pltpu.make_async_copy(
                result_ref.at[c - 1, :, rows], out_hbm.at[c, :, rows], sems.at[t, c - 1])
            for c in range(1, components)
        ]

    def half_of(incoming_ref, side):
        def of_tile(i, _):
            t = lax.rem(me + side, 2) * half + i
            rows = row_tile(t)
            scale = right_ref[cells - 1, rows]
            at = i * 2 * components
            lefts = [incoming_ref[at + c] for c in range(components)]
            rights = [incoming_ref[at + components + c] * scale for c in range(components)]
            for j in range(cells):
                left = left_ref[j, rows]
                right = right_ref[j, rows]
                for c in range(components):
                    value = base_ref[c, j, rows] + (right * lefts[c] + left * rights[c])
                    if c == 0:
                        plain_ref[j, rows] = value
                    else:
                        result_ref[c - 1, j, rows] = value
            for copy in copies(t):
                copy.start()
            return 0

        lax.fori_loop(0, half, of_tile, 0)

    half_of(own_ref, 0)
    half_of(other_ref, 1)
    for t in range(lines_y // SUB):
        for copy in copies(t):
            copy.wait()


def correct_kernel(count, goal_ref, unit_ref, *rest):
    tile_refs = rest[:count]
    plain_ref, _, out_hbm, result_ref, sems = rest[count:]
    totals = functools.reduce(jnp.add, [ref[0] for ref in tile_refs])
    flow = jnp.sum(totals[0:SUB // 2], keepdims=True)
    weight = jnp.sum(totals[SUB // 2:], keepdims=True)
    alpha = (goal_ref[0:1, 0:1] - flow) / weight
    cells, lines_y, _ = plain_ref.shape

    def copy(t):
        rows = row_tile(t)
        return pltpu.make_async_copy(result_ref.at[:, rows], out_hbm.at[0, :, rows], sems.at[t])

    def of_tile(t, _):
        rows = row_tile(t)
        for j in range(cells):
            result_ref[j, rows] = plain_ref[j, rows] + alpha * unit_ref[j, rows]
        copy(t).start()
        return 0

    lax.fori_loop(0, lines_y // SUB, of_tile, 0)
    for t in range(lines_y // SUB):
        copy(t).wait()


def shards(velocity, diffusion, wall_types, stretch_index, bulk_target):
    blocks = lax.axis_size("gz")
    columns = lax.axis_size("gy")
    components, cells, lines_y, lines_x = velocity.shape
    chips = blocks // 2
    row_tiles = lines_y // SUB
    half = row_tiles // 2
    f32 = jnp.float32
    vmem = pl.BlockSpec(memory_space=pltpu.VMEM)
    anywhere = pl.BlockSpec(memory_space=pl.ANY)
    plane = (lines_y, lines_x)
    sheet = (SUB, lines_x)

    def shape(*dims):
        return jax.ShapeDtypeStruct(dims, f32)

    def in_hbm(array):
        return pltpu.with_memory_space_constraint(array, pltpu.HBM)

    def options(mib):
        return pltpu.CompilerParams(vmem_limit_bytes=mib * MIB)

    def cost(flops, transferred):
        return pl.CostEstimate(flops=flops, bytes_accessed=transferred, transcendentals=0)

    def send(array, route):
        flat = [(a * columns + b, c * columns + d) for (a, b), (c, d) in route]
        return lax.ppermute(array, ("gz", "gy"), flat)

    def to_block(array, other):
        return send(array, [
            ((z, y), (z ^ other, y)) for z in range(blocks) for y in range(columns)
        ])

    def to_mate(array):
        return to_block(array, 1)

    count = lines_x // LANES
    lines = float(lines_y * columns * lines_x)
    (mine, away, pair, chip_coefs, left, right, left_h, right_h, ends, volume,
     near_velocity) = pl.pallas_call(
        functools.partial(ladder_kernel, cells, blocks, chips, lines),
        out_shape=[
            shape(half * 2 * components * count, SUB, LANES),
            shape(half * (2 * components + 1) * count + 1, SUB, LANES),
            shape(3, *plane),
            shape(chips - 1, *plane),
            shape(cells, *plane),
            shape(cells, *plane),
            shape(cells, *plane),
            shape(cells, *plane),
            shape(2, *plane),
            shape(SUB, LANES),
            shape(*velocity.shape),
        ],
        in_specs=[anywhere] * 4,
        out_specs=[vmem] * 11,
        scratch_shapes=[
            pltpu.SMEM(stretch_index.shape, jnp.int32),
            pltpu.VMEM(plane, f32),
            pltpu.VMEM(plane, jnp.int32),
            pltpu.VMEM((blocks,) + plane, f32),
            pltpu.VMEM((STRETCHES,) + plane, f32),
            pltpu.VMEM((7,) + plane, f32),
            pltpu.SemaphoreType.DMA((3 + components,)),
        ],
        compiler_params=options(24),
        cost_estimate=cost(40_000_000, 6_000_000),
        name="ladder",
    )(in_hbm(stretch_index), in_hbm(diffusion), in_hbm(wall_types), in_hbm(velocity))

    mate = to_mate(away)
    *outgoing, near = pl.pallas_call(
        functools.partial(merge_kernel, chips, components),
        out_shape=[
            shape(half * components * count + m.bit_count(), SUB, LANES) for m in range(1, chips)
        ] + [shape(half * 2 * components * count + 1, SUB, LANES)],
        in_specs=[vmem] * 4,
        out_specs=[vmem] * chips,
        compiler_params=options(16),
        cost_estimate=cost(500_000, 1_600_000),
        name="merge",
    )(mine, away, mate, pair)
    order = sorted(range(1, chips), key=lambda m: -m.bit_count())
    incoming = [to_block(outgoing[m - 1], 2 * m) for m in order]
    profile = shape(cells, *plane)
    base, unit, goal = pl.pallas_call(
        inner_kernel,
        out_shape=[shape(*velocity.shape), profile, shape(SUB, LANES)],
        in_specs=[vmem] * 8 + [anywhere],
        out_specs=[vmem] * 3,
        compiler_params=options(16),
        cost_estimate=cost(8_000_000, 8_000_000),
        name="inner",
    )(near_velocity, left, right, left_h, right_h, ends, volume, bulk_target.reshape(1, 1),
      outgoing[0])
    rounds = plane_rounds(columns)
    own_in, other_out, *tile = pl.pallas_call(
        functools.partial(spread_kernel, order, components),
        out_shape=[shape(half * 2 * components, *sheet)] * 2
        + [shape(len(rounds) - i, SUB, LANES) for i in range(len(rounds))],
        in_specs=[vmem] * 3 + [anywhere] + [vmem] * (chips - 1),
        out_specs=[vmem] * (2 + len(rounds)),
        compiler_params=options(16),
        cost_estimate=cost(500_000, 1_600_000),
        name="spread",
    )(near, pair, chip_coefs, base, *incoming)
    other_in = to_mate(other_out)
    tiles = [tile[0]] + [
        send(array, [((z, a), (z, b)) for z in range(blocks) for a, b in route])
        for array, route in zip(tile, rounds)
    ]
    partial, plain = pl.pallas_call(
        finish_kernel,
        out_shape=[shape(*velocity.shape), profile],
        in_specs=[vmem] * 5,
        out_specs=[anywhere, vmem],
        scratch_shapes=[
            pltpu.VMEM((components - 1, cells) + plane, f32),
            pltpu.SemaphoreType.DMA((row_tiles, components - 1)),
        ],
        compiler_params=options(16),
        cost_estimate=cost(3_000_000, 6_000_000),
        name="finish",
    )(own_in, other_in, base, left, right)
    return pl.pallas_call(
        functools.partial(correct_kernel, len(tiles)),
        out_shape=shape(*velocity.shape),
        in_specs=[vmem] * (3 + len(tiles)) + [anywhere],
        out_specs=anywhere,
        scratch_shapes=[
            pltpu.VMEM((cells,) + plane, f32),
            pltpu.SemaphoreType.DMA((row_tiles,)),
        ],
        input_output_aliases={3 + len(tiles): 0},
        compiler_params=options(16),
        cost_estimate=cost(500_000, 1_600_000),
        name="correct",
    )(goal, unit, *tiles, plain, partial)


def solution(mesh):
    return jax.shard_map(
        shards,
        mesh=mesh,
        in_specs=(P(None, "gz", "gy", None), P("gy", None), P("gy", None), P(), P()),
        out_specs=P(None, "gz", "gy", None),
        check_vma=False,
    )
```

```python
import functools

import jax
import jax.numpy as jnp
from jax import lax
from jax.experimental import pallas as pl
from jax.experimental.pallas import tpu as pltpu
from jax.sharding import PartitionSpec as P

SUB = 8
STRETCHES = 7
LANES = 128
MIB = 1024 * 1024


def row_tile(t):
    return pl.ds(pl.multiple_of(t * SUB, SUB), SUB)


def inverted(array):
    guess = pl.reciprocal(array, approx=True)
    return guess * (2.0 - array * guess)


def put(ref, at, sheet):
    count = sheet.shape[1] // LANES
    for i in range(count):
        ref[at * count + i] = sheet[:, i * LANES:(i + 1) * LANES]


def get(ref, at, count):
    return jnp.concatenate([ref[at * count + i] for i in range(count)], axis=1)


def height(index_ref, k):
    return 0.5 + 0.25 * index_ref[k].astype(jnp.float32)


def half_sum(index_ref, k):
    return 0.5 * (height(index_ref, k) + height(index_ref, k + 1))


def ladder_kernel(
    cells, blocks, chips, lines,
    index_hbm, diffusion_hbm, walls_hbm, velocity_hbm,
    mine_ref, away_ref, pair_ref, through_ref, held_ref, left_ref, right_ref, left_h_ref, right_h_ref,
    ends_ref, volume_ref, velocity_ref,
    index_ref, diffusion_ref, walls_ref, table_ref, sems,
):
    total = cells * blocks
    components = velocity_ref.shape[0]
    row_tiles = diffusion_ref.shape[0] // SUB
    small = [
        pltpu.make_async_copy(index_hbm, index_ref, sems.at[0]),
        pltpu.make_async_copy(diffusion_hbm, diffusion_ref, sems.at[1]),
        pltpu.make_async_copy(walls_hbm, walls_ref, sems.at[2]),
    ]
    large = [
        pltpu.make_async_copy(velocity_hbm.at[c], velocity_ref.at[c], sems.at[3 + c])
        for c in range(components)
    ]
    for copy in small + large:
        copy.start()
    me = lax.axis_index("gz")
    chip = me // 2
    first = chip * 2
    for copy in small:
        copy.wait()
    diffusion = diffusion_ref[...]
    inverse = inverted(diffusion)
    for i in range(STRETCHES):
        table_ref[i] = (0.5 + 0.25 * i) * inverse
    walls = walls_ref[...]

    def wall(bits, k):
        face = 1.0 / jnp.full((SUB, diffusion.shape[1]), 0.5 * height(index_ref, k))
        return bits.astype(jnp.float32) * jnp.concatenate([face] * row_tiles, axis=0)

    lower = wall(walls & 1, 0)
    upper = wall(walls >> 1, total - 1)

    def forward(block, kappa, keep=None):
        start = block * cells
        flux = table_ref[index_ref[start]] + kappa
        value = jnp.ones_like(flux)
        for j in range(cells):
            if keep is not None:
                keep(j, flux, value)
            k = start + j
            if j < cells - 1:
                value = value + half_sum(index_ref, k) * flux
                flux = flux + table_ref[index_ref[k + 1]] * value
        k = jnp.minimum(start + cells - 1, total - 2)
        after = inverted(value + half_sum(index_ref, k) * flux)
        return flux * after, after

    def backward(block, kappa, scale=None, keep=None):
        start = block * cells
        flux = table_ref[index_ref[start + cells - 1]] + kappa
        value = jnp.ones_like(flux)
        if scale is not None:
            flux, value = flux * scale, scale
        for j in reversed(range(cells)):
            if keep is not None:
                keep(j, flux, value)
            k = start + j
            if j > 0:
                value = value + half_sum(index_ref, k - 1) * flux
                flux = flux + table_ref[index_ref[k - 1]] * value
        k = jnp.maximum(start - 1, 0)
        after = inverted(value + half_sum(index_ref, k) * flux)
        return flux * after, after

    def thickness(block):
        parts = [height(index_ref, block * cells + j) for j in range(cells)]
        return functools.reduce(jnp.add, parts)

    def sweep_forward(block, state):
        kappa, product, extent = state
        kappa, after = forward(block, kappa)
        through_ref[block] = after
        return kappa, product * after, extent + thickness(block)

    def sweep_backward(step, state):
        block = blocks - 1 - step
        kappa, product, extent = state
        kappa, after = backward(block, kappa)
        through_ref[block] = after
        return kappa, product * after, extent + thickness(block)

    ones = jnp.ones_like(diffusion)
    kappa_left, product, extent = lax.fori_loop(
        0, me, sweep_forward, (lower, ones, thickness(me))
    )
    ends_ref[0] = diffusion * lower * product
    state = {}

    def keep_left(j, flux, value):
        left_ref[j] = value
        left_h_ref[j] = height(index_ref, me * cells + j) * value
        state["flux"], state["value"] = flux, value

    _, own_forward = forward(me, kappa_left, keep_left)
    held_ref[1] = own_forward
    held_ref[3] = state["flux"]
    held_ref[4] = state["value"]
    held_ref[5] = state["flux"] - kappa_left

    kappa_right, product, extent = lax.fori_loop(
        0, blocks - 1 - me, sweep_backward, (upper, ones, extent)
    )
    ends_ref[1] = diffusion_ref[...] * upper * product
    scale = inverted(diffusion_ref[...] * (held_ref[3] + kappa_right * held_ref[4]))
    held_ref[0] = scale

    def keep_right(j, flux, value):
        right_ref[j] = value
        right_h_ref[j] = height(index_ref, me * cells + j) * value
        state["flux"] = flux

    _, own_backward = backward(me, kappa_right, scale, keep_right)
    held_ref[2] = own_backward
    held_ref[6] = state["flux"] - kappa_right * scale

    is_first = me == first
    forth, back = held_ref[1], own_backward * held_ref[0]
    pair_ref[0] = jnp.where(is_first, back, forth)
    pair_ref[1] = jnp.where(is_first, forth, through_ref[first])
    pair_ref[2] = jnp.where(is_first, through_ref[first + 1], back)

    def fold(array):
        parts = [array[:, i * LANES:(i + 1) * LANES] for i in range(array.shape[1] // LANES)]
        return functools.reduce(jnp.add, parts)

    for copy in large:
        copy.wait()
    volume_ref[...] = jnp.full(volume_ref.shape, extent * lines)
    half = row_tiles // 2
    own_extent = thickness(me)
    heights = [height(index_ref, me * cells + j) for j in range(cells)]

    def sums(ref, whose, parts):
        def of_tile(i, state):
            flow, weight = state
            rows = row_tile(whose * half + i)
            from_left = [0.0] * parts
            from_right = [0.0] * parts
            plain = 0.0
            for j in range(cells):
                left = left_h_ref[j, rows]
                right = right_h_ref[j, rows]
                for c in range(parts):
                    v = velocity_ref[c, j, rows]
                    from_left[c] = from_left[c] + left * v
                    from_right[c] = from_right[c] + right * v
                    if c == 0:
                        plain = plain + heights[j] * v
            for c in range(parts):
                at = i * 2 * parts + c
                put(ref, at, from_left[c] * held_ref[1, rows])
                put(ref, at + parts, from_right[c] * held_ref[2, rows])
            low_part = ends_ref[0, rows]
            high_part = ends_ref[1, rows] * held_ref[0, rows]
            totals = low_part * held_ref[6, rows] + high_part * held_ref[5, rows]
            return (
                flow + fold(plain - low_part * from_right[0] - high_part * from_left[0]),
                weight + fold(own_extent - diffusion_ref[rows] * totals),
            )

        return of_tile

    state = (jnp.zeros((SUB, LANES), jnp.float32),) * 2
    mates = 1 - (me - first)
    state = lax.fori_loop(0, half, sums(away_ref, mates, components), state)
    flow, weight = lax.fori_loop(0, half, sums(mine_ref, me - first, 1), state)
    for i in range(half):
        put(away_ref, half * 2 * components + i, pair_ref[0, row_tile(mates * half + i)])
    slot, middle = away_ref.shape[0] - 1, SUB // 2
    away_ref[slot, 0:middle] = flow[0:middle] + flow[middle:]
    away_ref[slot, middle:] = weight[0:middle] + weight[middle:]


def rest_kernel(
    chips, velocity_ref, left_h_ref, right_h_ref, held_ref, through_ref, sums_ref, chip_ref
):
    components, cells, _, lines_x = velocity_ref.shape
    me = lax.axis_index("gz")
    chip = me // 2
    half = sums_ref.shape[0] // (2 * (components - 1) * (lines_x // LANES))
    ones = jnp.ones(chip_ref.shape[1:], jnp.float32)
    for m in range(1, chips):
        other = chip ^ m
        low = jnp.minimum(chip, other)
        high = jnp.maximum(chip, other)
        chip_ref[m - 1] = lax.fori_loop(
            low + 1,
            high,
            lambda r, product: product * (through_ref[2 * r] * through_ref[2 * r + 1]),
            ones,
        )

    def of_tile(i, _):
        rows = row_tile((me - chip * 2) * half + i)
        from_left = [0.0] * (components - 1)
        from_right = [0.0] * (components - 1)
        for j in range(cells):
            left = left_h_ref[j, rows]
            right = right_h_ref[j, rows]
            for c in range(components - 1):
                v = velocity_ref[c + 1, j, rows]
                from_left[c] = from_left[c] + left * v
                from_right[c] = from_right[c] + right * v
        for c in range(components - 1):
            at = i * 2 * (components - 1) + c
            put(sums_ref, at, from_left[c] * held_ref[1, rows])
            put(sums_ref, at + components - 1, from_right[c] * held_ref[2, rows])
        return 0

    lax.fori_loop(0, half, of_tile, 0)


def merge_kernel(chips, components, mine_ref, sums_ref, away_ref, mate_ref, pair_ref, *rest):
    send_refs, near_ref = rest[:-1], rest[-1]
    me = lax.axis_index("gz")
    chip = me // 2
    is_first = me == chip * 2
    count = pair_ref.shape[2] // LANES
    half = mine_ref.shape[0] // (2 * count)
    slot = away_ref.shape[0] - 1
    tile = away_ref[slot] + mate_ref[slot]
    near_ref[near_ref.shape[0] - 1] = tile
    for ref in send_refs:
        for at in range(half * components * count, ref.shape[0]):
            ref[at] = tile
    for i in range(half):
        rows = row_tile((me - chip * 2) * half + i)
        mine, mate = pair_ref[0, rows], get(mate_ref, half * 2 * components + i, count)
        forth = jnp.where(is_first, mate, mine)
        back = jnp.where(is_first, mine, mate)
        for c in range(components):
            at = i * 2 * components + c
            if c == 0:
                own = [get(mine_ref, i * 2 + k, count) for k in range(2)]
            else:
                others = components - 1
                own = [
                    get(sums_ref, i * 2 * others + k * others + c - 1, count) for k in range(2)
                ]
            mine, mate = own[0], get(mate_ref, at, count)
            first = jnp.where(is_first, mine, mate)
            second = jnp.where(is_first, mate, mine)
            put(near_ref, at, first)
            to_right = second + forth * first
            at = at + components
            mine, mate = own[1], get(mate_ref, at, count)
            first = jnp.where(is_first, mine, mate)
            second = jnp.where(is_first, mate, mine)
            put(near_ref, at, second)
            to_left = first + back * second
            for m in range(1, chips):
                goes_right = (chip ^ m) > chip
                sheet = jnp.where(goes_right, to_right, to_left)
                put(send_refs[m - 1], i * components + c, sheet)


def spread_kernel(order, components, near_ref, pair_ref, chip_ref, *rest):
    recv_refs = rest[1:len(order) + 1]
    own_ref, other_ref, *tile_refs = rest[len(order) + 1:]
    me = lax.axis_index("gz")
    chip = me // 2
    is_first = me == chip * 2
    count = pair_ref.shape[2] // LANES
    half = near_ref.shape[0] // (2 * components * count)
    tiles = [ref[ref.shape[0] - 1] for ref in (near_ref, *recv_refs)]
    tile = functools.reduce(jnp.add, tiles)
    for ref in tile_refs:
        for i in range(ref.shape[0]):
            ref[i] = tile
    for i in range(half):
        rows = row_tile((me - chip * 2) * half + i)
        coefs = [chip_ref[m - 1, rows] for m in order]
        for c in range(components):
            left_in = jnp.zeros(own_ref.shape[1:], jnp.float32)
            right_in = jnp.zeros(own_ref.shape[1:], jnp.float32)
            for m, coef, ref in zip(order, coefs, recv_refs):
                term = coef * get(ref, i * components + c, count)
                from_left = (chip ^ m) < chip
                left_in = left_in + jnp.where(from_left, term, 0.0)
                right_in = right_in + jnp.where(from_left, 0.0, term)
            at = i * 2 * components + c
            left_second = get(near_ref, at, count) + pair_ref[1, rows] * left_in
            right_first = get(near_ref, at + components, count) + pair_ref[2, rows] * right_in
            own_ref[at] = jnp.where(is_first, left_in, left_second)
            other_ref[at] = jnp.where(is_first, left_second, left_in)
            at = at + components
            own_ref[at] = jnp.where(is_first, right_first, right_in)
            other_ref[at] = jnp.where(is_first, right_in, right_first)


def inner_kernel(
    velocity_ref, left_ref, right_ref, left_h_ref, right_h_ref, ends_ref, volume_ref, target_ref,
    _, base_ref, unit_ref, goal_ref,
):
    components, cells, lines_y, lines_x = velocity_ref.shape
    goal_ref[...] = target_ref[...] * volume_ref[...]

    def of_tile(t, _):
        rows = row_tile(t)
        gathered = [jnp.zeros((SUB, lines_x), jnp.float32)] * components
        for j in reversed(range(cells)):
            left = left_ref[j, rows]
            right = right_h_ref[j, rows]
            for c in range(components):
                base_ref[c, j, rows] = left * gathered[c]
                if j > 0:
                    gathered[c] = gathered[c] + right * velocity_ref[c, j, rows]
        gathered = [jnp.zeros((SUB, lines_x), jnp.float32)] * components
        low_part = ends_ref[0, rows]
        high_part = ends_ref[1, rows] * right_ref[cells - 1, rows]
        for j in range(cells):
            left = left_h_ref[j, rows]
            right = right_ref[j, rows]
            unit_ref[j, rows] = 1.0 - (low_part * right + high_part * left_ref[j, rows])
            for c in range(components):
                gathered[c] = gathered[c] + left * velocity_ref[c, j, rows]
                base_ref[c, j, rows] = base_ref[c, j, rows] + right * gathered[c]
        return 0

    lax.fori_loop(0, lines_y // SUB, of_tile, 0)


def finish_kernel(
    own_ref, other_ref, base_ref, left_ref, right_ref, out_hbm, plain_ref, result_ref, sems
):
    components, cells, lines_y, _ = base_ref.shape
    half = own_ref.shape[0] // (2 * components)
    me = lax.axis_index("gz")

    def copies(t):
        rows = row_tile(t)
        return [
            pltpu.make_async_copy(
                result_ref.at[c - 1, :, rows], out_hbm.at[c, :, rows], sems.at[t, c - 1])
            for c in range(1, components)
        ]

    def half_of(incoming_ref, side):
        def of_tile(i, _):
            t = lax.rem(me + side, 2) * half + i
            rows = row_tile(t)
            scale = right_ref[cells - 1, rows]
            at = i * 2 * components
            lefts = [incoming_ref[at + c] for c in range(components)]
            rights = [incoming_ref[at + components + c] * scale for c in range(components)]
            for j in range(cells):
                left = left_ref[j, rows]
                right = right_ref[j, rows]
                for c in range(components):
                    value = base_ref[c, j, rows] + (right * lefts[c] + left * rights[c])
                    if c == 0:
                        plain_ref[j, rows] = value
                    else:
                        result_ref[c - 1, j, rows] = value
            for copy in copies(t):
                copy.start()
            return 0

        lax.fori_loop(0, half, of_tile, 0)

    half_of(own_ref, 0)
    half_of(other_ref, 1)
    for t in range(lines_y // SUB):
        for copy in copies(t):
            copy.wait()


def correct_kernel(columns, goal_ref, unit_ref, *rest):
    tile_refs = rest[:columns]
    plain_ref, _, out_hbm, result_ref, sems = rest[columns:]
    totals = functools.reduce(jnp.add, [ref[0] for ref in tile_refs])
    flow = jnp.sum(totals[0:SUB // 2], keepdims=True)
    weight = jnp.sum(totals[SUB // 2:], keepdims=True)
    alpha = (goal_ref[0:1, 0:1] - flow) / weight
    cells = plain_ref.shape[0]
    pieces = sems.shape[0]
    step = cells // pieces

    def copy(i):
        part = pl.ds(i * step, step)
        return pltpu.make_async_copy(result_ref.at[part], out_hbm.at[0, part], sems.at[i])

    def of_piece(i, _):
        for j in range(step):
            at = i * step + j
            result_ref[at] = plain_ref[at] + alpha * unit_ref[at]
        copy(i).start()
        return 0

    lax.fori_loop(0, pieces, of_piece, 0)
    for i in range(pieces):
        copy(i).wait()


def shards(velocity, diffusion, wall_types, stretch_index, bulk_target):
    blocks = lax.axis_size("gz")
    columns = lax.axis_size("gy")
    components, cells, lines_y, lines_x = velocity.shape
    chips = blocks // 2
    row_tiles = lines_y // SUB
    half = row_tiles // 2
    f32 = jnp.float32
    vmem = pl.BlockSpec(memory_space=pltpu.VMEM)
    anywhere = pl.BlockSpec(memory_space=pl.ANY)
    plane = (lines_y, lines_x)
    sheet = (SUB, lines_x)

    def shape(*dims):
        return jax.ShapeDtypeStruct(dims, f32)

    def in_hbm(array):
        return pltpu.with_memory_space_constraint(array, pltpu.HBM)

    def options(mib):
        return pltpu.CompilerParams(vmem_limit_bytes=mib * MIB)

    def cost(flops, transferred):
        return pl.CostEstimate(flops=flops, bytes_accessed=transferred, transcendentals=0)

    def send(array, partner):
        pairs = [((z, y), partner(z, y)) for z in range(blocks) for y in range(columns)]
        route = [(a * columns + b, c * columns + d) for (a, b), (c, d) in pairs]
        return lax.ppermute(array, ("gz", "gy"), route)

    def to_mate(array):
        return send(array, lambda z, y: (z ^ 1, y))

    count = lines_x // LANES
    lines = float(lines_y * columns * lines_x)
    (mine, away, pair, through, held, left, right, left_h, right_h, ends, volume,
     near_velocity) = pl.pallas_call(
        functools.partial(ladder_kernel, cells, blocks, chips, lines),
        out_shape=[
            shape(half * 2 * count, SUB, LANES),
            shape(half * (2 * components + 1) * count + 1, SUB, LANES),
            shape(3, *plane),
            shape(blocks, *plane),
            shape(7, *plane),
            shape(cells, *plane),
            shape(cells, *plane),
            shape(cells, *plane),
            shape(cells, *plane),
            shape(2, *plane),
            shape(SUB, LANES),
            shape(*velocity.shape),
        ],
        in_specs=[anywhere] * 4,
        out_specs=[vmem] * 12,
        scratch_shapes=[
            pltpu.SMEM(stretch_index.shape, jnp.int32),
            pltpu.VMEM(plane, f32),
            pltpu.VMEM(plane, jnp.int32),
            pltpu.VMEM((STRETCHES,) + plane, f32),
            pltpu.SemaphoreType.DMA((3 + components,)),
        ],
        compiler_params=options(24),
        cost_estimate=cost(40_000_000, 6_000_000),
        name="ladder",
    )(in_hbm(stretch_index), in_hbm(diffusion), in_hbm(wall_types), in_hbm(velocity))

    mate = to_mate(away)
    sums, chip_coefs = pl.pallas_call(
        functools.partial(rest_kernel, chips),
        out_shape=[
            shape(half * 2 * (components - 1) * count, SUB, LANES),
            shape(chips - 1, *plane),
        ],
        in_specs=[vmem] * 5,
        out_specs=[vmem] * 2,
        compiler_params=options(16),
        cost_estimate=cost(2_000_000, 2_000_000),
        name="rest",
    )(near_velocity, left_h, right_h, held, through)
    *outgoing, near = pl.pallas_call(
        functools.partial(merge_kernel, chips, components),
        out_shape=[
            shape(half * components * count + m.bit_count(), SUB, LANES) for m in range(1, chips)
        ] + [shape(half * 2 * components * count + 1, SUB, LANES)],
        in_specs=[vmem] * 5,
        out_specs=[vmem] * chips,
        compiler_params=options(16),
        cost_estimate=cost(500_000, 1_600_000),
        name="merge",
    )(mine, sums, away, mate, pair)
    order = sorted(range(1, chips), key=lambda m: -m.bit_count())
    incoming = [send(outgoing[m - 1], lambda z, y: (z ^ (2 * m), y)) for m in order]
    profile = shape(cells, *plane)
    base, unit, goal = pl.pallas_call(
        inner_kernel,
        out_shape=[shape(*velocity.shape), profile, shape(SUB, LANES)],
        in_specs=[vmem] * 8 + [anywhere],
        out_specs=[vmem] * 3,
        compiler_params=options(16),
        cost_estimate=cost(8_000_000, 8_000_000),
        name="inner",
    )(near_velocity, left, right, left_h, right_h, ends, volume, bulk_target.reshape(1, 1),
      outgoing[0])
    own_in, other_out, *tile = pl.pallas_call(
        functools.partial(spread_kernel, order, components),
        out_shape=[shape(half * 2 * components, *sheet)] * 2
        + [shape(columns - shift, SUB, LANES) for shift in range(1, columns)],
        in_specs=[vmem] * 3 + [anywhere] + [vmem] * (chips - 1),
        out_specs=[vmem] * (1 + columns),
        compiler_params=options(16),
        cost_estimate=cost(500_000, 1_600_000),
        name="spread",
    )(near, pair, chip_coefs, base, *incoming)
    other_in = to_mate(other_out)
    tiles = [tile[0]] + [
        send(tile[shift - 1], lambda z, y: (z, (y + shift) % columns))
        for shift in range(1, columns)
    ]
    partial, plain = pl.pallas_call(
        finish_kernel,
        out_shape=[shape(*velocity.shape), profile],
        in_specs=[vmem] * 5,
        out_specs=[anywhere, vmem],
        scratch_shapes=[
            pltpu.VMEM((components - 1, cells) + plane, f32),
            pltpu.SemaphoreType.DMA((row_tiles, components - 1)),
        ],
        compiler_params=options(16),
        cost_estimate=cost(3_000_000, 6_000_000),
        name="finish",
    )(own_in, other_in, base, left, right)
    return pl.pallas_call(
        functools.partial(correct_kernel, columns),
        out_shape=shape(*velocity.shape),
        in_specs=[vmem] * (3 + columns) + [anywhere],
        out_specs=anywhere,
        scratch_shapes=[
            pltpu.VMEM((cells,) + plane, f32),
            pltpu.SemaphoreType.DMA((cells // 2,)),
        ],
        input_output_aliases={3 + columns: 0},
        compiler_params=options(16),
        cost_estimate=cost(500_000, 1_600_000),
        name="correct",
    )(goal, unit, *tiles, plain, partial)


def solution(mesh):
    return jax.shard_map(
        shards,
        mesh=mesh,
        in_specs=(P(None, "gz", "gy", None), P("gy", None), P("gy", None), P(), P()),
        out_specs=P(None, "gz", "gy", None),
        check_vma=False,
    )
```

```python
import functools

import jax
import jax.numpy as jnp
from jax import lax
from jax.experimental import pallas as pl
from jax.experimental.pallas import tpu as pltpu
from jax.sharding import PartitionSpec as P

SUB = 8
STRETCHES = 7
LANES = 128
MIB = 1024 * 1024


def plane_rounds(columns):
    if columns == 4:
        return [(1, 3, 2, 0), (2, 1, 0, 3), (3, 0, 1, 2), (0, 2, 3, 1)]
    return [[(y + shift) % columns for y in range(columns)] for shift in range(1, columns + 1)]


def row_tile(t):
    return pl.ds(pl.multiple_of(t * SUB, SUB), SUB)


def inverted(array):
    guess = pl.reciprocal(array, approx=True)
    return guess * (2.0 - array * guess)


def put(ref, at, sheet):
    count = sheet.shape[1] // LANES
    for i in range(count):
        ref[at * count + i] = sheet[:, i * LANES:(i + 1) * LANES]


def get(ref, at, count):
    return jnp.concatenate([ref[at * count + i] for i in range(count)], axis=1)


def height(index_ref, k):
    return 0.5 + 0.25 * index_ref[k].astype(jnp.float32)


def half_sum(index_ref, k):
    return 0.5 * (height(index_ref, k) + height(index_ref, k + 1))


def ladder_kernel(
    cells, blocks, chips, lines,
    index_hbm, diffusion_hbm, walls_hbm, velocity_hbm,
    mine_ref, away_ref, pair_ref, through_ref, held_ref, left_ref, right_ref, left_h_ref, right_h_ref,
    ends_ref, volume_ref, velocity_ref,
    index_ref, diffusion_ref, walls_ref, table_ref, sems,
):
    total = cells * blocks
    components = velocity_ref.shape[0]
    row_tiles = diffusion_ref.shape[0] // SUB
    small = [
        pltpu.make_async_copy(index_hbm, index_ref, sems.at[0]),
        pltpu.make_async_copy(diffusion_hbm, diffusion_ref, sems.at[1]),
        pltpu.make_async_copy(walls_hbm, walls_ref, sems.at[2]),
    ]
    large = [
        pltpu.make_async_copy(velocity_hbm.at[c], velocity_ref.at[c], sems.at[3 + c])
        for c in range(components)
    ]
    for copy in small + large:
        copy.start()
    me = lax.axis_index("gz")
    chip = me // 2
    first = chip * 2
    for copy in small:
        copy.wait()
    diffusion = diffusion_ref[...]
    inverse = inverted(diffusion)
    for i in range(STRETCHES):
        table_ref[i] = (0.5 + 0.25 * i) * inverse
    walls = walls_ref[...]

    def wall(bits, k):
        face = 1.0 / jnp.full((SUB, diffusion.shape[1]), 0.5 * height(index_ref, k))
        return bits.astype(jnp.float32) * jnp.concatenate([face] * row_tiles, axis=0)

    lower = wall(walls & 1, 0)
    upper = wall(walls >> 1, total - 1)

    def forward(block, kappa, keep=None):
        start = block * cells
        flux = table_ref[index_ref[start]] + kappa
        value = jnp.ones_like(flux)
        for j in range(cells):
            if keep is not None:
                keep(j, flux, value)
            k = start + j
            if j < cells - 1:
                value = value + half_sum(index_ref, k) * flux
                flux = flux + table_ref[index_ref[k + 1]] * value
        k = jnp.minimum(start + cells - 1, total - 2)
        after = inverted(value + half_sum(index_ref, k) * flux)
        return flux * after, after

    def backward(block, kappa, scale=None, keep=None):
        start = block * cells
        flux = table_ref[index_ref[start + cells - 1]] + kappa
        value = jnp.ones_like(flux)
        if scale is not None:
            flux, value = flux * scale, scale
        for j in reversed(range(cells)):
            if keep is not None:
                keep(j, flux, value)
            k = start + j
            if j > 0:
                value = value + half_sum(index_ref, k - 1) * flux
                flux = flux + table_ref[index_ref[k - 1]] * value
        k = jnp.maximum(start - 1, 0)
        after = inverted(value + half_sum(index_ref, k) * flux)
        return flux * after, after

    def thickness(block):
        parts = [height(index_ref, block * cells + j) for j in range(cells)]
        return functools.reduce(jnp.add, parts)

    def sweep_forward(block, state):
        kappa, product, extent = state
        kappa, after = forward(block, kappa)
        through_ref[block] = after
        return kappa, product * after, extent + thickness(block)

    def sweep_backward(step, state):
        block = blocks - 1 - step
        kappa, product, extent = state
        kappa, after = backward(block, kappa)
        through_ref[block] = after
        return kappa, product * after, extent + thickness(block)

    ones = jnp.ones_like(diffusion)
    kappa_left, product, extent = lax.fori_loop(
        0, me, sweep_forward, (lower, ones, thickness(me))
    )
    ends_ref[0] = diffusion * lower * product
    state = {}

    def keep_left(j, flux, value):
        left_ref[j] = value
        left_h_ref[j] = height(index_ref, me * cells + j) * value
        state["flux"], state["value"] = flux, value

    _, own_forward = forward(me, kappa_left, keep_left)
    held_ref[1] = own_forward
    held_ref[3] = state["flux"]
    held_ref[4] = state["value"]
    held_ref[5] = state["flux"] - kappa_left

    kappa_right, product, extent = lax.fori_loop(
        0, blocks - 1 - me, sweep_backward, (upper, ones, extent)
    )
    ends_ref[1] = diffusion_ref[...] * upper * product
    scale = inverted(diffusion_ref[...] * (held_ref[3] + kappa_right * held_ref[4]))
    held_ref[0] = scale

    def keep_right(j, flux, value):
        right_ref[j] = value
        right_h_ref[j] = height(index_ref, me * cells + j) * value
        state["flux"] = flux

    _, own_backward = backward(me, kappa_right, scale, keep_right)
    held_ref[2] = own_backward
    held_ref[6] = state["flux"] - kappa_right * scale

    is_first = me == first
    forth, back = held_ref[1], own_backward * held_ref[0]
    pair_ref[0] = jnp.where(is_first, back, forth)
    pair_ref[1] = jnp.where(is_first, forth, through_ref[first])
    pair_ref[2] = jnp.where(is_first, through_ref[first + 1], back)

    def fold(array):
        parts = [array[:, i * LANES:(i + 1) * LANES] for i in range(array.shape[1] // LANES)]
        return functools.reduce(jnp.add, parts)

    for copy in large:
        copy.wait()
    volume_ref[...] = jnp.full(volume_ref.shape, extent * lines)
    half = row_tiles // 2
    own_extent = thickness(me)
    heights = [height(index_ref, me * cells + j) for j in range(cells)]

    def sums(ref, whose, parts):
        def of_tile(i, state):
            flow, weight = state
            rows = row_tile(whose * half + i)
            from_left = [0.0] * parts
            from_right = [0.0] * parts
            plain = 0.0
            for j in range(cells):
                left = left_h_ref[j, rows]
                right = right_h_ref[j, rows]
                for c in range(parts):
                    v = velocity_ref[c, j, rows]
                    from_left[c] = from_left[c] + left * v
                    from_right[c] = from_right[c] + right * v
                    if c == 0:
                        plain = plain + heights[j] * v
            for c in range(parts):
                at = i * 2 * parts + c
                put(ref, at, from_left[c] * held_ref[1, rows])
                put(ref, at + parts, from_right[c] * held_ref[2, rows])
            low_part = ends_ref[0, rows]
            high_part = ends_ref[1, rows] * held_ref[0, rows]
            totals = low_part * held_ref[6, rows] + high_part * held_ref[5, rows]
            return (
                flow + fold(plain - low_part * from_right[0] - high_part * from_left[0]),
                weight + fold(own_extent - diffusion_ref[rows] * totals),
            )

        return of_tile

    state = (jnp.zeros((SUB, LANES), jnp.float32),) * 2
    mates = 1 - (me - first)
    state = lax.fori_loop(0, half, sums(away_ref, mates, components), state)
    flow, weight = lax.fori_loop(0, half, sums(mine_ref, me - first, 1), state)
    for i in range(half):
        put(away_ref, half * 2 * components + i, pair_ref[0, row_tile(mates * half + i)])
    slot, middle = away_ref.shape[0] - 1, SUB // 2
    away_ref[slot, 0:middle] = flow[0:middle] + flow[middle:]
    away_ref[slot, middle:] = weight[0:middle] + weight[middle:]


def rest_kernel(
    chips, velocity_ref, left_h_ref, right_h_ref, held_ref, through_ref, sums_ref, chip_ref
):
    components, cells, _, lines_x = velocity_ref.shape
    me = lax.axis_index("gz")
    chip = me // 2
    half = sums_ref.shape[0] // (2 * (components - 1) * (lines_x // LANES))
    ones = jnp.ones(chip_ref.shape[1:], jnp.float32)
    for m in range(1, chips):
        other = chip ^ m
        low = jnp.minimum(chip, other)
        high = jnp.maximum(chip, other)
        chip_ref[m - 1] = lax.fori_loop(
            low + 1,
            high,
            lambda r, product: product * (through_ref[2 * r] * through_ref[2 * r + 1]),
            ones,
        )

    def of_tile(i, _):
        rows = row_tile((me - chip * 2) * half + i)
        from_left = [0.0] * (components - 1)
        from_right = [0.0] * (components - 1)
        for j in range(cells):
            left = left_h_ref[j, rows]
            right = right_h_ref[j, rows]
            for c in range(components - 1):
                v = velocity_ref[c + 1, j, rows]
                from_left[c] = from_left[c] + left * v
                from_right[c] = from_right[c] + right * v
        for c in range(components - 1):
            at = i * 2 * (components - 1) + c
            put(sums_ref, at, from_left[c] * held_ref[1, rows])
            put(sums_ref, at + components - 1, from_right[c] * held_ref[2, rows])
        return 0

    lax.fori_loop(0, half, of_tile, 0)


def merge_kernel(chips, components, mine_ref, sums_ref, away_ref, mate_ref, pair_ref, *rest):
    send_refs, near_ref = rest[:-1], rest[-1]
    me = lax.axis_index("gz")
    chip = me // 2
    is_first = me == chip * 2
    count = pair_ref.shape[2] // LANES
    half = mine_ref.shape[0] // (2 * count)
    slot = away_ref.shape[0] - 1
    tile = away_ref[slot] + mate_ref[slot]
    near_ref[near_ref.shape[0] - 1] = tile
    for ref in send_refs:
        for at in range(half * components * count, ref.shape[0]):
            ref[at] = tile
    for i in range(half):
        rows = row_tile((me - chip * 2) * half + i)
        mine, mate = pair_ref[0, rows], get(mate_ref, half * 2 * components + i, count)
        forth = jnp.where(is_first, mate, mine)
        back = jnp.where(is_first, mine, mate)
        for c in range(components):
            at = i * 2 * components + c
            if c == 0:
                own = [get(mine_ref, i * 2 + k, count) for k in range(2)]
            else:
                others = components - 1
                own = [
                    get(sums_ref, i * 2 * others + k * others + c - 1, count) for k in range(2)
                ]
            mine, mate = own[0], get(mate_ref, at, count)
            first = jnp.where(is_first, mine, mate)
            second = jnp.where(is_first, mate, mine)
            put(near_ref, at, first)
            to_right = second + forth * first
            at = at + components
            mine, mate = own[1], get(mate_ref, at, count)
            first = jnp.where(is_first, mine, mate)
            second = jnp.where(is_first, mate, mine)
            put(near_ref, at, second)
            to_left = first + back * second
            for m in range(1, chips):
                goes_right = (chip ^ m) > chip
                sheet = jnp.where(goes_right, to_right, to_left)
                put(send_refs[m - 1], i * components + c, sheet)


def spread_kernel(order, components, near_ref, pair_ref, chip_ref, *rest):
    recv_refs = rest[1:len(order) + 1]
    own_ref, other_ref, *tile_refs = rest[len(order) + 1:]
    me = lax.axis_index("gz")
    chip = me // 2
    is_first = me == chip * 2
    count = pair_ref.shape[2] // LANES
    half = near_ref.shape[0] // (2 * components * count)
    tiles = [ref[ref.shape[0] - 1] for ref in (near_ref, *recv_refs)]
    tile = functools.reduce(jnp.add, tiles)
    for ref in tile_refs:
        for i in range(ref.shape[0]):
            ref[i] = tile
    for i in range(half):
        rows = row_tile((me - chip * 2) * half + i)
        coefs = [chip_ref[m - 1, rows] for m in order]
        for c in range(components):
            left_in = jnp.zeros(own_ref.shape[1:], jnp.float32)
            right_in = jnp.zeros(own_ref.shape[1:], jnp.float32)
            for m, coef, ref in zip(order, coefs, recv_refs):
                term = coef * get(ref, i * components + c, count)
                from_left = (chip ^ m) < chip
                left_in = left_in + jnp.where(from_left, term, 0.0)
                right_in = right_in + jnp.where(from_left, 0.0, term)
            at = i * 2 * components + c
            left_second = get(near_ref, at, count) + pair_ref[1, rows] * left_in
            right_first = get(near_ref, at + components, count) + pair_ref[2, rows] * right_in
            own_ref[at] = jnp.where(is_first, left_in, left_second)
            other_ref[at] = jnp.where(is_first, left_second, left_in)
            at = at + components
            own_ref[at] = jnp.where(is_first, right_first, right_in)
            other_ref[at] = jnp.where(is_first, right_in, right_first)


def inner_kernel(
    velocity_ref, left_ref, right_ref, left_h_ref, right_h_ref, ends_ref, volume_ref, target_ref,
    _, base_ref, unit_ref, goal_ref,
):
    components, cells, lines_y, lines_x = velocity_ref.shape
    goal_ref[...] = target_ref[...] * volume_ref[...]

    def of_tile(t, _):
        rows = row_tile(t)
        gathered = [jnp.zeros((SUB, lines_x), jnp.float32)] * components
        for j in reversed(range(cells)):
            left = left_ref[j, rows]
            right = right_h_ref[j, rows]
            for c in range(components):
                base_ref[c, j, rows] = left * gathered[c]
                if j > 0:
                    gathered[c] = gathered[c] + right * velocity_ref[c, j, rows]
        gathered = [jnp.zeros((SUB, lines_x), jnp.float32)] * components
        low_part = ends_ref[0, rows]
        high_part = ends_ref[1, rows] * right_ref[cells - 1, rows]
        for j in range(cells):
            left = left_h_ref[j, rows]
            right = right_ref[j, rows]
            unit_ref[j, rows] = 1.0 - (low_part * right + high_part * left_ref[j, rows])
            for c in range(components):
                gathered[c] = gathered[c] + left * velocity_ref[c, j, rows]
                base_ref[c, j, rows] = base_ref[c, j, rows] + right * gathered[c]
        return 0

    lax.fori_loop(0, lines_y // SUB, of_tile, 0)


def finish_kernel(
    own_ref, other_ref, base_ref, left_ref, right_ref, out_hbm, plain_ref, result_ref, sems
):
    components, cells, lines_y, _ = base_ref.shape
    half = own_ref.shape[0] // (2 * components)
    me = lax.axis_index("gz")

    def copies(t):
        rows = row_tile(t)
        return [
            pltpu.make_async_copy(
                result_ref.at[c - 1, :, rows], out_hbm.at[c, :, rows], sems.at[t, c - 1])
            for c in range(1, components)
        ]

    def half_of(incoming_ref, side):
        def of_tile(i, _):
            t = lax.rem(me + side, 2) * half + i
            rows = row_tile(t)
            scale = right_ref[cells - 1, rows]
            at = i * 2 * components
            lefts = [incoming_ref[at + c] for c in range(components)]
            rights = [incoming_ref[at + components + c] * scale for c in range(components)]
            for j in range(cells):
                left = left_ref[j, rows]
                right = right_ref[j, rows]
                for c in range(components):
                    value = base_ref[c, j, rows] + (right * lefts[c] + left * rights[c])
                    if c == 0:
                        plain_ref[j, rows] = value
                    else:
                        result_ref[c - 1, j, rows] = value
            for copy in copies(t):
                copy.start()
            return 0

        lax.fori_loop(0, half, of_tile, 0)

    half_of(own_ref, 0)
    half_of(other_ref, 1)
    for t in range(lines_y // SUB):
        for copy in copies(t):
            copy.wait()


def correct_kernel(count, goal_ref, unit_ref, *rest):
    tile_refs = rest[:count]
    plain_ref, _, out_hbm, result_ref, sems = rest[count:]
    totals = functools.reduce(jnp.add, [ref[0] for ref in tile_refs])
    flow = jnp.sum(totals[0:SUB // 2], keepdims=True)
    weight = jnp.sum(totals[SUB // 2:], keepdims=True)
    alpha = (goal_ref[0:1, 0:1] - flow) / weight
    cells, lines_y, _ = plain_ref.shape

    def copy(t):
        rows = row_tile(t)
        return pltpu.make_async_copy(result_ref.at[:, rows], out_hbm.at[0, :, rows], sems.at[t])

    def of_tile(t, _):
        rows = row_tile(t)
        for j in range(cells):
            result_ref[j, rows] = plain_ref[j, rows] + alpha * unit_ref[j, rows]
        copy(t).start()
        return 0

    lax.fori_loop(0, lines_y // SUB, of_tile, 0)
    for t in range(lines_y // SUB):
        copy(t).wait()


def shards(velocity, diffusion, wall_types, stretch_index, bulk_target):
    blocks = lax.axis_size("gz")
    columns = lax.axis_size("gy")
    components, cells, lines_y, lines_x = velocity.shape
    chips = blocks // 2
    row_tiles = lines_y // SUB
    half = row_tiles // 2
    f32 = jnp.float32
    vmem = pl.BlockSpec(memory_space=pltpu.VMEM)
    anywhere = pl.BlockSpec(memory_space=pl.ANY)
    plane = (lines_y, lines_x)
    sheet = (SUB, lines_x)

    def shape(*dims):
        return jax.ShapeDtypeStruct(dims, f32)

    def in_hbm(array):
        return pltpu.with_memory_space_constraint(array, pltpu.HBM)

    def options(mib):
        return pltpu.CompilerParams(vmem_limit_bytes=mib * MIB)

    def cost(flops, transferred):
        return pl.CostEstimate(flops=flops, bytes_accessed=transferred, transcendentals=0)

    def send(array, partner):
        pairs = [((z, y), partner(z, y)) for z in range(blocks) for y in range(columns)]
        route = [(a * columns + b, c * columns + d) for (a, b), (c, d) in pairs]
        return lax.ppermute(array, ("gz", "gy"), route)

    def to_mate(array):
        return send(array, lambda z, y: (z ^ 1, y))

    count = lines_x // LANES
    lines = float(lines_y * columns * lines_x)
    (mine, away, pair, through, held, left, right, left_h, right_h, ends, volume,
     near_velocity) = pl.pallas_call(
        functools.partial(ladder_kernel, cells, blocks, chips, lines),
        out_shape=[
            shape(half * 2 * count, SUB, LANES),
            shape(half * (2 * components + 1) * count + 1, SUB, LANES),
            shape(3, *plane),
            shape(blocks, *plane),
            shape(7, *plane),
            shape(cells, *plane),
            shape(cells, *plane),
            shape(cells, *plane),
            shape(cells, *plane),
            shape(2, *plane),
            shape(SUB, LANES),
            shape(*velocity.shape),
        ],
        in_specs=[anywhere] * 4,
        out_specs=[vmem] * 12,
        scratch_shapes=[
            pltpu.SMEM(stretch_index.shape, jnp.int32),
            pltpu.VMEM(plane, f32),
            pltpu.VMEM(plane, jnp.int32),
            pltpu.VMEM((STRETCHES,) + plane, f32),
            pltpu.SemaphoreType.DMA((3 + components,)),
        ],
        compiler_params=options(24),
        cost_estimate=cost(40_000_000, 6_000_000),
        name="ladder",
    )(in_hbm(stretch_index), in_hbm(diffusion), in_hbm(wall_types), in_hbm(velocity))

    mate = to_mate(away)
    sums, chip_coefs = pl.pallas_call(
        functools.partial(rest_kernel, chips),
        out_shape=[
            shape(half * 2 * (components - 1) * count, SUB, LANES),
            shape(chips - 1, *plane),
        ],
        in_specs=[vmem] * 5,
        out_specs=[vmem] * 2,
        compiler_params=options(16),
        cost_estimate=cost(2_000_000, 2_000_000),
        name="rest",
    )(near_velocity, left_h, right_h, held, through)
    *outgoing, near = pl.pallas_call(
        functools.partial(merge_kernel, chips, components),
        out_shape=[
            shape(half * components * count + m.bit_count(), SUB, LANES) for m in range(1, chips)
        ] + [shape(half * 2 * components * count + 1, SUB, LANES)],
        in_specs=[vmem] * 5,
        out_specs=[vmem] * chips,
        compiler_params=options(16),
        cost_estimate=cost(500_000, 1_600_000),
        name="merge",
    )(mine, sums, away, mate, pair)
    order = sorted(range(1, chips), key=lambda m: -m.bit_count())
    incoming = [send(outgoing[m - 1], lambda z, y: (z ^ (2 * m), y)) for m in order]
    profile = shape(cells, *plane)
    base, unit, goal = pl.pallas_call(
        inner_kernel,
        out_shape=[shape(*velocity.shape), profile, shape(SUB, LANES)],
        in_specs=[vmem] * 8 + [anywhere],
        out_specs=[vmem] * 3,
        compiler_params=options(16),
        cost_estimate=cost(8_000_000, 8_000_000),
        name="inner",
    )(near_velocity, left, right, left_h, right_h, ends, volume, bulk_target.reshape(1, 1),
      outgoing[0])
    rounds = plane_rounds(columns)
    own_in, other_out, *tile = pl.pallas_call(
        functools.partial(spread_kernel, order, components),
        out_shape=[shape(half * 2 * components, *sheet)] * 2
        + [shape(len(rounds) - i, SUB, LANES) for i in range(len(rounds))],
        in_specs=[vmem] * 3 + [anywhere] + [vmem] * (chips - 1),
        out_specs=[vmem] * (2 + len(rounds)),
        compiler_params=options(16),
        cost_estimate=cost(500_000, 1_600_000),
        name="spread",
    )(near, pair, chip_coefs, base, *incoming)
    other_in = to_mate(other_out)
    tiles = [
        send(array, lambda z, y: (z, targets[y])) for array, targets in zip(tile, rounds)
    ]
    partial, plain = pl.pallas_call(
        finish_kernel,
        out_shape=[shape(*velocity.shape), profile],
        in_specs=[vmem] * 5,
        out_specs=[anywhere, vmem],
        scratch_shapes=[
            pltpu.VMEM((components - 1, cells) + plane, f32),
            pltpu.SemaphoreType.DMA((row_tiles, components - 1)),
        ],
        compiler_params=options(16),
        cost_estimate=cost(3_000_000, 6_000_000),
        name="finish",
    )(own_in, other_in, base, left, right)
    return pl.pallas_call(
        functools.partial(correct_kernel, len(tiles)),
        out_shape=shape(*velocity.shape),
        in_specs=[vmem] * (3 + len(tiles)) + [anywhere],
        out_specs=anywhere,
        scratch_shapes=[
            pltpu.VMEM((cells,) + plane, f32),
            pltpu.SemaphoreType.DMA((row_tiles,)),
        ],
        input_output_aliases={3 + len(tiles): 0},
        compiler_params=options(16),
        cost_estimate=cost(500_000, 1_600_000),
        name="correct",
    )(goal, unit, *tiles, plain, partial)


def solution(mesh):
    return jax.shard_map(
        shards,
        mesh=mesh,
        in_specs=(P(None, "gz", "gy", None), P("gy", None), P("gy", None), P(), P()),
        out_specs=P(None, "gz", "gy", None),
        check_vma=False,
    )
```

```python
import functools

import jax
import jax.numpy as jnp
from jax import lax
from jax.experimental import pallas as pl
from jax.experimental.pallas import tpu as pltpu
from jax.sharding import PartitionSpec as P

SUB = 8
STRETCHES = 7
LANES = 128
MIB = 1024 * 1024


def plane_rounds(columns):
    if columns == 4:
        return [(1, 0, 3, 2), (1, 2, 3, 0), (3, 2, 0, 1), (2, 3, 1, 0)]
    return [[(y + shift) % columns for y in range(columns)] for shift in range(1, columns)]


def repeated(rounds):
    seen, again = set(), []
    for targets in rounds:
        pairs = list(enumerate(targets))
        again.append([b for a, b in pairs if (a, b) in seen])
        seen.update(pairs)
    return again


def row_tile(t):
    return pl.ds(pl.multiple_of(t * SUB, SUB), SUB)


def inverted(array):
    guess = pl.reciprocal(array, approx=True)
    return guess * (2.0 - array * guess)


def put(ref, at, sheet):
    count = sheet.shape[1] // LANES
    for i in range(count):
        ref[at * count + i] = sheet[:, i * LANES:(i + 1) * LANES]


def get(ref, at, count):
    return jnp.concatenate([ref[at * count + i] for i in range(count)], axis=1)


def height(index_ref, k):
    return 0.5 + 0.25 * index_ref[k].astype(jnp.float32)


def half_sum(index_ref, k):
    return 0.5 * (height(index_ref, k) + height(index_ref, k + 1))


def ladder_kernel(
    cells, blocks, chips, lines,
    index_hbm, diffusion_hbm, walls_hbm, velocity_hbm,
    mine_ref, away_ref, pair_ref, through_ref, held_ref, left_ref, right_ref, left_h_ref, right_h_ref,
    ends_ref, volume_ref, velocity_ref,
    index_ref, diffusion_ref, walls_ref, table_ref, sems,
):
    total = cells * blocks
    components = velocity_ref.shape[0]
    row_tiles = diffusion_ref.shape[0] // SUB
    small = [
        pltpu.make_async_copy(index_hbm, index_ref, sems.at[0]),
        pltpu.make_async_copy(diffusion_hbm, diffusion_ref, sems.at[1]),
        pltpu.make_async_copy(walls_hbm, walls_ref, sems.at[2]),
    ]
    large = [
        pltpu.make_async_copy(velocity_hbm.at[c], velocity_ref.at[c], sems.at[3 + c])
        for c in range(components)
    ]
    for copy in small + large:
        copy.start()
    me = lax.axis_index("gz")
    chip = me // 2
    first = chip * 2
    for copy in small:
        copy.wait()
    diffusion = diffusion_ref[...]
    inverse = inverted(diffusion)
    for i in range(STRETCHES):
        table_ref[i] = (0.5 + 0.25 * i) * inverse
    walls = walls_ref[...]

    def wall(bits, k):
        face = 1.0 / jnp.full((SUB, diffusion.shape[1]), 0.5 * height(index_ref, k))
        return bits.astype(jnp.float32) * jnp.concatenate([face] * row_tiles, axis=0)

    lower = wall(walls & 1, 0)
    upper = wall(walls >> 1, total - 1)

    def forward(block, kappa, keep=None):
        start = block * cells
        flux = table_ref[index_ref[start]] + kappa
        value = jnp.ones_like(flux)
        for j in range(cells):
            if keep is not None:
                keep(j, flux, value)
            k = start + j
            if j < cells - 1:
                value = value + half_sum(index_ref, k) * flux
                flux = flux + table_ref[index_ref[k + 1]] * value
        k = jnp.minimum(start + cells - 1, total - 2)
        after = inverted(value + half_sum(index_ref, k) * flux)
        return flux * after, after

    def backward(block, kappa, scale=None, keep=None):
        start = block * cells
        flux = table_ref[index_ref[start + cells - 1]] + kappa
        value = jnp.ones_like(flux)
        if scale is not None:
            flux, value = flux * scale, scale
        for j in reversed(range(cells)):
            if keep is not None:
                keep(j, flux, value)
            k = start + j
            if j > 0:
                value = value + half_sum(index_ref, k - 1) * flux
                flux = flux + table_ref[index_ref[k - 1]] * value
        k = jnp.maximum(start - 1, 0)
        after = inverted(value + half_sum(index_ref, k) * flux)
        return flux * after, after

    def thickness(block):
        parts = [height(index_ref, block * cells + j) for j in range(cells)]
        return functools.reduce(jnp.add, parts)

    def sweep_forward(block, state):
        kappa, product, extent = state
        kappa, after = forward(block, kappa)
        through_ref[block] = after
        return kappa, product * after, extent + thickness(block)

    def sweep_backward(step, state):
        block = blocks - 1 - step
        kappa, product, extent = state
        kappa, after = backward(block, kappa)
        through_ref[block] = after
        return kappa, product * after, extent + thickness(block)

    ones = jnp.ones_like(diffusion)
    kappa_left, product, extent = lax.fori_loop(
        0, me, sweep_forward, (lower, ones, thickness(me))
    )
    ends_ref[0] = diffusion * lower * product
    state = {}

    def keep_left(j, flux, value):
        left_ref[j] = value
        left_h_ref[j] = height(index_ref, me * cells + j) * value
        state["flux"], state["value"] = flux, value

    _, own_forward = forward(me, kappa_left, keep_left)
    held_ref[1] = own_forward
    held_ref[3] = state["flux"]
    held_ref[4] = state["value"]
    held_ref[5] = state["flux"] - kappa_left

    kappa_right, product, extent = lax.fori_loop(
        0, blocks - 1 - me, sweep_backward, (upper, ones, extent)
    )
    ends_ref[1] = diffusion_ref[...] * upper * product
    scale = inverted(diffusion_ref[...] * (held_ref[3] + kappa_right * held_ref[4]))
    held_ref[0] = scale

    def keep_right(j, flux, value):
        right_ref[j] = value
        right_h_ref[j] = height(index_ref, me * cells + j) * value
        state["flux"] = flux

    _, own_backward = backward(me, kappa_right, scale, keep_right)
    held_ref[2] = own_backward
    held_ref[6] = state["flux"] - kappa_right * scale

    is_first = me == first
    forth, back = held_ref[1], own_backward * held_ref[0]
    pair_ref[0] = jnp.where(is_first, back, forth)
    pair_ref[1] = jnp.where(is_first, forth, through_ref[first])
    pair_ref[2] = jnp.where(is_first, through_ref[first + 1], back)

    def fold(array):
        parts = [array[:, i * LANES:(i + 1) * LANES] for i in range(array.shape[1] // LANES)]
        return functools.reduce(jnp.add, parts)

    for copy in large:
        copy.wait()
    volume_ref[...] = jnp.full(volume_ref.shape, extent * lines)
    half = row_tiles // 2
    own_extent = thickness(me)
    heights = [height(index_ref, me * cells + j) for j in range(cells)]

    def sums(ref, whose, parts):
        def of_tile(i, state):
            flow, weight = state
            rows = row_tile(whose * half + i)
            from_left = [0.0] * parts
            from_right = [0.0] * parts
            plain = 0.0
            for j in range(cells):
                left = left_h_ref[j, rows]
                right = right_h_ref[j, rows]
                for c in range(parts):
                    v = velocity_ref[c, j, rows]
                    from_left[c] = from_left[c] + left * v
                    from_right[c] = from_right[c] + right * v
                    if c == 0:
                        plain = plain + heights[j] * v
            for c in range(parts):
                at = i * 2 * parts + c
                put(ref, at, from_left[c] * held_ref[1, rows])
                put(ref, at + parts, from_right[c] * held_ref[2, rows])
            low_part = ends_ref[0, rows]
            high_part = ends_ref[1, rows] * held_ref[0, rows]
            totals = low_part * held_ref[6, rows] + high_part * held_ref[5, rows]
            return (
                flow + fold(plain - low_part * from_right[0] - high_part * from_left[0]),
                weight + fold(own_extent - diffusion_ref[rows] * totals),
            )

        return of_tile

    state = (jnp.zeros((SUB, LANES), jnp.float32),) * 2
    mates = 1 - (me - first)
    state = lax.fori_loop(0, half, sums(away_ref, mates, components), state)
    flow, weight = lax.fori_loop(0, half, sums(mine_ref, me - first, 1), state)
    for i in range(half):
        put(away_ref, half * 2 * components + i, pair_ref[0, row_tile(mates * half + i)])
    slot, middle = away_ref.shape[0] - 1, SUB // 2
    away_ref[slot, 0:middle] = flow[0:middle] + flow[middle:]
    away_ref[slot, middle:] = weight[0:middle] + weight[middle:]


def rest_kernel(
    chips, velocity_ref, left_h_ref, right_h_ref, held_ref, through_ref, sums_ref, chip_ref
):
    components, cells, _, lines_x = velocity_ref.shape
    me = lax.axis_index("gz")
    chip = me // 2
    half = sums_ref.shape[0] // (2 * (components - 1) * (lines_x // LANES))
    ones = jnp.ones(chip_ref.shape[1:], jnp.float32)
    for m in range(1, chips):
        other = chip ^ m
        low = jnp.minimum(chip, other)
        high = jnp.maximum(chip, other)
        chip_ref[m - 1] = lax.fori_loop(
            low + 1,
            high,
            lambda r, product: product * (through_ref[2 * r] * through_ref[2 * r + 1]),
            ones,
        )

    def of_tile(i, _):
        rows = row_tile((me - chip * 2) * half + i)
        from_left = [0.0] * (components - 1)
        from_right = [0.0] * (components - 1)
        for j in range(cells):
            left = left_h_ref[j, rows]
            right = right_h_ref[j, rows]
            for c in range(components - 1):
                v = velocity_ref[c + 1, j, rows]
                from_left[c] = from_left[c] + left * v
                from_right[c] = from_right[c] + right * v
        for c in range(components - 1):
            at = i * 2 * (components - 1) + c
            put(sums_ref, at, from_left[c] * held_ref[1, rows])
            put(sums_ref, at + components - 1, from_right[c] * held_ref[2, rows])
        return 0

    lax.fori_loop(0, half, of_tile, 0)


def merge_kernel(chips, components, mine_ref, sums_ref, away_ref, mate_ref, pair_ref, *rest):
    send_refs, near_ref = rest[:-1], rest[-1]
    me = lax.axis_index("gz")
    chip = me // 2
    is_first = me == chip * 2
    count = pair_ref.shape[2] // LANES
    half = mine_ref.shape[0] // (2 * count)
    slot = away_ref.shape[0] - 1
    tile = away_ref[slot] + mate_ref[slot]
    near_ref[near_ref.shape[0] - 1] = tile
    for ref in send_refs:
        for at in range(half * components * count, ref.shape[0]):
            ref[at] = tile
    for i in range(half):
        rows = row_tile((me - chip * 2) * half + i)
        mine, mate = pair_ref[0, rows], get(mate_ref, half * 2 * components + i, count)
        forth = jnp.where(is_first, mate, mine)
        back = jnp.where(is_first, mine, mate)
        for c in range(components):
            at = i * 2 * components + c
            if c == 0:
                own = [get(mine_ref, i * 2 + k, count) for k in range(2)]
            else:
                others = components - 1
                own = [
                    get(sums_ref, i * 2 * others + k * others + c - 1, count) for k in range(2)
                ]
            mine, mate = own[0], get(mate_ref, at, count)
            first = jnp.where(is_first, mine, mate)
            second = jnp.where(is_first, mate, mine)
            put(near_ref, at, first)
            to_right = second + forth * first
            at = at + components
            mine, mate = own[1], get(mate_ref, at, count)
            first = jnp.where(is_first, mine, mate)
            second = jnp.where(is_first, mate, mine)
            put(near_ref, at, second)
            to_left = first + back * second
            for m in range(1, chips):
                goes_right = (chip ^ m) > chip
                sheet = jnp.where(goes_right, to_right, to_left)
                put(send_refs[m - 1], i * components + c, sheet)


def spread_kernel(order, components, near_ref, pair_ref, chip_ref, *rest):
    recv_refs = rest[1:len(order) + 1]
    own_ref, other_ref, *tile_refs = rest[len(order) + 1:]
    me = lax.axis_index("gz")
    chip = me // 2
    is_first = me == chip * 2
    count = pair_ref.shape[2] // LANES
    half = near_ref.shape[0] // (2 * components * count)
    tiles = [ref[ref.shape[0] - 1] for ref in (near_ref, *recv_refs)]
    tile = functools.reduce(jnp.add, tiles)
    for ref in tile_refs:
        for i in range(ref.shape[0]):
            ref[i] = tile
    for i in range(half):
        rows = row_tile((me - chip * 2) * half + i)
        coefs = [chip_ref[m - 1, rows] for m in order]
        for c in range(components):
            left_in = jnp.zeros(own_ref.shape[1:], jnp.float32)
            right_in = jnp.zeros(own_ref.shape[1:], jnp.float32)
            for m, coef, ref in zip(order, coefs, recv_refs):
                term = coef * get(ref, i * components + c, count)
                from_left = (chip ^ m) < chip
                left_in = left_in + jnp.where(from_left, term, 0.0)
                right_in = right_in + jnp.where(from_left, 0.0, term)
            at = i * 2 * components + c
            left_second = get(near_ref, at, count) + pair_ref[1, rows] * left_in
            right_first = get(near_ref, at + components, count) + pair_ref[2, rows] * right_in
            own_ref[at] = jnp.where(is_first, left_in, left_second)
            other_ref[at] = jnp.where(is_first, left_second, left_in)
            at = at + components
            own_ref[at] = jnp.where(is_first, right_first, right_in)
            other_ref[at] = jnp.where(is_first, right_in, right_first)


def inner_kernel(
    velocity_ref, left_ref, right_ref, left_h_ref, right_h_ref, ends_ref, volume_ref, target_ref,
    _, base_ref, unit_ref, goal_ref,
):
    components, cells, lines_y, lines_x = velocity_ref.shape
    goal_ref[...] = target_ref[...] * volume_ref[...]

    def of_tile(t, _):
        rows = row_tile(t)
        gathered = [jnp.zeros((SUB, lines_x), jnp.float32)] * components
        for j in reversed(range(cells)):
            left = left_ref[j, rows]
            right = right_h_ref[j, rows]
            for c in range(components):
                base_ref[c, j, rows] = left * gathered[c]
                if j > 0:
                    gathered[c] = gathered[c] + right * velocity_ref[c, j, rows]
        gathered = [jnp.zeros((SUB, lines_x), jnp.float32)] * components
        low_part = ends_ref[0, rows]
        high_part = ends_ref[1, rows] * right_ref[cells - 1, rows]
        for j in range(cells):
            left = left_h_ref[j, rows]
            right = right_ref[j, rows]
            unit_ref[j, rows] = 1.0 - (low_part * right + high_part * left_ref[j, rows])
            for c in range(components):
                gathered[c] = gathered[c] + left * velocity_ref[c, j, rows]
                base_ref[c, j, rows] = base_ref[c, j, rows] + right * gathered[c]
        return 0

    lax.fori_loop(0, lines_y // SUB, of_tile, 0)


def finish_kernel(
    own_ref, other_ref, base_ref, left_ref, right_ref, out_hbm, plain_ref, result_ref, sems
):
    components, cells, lines_y, _ = base_ref.shape
    half = own_ref.shape[0] // (2 * components)
    me = lax.axis_index("gz")

    def copies(t):
        rows = row_tile(t)
        return [
            pltpu.make_async_copy(
                result_ref.at[c - 1, :, rows], out_hbm.at[c, :, rows], sems.at[t, c - 1])
            for c in range(1, components)
        ]

    def half_of(incoming_ref, side):
        def of_tile(i, _):
            t = lax.rem(me + side, 2) * half + i
            rows = row_tile(t)
            scale = right_ref[cells - 1, rows]
            at = i * 2 * components
            lefts = [incoming_ref[at + c] for c in range(components)]
            rights = [incoming_ref[at + components + c] * scale for c in range(components)]
            for j in range(cells):
                left = left_ref[j, rows]
                right = right_ref[j, rows]
                for c in range(components):
                    value = base_ref[c, j, rows] + (right * lefts[c] + left * rights[c])
                    if c == 0:
                        plain_ref[j, rows] = value
                    else:
                        result_ref[c - 1, j, rows] = value
            for copy in copies(t):
                copy.start()
            return 0

        lax.fori_loop(0, half, of_tile, 0)

    half_of(own_ref, 0)
    half_of(other_ref, 1)
    for t in range(lines_y // SUB):
        for copy in copies(t):
            copy.wait()


def correct_kernel(again, goal_ref, unit_ref, *rest):
    tile_refs = rest[:len(again) + 1]
    plain_ref, _, out_hbm, result_ref, sems = rest[len(again) + 1:]
    me = lax.axis_index("gy")
    totals = tile_refs[0][0]
    for planes, ref in zip(again, tile_refs[1:]):
        term = ref[0]
        for y in planes:
            term = jnp.where(me == y, 0.0, term)
        totals = totals + term
    flow = jnp.sum(totals[0:SUB // 2], keepdims=True)
    weight = jnp.sum(totals[SUB // 2:], keepdims=True)
    alpha = (goal_ref[0:1, 0:1] - flow) / weight
    cells, lines_y, _ = plain_ref.shape

    def copy(t):
        rows = row_tile(t)
        return pltpu.make_async_copy(result_ref.at[:, rows], out_hbm.at[0, :, rows], sems.at[t])

    def of_tile(t, _):
        rows = row_tile(t)
        for j in range(cells):
            result_ref[j, rows] = plain_ref[j, rows] + alpha * unit_ref[j, rows]
        copy(t).start()
        return 0

    lax.fori_loop(0, lines_y // SUB, of_tile, 0)
    for t in range(lines_y // SUB):
        copy(t).wait()


def shards(velocity, diffusion, wall_types, stretch_index, bulk_target):
    blocks = lax.axis_size("gz")
    columns = lax.axis_size("gy")
    components, cells, lines_y, lines_x = velocity.shape
    chips = blocks // 2
    row_tiles = lines_y // SUB
    half = row_tiles // 2
    f32 = jnp.float32
    vmem = pl.BlockSpec(memory_space=pltpu.VMEM)
    anywhere = pl.BlockSpec(memory_space=pl.ANY)
    plane = (lines_y, lines_x)
    sheet = (SUB, lines_x)

    def shape(*dims):
        return jax.ShapeDtypeStruct(dims, f32)

    def in_hbm(array):
        return pltpu.with_memory_space_constraint(array, pltpu.HBM)

    def options(mib):
        return pltpu.CompilerParams(vmem_limit_bytes=mib * MIB)

    def cost(flops, transferred):
        return pl.CostEstimate(flops=flops, bytes_accessed=transferred, transcendentals=0)

    def send(array, partner):
        pairs = [((z, y), partner(z, y)) for z in range(blocks) for y in range(columns)]
        route = [(a * columns + b, c * columns + d) for (a, b), (c, d) in pairs]
        return lax.ppermute(array, ("gz", "gy"), route)

    def to_mate(array):
        return send(array, lambda z, y: (z ^ 1, y))

    count = lines_x // LANES
    lines = float(lines_y * columns * lines_x)
    (mine, away, pair, through, held, left, right, left_h, right_h, ends, volume,
     near_velocity) = pl.pallas_call(
        functools.partial(ladder_kernel, cells, blocks, chips, lines),
        out_shape=[
            shape(half * 2 * count, SUB, LANES),
            shape(half * (2 * components + 1) * count + 1, SUB, LANES),
            shape(3, *plane),
            shape(blocks, *plane),
            shape(7, *plane),
            shape(cells, *plane),
            shape(cells, *plane),
            shape(cells, *plane),
            shape(cells, *plane),
            shape(2, *plane),
            shape(SUB, LANES),
            shape(*velocity.shape),
        ],
        in_specs=[anywhere] * 4,
        out_specs=[vmem] * 12,
        scratch_shapes=[
            pltpu.SMEM(stretch_index.shape, jnp.int32),
            pltpu.VMEM(plane, f32),
            pltpu.VMEM(plane, jnp.int32),
            pltpu.VMEM((STRETCHES,) + plane, f32),
            pltpu.SemaphoreType.DMA((3 + components,)),
        ],
        compiler_params=options(24),
        cost_estimate=cost(40_000_000, 6_000_000),
        name="ladder",
    )(in_hbm(stretch_index), in_hbm(diffusion), in_hbm(wall_types), in_hbm(velocity))

    mate = to_mate(away)
    sums, chip_coefs = pl.pallas_call(
        functools.partial(rest_kernel, chips),
        out_shape=[
            shape(half * 2 * (components - 1) * count, SUB, LANES),
            shape(chips - 1, *plane),
        ],
        in_specs=[vmem] * 5,
        out_specs=[vmem] * 2,
        compiler_params=options(16),
        cost_estimate=cost(2_000_000, 2_000_000),
        name="rest",
    )(near_velocity, left_h, right_h, held, through)
    *outgoing, near = pl.pallas_call(
        functools.partial(merge_kernel, chips, components),
        out_shape=[
            shape(half * components * count + m.bit_count(), SUB, LANES) for m in range(1, chips)
        ] + [shape(half * 2 * components * count + 1, SUB, LANES)],
        in_specs=[vmem] * 5,
        out_specs=[vmem] * chips,
        compiler_params=options(16),
        cost_estimate=cost(500_000, 1_600_000),
        name="merge",
    )(mine, sums, away, mate, pair)
    order = sorted(range(1, chips), key=lambda m: -m.bit_count())
    incoming = [send(outgoing[m - 1], lambda z, y: (z ^ (2 * m), y)) for m in order]
    profile = shape(cells, *plane)
    base, unit, goal = pl.pallas_call(
        inner_kernel,
        out_shape=[shape(*velocity.shape), profile, shape(SUB, LANES)],
        in_specs=[vmem] * 8 + [anywhere],
        out_specs=[vmem] * 3,
        compiler_params=options(16),
        cost_estimate=cost(8_000_000, 8_000_000),
        name="inner",
    )(near_velocity, left, right, left_h, right_h, ends, volume, bulk_target.reshape(1, 1),
      outgoing[0])
    rounds = plane_rounds(columns)
    own_in, other_out, *tile = pl.pallas_call(
        functools.partial(spread_kernel, order, components),
        out_shape=[shape(half * 2 * components, *sheet)] * 2
        + [shape(len(rounds) - i, SUB, LANES) for i in range(len(rounds))],
        in_specs=[vmem] * 3 + [anywhere] + [vmem] * (chips - 1),
        out_specs=[vmem] * (2 + len(rounds)),
        compiler_params=options(16),
        cost_estimate=cost(500_000, 1_600_000),
        name="spread",
    )(near, pair, chip_coefs, base, *incoming)
    other_in = to_mate(other_out)
    tiles = [tile[0]] + [
        send(array, lambda z, y: (z, targets[y])) for array, targets in zip(tile, rounds)
    ]
    partial, plain = pl.pallas_call(
        finish_kernel,
        out_shape=[shape(*velocity.shape), profile],
        in_specs=[vmem] * 5,
        out_specs=[anywhere, vmem],
        scratch_shapes=[
            pltpu.VMEM((components - 1, cells) + plane, f32),
            pltpu.SemaphoreType.DMA((row_tiles, components - 1)),
        ],
        compiler_params=options(16),
        cost_estimate=cost(3_000_000, 6_000_000),
        name="finish",
    )(own_in, other_in, base, left, right)
    return pl.pallas_call(
        functools.partial(correct_kernel, repeated(rounds)),
        out_shape=shape(*velocity.shape),
        in_specs=[vmem] * (3 + len(tiles)) + [anywhere],
        out_specs=anywhere,
        scratch_shapes=[
            pltpu.VMEM((cells,) + plane, f32),
            pltpu.SemaphoreType.DMA((row_tiles,)),
        ],
        input_output_aliases={3 + len(tiles): 0},
        compiler_params=options(16),
        cost_estimate=cost(500_000, 1_600_000),
        name="correct",
    )(goal, unit, *tiles, plain, partial)


def solution(mesh):
    return jax.shard_map(
        shards,
        mesh=mesh,
        in_specs=(P(None, "gz", "gy", None), P("gy", None), P("gy", None), P(), P()),
        out_specs=P(None, "gz", "gy", None),
        check_vma=False,
    )
```

```python
import functools

import jax
import jax.numpy as jnp
from jax import lax
from jax.experimental import pallas as pl
from jax.experimental.pallas import tpu as pltpu
from jax.sharding import PartitionSpec as P

SUB = 8
STRETCHES = 7
LANES = 128
MIB = 1024 * 1024


def plane_rounds(columns):
    if columns == 4:
        return [(2, 3, 1, 0), (3, 2, 0, 1), (1, 0, 3, 2)]
    return [[(y + shift) % columns for y in range(columns)] for shift in range(1, columns)]


def row_tile(t):
    return pl.ds(pl.multiple_of(t * SUB, SUB), SUB)


def inverted(array):
    guess = pl.reciprocal(array, approx=True)
    return guess * (2.0 - array * guess)


def put(ref, at, sheet):
    count = sheet.shape[1] // LANES
    for i in range(count):
        ref[at * count + i] = sheet[:, i * LANES:(i + 1) * LANES]


def get(ref, at, count):
    return jnp.concatenate([ref[at * count + i] for i in range(count)], axis=1)


def height(index_ref, k):
    return 0.5 + 0.25 * index_ref[k].astype(jnp.float32)


def half_sum(index_ref, k):
    return 0.5 * (height(index_ref, k) + height(index_ref, k + 1))


def ladder_kernel(
    cells, blocks, chips, lines,
    index_hbm, diffusion_hbm, walls_hbm, velocity_hbm,
    mine_ref, away_ref, pair_ref, through_ref, held_ref, left_ref, right_ref, left_h_ref, right_h_ref,
    ends_ref, volume_ref, velocity_ref,
    index_ref, diffusion_ref, walls_ref, table_ref, sems,
):
    total = cells * blocks
    components = velocity_ref.shape[0]
    row_tiles = diffusion_ref.shape[0] // SUB
    small = [
        pltpu.make_async_copy(index_hbm, index_ref, sems.at[0]),
        pltpu.make_async_copy(diffusion_hbm, diffusion_ref, sems.at[1]),
        pltpu.make_async_copy(walls_hbm, walls_ref, sems.at[2]),
    ]
    large = [
        pltpu.make_async_copy(velocity_hbm.at[c], velocity_ref.at[c], sems.at[3 + c])
        for c in range(components)
    ]
    for copy in small + large:
        copy.start()
    me = lax.axis_index("gz")
    chip = me // 2
    first = chip * 2
    for copy in small:
        copy.wait()
    diffusion = diffusion_ref[...]
    inverse = inverted(diffusion)
    for i in range(STRETCHES):
        table_ref[i] = (0.5 + 0.25 * i) * inverse
    walls = walls_ref[...]

    def wall(bits, k):
        face = 1.0 / jnp.full((SUB, diffusion.shape[1]), 0.5 * height(index_ref, k))
        return bits.astype(jnp.float32) * jnp.concatenate([face] * row_tiles, axis=0)

    lower = wall(walls & 1, 0)
    upper = wall(walls >> 1, total - 1)

    def forward(block, kappa, keep=None):
        start = block * cells
        flux = table_ref[index_ref[start]] + kappa
        value = jnp.ones_like(flux)
        for j in range(cells):
            if keep is not None:
                keep(j, flux, value)
            k = start + j
            if j < cells - 1:
                value = value + half_sum(index_ref, k) * flux
                flux = flux + table_ref[index_ref[k + 1]] * value
        k = jnp.minimum(start + cells - 1, total - 2)
        after = inverted(value + half_sum(index_ref, k) * flux)
        return flux * after, after

    def backward(block, kappa, scale=None, keep=None):
        start = block * cells
        flux = table_ref[index_ref[start + cells - 1]] + kappa
        value = jnp.ones_like(flux)
        if scale is not None:
            flux, value = flux * scale, scale
        for j in reversed(range(cells)):
            if keep is not None:
                keep(j, flux, value)
            k = start + j
            if j > 0:
                value = value + half_sum(index_ref, k - 1) * flux
                flux = flux + table_ref[index_ref[k - 1]] * value
        k = jnp.maximum(start - 1, 0)
        after = inverted(value + half_sum(index_ref, k) * flux)
        return flux * after, after

    def thickness(block):
        parts = [height(index_ref, block * cells + j) for j in range(cells)]
        return functools.reduce(jnp.add, parts)

    def sweep_forward(block, state):
        kappa, product, extent = state
        kappa, after = forward(block, kappa)
        through_ref[block] = after
        return kappa, product * after, extent + thickness(block)

    def sweep_backward(step, state):
        block = blocks - 1 - step
        kappa, product, extent = state
        kappa, after = backward(block, kappa)
        through_ref[block] = after
        return kappa, product * after, extent + thickness(block)

    ones = jnp.ones_like(diffusion)
    kappa_left, product, extent = lax.fori_loop(
        0, me, sweep_forward, (lower, ones, thickness(me))
    )
    ends_ref[0] = diffusion * lower * product
    state = {}

    def keep_left(j, flux, value):
        left_ref[j] = value
        left_h_ref[j] = height(index_ref, me * cells + j) * value
        state["flux"], state["value"] = flux, value

    _, own_forward = forward(me, kappa_left, keep_left)
    held_ref[1] = own_forward
    held_ref[3] = state["flux"]
    held_ref[4] = state["value"]
    held_ref[5] = state["flux"] - kappa_left

    kappa_right, product, extent = lax.fori_loop(
        0, blocks - 1 - me, sweep_backward, (upper, ones, extent)
    )
    ends_ref[1] = diffusion_ref[...] * upper * product
    scale = inverted(diffusion_ref[...] * (held_ref[3] + kappa_right * held_ref[4]))
    held_ref[0] = scale

    def keep_right(j, flux, value):
        right_ref[j] = value
        right_h_ref[j] = height(index_ref, me * cells + j) * value
        state["flux"] = flux

    _, own_backward = backward(me, kappa_right, scale, keep_right)
    held_ref[2] = own_backward
    held_ref[6] = state["flux"] - kappa_right * scale

    is_first = me == first
    forth, back = held_ref[1], own_backward * held_ref[0]
    pair_ref[0] = jnp.where(is_first, back, forth)
    pair_ref[1] = jnp.where(is_first, forth, through_ref[first])
    pair_ref[2] = jnp.where(is_first, through_ref[first + 1], back)

    def fold(array):
        parts = [array[:, i * LANES:(i + 1) * LANES] for i in range(array.shape[1] // LANES)]
        return functools.reduce(jnp.add, parts)

    for copy in large:
        copy.wait()
    volume_ref[...] = jnp.full(volume_ref.shape, extent * lines)
    half = row_tiles // 2
    own_extent = thickness(me)
    heights = [height(index_ref, me * cells + j) for j in range(cells)]

    def sums(ref, whose, parts):
        def of_tile(i, state):
            flow, weight = state
            rows = row_tile(whose * half + i)
            from_left = [0.0] * parts
            from_right = [0.0] * parts
            plain = 0.0
            for j in range(cells):
                left = left_h_ref[j, rows]
                right = right_h_ref[j, rows]
                for c in range(parts):
                    v = velocity_ref[c, j, rows]
                    from_left[c] = from_left[c] + left * v
                    from_right[c] = from_right[c] + right * v
                    if c == 0:
                        plain = plain + heights[j] * v
            for c in range(parts):
                at = i * 2 * parts + c
                put(ref, at, from_left[c] * held_ref[1, rows])
                put(ref, at + parts, from_right[c] * held_ref[2, rows])
            low_part = ends_ref[0, rows]
            high_part = ends_ref[1, rows] * held_ref[0, rows]
            totals = low_part * held_ref[6, rows] + high_part * held_ref[5, rows]
            return (
                flow + fold(plain - low_part * from_right[0] - high_part * from_left[0]),
                weight + fold(own_extent - diffusion_ref[rows] * totals),
            )

        return of_tile

    state = (jnp.zeros((SUB, LANES), jnp.float32),) * 2
    mates = 1 - (me - first)
    state = lax.fori_loop(0, half, sums(away_ref, mates, components), state)
    flow, weight = lax.fori_loop(0, half, sums(mine_ref, me - first, 1), state)
    for i in range(half):
        put(away_ref, half * 2 * components + i, pair_ref[0, row_tile(mates * half + i)])
    slot, middle = away_ref.shape[0] - 1, SUB // 2
    away_ref[slot, 0:middle] = flow[0:middle] + flow[middle:]
    away_ref[slot, middle:] = weight[0:middle] + weight[middle:]


def rest_kernel(
    chips, velocity_ref, left_h_ref, right_h_ref, held_ref, through_ref, sums_ref, chip_ref
):
    components, cells, _, lines_x = velocity_ref.shape
    me = lax.axis_index("gz")
    chip = me // 2
    half = sums_ref.shape[0] // (2 * (components - 1) * (lines_x // LANES))
    ones = jnp.ones(chip_ref.shape[1:], jnp.float32)
    for m in range(1, chips):
        other = chip ^ m
        low = jnp.minimum(chip, other)
        high = jnp.maximum(chip, other)
        chip_ref[m - 1] = lax.fori_loop(
            low + 1,
            high,
            lambda r, product: product * (through_ref[2 * r] * through_ref[2 * r + 1]),
            ones,
        )

    def of_tile(i, _):
        rows = row_tile((me - chip * 2) * half + i)
        from_left = [0.0] * (components - 1)
        from_right = [0.0] * (components - 1)
        for j in range(cells):
            left = left_h_ref[j, rows]
            right = right_h_ref[j, rows]
            for c in range(components - 1):
                v = velocity_ref[c + 1, j, rows]
                from_left[c] = from_left[c] + left * v
                from_right[c] = from_right[c] + right * v
        for c in range(components - 1):
            at = i * 2 * (components - 1) + c
            put(sums_ref, at, from_left[c] * held_ref[1, rows])
            put(sums_ref, at + components - 1, from_right[c] * held_ref[2, rows])
        return 0

    lax.fori_loop(0, half, of_tile, 0)


def merge_kernel(chips, components, mine_ref, sums_ref, away_ref, mate_ref, pair_ref, *rest):
    send_refs, near_ref = rest[:-1], rest[-1]
    me = lax.axis_index("gz")
    chip = me // 2
    is_first = me == chip * 2
    count = pair_ref.shape[2] // LANES
    half = mine_ref.shape[0] // (2 * count)
    slot = away_ref.shape[0] - 1
    tile = away_ref[slot] + mate_ref[slot]
    near_ref[near_ref.shape[0] - 1] = tile
    for ref in send_refs:
        for at in range(half * components * count, ref.shape[0]):
            ref[at] = tile
    for i in range(half):
        rows = row_tile((me - chip * 2) * half + i)
        mine, mate = pair_ref[0, rows], get(mate_ref, half * 2 * components + i, count)
        forth = jnp.where(is_first, mate, mine)
        back = jnp.where(is_first, mine, mate)
        for c in range(components):
            at = i * 2 * components + c
            if c == 0:
                own = [get(mine_ref, i * 2 + k, count) for k in range(2)]
            else:
                others = components - 1
                own = [
                    get(sums_ref, i * 2 * others + k * others + c - 1, count) for k in range(2)
                ]
            mine, mate = own[0], get(mate_ref, at, count)
            first = jnp.where(is_first, mine, mate)
            second = jnp.where(is_first, mate, mine)
            put(near_ref, at, first)
            to_right = second + forth * first
            at = at + components
            mine, mate = own[1], get(mate_ref, at, count)
            first = jnp.where(is_first, mine, mate)
            second = jnp.where(is_first, mate, mine)
            put(near_ref, at, second)
            to_left = first + back * second
            for m in range(1, chips):
                goes_right = (chip ^ m) > chip
                sheet = jnp.where(goes_right, to_right, to_left)
                put(send_refs[m - 1], i * components + c, sheet)


def spread_kernel(order, components, near_ref, pair_ref, chip_ref, *rest):
    recv_refs = rest[1:len(order) + 1]
    own_ref, other_ref, *tile_refs = rest[len(order) + 1:]
    me = lax.axis_index("gz")
    chip = me // 2
    is_first = me == chip * 2
    count = pair_ref.shape[2] // LANES
    half = near_ref.shape[0] // (2 * components * count)
    tiles = [ref[ref.shape[0] - 1] for ref in (near_ref, *recv_refs)]
    tile = functools.reduce(jnp.add, tiles)
    for ref in tile_refs:
        for i in range(ref.shape[0]):
            ref[i] = tile
    for i in range(half):
        rows = row_tile((me - chip * 2) * half + i)
        coefs = [chip_ref[m - 1, rows] for m in order]
        for c in range(components):
            left_in = jnp.zeros(own_ref.shape[1:], jnp.float32)
            right_in = jnp.zeros(own_ref.shape[1:], jnp.float32)
            for m, coef, ref in zip(order, coefs, recv_refs):
                term = coef * get(ref, i * components + c, count)
                from_left = (chip ^ m) < chip
                left_in = left_in + jnp.where(from_left, term, 0.0)
                right_in = right_in + jnp.where(from_left, 0.0, term)
            at = i * 2 * components + c
            left_second = get(near_ref, at, count) + pair_ref[1, rows] * left_in
            right_first = get(near_ref, at + components, count) + pair_ref[2, rows] * right_in
            own_ref[at] = jnp.where(is_first, left_in, left_second)
            other_ref[at] = jnp.where(is_first, left_second, left_in)
            at = at + components
            own_ref[at] = jnp.where(is_first, right_first, right_in)
            other_ref[at] = jnp.where(is_first, right_in, right_first)


def inner_kernel(
    velocity_ref, left_ref, right_ref, left_h_ref, right_h_ref, ends_ref, volume_ref, target_ref,
    _, base_ref, unit_ref, goal_ref,
):
    components, cells, lines_y, lines_x = velocity_ref.shape
    goal_ref[...] = target_ref[...] * volume_ref[...]

    def of_tile(t, _):
        rows = row_tile(t)
        gathered = [jnp.zeros((SUB, lines_x), jnp.float32)] * components
        for j in reversed(range(cells)):
            left = left_ref[j, rows]
            right = right_h_ref[j, rows]
            for c in range(components):
                base_ref[c, j, rows] = left * gathered[c]
                if j > 0:
                    gathered[c] = gathered[c] + right * velocity_ref[c, j, rows]
        gathered = [jnp.zeros((SUB, lines_x), jnp.float32)] * components
        low_part = ends_ref[0, rows]
        high_part = ends_ref[1, rows] * right_ref[cells - 1, rows]
        for j in range(cells):
            left = left_h_ref[j, rows]
            right = right_ref[j, rows]
            unit_ref[j, rows] = 1.0 - (low_part * right + high_part * left_ref[j, rows])
            for c in range(components):
                gathered[c] = gathered[c] + left * velocity_ref[c, j, rows]
                base_ref[c, j, rows] = base_ref[c, j, rows] + right * gathered[c]
        return 0

    lax.fori_loop(0, lines_y // SUB, of_tile, 0)


def finish_kernel(
    own_ref, other_ref, base_ref, left_ref, right_ref, out_hbm, plain_ref, result_ref, sems
):
    components, cells, lines_y, _ = base_ref.shape
    half = own_ref.shape[0] // (2 * components)
    me = lax.axis_index("gz")

    def copies(t):
        rows = row_tile(t)
        return [
            pltpu.make_async_copy(
                result_ref.at[c - 1, :, rows], out_hbm.at[c, :, rows], sems.at[t, c - 1])
            for c in range(1, components)
        ]

    def half_of(incoming_ref, side):
        def of_tile(i, _):
            t = lax.rem(me + side, 2) * half + i
            rows = row_tile(t)
            scale = right_ref[cells - 1, rows]
            at = i * 2 * components
            lefts = [incoming_ref[at + c] for c in range(components)]
            rights = [incoming_ref[at + components + c] * scale for c in range(components)]
            for j in range(cells):
                left = left_ref[j, rows]
                right = right_ref[j, rows]
                for c in range(components):
                    value = base_ref[c, j, rows] + (right * lefts[c] + left * rights[c])
                    if c == 0:
                        plain_ref[j, rows] = value
                    else:
                        result_ref[c - 1, j, rows] = value
            for copy in copies(t):
                copy.start()
            return 0

        lax.fori_loop(0, half, of_tile, 0)

    half_of(own_ref, 0)
    half_of(other_ref, 1)
    for t in range(lines_y // SUB):
        for copy in copies(t):
            copy.wait()


def correct_kernel(count, goal_ref, unit_ref, *rest):
    tile_refs = rest[:count]
    plain_ref, _, out_hbm, result_ref, sems = rest[count:]
    totals = functools.reduce(jnp.add, [ref[0] for ref in tile_refs])
    flow = jnp.sum(totals[0:SUB // 2], keepdims=True)
    weight = jnp.sum(totals[SUB // 2:], keepdims=True)
    alpha = (goal_ref[0:1, 0:1] - flow) / weight
    cells, lines_y, _ = plain_ref.shape

    def copy(t):
        rows = row_tile(t)
        return pltpu.make_async_copy(result_ref.at[:, rows], out_hbm.at[0, :, rows], sems.at[t])

    def of_tile(t, _):
        rows = row_tile(t)
        for j in range(cells):
            result_ref[j, rows] = plain_ref[j, rows] + alpha * unit_ref[j, rows]
        copy(t).start()
        return 0

    lax.fori_loop(0, lines_y // SUB, of_tile, 0)
    for t in range(lines_y // SUB):
        copy(t).wait()


def shards(velocity, diffusion, wall_types, stretch_index, bulk_target):
    blocks = lax.axis_size("gz")
    columns = lax.axis_size("gy")
    components, cells, lines_y, lines_x = velocity.shape
    chips = blocks // 2
    row_tiles = lines_y // SUB
    half = row_tiles // 2
    f32 = jnp.float32
    vmem = pl.BlockSpec(memory_space=pltpu.VMEM)
    anywhere = pl.BlockSpec(memory_space=pl.ANY)
    plane = (lines_y, lines_x)
    sheet = (SUB, lines_x)

    def shape(*dims):
        return jax.ShapeDtypeStruct(dims, f32)

    def in_hbm(array):
        return pltpu.with_memory_space_constraint(array, pltpu.HBM)

    def options(mib):
        return pltpu.CompilerParams(vmem_limit_bytes=mib * MIB)

    def cost(flops, transferred):
        return pl.CostEstimate(flops=flops, bytes_accessed=transferred, transcendentals=0)

    def send(array, partner):
        pairs = [((z, y), partner(z, y)) for z in range(blocks) for y in range(columns)]
        route = [(a * columns + b, c * columns + d) for (a, b), (c, d) in pairs]
        return lax.ppermute(array, ("gz", "gy"), route)

    def to_mate(array):
        return send(array, lambda z, y: (z ^ 1, y))

    count = lines_x // LANES
    lines = float(lines_y * columns * lines_x)
    (mine, away, pair, through, held, left, right, left_h, right_h, ends, volume,
     near_velocity) = pl.pallas_call(
        functools.partial(ladder_kernel, cells, blocks, chips, lines),
        out_shape=[
            shape(half * 2 * count, SUB, LANES),
            shape(half * (2 * components + 1) * count + 1, SUB, LANES),
            shape(3, *plane),
            shape(blocks, *plane),
            shape(7, *plane),
            shape(cells, *plane),
            shape(cells, *plane),
            shape(cells, *plane),
            shape(cells, *plane),
            shape(2, *plane),
            shape(SUB, LANES),
            shape(*velocity.shape),
        ],
        in_specs=[anywhere] * 4,
        out_specs=[vmem] * 12,
        scratch_shapes=[
            pltpu.SMEM(stretch_index.shape, jnp.int32),
            pltpu.VMEM(plane, f32),
            pltpu.VMEM(plane, jnp.int32),
            pltpu.VMEM((STRETCHES,) + plane, f32),
            pltpu.SemaphoreType.DMA((3 + components,)),
        ],
        compiler_params=options(24),
        cost_estimate=cost(40_000_000, 6_000_000),
        name="ladder",
    )(in_hbm(stretch_index), in_hbm(diffusion), in_hbm(wall_types), in_hbm(velocity))

    mate = to_mate(away)
    sums, chip_coefs = pl.pallas_call(
        functools.partial(rest_kernel, chips),
        out_shape=[
            shape(half * 2 * (components - 1) * count, SUB, LANES),
            shape(chips - 1, *plane),
        ],
        in_specs=[vmem] * 5,
        out_specs=[vmem] * 2,
        compiler_params=options(16),
        cost_estimate=cost(2_000_000, 2_000_000),
        name="rest",
    )(near_velocity, left_h, right_h, held, through)
    *outgoing, near = pl.pallas_call(
        functools.partial(merge_kernel, chips, components),
        out_shape=[
            shape(half * components * count + m.bit_count(), SUB, LANES) for m in range(1, chips)
        ] + [shape(half * 2 * components * count + 1, SUB, LANES)],
        in_specs=[vmem] * 5,
        out_specs=[vmem] * chips,
        compiler_params=options(16),
        cost_estimate=cost(500_000, 1_600_000),
        name="merge",
    )(mine, sums, away, mate, pair)
    order = sorted(range(1, chips), key=lambda m: -m.bit_count())
    incoming = [send(outgoing[m - 1], lambda z, y: (z ^ (2 * m), y)) for m in order]
    profile = shape(cells, *plane)
    base, unit, goal = pl.pallas_call(
        inner_kernel,
        out_shape=[shape(*velocity.shape), profile, shape(SUB, LANES)],
        in_specs=[vmem] * 8 + [anywhere],
        out_specs=[vmem] * 3,
        compiler_params=options(16),
        cost_estimate=cost(8_000_000, 8_000_000),
        name="inner",
    )(near_velocity, left, right, left_h, right_h, ends, volume, bulk_target.reshape(1, 1),
      outgoing[0])
    rounds = plane_rounds(columns)
    own_in, other_out, *tile = pl.pallas_call(
        functools.partial(spread_kernel, order, components),
        out_shape=[shape(half * 2 * components, *sheet)] * 2
        + [shape(len(rounds) - i, SUB, LANES) for i in range(len(rounds))],
        in_specs=[vmem] * 3 + [anywhere] + [vmem] * (chips - 1),
        out_specs=[vmem] * (2 + len(rounds)),
        compiler_params=options(16),
        cost_estimate=cost(500_000, 1_600_000),
        name="spread",
    )(near, pair, chip_coefs, base, *incoming)
    other_in = to_mate(other_out)
    tiles = [tile[0]] + [
        send(array, lambda z, y: (z, targets[y])) for array, targets in zip(tile, rounds)
    ]
    partial, plain = pl.pallas_call(
        finish_kernel,
        out_shape=[shape(*velocity.shape), profile],
        in_specs=[vmem] * 5,
        out_specs=[anywhere, vmem],
        scratch_shapes=[
            pltpu.VMEM((components - 1, cells) + plane, f32),
            pltpu.SemaphoreType.DMA((row_tiles, components - 1)),
        ],
        compiler_params=options(16),
        cost_estimate=cost(3_000_000, 6_000_000),
        name="finish",
    )(own_in, other_in, base, left, right)
    return pl.pallas_call(
        functools.partial(correct_kernel, len(tiles)),
        out_shape=shape(*velocity.shape),
        in_specs=[vmem] * (3 + len(tiles)) + [anywhere],
        out_specs=anywhere,
        scratch_shapes=[
            pltpu.VMEM((cells,) + plane, f32),
            pltpu.SemaphoreType.DMA((row_tiles,)),
        ],
        input_output_aliases={3 + len(tiles): 0},
        compiler_params=options(16),
        cost_estimate=cost(500_000, 1_600_000),
        name="correct",
    )(goal, unit, *tiles, plain, partial)


def solution(mesh):
    return jax.shard_map(
        shards,
        mesh=mesh,
        in_specs=(P(None, "gz", "gy", None), P("gy", None), P("gy", None), P(), P()),
        out_specs=P(None, "gz", "gy", None),
        check_vma=False,
    )
```

```python
import functools

import jax
import jax.numpy as jnp
from jax import lax
from jax.experimental import pallas as pl
from jax.experimental.pallas import tpu as pltpu
from jax.sharding import PartitionSpec as P

SUB = 8
STRETCHES = 7
LANES = 128
MIB = 1024 * 1024


def extra(m):
    return 2 if m % 2 == 0 else int(m > 1)


def plane_rounds(columns):
    if columns == 4:
        return [(2, 3, 1, 0), (3, 2, 0, 1), (1, 0, 3, 2)]
    return [[(y + shift) % columns for y in range(columns)] for shift in range(1, columns)]


def row_tile(t):
    return pl.ds(pl.multiple_of(t * SUB, SUB), SUB)


def inverted(array):
    guess = pl.reciprocal(array, approx=True)
    return guess * (2.0 - array * guess)


def put(ref, at, sheet):
    count = sheet.shape[1] // LANES
    for i in range(count):
        ref[at * count + i] = sheet[:, i * LANES:(i + 1) * LANES]


def get(ref, at, count):
    return jnp.concatenate([ref[at * count + i] for i in range(count)], axis=1)


def height(index_ref, k):
    return 0.5 + 0.25 * index_ref[k].astype(jnp.float32)


def half_sum(index_ref, k):
    return 0.5 * (height(index_ref, k) + height(index_ref, k + 1))


def ladder_kernel(
    cells, blocks, chips, lines,
    index_hbm, diffusion_hbm, walls_hbm, velocity_hbm,
    mine_ref, away_ref, pair_ref, through_ref, held_ref, left_ref, right_ref, left_h_ref, right_h_ref,
    ends_ref, volume_ref, velocity_ref,
    index_ref, diffusion_ref, walls_ref, table_ref, sems,
):
    total = cells * blocks
    components = velocity_ref.shape[0]
    row_tiles = diffusion_ref.shape[0] // SUB
    small = [
        pltpu.make_async_copy(index_hbm, index_ref, sems.at[0]),
        pltpu.make_async_copy(diffusion_hbm, diffusion_ref, sems.at[1]),
        pltpu.make_async_copy(walls_hbm, walls_ref, sems.at[2]),
    ]
    large = [
        pltpu.make_async_copy(velocity_hbm.at[c], velocity_ref.at[c], sems.at[3 + c])
        for c in range(components)
    ]
    for copy in small + large:
        copy.start()
    me = lax.axis_index("gz")
    chip = me // 2
    first = chip * 2
    for copy in small:
        copy.wait()
    diffusion = diffusion_ref[...]
    inverse = inverted(diffusion)
    for i in range(STRETCHES):
        table_ref[i] = (0.5 + 0.25 * i) * inverse
    walls = walls_ref[...]

    def wall(bits, k):
        face = 1.0 / jnp.full((SUB, diffusion.shape[1]), 0.5 * height(index_ref, k))
        return bits.astype(jnp.float32) * jnp.concatenate([face] * row_tiles, axis=0)

    lower = wall(walls & 1, 0)
    upper = wall(walls >> 1, total - 1)

    def forward(block, kappa, keep=None):
        start = block * cells
        flux = table_ref[index_ref[start]] + kappa
        value = jnp.ones_like(flux)
        for j in range(cells):
            if keep is not None:
                keep(j, flux, value)
            k = start + j
            if j < cells - 1:
                value = value + half_sum(index_ref, k) * flux
                flux = flux + table_ref[index_ref[k + 1]] * value
        k = jnp.minimum(start + cells - 1, total - 2)
        after = inverted(value + half_sum(index_ref, k) * flux)
        return flux * after, after

    def backward(block, kappa, scale=None, keep=None):
        start = block * cells
        flux = table_ref[index_ref[start + cells - 1]] + kappa
        value = jnp.ones_like(flux)
        if scale is not None:
            flux, value = flux * scale, scale
        for j in reversed(range(cells)):
            if keep is not None:
                keep(j, flux, value)
            k = start + j
            if j > 0:
                value = value + half_sum(index_ref, k - 1) * flux
                flux = flux + table_ref[index_ref[k - 1]] * value
        k = jnp.maximum(start - 1, 0)
        after = inverted(value + half_sum(index_ref, k) * flux)
        return flux * after, after

    def thickness(block):
        parts = [height(index_ref, block * cells + j) for j in range(cells)]
        return functools.reduce(jnp.add, parts)

    def sweep_forward(block, state):
        kappa, product, extent = state
        kappa, after = forward(block, kappa)
        through_ref[block] = after
        return kappa, product * after, extent + thickness(block)

    def sweep_backward(step, state):
        block = blocks - 1 - step
        kappa, product, extent = state
        kappa, after = backward(block, kappa)
        through_ref[block] = after
        return kappa, product * after, extent + thickness(block)

    ones = jnp.ones_like(diffusion)
    kappa_left, product, extent = lax.fori_loop(
        0, me, sweep_forward, (lower, ones, thickness(me))
    )
    ends_ref[0] = diffusion * lower * product
    state = {}

    def keep_left(j, flux, value):
        left_ref[j] = value
        left_h_ref[j] = height(index_ref, me * cells + j) * value
        state["flux"], state["value"] = flux, value

    _, own_forward = forward(me, kappa_left, keep_left)
    held_ref[1] = own_forward
    held_ref[3] = state["flux"]
    held_ref[4] = state["value"]
    held_ref[5] = state["flux"] - kappa_left

    kappa_right, product, extent = lax.fori_loop(
        0, blocks - 1 - me, sweep_backward, (upper, ones, extent)
    )
    ends_ref[1] = diffusion_ref[...] * upper * product
    scale = inverted(diffusion_ref[...] * (held_ref[3] + kappa_right * held_ref[4]))
    held_ref[0] = scale

    def keep_right(j, flux, value):
        right_ref[j] = value
        right_h_ref[j] = height(index_ref, me * cells + j) * value
        state["flux"] = flux

    _, own_backward = backward(me, kappa_right, scale, keep_right)
    held_ref[2] = own_backward
    held_ref[6] = state["flux"] - kappa_right * scale

    is_first = me == first
    forth, back = held_ref[1], own_backward * held_ref[0]
    pair_ref[0] = jnp.where(is_first, back, forth)
    pair_ref[1] = jnp.where(is_first, forth, through_ref[first])
    pair_ref[2] = jnp.where(is_first, through_ref[first + 1], back)

    def fold(array):
        parts = [array[:, i * LANES:(i + 1) * LANES] for i in range(array.shape[1] // LANES)]
        return functools.reduce(jnp.add, parts)

    for copy in large:
        copy.wait()
    volume_ref[...] = jnp.full(volume_ref.shape, extent * lines)
    half = row_tiles // 2
    own_extent = thickness(me)
    heights = [height(index_ref, me * cells + j) for j in range(cells)]

    def sums(ref, whose, parts):
        def of_tile(i, state):
            flow, weight = state
            rows = row_tile(whose * half + i)
            from_left = [0.0] * parts
            from_right = [0.0] * parts
            plain = 0.0
            for j in range(cells):
                left = left_h_ref[j, rows]
                right = right_h_ref[j, rows]
                for c in range(parts):
                    v = velocity_ref[c, j, rows]
                    from_left[c] = from_left[c] + left * v
                    from_right[c] = from_right[c] + right * v
                    if c == 0:
                        plain = plain + heights[j] * v
            for c in range(parts):
                at = i * 2 * parts + c
                put(ref, at, from_left[c] * held_ref[1, rows])
                put(ref, at + parts, from_right[c] * held_ref[2, rows])
            low_part = ends_ref[0, rows]
            high_part = ends_ref[1, rows] * held_ref[0, rows]
            totals = low_part * held_ref[6, rows] + high_part * held_ref[5, rows]
            return (
                flow + fold(plain - low_part * from_right[0] - high_part * from_left[0]),
                weight + fold(own_extent - diffusion_ref[rows] * totals),
            )

        return of_tile

    state = (jnp.zeros((SUB, LANES), jnp.float32),) * 2
    mates = 1 - (me - first)
    state = lax.fori_loop(0, half, sums(away_ref, mates, components), state)
    flow, weight = lax.fori_loop(0, half, sums(mine_ref, me - first, 1), state)
    for i in range(half):
        put(away_ref, half * 2 * components + i, pair_ref[0, row_tile(mates * half + i)])
    slot, middle = away_ref.shape[0] - 1, SUB // 2
    away_ref[slot, 0:middle] = flow[0:middle] + flow[middle:]
    away_ref[slot, middle:] = weight[0:middle] + weight[middle:]


def rest_kernel(
    chips, velocity_ref, left_h_ref, right_h_ref, held_ref, through_ref, sums_ref, chip_ref
):
    components, cells, _, lines_x = velocity_ref.shape
    me = lax.axis_index("gz")
    chip = me // 2
    half = sums_ref.shape[0] // (2 * (components - 1) * (lines_x // LANES))
    ones = jnp.ones(chip_ref.shape[1:], jnp.float32)
    for m in range(1, chips):
        other = chip ^ m
        low = jnp.minimum(chip, other)
        high = jnp.maximum(chip, other)
        chip_ref[m - 1] = lax.fori_loop(
            low + 1,
            high,
            lambda r, product: product * (through_ref[2 * r] * through_ref[2 * r + 1]),
            ones,
        )

    def of_tile(i, _):
        rows = row_tile((me - chip * 2) * half + i)
        from_left = [0.0] * (components - 1)
        from_right = [0.0] * (components - 1)
        for j in range(cells):
            left = left_h_ref[j, rows]
            right = right_h_ref[j, rows]
            for c in range(components - 1):
                v = velocity_ref[c + 1, j, rows]
                from_left[c] = from_left[c] + left * v
                from_right[c] = from_right[c] + right * v
        for c in range(components - 1):
            at = i * 2 * (components - 1) + c
            put(sums_ref, at, from_left[c] * held_ref[1, rows])
            put(sums_ref, at + components - 1, from_right[c] * held_ref[2, rows])
        return 0

    lax.fori_loop(0, half, of_tile, 0)


def merge_kernel(chips, components, mine_ref, sums_ref, away_ref, mate_ref, pair_ref, *rest):
    send_refs, near_ref = rest[:-1], rest[-1]
    me = lax.axis_index("gz")
    chip = me // 2
    is_first = me == chip * 2
    count = pair_ref.shape[2] // LANES
    half = mine_ref.shape[0] // (2 * count)
    slot = away_ref.shape[0] - 1
    tile = away_ref[slot] + mate_ref[slot]
    near_ref[near_ref.shape[0] - 1] = tile
    for ref in send_refs:
        for at in range(half * components * count, ref.shape[0]):
            ref[at] = tile
    for i in range(half):
        rows = row_tile((me - chip * 2) * half + i)
        mine, mate = pair_ref[0, rows], get(mate_ref, half * 2 * components + i, count)
        forth = jnp.where(is_first, mate, mine)
        back = jnp.where(is_first, mine, mate)
        for c in range(components):
            at = i * 2 * components + c
            if c == 0:
                own = [get(mine_ref, i * 2 + k, count) for k in range(2)]
            else:
                others = components - 1
                own = [
                    get(sums_ref, i * 2 * others + k * others + c - 1, count) for k in range(2)
                ]
            mine, mate = own[0], get(mate_ref, at, count)
            first = jnp.where(is_first, mine, mate)
            second = jnp.where(is_first, mate, mine)
            put(near_ref, at, first)
            to_right = second + forth * first
            at = at + components
            mine, mate = own[1], get(mate_ref, at, count)
            first = jnp.where(is_first, mine, mate)
            second = jnp.where(is_first, mate, mine)
            put(near_ref, at, second)
            to_left = first + back * second
            for m in range(1, chips):
                goes_right = (chip ^ m) > chip
                sheet = jnp.where(goes_right, to_right, to_left)
                put(send_refs[m - 1], i * components + c, sheet)


def spread_kernel(order, components, near_ref, pair_ref, chip_ref, *rest):
    recv_refs = rest[1:len(order) + 1]
    own_ref, other_ref, *tile_refs = rest[len(order) + 1:]
    me = lax.axis_index("gz")
    chip = me // 2
    is_first = me == chip * 2
    count = pair_ref.shape[2] // LANES
    half = near_ref.shape[0] // (2 * components * count)
    tiles = [ref[ref.shape[0] - 1] for ref in (near_ref, *recv_refs)]
    tile = functools.reduce(jnp.add, tiles)
    for ref in tile_refs:
        for i in range(ref.shape[0]):
            ref[i] = tile
    for i in range(half):
        rows = row_tile((me - chip * 2) * half + i)
        coefs = [chip_ref[m - 1, rows] for m in order]
        for c in range(components):
            left_in = jnp.zeros(own_ref.shape[1:], jnp.float32)
            right_in = jnp.zeros(own_ref.shape[1:], jnp.float32)
            for m, coef, ref in zip(order, coefs, recv_refs):
                term = coef * get(ref, i * components + c, count)
                from_left = (chip ^ m) < chip
                left_in = left_in + jnp.where(from_left, term, 0.0)
                right_in = right_in + jnp.where(from_left, 0.0, term)
            at = i * 2 * components + c
            left_second = get(near_ref, at, count) + pair_ref[1, rows] * left_in
            right_first = get(near_ref, at + components, count) + pair_ref[2, rows] * right_in
            own_ref[at] = jnp.where(is_first, left_in, left_second)
            other_ref[at] = jnp.where(is_first, left_second, left_in)
            at = at + components
            own_ref[at] = jnp.where(is_first, right_first, right_in)
            other_ref[at] = jnp.where(is_first, right_in, right_first)


def inner_kernel(
    velocity_ref, left_ref, right_ref, left_h_ref, right_h_ref, ends_ref, volume_ref, target_ref,
    _, base_ref, unit_ref, goal_ref,
):
    components, cells, lines_y, lines_x = velocity_ref.shape
    goal_ref[...] = target_ref[...] * volume_ref[...]

    def of_tile(t, _):
        rows = row_tile(t)
        gathered = [jnp.zeros((SUB, lines_x), jnp.float32)] * components
        for j in reversed(range(cells)):
            left = left_ref[j, rows]
            right = right_h_ref[j, rows]
            for c in range(components):
                base_ref[c, j, rows] = left * gathered[c]
                if j > 0:
                    gathered[c] = gathered[c] + right * velocity_ref[c, j, rows]
        gathered = [jnp.zeros((SUB, lines_x), jnp.float32)] * components
        low_part = ends_ref[0, rows]
        high_part = ends_ref[1, rows] * right_ref[cells - 1, rows]
        for j in range(cells):
            left = left_h_ref[j, rows]
            right = right_ref[j, rows]
            unit_ref[j, rows] = 1.0 - (low_part * right + high_part * left_ref[j, rows])
            for c in range(components):
                gathered[c] = gathered[c] + left * velocity_ref[c, j, rows]
                base_ref[c, j, rows] = base_ref[c, j, rows] + right * gathered[c]
        return 0

    lax.fori_loop(0, lines_y // SUB, of_tile, 0)


def finish_kernel(
    own_ref, other_ref, base_ref, left_ref, right_ref, out_hbm, plain_ref, result_ref, sems
):
    components, cells, lines_y, _ = base_ref.shape
    half = own_ref.shape[0] // (2 * components)
    me = lax.axis_index("gz")

    def copies(t):
        rows = row_tile(t)
        return [
            pltpu.make_async_copy(
                result_ref.at[c - 1, :, rows], out_hbm.at[c, :, rows], sems.at[t, c - 1])
            for c in range(1, components)
        ]

    def half_of(incoming_ref, side):
        def of_tile(i, _):
            t = lax.rem(me + side, 2) * half + i
            rows = row_tile(t)
            scale = right_ref[cells - 1, rows]
            at = i * 2 * components
            lefts = [incoming_ref[at + c] for c in range(components)]
            rights = [incoming_ref[at + components + c] * scale for c in range(components)]
            for j in range(cells):
                left = left_ref[j, rows]
                right = right_ref[j, rows]
                for c in range(components):
                    value = base_ref[c, j, rows] + (right * lefts[c] + left * rights[c])
                    if c == 0:
                        plain_ref[j, rows] = value
                    else:
                        result_ref[c - 1, j, rows] = value
            for copy in copies(t):
                copy.start()
            return 0

        lax.fori_loop(0, half, of_tile, 0)

    half_of(own_ref, 0)
    half_of(other_ref, 1)
    for t in range(lines_y // SUB):
        for copy in copies(t):
            copy.wait()


def correct_kernel(count, goal_ref, unit_ref, *rest):
    tile_refs = rest[:count]
    plain_ref, _, out_hbm, result_ref, sems = rest[count:]
    totals = functools.reduce(jnp.add, [ref[0] for ref in tile_refs])
    flow = jnp.sum(totals[0:SUB // 2], keepdims=True)
    weight = jnp.sum(totals[SUB // 2:], keepdims=True)
    alpha = (goal_ref[0:1, 0:1] - flow) / weight
    cells, lines_y, _ = plain_ref.shape

    def copy(t):
        rows = row_tile(t)
        return pltpu.make_async_copy(result_ref.at[:, rows], out_hbm.at[0, :, rows], sems.at[t])

    def of_tile(t, _):
        rows = row_tile(t)
        for j in range(cells):
            result_ref[j, rows] = plain_ref[j, rows] + alpha * unit_ref[j, rows]
        copy(t).start()
        return 0

    lax.fori_loop(0, lines_y // SUB, of_tile, 0)
    for t in range(lines_y // SUB):
        copy(t).wait()


def shards(velocity, diffusion, wall_types, stretch_index, bulk_target):
    blocks = lax.axis_size("gz")
    columns = lax.axis_size("gy")
    components, cells, lines_y, lines_x = velocity.shape
    chips = blocks // 2
    row_tiles = lines_y // SUB
    half = row_tiles // 2
    f32 = jnp.float32
    vmem = pl.BlockSpec(memory_space=pltpu.VMEM)
    anywhere = pl.BlockSpec(memory_space=pl.ANY)
    plane = (lines_y, lines_x)
    sheet = (SUB, lines_x)

    def shape(*dims):
        return jax.ShapeDtypeStruct(dims, f32)

    def in_hbm(array):
        return pltpu.with_memory_space_constraint(array, pltpu.HBM)

    def options(mib):
        return pltpu.CompilerParams(vmem_limit_bytes=mib * MIB)

    def cost(flops, transferred):
        return pl.CostEstimate(flops=flops, bytes_accessed=transferred, transcendentals=0)

    def send(array, partner):
        pairs = [((z, y), partner(z, y)) for z in range(blocks) for y in range(columns)]
        route = [(a * columns + b, c * columns + d) for (a, b), (c, d) in pairs]
        return lax.ppermute(array, ("gz", "gy"), route)

    def to_mate(array):
        return send(array, lambda z, y: (z ^ 1, y))

    count = lines_x // LANES
    lines = float(lines_y * columns * lines_x)
    (mine, away, pair, through, held, left, right, left_h, right_h, ends, volume,
     near_velocity) = pl.pallas_call(
        functools.partial(ladder_kernel, cells, blocks, chips, lines),
        out_shape=[
            shape(half * 2 * count, SUB, LANES),
            shape(half * (2 * components + 1) * count + 1, SUB, LANES),
            shape(3, *plane),
            shape(blocks, *plane),
            shape(7, *plane),
            shape(cells, *plane),
            shape(cells, *plane),
            shape(cells, *plane),
            shape(cells, *plane),
            shape(2, *plane),
            shape(SUB, LANES),
            shape(*velocity.shape),
        ],
        in_specs=[anywhere] * 4,
        out_specs=[vmem] * 12,
        scratch_shapes=[
            pltpu.SMEM(stretch_index.shape, jnp.int32),
            pltpu.VMEM(plane, f32),
            pltpu.VMEM(plane, jnp.int32),
            pltpu.VMEM((STRETCHES,) + plane, f32),
            pltpu.SemaphoreType.DMA((3 + components,)),
        ],
        compiler_params=options(24),
        cost_estimate=cost(40_000_000, 6_000_000),
        name="ladder",
    )(in_hbm(stretch_index), in_hbm(diffusion), in_hbm(wall_types), in_hbm(velocity))

    mate = to_mate(away)
    sums, chip_coefs = pl.pallas_call(
        functools.partial(rest_kernel, chips),
        out_shape=[
            shape(half * 2 * (components - 1) * count, SUB, LANES),
            shape(chips - 1, *plane),
        ],
        in_specs=[vmem] * 5,
        out_specs=[vmem] * 2,
        compiler_params=options(16),
        cost_estimate=cost(2_000_000, 2_000_000),
        name="rest",
    )(near_velocity, left_h, right_h, held, through)
    *outgoing, near = pl.pallas_call(
        functools.partial(merge_kernel, chips, components),
        out_shape=[
            shape(half * components * count + 1 + extra(m), SUB, LANES) for m in range(1, chips)
        ] + [shape(half * 2 * components * count + 1, SUB, LANES)],
        in_specs=[vmem] * 5,
        out_specs=[vmem] * chips,
        compiler_params=options(16),
        cost_estimate=cost(500_000, 1_600_000),
        name="merge",
    )(mine, sums, away, mate, pair)
    order = sorted(range(1, chips), key=extra, reverse=True)
    incoming = [send(outgoing[m - 1], lambda z, y: (z ^ (2 * m), y)) for m in order]
    profile = shape(cells, *plane)
    base, unit, goal = pl.pallas_call(
        inner_kernel,
        out_shape=[shape(*velocity.shape), profile, shape(SUB, LANES)],
        in_specs=[vmem] * 8 + [anywhere],
        out_specs=[vmem] * 3,
        compiler_params=options(16),
        cost_estimate=cost(8_000_000, 8_000_000),
        name="inner",
    )(near_velocity, left, right, left_h, right_h, ends, volume, bulk_target.reshape(1, 1),
      outgoing[0])
    rounds = plane_rounds(columns)
    own_in, other_out, *tile = pl.pallas_call(
        functools.partial(spread_kernel, order, components),
        out_shape=[shape(half * 2 * components, *sheet)] * 2
        + [shape(len(rounds) - i, SUB, LANES) for i in range(len(rounds))],
        in_specs=[vmem] * 3 + [anywhere] + [vmem] * (chips - 1),
        out_specs=[vmem] * (2 + len(rounds)),
        compiler_params=options(16),
        cost_estimate=cost(500_000, 1_600_000),
        name="spread",
    )(near, pair, chip_coefs, base, *incoming)
    other_in = to_mate(other_out)
    tiles = [tile[0]] + [
        send(array, lambda z, y: (z, targets[y])) for array, targets in zip(tile, rounds)
    ]
    partial, plain = pl.pallas_call(
        finish_kernel,
        out_shape=[shape(*velocity.shape), profile],
        in_specs=[vmem] * 5,
        out_specs=[anywhere, vmem],
        scratch_shapes=[
            pltpu.VMEM((components - 1, cells) + plane, f32),
            pltpu.SemaphoreType.DMA((row_tiles, components - 1)),
        ],
        compiler_params=options(16),
        cost_estimate=cost(3_000_000, 6_000_000),
        name="finish",
    )(own_in, other_in, base, left, right)
    return pl.pallas_call(
        functools.partial(correct_kernel, len(tiles)),
        out_shape=shape(*velocity.shape),
        in_specs=[vmem] * (3 + len(tiles)) + [anywhere],
        out_specs=anywhere,
        scratch_shapes=[
            pltpu.VMEM((cells,) + plane, f32),
            pltpu.SemaphoreType.DMA((row_tiles,)),
        ],
        input_output_aliases={3 + len(tiles): 0},
        compiler_params=options(16),
        cost_estimate=cost(500_000, 1_600_000),
        name="correct",
    )(goal, unit, *tiles, plain, partial)


def solution(mesh):
    return jax.shard_map(
        shards,
        mesh=mesh,
        in_specs=(P(None, "gz", "gy", None), P("gy", None), P("gy", None), P(), P()),
        out_specs=P(None, "gz", "gy", None),
        check_vma=False,
    )
```

```python
import functools

import jax
import jax.numpy as jnp
from jax import lax
from jax.experimental import pallas as pl
from jax.experimental.pallas import tpu as pltpu
from jax.sharding import PartitionSpec as P

SUB = 8
STRETCHES = 7
LANES = 128
MIB = 1024 * 1024


def plane_rounds(columns):
    if columns == 4:
        return [(2, 3, 1, 0), (3, 2, 0, 1), (1, 0, 3, 2)]
    return [[(y + shift) % columns for y in range(columns)] for shift in range(1, columns)]


def row_tile(t):
    return pl.ds(pl.multiple_of(t * SUB, SUB), SUB)


def inverted(array):
    guess = pl.reciprocal(array, approx=True)
    return guess * (2.0 - array * guess)


def put(ref, at, sheet):
    count = sheet.shape[1] // LANES
    for i in range(count):
        ref[at * count + i] = sheet[:, i * LANES:(i + 1) * LANES]


def get(ref, at, count):
    return jnp.concatenate([ref[at * count + i] for i in range(count)], axis=1)


def height(index_ref, k):
    return 0.5 + 0.25 * index_ref[k].astype(jnp.float32)


def half_sum(index_ref, k):
    return 0.5 * (height(index_ref, k) + height(index_ref, k + 1))


def ladder_kernel(
    cells, blocks, chips, lines,
    index_hbm, diffusion_hbm, walls_hbm, velocity_hbm,
    mine_ref, away_ref, pair_ref, through_ref, held_ref, left_ref, right_ref, left_h_ref, right_h_ref,
    ends_ref, volume_ref, velocity_ref,
    index_ref, diffusion_ref, walls_ref, table_ref, sems,
):
    total = cells * blocks
    components = velocity_ref.shape[0]
    row_tiles = diffusion_ref.shape[0] // SUB
    small = [
        pltpu.make_async_copy(index_hbm, index_ref, sems.at[0]),
        pltpu.make_async_copy(diffusion_hbm, diffusion_ref, sems.at[1]),
        pltpu.make_async_copy(walls_hbm, walls_ref, sems.at[2]),
    ]
    large = [
        pltpu.make_async_copy(velocity_hbm.at[c], velocity_ref.at[c], sems.at[3 + c])
        for c in range(components)
    ]
    for copy in small + large:
        copy.start()
    me = lax.axis_index("gz")
    chip = me // 2
    first = chip * 2
    for copy in small:
        copy.wait()
    diffusion = diffusion_ref[...]
    inverse = inverted(diffusion)
    for i in range(STRETCHES):
        table_ref[i] = (0.5 + 0.25 * i) * inverse
    walls = walls_ref[...]

    def wall(bits, k):
        face = 1.0 / jnp.full((SUB, diffusion.shape[1]), 0.5 * height(index_ref, k))
        return bits.astype(jnp.float32) * jnp.concatenate([face] * row_tiles, axis=0)

    lower = wall(walls & 1, 0)
    upper = wall(walls >> 1, total - 1)

    def forward(block, kappa, keep=None):
        start = block * cells
        flux = table_ref[index_ref[start]] + kappa
        value = jnp.ones_like(flux)
        for j in range(cells):
            if keep is not None:
                keep(j, flux, value)
            k = start + j
            if j < cells - 1:
                value = value + half_sum(index_ref, k) * flux
                flux = flux + table_ref[index_ref[k + 1]] * value
        k = jnp.minimum(start + cells - 1, total - 2)
        after = inverted(value + half_sum(index_ref, k) * flux)
        return flux * after, after

    def backward(block, kappa, scale=None, keep=None):
        start = block * cells
        flux = table_ref[index_ref[start + cells - 1]] + kappa
        value = jnp.ones_like(flux)
        if scale is not None:
            flux, value = flux * scale, scale
        for j in reversed(range(cells)):
            if keep is not None:
                keep(j, flux, value)
            k = start + j
            if j > 0:
                value = value + half_sum(index_ref, k - 1) * flux
                flux = flux + table_ref[index_ref[k - 1]] * value
        k = jnp.maximum(start - 1, 0)
        after = inverted(value + half_sum(index_ref, k) * flux)
        return flux * after, after

    def thickness(block):
        parts = [height(index_ref, block * cells + j) for j in range(cells)]
        return functools.reduce(jnp.add, parts)

    def sweep_forward(block, state):
        kappa, product, extent = state
        kappa, after = forward(block, kappa)
        through_ref[block] = after
        return kappa, product * after, extent + thickness(block)

    def sweep_backward(step, state):
        block = blocks - 1 - step
        kappa, product, extent = state
        kappa, after = backward(block, kappa)
        through_ref[block] = after
        return kappa, product * after, extent + thickness(block)

    ones = jnp.ones_like(diffusion)
    kappa_left, product, extent = lax.fori_loop(
        0, me, sweep_forward, (lower, ones, thickness(me))
    )
    ends_ref[0] = diffusion * lower * product
    state = {}

    def keep_left(j, flux, value):
        left_ref[j] = value
        left_h_ref[j] = height(index_ref, me * cells + j) * value
        state["flux"], state["value"] = flux, value

    _, own_forward = forward(me, kappa_left, keep_left)
    held_ref[1] = own_forward
    held_ref[3] = state["flux"]
    held_ref[4] = state["value"]
    held_ref[5] = state["flux"] - kappa_left

    kappa_right, product, extent = lax.fori_loop(
        0, blocks - 1 - me, sweep_backward, (upper, ones, extent)
    )
    ends_ref[1] = diffusion_ref[...] * upper * product
    scale = inverted(diffusion_ref[...] * (held_ref[3] + kappa_right * held_ref[4]))
    held_ref[0] = scale

    def keep_right(j, flux, value):
        right_ref[j] = value
        right_h_ref[j] = height(index_ref, me * cells + j) * value
        state["flux"] = flux

    _, own_backward = backward(me, kappa_right, scale, keep_right)
    held_ref[2] = own_backward
    held_ref[6] = state["flux"] - kappa_right * scale

    is_first = me == first
    forth, back = held_ref[1], own_backward * held_ref[0]
    pair_ref[0] = jnp.where(is_first, back, forth)
    pair_ref[1] = jnp.where(is_first, forth, through_ref[first])
    pair_ref[2] = jnp.where(is_first, through_ref[first + 1], back)

    def fold(array):
        parts = [array[:, i * LANES:(i + 1) * LANES] for i in range(array.shape[1] // LANES)]
        return functools.reduce(jnp.add, parts)

    for copy in large:
        copy.wait()
    volume_ref[...] = jnp.full(volume_ref.shape, extent * lines)
    half = row_tiles // 2
    own_extent = thickness(me)
    heights = [height(index_ref, me * cells + j) for j in range(cells)]

    def sums(ref, whose, parts):
        def of_tile(i, state):
            flow, weight = state
            rows = row_tile(whose * half + i)
            from_left = [0.0] * parts
            from_right = [0.0] * parts
            plain = 0.0
            for j in range(cells):
                left = left_h_ref[j, rows]
                right = right_h_ref[j, rows]
                for c in range(parts):
                    v = velocity_ref[c, j, rows]
                    from_left[c] = from_left[c] + left * v
                    from_right[c] = from_right[c] + right * v
                    if c == 0:
                        plain = plain + heights[j] * v
            for c in range(parts):
                at = i * 2 * parts + c
                put(ref, at, from_left[c] * held_ref[1, rows])
                put(ref, at + parts, from_right[c] * held_ref[2, rows])
            low_part = ends_ref[0, rows]
            high_part = ends_ref[1, rows] * held_ref[0, rows]
            totals = low_part * held_ref[6, rows] + high_part * held_ref[5, rows]
            return (
                flow + fold(plain - low_part * from_right[0] - high_part * from_left[0]),
                weight + fold(own_extent - diffusion_ref[rows] * totals),
            )

        return of_tile

    state = (jnp.zeros((SUB, LANES), jnp.float32),) * 2
    mates = 1 - (me - first)
    state = lax.fori_loop(0, half, sums(away_ref, mates, components), state)
    flow, weight = lax.fori_loop(0, half, sums(mine_ref, me - first, 1), state)
    for i in range(half):
        put(away_ref, half * 2 * components + i, pair_ref[0, row_tile(mates * half + i)])
    slot, middle = away_ref.shape[0] - 1, SUB // 2
    away_ref[slot, 0:middle] = flow[0:middle] + flow[middle:]
    away_ref[slot, middle:] = weight[0:middle] + weight[middle:]


def rest_kernel(
    chips, velocity_ref, left_h_ref, right_h_ref, held_ref, through_ref, sums_ref, chip_ref
):
    components, cells, _, lines_x = velocity_ref.shape
    me = lax.axis_index("gz")
    chip = me // 2
    half = sums_ref.shape[0] // (2 * (components - 1) * (lines_x // LANES))
    ones = jnp.ones(chip_ref.shape[1:], jnp.float32)
    for m in range(1, chips):
        other = chip ^ m
        low = jnp.minimum(chip, other)
        high = jnp.maximum(chip, other)
        chip_ref[m - 1] = lax.fori_loop(
            low + 1,
            high,
            lambda r, product: product * (through_ref[2 * r] * through_ref[2 * r + 1]),
            ones,
        )

    def of_tile(i, _):
        rows = row_tile((me - chip * 2) * half + i)
        from_left = [0.0] * (components - 1)
        from_right = [0.0] * (components - 1)
        for j in range(cells):
            left = left_h_ref[j, rows]
            right = right_h_ref[j, rows]
            for c in range(components - 1):
                v = velocity_ref[c + 1, j, rows]
                from_left[c] = from_left[c] + left * v
                from_right[c] = from_right[c] + right * v
        for c in range(components - 1):
            at = i * 2 * (components - 1) + c
            put(sums_ref, at, from_left[c] * held_ref[1, rows])
            put(sums_ref, at + components - 1, from_right[c] * held_ref[2, rows])
        return 0

    lax.fori_loop(0, half, of_tile, 0)


def merge_kernel(orders, components, mine_ref, sums_ref, away_ref, mate_ref, pair_ref, *rest):
    send_refs, near_ref = rest[:-1], rest[-1]
    me = lax.axis_index("gz")
    chip = me // 2
    is_first = me == chip * 2
    steps = [jnp.where(is_first, a, b) for a, b in zip(*orders)]
    count = pair_ref.shape[2] // LANES
    half = mine_ref.shape[0] // (2 * count)
    slot = away_ref.shape[0] - 1
    tile = away_ref[slot] + mate_ref[slot]
    near_ref[near_ref.shape[0] - 1] = tile
    for ref in send_refs:
        for at in range(half * components * count, ref.shape[0]):
            ref[at] = tile
    for i in range(half):
        rows = row_tile((me - chip * 2) * half + i)
        mine, mate = pair_ref[0, rows], get(mate_ref, half * 2 * components + i, count)
        forth = jnp.where(is_first, mate, mine)
        back = jnp.where(is_first, mine, mate)
        for c in range(components):
            at = i * 2 * components + c
            if c == 0:
                own = [get(mine_ref, i * 2 + k, count) for k in range(2)]
            else:
                others = components - 1
                own = [
                    get(sums_ref, i * 2 * others + k * others + c - 1, count) for k in range(2)
                ]
            mine, mate = own[0], get(mate_ref, at, count)
            first = jnp.where(is_first, mine, mate)
            second = jnp.where(is_first, mate, mine)
            put(near_ref, at, first)
            to_right = second + forth * first
            at = at + components
            mine, mate = own[1], get(mate_ref, at, count)
            first = jnp.where(is_first, mine, mate)
            second = jnp.where(is_first, mate, mine)
            put(near_ref, at, second)
            to_left = first + back * second
            for m, ref in zip(steps, send_refs):
                goes_right = (chip ^ m) > chip
                put(ref, i * components + c, jnp.where(goes_right, to_right, to_left))


def spread_kernel(orders, components, near_ref, pair_ref, chip_ref, *rest):
    count = len(orders[0])
    recv_refs = rest[1:count + 1]
    own_ref, other_ref, *tile_refs = rest[count + 1:]
    me = lax.axis_index("gz")
    chip = me // 2
    is_first = me == chip * 2
    steps = [jnp.where(is_first, a, b) for a, b in zip(*orders)]
    count = pair_ref.shape[2] // LANES
    half = near_ref.shape[0] // (2 * components * count)
    tiles = [ref[ref.shape[0] - 1] for ref in (near_ref, *recv_refs)]
    tile = functools.reduce(jnp.add, tiles)
    for ref in tile_refs:
        for i in range(ref.shape[0]):
            ref[i] = tile
    for i in range(half):
        rows = row_tile((me - chip * 2) * half + i)
        coefs = [chip_ref[m - 1, rows] for m in steps]
        for c in range(components):
            left_in = jnp.zeros(own_ref.shape[1:], jnp.float32)
            right_in = jnp.zeros(own_ref.shape[1:], jnp.float32)
            for m, coef, ref in zip(steps, coefs, recv_refs):
                term = coef * get(ref, i * components + c, count)
                from_left = (chip ^ m) < chip
                left_in = left_in + jnp.where(from_left, term, 0.0)
                right_in = right_in + jnp.where(from_left, 0.0, term)
            at = i * 2 * components + c
            left_second = get(near_ref, at, count) + pair_ref[1, rows] * left_in
            right_first = get(near_ref, at + components, count) + pair_ref[2, rows] * right_in
            own_ref[at] = jnp.where(is_first, left_in, left_second)
            other_ref[at] = jnp.where(is_first, left_second, left_in)
            at = at + components
            own_ref[at] = jnp.where(is_first, right_first, right_in)
            other_ref[at] = jnp.where(is_first, right_in, right_first)


def inner_kernel(
    velocity_ref, left_ref, right_ref, left_h_ref, right_h_ref, ends_ref, volume_ref, target_ref,
    _, base_ref, unit_ref, goal_ref,
):
    components, cells, lines_y, lines_x = velocity_ref.shape
    goal_ref[...] = target_ref[...] * volume_ref[...]

    def of_tile(t, _):
        rows = row_tile(t)
        gathered = [jnp.zeros((SUB, lines_x), jnp.float32)] * components
        for j in reversed(range(cells)):
            left = left_ref[j, rows]
            right = right_h_ref[j, rows]
            for c in range(components):
                base_ref[c, j, rows] = left * gathered[c]
                if j > 0:
                    gathered[c] = gathered[c] + right * velocity_ref[c, j, rows]
        gathered = [jnp.zeros((SUB, lines_x), jnp.float32)] * components
        low_part = ends_ref[0, rows]
        high_part = ends_ref[1, rows] * right_ref[cells - 1, rows]
        for j in range(cells):
            left = left_h_ref[j, rows]
            right = right_ref[j, rows]
            unit_ref[j, rows] = 1.0 - (low_part * right + high_part * left_ref[j, rows])
            for c in range(components):
                gathered[c] = gathered[c] + left * velocity_ref[c, j, rows]
                base_ref[c, j, rows] = base_ref[c, j, rows] + right * gathered[c]
        return 0

    lax.fori_loop(0, lines_y // SUB, of_tile, 0)


def finish_kernel(
    own_ref, other_ref, base_ref, left_ref, right_ref, out_hbm, plain_ref, result_ref, sems
):
    components, cells, lines_y, _ = base_ref.shape
    half = own_ref.shape[0] // (2 * components)
    me = lax.axis_index("gz")

    def copies(t):
        rows = row_tile(t)
        return [
            pltpu.make_async_copy(
                result_ref.at[c - 1, :, rows], out_hbm.at[c, :, rows], sems.at[t, c - 1])
            for c in range(1, components)
        ]

    def half_of(incoming_ref, side):
        def of_tile(i, _):
            t = lax.rem(me + side, 2) * half + i
            rows = row_tile(t)
            scale = right_ref[cells - 1, rows]
            at = i * 2 * components
            lefts = [incoming_ref[at + c] for c in range(components)]
            rights = [incoming_ref[at + components + c] * scale for c in range(components)]
            for j in range(cells):
                left = left_ref[j, rows]
                right = right_ref[j, rows]
                for c in range(components):
                    value = base_ref[c, j, rows] + (right * lefts[c] + left * rights[c])
                    if c == 0:
                        plain_ref[j, rows] = value
                    else:
                        result_ref[c - 1, j, rows] = value
            for copy in copies(t):
                copy.start()
            return 0

        lax.fori_loop(0, half, of_tile, 0)

    half_of(own_ref, 0)
    half_of(other_ref, 1)
    for t in range(lines_y // SUB):
        for copy in copies(t):
            copy.wait()


def correct_kernel(count, goal_ref, unit_ref, *rest):
    tile_refs = rest[:count]
    plain_ref, _, out_hbm, result_ref, sems = rest[count:]
    totals = functools.reduce(jnp.add, [ref[0] for ref in tile_refs])
    flow = jnp.sum(totals[0:SUB // 2], keepdims=True)
    weight = jnp.sum(totals[SUB // 2:], keepdims=True)
    alpha = (goal_ref[0:1, 0:1] - flow) / weight
    cells, lines_y, _ = plain_ref.shape

    def copy(t):
        rows = row_tile(t)
        return pltpu.make_async_copy(result_ref.at[:, rows], out_hbm.at[0, :, rows], sems.at[t])

    def of_tile(t, _):
        rows = row_tile(t)
        for j in range(cells):
            result_ref[j, rows] = plain_ref[j, rows] + alpha * unit_ref[j, rows]
        copy(t).start()
        return 0

    lax.fori_loop(0, lines_y // SUB, of_tile, 0)
    for t in range(lines_y // SUB):
        copy(t).wait()


def shards(velocity, diffusion, wall_types, stretch_index, bulk_target):
    blocks = lax.axis_size("gz")
    columns = lax.axis_size("gy")
    components, cells, lines_y, lines_x = velocity.shape
    chips = blocks // 2
    row_tiles = lines_y // SUB
    half = row_tiles // 2
    f32 = jnp.float32
    vmem = pl.BlockSpec(memory_space=pltpu.VMEM)
    anywhere = pl.BlockSpec(memory_space=pl.ANY)
    plane = (lines_y, lines_x)
    sheet = (SUB, lines_x)

    def shape(*dims):
        return jax.ShapeDtypeStruct(dims, f32)

    def in_hbm(array):
        return pltpu.with_memory_space_constraint(array, pltpu.HBM)

    def options(mib):
        return pltpu.CompilerParams(vmem_limit_bytes=mib * MIB)

    def cost(flops, transferred):
        return pl.CostEstimate(flops=flops, bytes_accessed=transferred, transcendentals=0)

    def send(array, partner):
        pairs = [((z, y), partner(z, y)) for z in range(blocks) for y in range(columns)]
        route = [(a * columns + b, c * columns + d) for (a, b), (c, d) in pairs]
        return lax.ppermute(array, ("gz", "gy"), route)

    def to_mate(array):
        return send(array, lambda z, y: (z ^ 1, y))

    count = lines_x // LANES
    lines = float(lines_y * columns * lines_x)
    (mine, away, pair, through, held, left, right, left_h, right_h, ends, volume,
     near_velocity) = pl.pallas_call(
        functools.partial(ladder_kernel, cells, blocks, chips, lines),
        out_shape=[
            shape(half * 2 * count, SUB, LANES),
            shape(half * (2 * components + 1) * count + 1, SUB, LANES),
            shape(3, *plane),
            shape(blocks, *plane),
            shape(7, *plane),
            shape(cells, *plane),
            shape(cells, *plane),
            shape(cells, *plane),
            shape(cells, *plane),
            shape(2, *plane),
            shape(SUB, LANES),
            shape(*velocity.shape),
        ],
        in_specs=[anywhere] * 4,
        out_specs=[vmem] * 12,
        scratch_shapes=[
            pltpu.SMEM(stretch_index.shape, jnp.int32),
            pltpu.VMEM(plane, f32),
            pltpu.VMEM(plane, jnp.int32),
            pltpu.VMEM((STRETCHES,) + plane, f32),
            pltpu.SemaphoreType.DMA((3 + components,)),
        ],
        compiler_params=options(24),
        cost_estimate=cost(40_000_000, 6_000_000),
        name="ladder",
    )(in_hbm(stretch_index), in_hbm(diffusion), in_hbm(wall_types), in_hbm(velocity))

    mate = to_mate(away)
    sums, chip_coefs = pl.pallas_call(
        functools.partial(rest_kernel, chips),
        out_shape=[
            shape(half * 2 * (components - 1) * count, SUB, LANES),
            shape(chips - 1, *plane),
        ],
        in_specs=[vmem] * 5,
        out_specs=[vmem] * 2,
        compiler_params=options(16),
        cost_estimate=cost(2_000_000, 2_000_000),
        name="rest",
    )(near_velocity, left_h, right_h, held, through)
    even = sorted(range(1, chips), key=lambda m: (m.bit_count(), m), reverse=True)
    odd = even[-1:] + even[:-1]
    orders = (even, odd)
    *outgoing, near = pl.pallas_call(
        functools.partial(merge_kernel, orders, components),
        out_shape=[
            shape(half * components * count + 1 + max(0, 2 - k), SUB, LANES)
            for k in range(chips - 1)
        ] + [shape(half * 2 * components * count + 1, SUB, LANES)],
        in_specs=[vmem] * 5,
        out_specs=[vmem] * chips,
        compiler_params=options(16),
        cost_estimate=cost(500_000, 1_600_000),
        name="merge",
    )(mine, sums, away, mate, pair)
    incoming = [
        send(array, lambda z, y: (z ^ (2 * orders[z % 2][k]), y))
        for k, array in enumerate(outgoing)
    ]
    profile = shape(cells, *plane)
    base, unit, goal = pl.pallas_call(
        inner_kernel,
        out_shape=[shape(*velocity.shape), profile, shape(SUB, LANES)],
        in_specs=[vmem] * 8 + [anywhere],
        out_specs=[vmem] * 3,
        compiler_params=options(16),
        cost_estimate=cost(8_000_000, 8_000_000),
        name="inner",
    )(near_velocity, left, right, left_h, right_h, ends, volume, bulk_target.reshape(1, 1),
      outgoing[0])
    rounds = plane_rounds(columns)
    own_in, other_out, *tile = pl.pallas_call(
        functools.partial(spread_kernel, orders, components),
        out_shape=[shape(half * 2 * components, *sheet)] * 2
        + [shape(len(rounds) - i, SUB, LANES) for i in range(len(rounds))],
        in_specs=[vmem] * 3 + [anywhere] + [vmem] * (chips - 1),
        out_specs=[vmem] * (2 + len(rounds)),
        compiler_params=options(16),
        cost_estimate=cost(500_000, 1_600_000),
        name="spread",
    )(near, pair, chip_coefs, base, *incoming)
    other_in = to_mate(other_out)
    tiles = [tile[0]] + [
        send(array, lambda z, y: (z, targets[y])) for array, targets in zip(tile, rounds)
    ]
    partial, plain = pl.pallas_call(
        finish_kernel,
        out_shape=[shape(*velocity.shape), profile],
        in_specs=[vmem] * 5,
        out_specs=[anywhere, vmem],
        scratch_shapes=[
            pltpu.VMEM((components - 1, cells) + plane, f32),
            pltpu.SemaphoreType.DMA((row_tiles, components - 1)),
        ],
        compiler_params=options(16),
        cost_estimate=cost(3_000_000, 6_000_000),
        name="finish",
    )(own_in, other_in, base, left, right)
    return pl.pallas_call(
        functools.partial(correct_kernel, len(tiles)),
        out_shape=shape(*velocity.shape),
        in_specs=[vmem] * (3 + len(tiles)) + [anywhere],
        out_specs=anywhere,
        scratch_shapes=[
            pltpu.VMEM((cells,) + plane, f32),
            pltpu.SemaphoreType.DMA((row_tiles,)),
        ],
        input_output_aliases={3 + len(tiles): 0},
        compiler_params=options(16),
        cost_estimate=cost(500_000, 1_600_000),
        name="correct",
    )(goal, unit, *tiles, plain, partial)


def solution(mesh):
    return jax.shard_map(
        shards,
        mesh=mesh,
        in_specs=(P(None, "gz", "gy", None), P("gy", None), P("gy", None), P(), P()),
        out_specs=P(None, "gz", "gy", None),
        check_vma=False,
    )
```

```python
import functools

import jax
import jax.numpy as jnp
from jax import lax
from jax.experimental import pallas as pl
from jax.experimental.pallas import tpu as pltpu
from jax.sharding import PartitionSpec as P

SUB = 8
STRETCHES = 7
LANES = 128
MIB = 1024 * 1024


def plane_rounds(columns):
    if columns == 4:
        return [(2, 3, 1, 0), (3, 2, 0, 1), (1, 0, 3, 2)]
    return [[(y + shift) % columns for y in range(columns)] for shift in range(1, columns)]


def row_tile(t):
    return pl.ds(pl.multiple_of(t * SUB, SUB), SUB)


def inverted(array):
    guess = pl.reciprocal(array, approx=True)
    return guess * (2.0 - array * guess)


def put(ref, at, sheet):
    count = sheet.shape[1] // LANES
    for i in range(count):
        ref[at * count + i] = sheet[:, i * LANES:(i + 1) * LANES]


def get(ref, at, count):
    return jnp.concatenate([ref[at * count + i] for i in range(count)], axis=1)


def height(index_ref, k):
    return 0.5 + 0.25 * index_ref[k].astype(jnp.float32)


def half_sum(index_ref, k):
    return 0.5 * (height(index_ref, k) + height(index_ref, k + 1))


def ladder_kernel(
    cells, blocks, chips, lines,
    index_hbm, diffusion_hbm, walls_hbm, velocity_hbm,
    mine_ref, away_ref, pair_ref, through_ref, held_ref, left_ref, right_ref, left_h_ref, right_h_ref,
    ends_ref, volume_ref, velocity_ref,
    index_ref, diffusion_ref, walls_ref, table_ref, sems,
):
    total = cells * blocks
    components = velocity_ref.shape[0]
    row_tiles = diffusion_ref.shape[0] // SUB
    small = [
        pltpu.make_async_copy(index_hbm, index_ref, sems.at[0]),
        pltpu.make_async_copy(diffusion_hbm, diffusion_ref, sems.at[1]),
        pltpu.make_async_copy(walls_hbm, walls_ref, sems.at[2]),
    ]
    large = [
        pltpu.make_async_copy(velocity_hbm.at[c], velocity_ref.at[c], sems.at[3 + c])
        for c in range(components)
    ]
    for copy in small + large:
        copy.start()
    me = lax.axis_index("gz")
    chip = me // 2
    first = chip * 2
    for copy in small:
        copy.wait()
    diffusion = diffusion_ref[...]
    inverse = inverted(diffusion)
    for i in range(STRETCHES):
        table_ref[i] = (0.5 + 0.25 * i) * inverse
    walls = walls_ref[...]

    def wall(bits, k):
        face = 1.0 / jnp.full((SUB, diffusion.shape[1]), 0.5 * height(index_ref, k))
        return bits.astype(jnp.float32) * jnp.concatenate([face] * row_tiles, axis=0)

    lower = wall(walls & 1, 0)
    upper = wall(walls >> 1, total - 1)

    def forward(block, kappa, part=slice(None), keep=None):
        start = block * cells
        flux = table_ref[index_ref[start], part] + kappa
        value = jnp.ones_like(flux)
        for j in range(cells):
            if keep is not None:
                keep(j, flux, value)
            k = start + j
            if j < cells - 1:
                value = value + half_sum(index_ref, k) * flux
                flux = flux + table_ref[index_ref[k + 1], part] * value
        k = jnp.minimum(start + cells - 1, total - 2)
        after = inverted(value + half_sum(index_ref, k) * flux)
        return flux * after, after

    def backward(block, kappa, part=slice(None), scale=None, keep=None):
        start = block * cells
        flux = table_ref[index_ref[start + cells - 1], part] + kappa
        value = jnp.ones_like(flux)
        if scale is not None:
            flux, value = flux * scale, scale
        for j in reversed(range(cells)):
            if keep is not None:
                keep(j, flux, value)
            k = start + j
            if j > 0:
                value = value + half_sum(index_ref, k - 1) * flux
                flux = flux + table_ref[index_ref[k - 1], part] * value
        k = jnp.maximum(start - 1, 0)
        after = inverted(value + half_sum(index_ref, k) * flux)
        return flux * after, after

    def thickness(block):
        parts = [height(index_ref, block * cells + j) for j in range(cells)]
        return functools.reduce(jnp.add, parts)

    def sweeps(count, step, ends, extent):
        size = diffusion.shape[0] // 2
        parts = []
        for start in (0, size):
            part = slice(start, start + size)

            def sweep(i, state, part=part):
                kappa, product, extent = state
                block, (kappa, after) = step(i, kappa, part)
                through_ref[block, part] = after
                if part.start == 0:
                    extent = extent + thickness(block)
                return kappa, product * after, extent

            state = (ends[part], jnp.ones_like(ends[part]), extent)
            *arrays, extent = lax.fori_loop(0, count, sweep, state)
            parts.append(arrays)
        return [jnp.concatenate(pair, axis=0) for pair in zip(*parts)] + [extent]

    def step_forward(block, kappa, part):
        return block, forward(block, kappa, part)

    def step_backward(i, kappa, part):
        return blocks - 1 - i, backward(blocks - 1 - i, kappa, part)

    kappa_left, product, extent = sweeps(me, step_forward, lower, thickness(me))
    ends_ref[0] = diffusion * lower * product
    state = {}

    def keep_left(j, flux, value):
        left_ref[j] = value
        left_h_ref[j] = height(index_ref, me * cells + j) * value
        state["flux"], state["value"] = flux, value

    _, own_forward = forward(me, kappa_left, keep=keep_left)
    held_ref[1] = own_forward
    held_ref[3] = state["flux"]
    held_ref[4] = state["value"]
    held_ref[5] = state["flux"] - kappa_left

    kappa_right, product, extent = sweeps(blocks - 1 - me, step_backward, upper, extent)
    ends_ref[1] = diffusion_ref[...] * upper * product
    scale = inverted(diffusion_ref[...] * (held_ref[3] + kappa_right * held_ref[4]))
    held_ref[0] = scale

    def keep_right(j, flux, value):
        right_ref[j] = value
        right_h_ref[j] = height(index_ref, me * cells + j) * value
        state["flux"] = flux

    _, own_backward = backward(me, kappa_right, scale=scale, keep=keep_right)
    held_ref[2] = own_backward
    held_ref[6] = state["flux"] - kappa_right * scale

    is_first = me == first
    forth, back = held_ref[1], own_backward * held_ref[0]
    pair_ref[0] = jnp.where(is_first, back, forth)
    pair_ref[1] = jnp.where(is_first, forth, through_ref[first])
    pair_ref[2] = jnp.where(is_first, through_ref[first + 1], back)

    def fold(array):
        parts = [array[:, i * LANES:(i + 1) * LANES] for i in range(array.shape[1] // LANES)]
        return functools.reduce(jnp.add, parts)

    for copy in large:
        copy.wait()
    volume_ref[...] = jnp.full(volume_ref.shape, extent * lines)
    half = row_tiles // 2
    own_extent = thickness(me)
    heights = [height(index_ref, me * cells + j) for j in range(cells)]

    def sums(ref, whose, parts):
        def of_tile(i, state):
            flow, weight = state
            rows = row_tile(whose * half + i)
            from_left = [0.0] * parts
            from_right = [0.0] * parts
            plain = 0.0
            for j in range(cells):
                left = left_h_ref[j, rows]
                right = right_h_ref[j, rows]
                for c in range(parts):
                    v = velocity_ref[c, j, rows]
                    from_left[c] = from_left[c] + left * v
                    from_right[c] = from_right[c] + right * v
                    if c == 0:
                        plain = plain + heights[j] * v
            for c in range(parts):
                at = i * 2 * parts + c
                put(ref, at, from_left[c] * held_ref[1, rows])
                put(ref, at + parts, from_right[c] * held_ref[2, rows])
            low_part = ends_ref[0, rows]
            high_part = ends_ref[1, rows] * held_ref[0, rows]
            totals = low_part * held_ref[6, rows] + high_part * held_ref[5, rows]
            return (
                flow + fold(plain - low_part * from_right[0] - high_part * from_left[0]),
                weight + fold(own_extent - diffusion_ref[rows] * totals),
            )

        return of_tile

    state = (jnp.zeros((SUB, LANES), jnp.float32),) * 2
    mates = 1 - (me - first)
    state = lax.fori_loop(0, half, sums(away_ref, mates, components), state)
    flow, weight = lax.fori_loop(0, half, sums(mine_ref, me - first, 1), state)
    for i in range(half):
        put(away_ref, half * 2 * components + i, pair_ref[0, row_tile(mates * half + i)])
    slot, middle = away_ref.shape[0] - 1, SUB // 2
    away_ref[slot, 0:middle] = flow[0:middle] + flow[middle:]
    away_ref[slot, middle:] = weight[0:middle] + weight[middle:]


def rest_kernel(
    chips, velocity_ref, left_h_ref, right_h_ref, held_ref, through_ref, sums_ref, chip_ref
):
    components, cells, _, lines_x = velocity_ref.shape
    me = lax.axis_index("gz")
    chip = me // 2
    half = sums_ref.shape[0] // (2 * (components - 1) * (lines_x // LANES))
    ones = jnp.ones(chip_ref.shape[1:], jnp.float32)
    for m in range(1, chips):
        other = chip ^ m
        low = jnp.minimum(chip, other)
        high = jnp.maximum(chip, other)
        chip_ref[m - 1] = lax.fori_loop(
            low + 1,
            high,
            lambda r, product: product * (through_ref[2 * r] * through_ref[2 * r + 1]),
            ones,
        )

    def of_tile(i, _):
        rows = row_tile((me - chip * 2) * half + i)
        from_left = [0.0] * (components - 1)
        from_right = [0.0] * (components - 1)
        for j in range(cells):
            left = left_h_ref[j, rows]
            right = right_h_ref[j, rows]
            for c in range(components - 1):
                v = velocity_ref[c + 1, j, rows]
                from_left[c] = from_left[c] + left * v
                from_right[c] = from_right[c] + right * v
        for c in range(components - 1):
            at = i * 2 * (components - 1) + c
            put(sums_ref, at, from_left[c] * held_ref[1, rows])
            put(sums_ref, at + components - 1, from_right[c] * held_ref[2, rows])
        return 0

    lax.fori_loop(0, half, of_tile, 0)


def merge_kernel(chips, components, mine_ref, sums_ref, away_ref, mate_ref, pair_ref, *rest):
    send_refs, near_ref = rest[:-1], rest[-1]
    me = lax.axis_index("gz")
    chip = me // 2
    is_first = me == chip * 2
    count = pair_ref.shape[2] // LANES
    half = mine_ref.shape[0] // (2 * count)
    slot = away_ref.shape[0] - 1
    tile = away_ref[slot] + mate_ref[slot]
    near_ref[near_ref.shape[0] - 1] = tile
    for ref in send_refs:
        for at in range(half * components * count, ref.shape[0]):
            ref[at] = tile
    for i in range(half):
        rows = row_tile((me - chip * 2) * half + i)
        mine, mate = pair_ref[0, rows], get(mate_ref, half * 2 * components + i, count)
        forth = jnp.where(is_first, mate, mine)
        back = jnp.where(is_first, mine, mate)
        for c in range(components):
            at = i * 2 * components + c
            if c == 0:
                own = [get(mine_ref, i * 2 + k, count) for k in range(2)]
            else:
                others = components - 1
                own = [
                    get(sums_ref, i * 2 * others + k * others + c - 1, count) for k in range(2)
                ]
            mine, mate = own[0], get(mate_ref, at, count)
            first = jnp.where(is_first, mine, mate)
            second = jnp.where(is_first, mate, mine)
            put(near_ref, at, first)
            to_right = second + forth * first
            at = at + components
            mine, mate = own[1], get(mate_ref, at, count)
            first = jnp.where(is_first, mine, mate)
            second = jnp.where(is_first, mate, mine)
            put(near_ref, at, second)
            to_left = first + back * second
            for m in range(1, chips):
                goes_right = (chip ^ m) > chip
                sheet = jnp.where(goes_right, to_right, to_left)
                put(send_refs[m - 1], i * components + c, sheet)


def spread_kernel(order, components, near_ref, pair_ref, chip_ref, *rest):
    recv_refs = rest[1:len(order) + 1]
    own_ref, other_ref, *tile_refs = rest[len(order) + 1:]
    me = lax.axis_index("gz")
    chip = me // 2
    is_first = me == chip * 2
    count = pair_ref.shape[2] // LANES
    half = near_ref.shape[0] // (2 * components * count)
    tiles = [ref[ref.shape[0] - 1] for ref in (near_ref, *recv_refs)]
    tile = functools.reduce(jnp.add, tiles)
    for ref in tile_refs:
        for i in range(ref.shape[0]):
            ref[i] = tile
    for i in range(half):
        rows = row_tile((me - chip * 2) * half + i)
        coefs = [chip_ref[m - 1, rows] for m in order]
        for c in range(components):
            left_in = jnp.zeros(own_ref.shape[1:], jnp.float32)
            right_in = jnp.zeros(own_ref.shape[1:], jnp.float32)
            for m, coef, ref in zip(order, coefs, recv_refs):
                term = coef * get(ref, i * components + c, count)
                from_left = (chip ^ m) < chip
                left_in = left_in + jnp.where(from_left, term, 0.0)
                right_in = right_in + jnp.where(from_left, 0.0, term)
            at = i * 2 * components + c
            left_second = get(near_ref, at, count) + pair_ref[1, rows] * left_in
            right_first = get(near_ref, at + components, count) + pair_ref[2, rows] * right_in
            own_ref[at] = jnp.where(is_first, left_in, left_second)
            other_ref[at] = jnp.where(is_first, left_second, left_in)
            at = at + components
            own_ref[at] = jnp.where(is_first, right_first, right_in)
            other_ref[at] = jnp.where(is_first, right_in, right_first)


def inner_kernel(
    velocity_ref, left_ref, right_ref, left_h_ref, right_h_ref, ends_ref, volume_ref, target_ref,
    _, base_ref, unit_ref, goal_ref,
):
    components, cells, lines_y, lines_x = velocity_ref.shape
    goal_ref[...] = target_ref[...] * volume_ref[...]

    def of_tile(t, _):
        rows = row_tile(t)
        gathered = [jnp.zeros((SUB, lines_x), jnp.float32)] * components
        for j in reversed(range(cells)):
            left = left_ref[j, rows]
            right = right_h_ref[j, rows]
            for c in range(components):
                base_ref[c, j, rows] = left * gathered[c]
                if j > 0:
                    gathered[c] = gathered[c] + right * velocity_ref[c, j, rows]
        gathered = [jnp.zeros((SUB, lines_x), jnp.float32)] * components
        low_part = ends_ref[0, rows]
        high_part = ends_ref[1, rows] * right_ref[cells - 1, rows]
        for j in range(cells):
            left = left_h_ref[j, rows]
            right = right_ref[j, rows]
            unit_ref[j, rows] = 1.0 - (low_part * right + high_part * left_ref[j, rows])
            for c in range(components):
                gathered[c] = gathered[c] + left * velocity_ref[c, j, rows]
                base_ref[c, j, rows] = base_ref[c, j, rows] + right * gathered[c]
        return 0

    lax.fori_loop(0, lines_y // SUB, of_tile, 0)


def finish_kernel(
    own_ref, other_ref, base_ref, left_ref, right_ref, out_hbm, plain_ref, result_ref, sems
):
    components, cells, lines_y, _ = base_ref.shape
    half = own_ref.shape[0] // (2 * components)
    me = lax.axis_index("gz")

    def copies(t):
        rows = row_tile(t)
        return [
            pltpu.make_async_copy(
                result_ref.at[c - 1, :, rows], out_hbm.at[c, :, rows], sems.at[t, c - 1])
            for c in range(1, components)
        ]

    def half_of(incoming_ref, side):
        def of_tile(i, _):
            t = lax.rem(me + side, 2) * half + i
            rows = row_tile(t)
            scale = right_ref[cells - 1, rows]
            at = i * 2 * components
            lefts = [incoming_ref[at + c] for c in range(components)]
            rights = [incoming_ref[at + components + c] * scale for c in range(components)]
            for j in range(cells):
                left = left_ref[j, rows]
                right = right_ref[j, rows]
                for c in range(components):
                    value = base_ref[c, j, rows] + (right * lefts[c] + left * rights[c])
                    if c == 0:
                        plain_ref[j, rows] = value
                    else:
                        result_ref[c - 1, j, rows] = value
            for copy in copies(t):
                copy.start()
            return 0

        lax.fori_loop(0, half, of_tile, 0)

    half_of(own_ref, 0)
    half_of(other_ref, 1)
    for t in range(lines_y // SUB):
        for copy in copies(t):
            copy.wait()


def correct_kernel(count, goal_ref, unit_ref, *rest):
    tile_refs = rest[:count]
    plain_ref, _, out_hbm, result_ref, sems = rest[count:]
    totals = functools.reduce(jnp.add, [ref[0] for ref in tile_refs])
    flow = jnp.sum(totals[0:SUB // 2], keepdims=True)
    weight = jnp.sum(totals[SUB // 2:], keepdims=True)
    alpha = (goal_ref[0:1, 0:1] - flow) / weight
    cells, lines_y, _ = plain_ref.shape

    def copy(t):
        rows = row_tile(t)
        return pltpu.make_async_copy(result_ref.at[:, rows], out_hbm.at[0, :, rows], sems.at[t])

    def of_tile(t, _):
        rows = row_tile(t)
        for j in range(cells):
            result_ref[j, rows] = plain_ref[j, rows] + alpha * unit_ref[j, rows]
        copy(t).start()
        return 0

    lax.fori_loop(0, lines_y // SUB, of_tile, 0)
    for t in range(lines_y // SUB):
        copy(t).wait()


def shards(velocity, diffusion, wall_types, stretch_index, bulk_target):
    blocks = lax.axis_size("gz")
    columns = lax.axis_size("gy")
    components, cells, lines_y, lines_x = velocity.shape
    chips = blocks // 2
    row_tiles = lines_y // SUB
    half = row_tiles // 2
    f32 = jnp.float32
    vmem = pl.BlockSpec(memory_space=pltpu.VMEM)
    anywhere = pl.BlockSpec(memory_space=pl.ANY)
    plane = (lines_y, lines_x)
    sheet = (SUB, lines_x)

    def shape(*dims):
        return jax.ShapeDtypeStruct(dims, f32)

    def in_hbm(array):
        return pltpu.with_memory_space_constraint(array, pltpu.HBM)

    def options(mib):
        return pltpu.CompilerParams(vmem_limit_bytes=mib * MIB)

    def cost(flops, transferred):
        return pl.CostEstimate(flops=flops, bytes_accessed=transferred, transcendentals=0)

    def send(array, partner):
        pairs = [((z, y), partner(z, y)) for z in range(blocks) for y in range(columns)]
        route = [(a * columns + b, c * columns + d) for (a, b), (c, d) in pairs]
        return lax.ppermute(array, ("gz", "gy"), route)

    def to_mate(array):
        return send(array, lambda z, y: (z ^ 1, y))

    count = lines_x // LANES
    lines = float(lines_y * columns * lines_x)
    (mine, away, pair, through, held, left, right, left_h, right_h, ends, volume,
     near_velocity) = pl.pallas_call(
        functools.partial(ladder_kernel, cells, blocks, chips, lines),
        out_shape=[
            shape(half * 2 * count, SUB, LANES),
            shape(half * (2 * components + 1) * count + 1, SUB, LANES),
            shape(3, *plane),
            shape(blocks, *plane),
            shape(7, *plane),
            shape(cells, *plane),
            shape(cells, *plane),
            shape(cells, *plane),
            shape(cells, *plane),
            shape(2, *plane),
            shape(SUB, LANES),
            shape(*velocity.shape),
        ],
        in_specs=[anywhere] * 4,
        out_specs=[vmem] * 12,
        scratch_shapes=[
            pltpu.SMEM(stretch_index.shape, jnp.int32),
            pltpu.VMEM(plane, f32),
            pltpu.VMEM(plane, jnp.int32),
            pltpu.VMEM((STRETCHES,) + plane, f32),
            pltpu.SemaphoreType.DMA((3 + components,)),
        ],
        compiler_params=options(24),
        cost_estimate=cost(40_000_000, 6_000_000),
        name="ladder",
    )(in_hbm(stretch_index), in_hbm(diffusion), in_hbm(wall_types), in_hbm(velocity))

    mate = to_mate(away)
    sums, chip_coefs = pl.pallas_call(
        functools.partial(rest_kernel, chips),
        out_shape=[
            shape(half * 2 * (components - 1) * count, SUB, LANES),
            shape(chips - 1, *plane),
        ],
        in_specs=[vmem] * 5,
        out_specs=[vmem] * 2,
        compiler_params=options(16),
        cost_estimate=cost(2_000_000, 2_000_000),
        name="rest",
    )(near_velocity, left_h, right_h, held, through)
    *outgoing, near = pl.pallas_call(
        functools.partial(merge_kernel, chips, components),
        out_shape=[
            shape(half * components * count + m.bit_count(), SUB, LANES) for m in range(1, chips)
        ] + [shape(half * 2 * components * count + 1, SUB, LANES)],
        in_specs=[vmem] * 5,
        out_specs=[vmem] * chips,
        compiler_params=options(16),
        cost_estimate=cost(500_000, 1_600_000),
        name="merge",
    )(mine, sums, away, mate, pair)
    order = sorted(range(1, chips), key=lambda m: -m.bit_count())
    incoming = [send(outgoing[m - 1], lambda z, y: (z ^ (2 * m), y)) for m in order]
    profile = shape(cells, *plane)
    base, unit, goal = pl.pallas_call(
        inner_kernel,
        out_shape=[shape(*velocity.shape), profile, shape(SUB, LANES)],
        in_specs=[vmem] * 8 + [anywhere],
        out_specs=[vmem] * 3,
        compiler_params=options(16),
        cost_estimate=cost(8_000_000, 8_000_000),
        name="inner",
    )(near_velocity, left, right, left_h, right_h, ends, volume, bulk_target.reshape(1, 1),
      outgoing[0])
    rounds = plane_rounds(columns)
    own_in, other_out, *tile = pl.pallas_call(
        functools.partial(spread_kernel, order, components),
        out_shape=[shape(half * 2 * components, *sheet)] * 2
        + [shape(len(rounds) - i, SUB, LANES) for i in range(len(rounds))],
        in_specs=[vmem] * 3 + [anywhere] + [vmem] * (chips - 1),
        out_specs=[vmem] * (2 + len(rounds)),
        compiler_params=options(16),
        cost_estimate=cost(500_000, 1_600_000),
        name="spread",
    )(near, pair, chip_coefs, base, *incoming)
    other_in = to_mate(other_out)
    tiles = [tile[0]] + [
        send(array, lambda z, y: (z, targets[y])) for array, targets in zip(tile, rounds)
    ]
    partial, plain = pl.pallas_call(
        finish_kernel,
        out_shape=[shape(*velocity.shape), profile],
        in_specs=[vmem] * 5,
        out_specs=[anywhere, vmem],
        scratch_shapes=[
            pltpu.VMEM((components - 1, cells) + plane, f32),
            pltpu.SemaphoreType.DMA((row_tiles, components - 1)),
        ],
        compiler_params=options(16),
        cost_estimate=cost(3_000_000, 6_000_000),
        name="finish",
    )(own_in, other_in, base, left, right)
    return pl.pallas_call(
        functools.partial(correct_kernel, len(tiles)),
        out_shape=shape(*velocity.shape),
        in_specs=[vmem] * (3 + len(tiles)) + [anywhere],
        out_specs=anywhere,
        scratch_shapes=[
            pltpu.VMEM((cells,) + plane, f32),
            pltpu.SemaphoreType.DMA((row_tiles,)),
        ],
        input_output_aliases={3 + len(tiles): 0},
        compiler_params=options(16),
        cost_estimate=cost(500_000, 1_600_000),
        name="correct",
    )(goal, unit, *tiles, plain, partial)


def solution(mesh):
    return jax.shard_map(
        shards,
        mesh=mesh,
        in_specs=(P(None, "gz", "gy", None), P("gy", None), P("gy", None), P(), P()),
        out_specs=P(None, "gz", "gy", None),
        check_vma=False,
    )
```

```python
import functools

import jax
import jax.numpy as jnp
from jax import lax
from jax.experimental import pallas as pl
from jax.experimental.pallas import tpu as pltpu
from jax.sharding import PartitionSpec as P

SUB = 8
STRETCHES = 7
LANES = 128
MIB = 1024 * 1024


def plane_rounds(columns):
    if columns == 4:
        return [(2, 3, 1, 0), (3, 2, 0, 1), (1, 0, 3, 2)]
    return [[(y + shift) % columns for y in range(columns)] for shift in range(1, columns)]


def row_tile(t):
    return pl.ds(pl.multiple_of(t * SUB, SUB), SUB)


def inverted(array):
    guess = pl.reciprocal(array, approx=True)
    return guess * (2.0 - array * guess)


def put(ref, at, sheet):
    count = sheet.shape[1] // LANES
    for i in range(count):
        ref[at * count + i] = sheet[:, i * LANES:(i + 1) * LANES]


def get(ref, at, count):
    return jnp.concatenate([ref[at * count + i] for i in range(count)], axis=1)


def height(index_ref, k):
    return 0.5 + 0.25 * index_ref[k].astype(jnp.float32)


def half_sum(index_ref, k):
    return 0.5 * (height(index_ref, k) + height(index_ref, k + 1))


def ladder_kernel(
    cells, blocks, chips, lines,
    index_hbm, diffusion_hbm, walls_hbm, velocity_hbm,
    mine_ref, away_ref, pair_ref, through_ref, held_ref, left_ref, right_ref, left_h_ref, right_h_ref,
    ends_ref, volume_ref, velocity_ref,
    index_ref, diffusion_ref, walls_ref, table_ref, sems,
):
    total = cells * blocks
    components = velocity_ref.shape[0]
    row_tiles = diffusion_ref.shape[0] // SUB
    small = [
        pltpu.make_async_copy(index_hbm, index_ref, sems.at[0]),
        pltpu.make_async_copy(diffusion_hbm, diffusion_ref, sems.at[1]),
        pltpu.make_async_copy(walls_hbm, walls_ref, sems.at[2]),
    ]
    large = [
        pltpu.make_async_copy(velocity_hbm.at[c], velocity_ref.at[c], sems.at[3 + c])
        for c in range(components)
    ]
    for copy in small + large:
        copy.start()
    me = lax.axis_index("gz")
    chip = me // 2
    first = chip * 2
    for copy in small:
        copy.wait()
    diffusion = diffusion_ref[...]
    inverse = inverted(diffusion)
    for i in range(STRETCHES):
        table_ref[i] = (0.5 + 0.25 * i) * inverse
    walls = walls_ref[...]

    def wall(bits, k):
        face = 1.0 / jnp.full((SUB, diffusion.shape[1]), 0.5 * height(index_ref, k))
        return bits.astype(jnp.float32) * jnp.concatenate([face] * row_tiles, axis=0)

    lower = wall(walls & 1, 0)
    upper = wall(walls >> 1, total - 1)

    def forward(block, kappa, keep=None):
        start = block * cells
        flux = table_ref[index_ref[start]] + kappa
        value = jnp.ones_like(flux)
        for j in range(cells):
            if keep is not None:
                keep(j, flux, value)
            k = start + j
            if j < cells - 1:
                value = value + half_sum(index_ref, k) * flux
                flux = flux + table_ref[index_ref[k + 1]] * value
        k = jnp.minimum(start + cells - 1, total - 2)
        after = inverted(value + half_sum(index_ref, k) * flux)
        return flux * after, after

    def backward(block, kappa, scale=None, keep=None):
        start = block * cells
        flux = table_ref[index_ref[start + cells - 1]] + kappa
        value = jnp.ones_like(flux)
        if scale is not None:
            flux, value = flux * scale, scale
        for j in reversed(range(cells)):
            if keep is not None:
                keep(j, flux, value)
            k = start + j
            if j > 0:
                value = value + half_sum(index_ref, k - 1) * flux
                flux = flux + table_ref[index_ref[k - 1]] * value
        k = jnp.maximum(start - 1, 0)
        after = inverted(value + half_sum(index_ref, k) * flux)
        return flux * after, after

    def thickness(block):
        parts = [height(index_ref, block * cells + j) for j in range(cells)]
        return functools.reduce(jnp.add, parts)

    def sweep_forward(block, state):
        kappa, product, extent = state
        kappa, after = forward(block, kappa)
        through_ref[block] = after
        return kappa, product * after, extent + thickness(block)

    def sweep_backward(step, state):
        block = blocks - 1 - step
        kappa, product, extent = state
        kappa, after = backward(block, kappa)
        through_ref[block] = after
        return kappa, product * after, extent + thickness(block)

    ones = jnp.ones_like(diffusion)
    kappa_left, product, extent = lax.fori_loop(
        0, me, sweep_forward, (lower, ones, thickness(me))
    )
    ends_ref[0] = diffusion * lower * product
    state = {}

    def keep_left(j, flux, value):
        left_ref[j] = value
        left_h_ref[j] = height(index_ref, me * cells + j) * value
        state["flux"], state["value"] = flux, value

    _, own_forward = forward(me, kappa_left, keep_left)
    held_ref[1] = own_forward
    held_ref[3] = state["flux"]
    held_ref[4] = state["value"]
    held_ref[5] = state["flux"] - kappa_left

    kappa_right, product, extent = lax.fori_loop(
        0, blocks - 1 - me, sweep_backward, (upper, ones, extent)
    )
    ends_ref[1] = diffusion_ref[...] * upper * product
    scale = inverted(diffusion_ref[...] * (held_ref[3] + kappa_right * held_ref[4]))
    held_ref[0] = scale

    def keep_right(j, flux, value):
        right_ref[j] = value
        right_h_ref[j] = height(index_ref, me * cells + j) * value
        state["flux"] = flux

    _, own_backward = backward(me, kappa_right, scale, keep_right)
    held_ref[2] = own_backward
    held_ref[6] = state["flux"] - kappa_right * scale

    is_first = me == first
    forth, back = held_ref[1], own_backward * held_ref[0]
    pair_ref[0] = jnp.where(is_first, back, forth)
    pair_ref[1] = jnp.where(is_first, forth, through_ref[first])
    pair_ref[2] = jnp.where(is_first, through_ref[first + 1], back)

    def fold(array):
        parts = [array[:, i * LANES:(i + 1) * LANES] for i in range(array.shape[1] // LANES)]
        return functools.reduce(jnp.add, parts)

    for copy in large:
        copy.wait()
    volume_ref[...] = jnp.full(volume_ref.shape, extent * lines)
    half = row_tiles // 2
    own_extent = thickness(me)
    heights = [height(index_ref, me * cells + j) for j in range(cells)]

    def sums(ref, whose, parts):
        def of_tile(i, state):
            flow, weight = state
            rows = row_tile(whose * half + i)
            from_left = [0.0] * parts
            from_right = [0.0] * parts
            plain = 0.0
            for j in range(cells):
                left = left_h_ref[j, rows]
                right = right_h_ref[j, rows]
                for c in range(parts):
                    v = velocity_ref[c, j, rows]
                    from_left[c] = from_left[c] + left * v
                    from_right[c] = from_right[c] + right * v
                    if c == 0:
                        plain = plain + heights[j] * v
            for c in range(parts):
                at = i * 2 * parts + c
                put(ref, at, from_left[c] * held_ref[1, rows])
                put(ref, at + parts, from_right[c] * held_ref[2, rows])
            low_part = ends_ref[0, rows]
            high_part = ends_ref[1, rows] * held_ref[0, rows]
            totals = low_part * held_ref[6, rows] + high_part * held_ref[5, rows]
            return (
                flow + fold(plain - low_part * from_right[0] - high_part * from_left[0]),
                weight + fold(own_extent - diffusion_ref[rows] * totals),
            )

        return of_tile

    state = (jnp.zeros((SUB, LANES), jnp.float32),) * 2
    mates = 1 - (me - first)
    state = lax.fori_loop(0, half, sums(away_ref, mates, components), state)
    flow, weight = lax.fori_loop(0, half, sums(mine_ref, me - first, 1), state)
    for i in range(half):
        put(away_ref, half * 2 * components + i, pair_ref[0, row_tile(mates * half + i)])
    slot, middle = away_ref.shape[0] - 1, SUB // 2
    away_ref[slot, 0:middle] = flow[0:middle] + flow[middle:]
    away_ref[slot, middle:] = weight[0:middle] + weight[middle:]


def rest_kernel(
    chips, velocity_ref, left_h_ref, right_h_ref, held_ref, through_ref, sums_ref, chip_ref
):
    components, cells, _, lines_x = velocity_ref.shape
    me = lax.axis_index("gz")
    chip = me // 2
    half = sums_ref.shape[0] // (2 * (components - 1) * (lines_x // LANES))
    ones = jnp.ones(chip_ref.shape[1:], jnp.float32)
    for m in range(1, chips):
        other = chip ^ m
        low = jnp.minimum(chip, other)
        high = jnp.maximum(chip, other)
        chip_ref[m - 1] = lax.fori_loop(
            low + 1,
            high,
            lambda r, product: product * (through_ref[2 * r] * through_ref[2 * r + 1]),
            ones,
        )

    def of_tile(i, _):
        rows = row_tile((me - chip * 2) * half + i)
        from_left = [0.0] * (components - 1)
        from_right = [0.0] * (components - 1)
        for j in range(cells):
            left = left_h_ref[j, rows]
            right = right_h_ref[j, rows]
            for c in range(components - 1):
                v = velocity_ref[c + 1, j, rows]
                from_left[c] = from_left[c] + left * v
                from_right[c] = from_right[c] + right * v
        for c in range(components - 1):
            at = i * 2 * (components - 1) + c
            put(sums_ref, at, from_left[c] * held_ref[1, rows])
            put(sums_ref, at + components - 1, from_right[c] * held_ref[2, rows])
        return 0

    lax.fori_loop(0, half, of_tile, 0)


def merge_kernel(chips, components, mine_ref, sums_ref, away_ref, mate_ref, pair_ref, *rest):
    send_refs, near_ref = rest[:-1], rest[-1]
    me = lax.axis_index("gz")
    chip = me // 2
    is_first = me == chip * 2
    count = pair_ref.shape[2] // LANES
    half = mine_ref.shape[0] // (2 * count)
    slot = away_ref.shape[0] - 1
    tile = away_ref[slot] + mate_ref[slot]
    near_ref[near_ref.shape[0] - 1] = tile
    for ref in send_refs:
        for at in range(half * components * count, ref.shape[0]):
            ref[at] = tile
    for i in range(half):
        rows = row_tile((me - chip * 2) * half + i)
        mine, mate = pair_ref[0, rows], get(mate_ref, half * 2 * components + i, count)
        forth = jnp.where(is_first, mate, mine)
        back = jnp.where(is_first, mine, mate)
        for c in range(components):
            at = i * 2 * components + c
            if c == 0:
                own = [get(mine_ref, i * 2 + k, count) for k in range(2)]
            else:
                others = components - 1
                own = [
                    get(sums_ref, i * 2 * others + k * others + c - 1, count) for k in range(2)
                ]
            mine, mate = own[0], get(mate_ref, at, count)
            first = jnp.where(is_first, mine, mate)
            second = jnp.where(is_first, mate, mine)
            put(near_ref, at, first)
            to_right = second + forth * first
            at = at + components
            mine, mate = own[1], get(mate_ref, at, count)
            first = jnp.where(is_first, mine, mate)
            second = jnp.where(is_first, mate, mine)
            put(near_ref, at, second)
            to_left = first + back * second
            for m in range(1, chips):
                goes_right = (chip ^ m) > chip
                sheet = jnp.where(goes_right, to_right, to_left)
                put(send_refs[m - 1], i * components + c, sheet)


def spread_kernel(order, components, near_ref, pair_ref, chip_ref, *rest):
    recv_refs = rest[1:len(order) + 1]
    own_ref, other_ref, *tile_refs = rest[len(order) + 1:]
    me = lax.axis_index("gz")
    chip = me // 2
    is_first = me == chip * 2
    count = pair_ref.shape[2] // LANES
    half = near_ref.shape[0] // (2 * components * count)
    tiles = [ref[ref.shape[0] - 1] for ref in (near_ref, *recv_refs)]
    tile = functools.reduce(jnp.add, tiles)
    for ref in tile_refs:
        for i in range(ref.shape[0]):
            ref[i] = tile
    for i in range(half):
        rows = row_tile((me - chip * 2) * half + i)
        coefs = [chip_ref[m - 1, rows] for m in order]
        for c in range(components):
            left_in = jnp.zeros(own_ref.shape[1:], jnp.float32)
            right_in = jnp.zeros(own_ref.shape[1:], jnp.float32)
            for m, coef, ref in zip(order, coefs, recv_refs):
                term = coef * get(ref, i * components + c, count)
                from_left = (chip ^ m) < chip
                left_in = left_in + jnp.where(from_left, term, 0.0)
                right_in = right_in + jnp.where(from_left, 0.0, term)
            at = i * 2 * components + c
            left_second = get(near_ref, at, count) + pair_ref[1, rows] * left_in
            right_first = get(near_ref, at + components, count) + pair_ref[2, rows] * right_in
            own_ref[at] = jnp.where(is_first, left_in, left_second)
            other_ref[at] = jnp.where(is_first, left_second, left_in)
            at = at + components
            own_ref[at] = jnp.where(is_first, right_first, right_in)
            other_ref[at] = jnp.where(is_first, right_in, right_first)


def inner_kernel(
    velocity_ref, left_ref, right_ref, left_h_ref, right_h_ref, ends_ref, volume_ref, target_ref,
    _, base_ref, unit_ref, goal_ref,
):
    components, cells, lines_y, lines_x = velocity_ref.shape
    goal_ref[...] = target_ref[...] * volume_ref[...]

    def of_tile(t, _):
        rows = row_tile(t)
        gathered = [jnp.zeros((SUB, lines_x), jnp.float32)] * components
        for j in reversed(range(cells)):
            left = left_ref[j, rows]
            right = right_h_ref[j, rows]
            for c in range(components):
                base_ref[c, j, rows] = left * gathered[c]
                if j > 0:
                    gathered[c] = gathered[c] + right * velocity_ref[c, j, rows]
        gathered = [jnp.zeros((SUB, lines_x), jnp.float32)] * components
        low_part = ends_ref[0, rows]
        high_part = ends_ref[1, rows] * right_ref[cells - 1, rows]
        for j in range(cells):
            left = left_h_ref[j, rows]
            right = right_ref[j, rows]
            unit_ref[j, rows] = 1.0 - (low_part * right + high_part * left_ref[j, rows])
            for c in range(components):
                gathered[c] = gathered[c] + left * velocity_ref[c, j, rows]
                base_ref[c, j, rows] = base_ref[c, j, rows] + right * gathered[c]
        return 0

    lax.fori_loop(0, lines_y // SUB, of_tile, 0)


def finish_kernel(
    own_ref, other_ref, base_ref, left_ref, right_ref, out_hbm, plain_ref, result_ref, sems
):
    components, cells, lines_y, _ = base_ref.shape
    half = own_ref.shape[0] // (2 * components)
    me = lax.axis_index("gz")

    def copies(t):
        rows = row_tile(t)
        return [
            pltpu.make_async_copy(
                result_ref.at[c - 1, :, rows], out_hbm.at[c, :, rows], sems.at[t, c - 1])
            for c in range(1, components)
        ]

    def half_of(incoming_ref, side):
        def of_tile(i, _):
            t = lax.rem(me + side, 2) * half + i
            rows = row_tile(t)
            scale = right_ref[cells - 1, rows]
            at = i * 2 * components
            lefts = [incoming_ref[at + c] for c in range(components)]
            rights = [incoming_ref[at + components + c] * scale for c in range(components)]
            for j in range(cells):
                left = left_ref[j, rows]
                right = right_ref[j, rows]
                for c in range(components):
                    value = base_ref[c, j, rows] + (right * lefts[c] + left * rights[c])
                    if c == 0:
                        plain_ref[j, rows] = value
                    else:
                        result_ref[c - 1, j, rows] = value
            for copy in copies(t):
                copy.start()
            return 0

        lax.fori_loop(0, half, of_tile, 0)

    half_of(own_ref, 0)
    half_of(other_ref, 1)
    for t in range(lines_y // SUB):
        for copy in copies(t):
            copy.wait()


def correct_kernel(count, goal_ref, unit_ref, *rest):
    tile_refs = rest[:count]
    plain_ref, _, out_hbm, result_ref, sems = rest[count:]
    totals = functools.reduce(jnp.add, [ref[0] for ref in tile_refs])
    lanes = jnp.sum(totals, axis=1, keepdims=True)
    flow = jnp.sum(lanes[0:SUB // 2], axis=0, keepdims=True)
    weight = jnp.sum(lanes[SUB // 2:], axis=0, keepdims=True)
    alpha = (goal_ref[0:1, 0:1] - flow) / weight
    cells, lines_y, _ = plain_ref.shape

    def copy(t):
        rows = row_tile(t)
        return pltpu.make_async_copy(result_ref.at[:, rows], out_hbm.at[0, :, rows], sems.at[t])

    for t in range(lines_y // SUB):
        rows = row_tile(t)
        for j in range(cells):
            result_ref[j, rows] = plain_ref[j, rows] + alpha * unit_ref[j, rows]
        copy(t).start()
    for t in range(lines_y // SUB):
        copy(t).wait()


def shards(velocity, diffusion, wall_types, stretch_index, bulk_target):
    blocks = lax.axis_size("gz")
    columns = lax.axis_size("gy")
    components, cells, lines_y, lines_x = velocity.shape
    chips = blocks // 2
    row_tiles = lines_y // SUB
    half = row_tiles // 2
    f32 = jnp.float32
    vmem = pl.BlockSpec(memory_space=pltpu.VMEM)
    anywhere = pl.BlockSpec(memory_space=pl.ANY)
    plane = (lines_y, lines_x)
    sheet = (SUB, lines_x)

    def shape(*dims):
        return jax.ShapeDtypeStruct(dims, f32)

    def in_hbm(array):
        return pltpu.with_memory_space_constraint(array, pltpu.HBM)

    def options(mib):
        return pltpu.CompilerParams(vmem_limit_bytes=mib * MIB)

    def cost(flops, transferred):
        return pl.CostEstimate(flops=flops, bytes_accessed=transferred, transcendentals=0)

    def send(array, partner):
        pairs = [((z, y), partner(z, y)) for z in range(blocks) for y in range(columns)]
        route = [(a * columns + b, c * columns + d) for (a, b), (c, d) in pairs]
        return lax.ppermute(array, ("gz", "gy"), route)

    def to_mate(array):
        return send(array, lambda z, y: (z ^ 1, y))

    count = lines_x // LANES
    lines = float(lines_y * columns * lines_x)
    (mine, away, pair, through, held, left, right, left_h, right_h, ends, volume,
     near_velocity) = pl.pallas_call(
        functools.partial(ladder_kernel, cells, blocks, chips, lines),
        out_shape=[
            shape(half * 2 * count, SUB, LANES),
            shape(half * (2 * components + 1) * count + 1, SUB, LANES),
            shape(3, *plane),
            shape(blocks, *plane),
            shape(7, *plane),
            shape(cells, *plane),
            shape(cells, *plane),
            shape(cells, *plane),
            shape(cells, *plane),
            shape(2, *plane),
            shape(SUB, LANES),
            shape(*velocity.shape),
        ],
        in_specs=[anywhere] * 4,
        out_specs=[vmem] * 12,
        scratch_shapes=[
            pltpu.SMEM(stretch_index.shape, jnp.int32),
            pltpu.VMEM(plane, f32),
            pltpu.VMEM(plane, jnp.int32),
            pltpu.VMEM((STRETCHES,) + plane, f32),
            pltpu.SemaphoreType.DMA((3 + components,)),
        ],
        compiler_params=options(24),
        cost_estimate=cost(40_000_000, 6_000_000),
        name="ladder",
    )(in_hbm(stretch_index), in_hbm(diffusion), in_hbm(wall_types), in_hbm(velocity))

    mate = to_mate(away)
    sums, chip_coefs = pl.pallas_call(
        functools.partial(rest_kernel, chips),
        out_shape=[
            shape(half * 2 * (components - 1) * count, SUB, LANES),
            shape(chips - 1, *plane),
        ],
        in_specs=[vmem] * 5,
        out_specs=[vmem] * 2,
        compiler_params=options(16),
        cost_estimate=cost(2_000_000, 2_000_000),
        name="rest",
    )(near_velocity, left_h, right_h, held, through)
    *outgoing, near = pl.pallas_call(
        functools.partial(merge_kernel, chips, components),
        out_shape=[
            shape(half * components * count + m.bit_count(), SUB, LANES) for m in range(1, chips)
        ] + [shape(half * 2 * components * count + 1, SUB, LANES)],
        in_specs=[vmem] * 5,
        out_specs=[vmem] * chips,
        compiler_params=options(16),
        cost_estimate=cost(500_000, 1_600_000),
        name="merge",
    )(mine, sums, away, mate, pair)
    order = sorted(range(1, chips), key=lambda m: -m.bit_count())
    incoming = [send(outgoing[m - 1], lambda z, y: (z ^ (2 * m), y)) for m in order]
    profile = shape(cells, *plane)
    base, unit, goal = pl.pallas_call(
        inner_kernel,
        out_shape=[shape(*velocity.shape), profile, shape(SUB, LANES)],
        in_specs=[vmem] * 8 + [anywhere],
        out_specs=[vmem] * 3,
        compiler_params=options(16),
        cost_estimate=cost(8_000_000, 8_000_000),
        name="inner",
    )(near_velocity, left, right, left_h, right_h, ends, volume, bulk_target.reshape(1, 1),
      outgoing[0])
    rounds = plane_rounds(columns)
    own_in, other_out, *tile = pl.pallas_call(
        functools.partial(spread_kernel, order, components),
        out_shape=[shape(half * 2 * components, *sheet)] * 2
        + [shape(len(rounds) - i, SUB, LANES) for i in range(len(rounds))],
        in_specs=[vmem] * 3 + [anywhere] + [vmem] * (chips - 1),
        out_specs=[vmem] * (2 + len(rounds)),
        compiler_params=options(16),
        cost_estimate=cost(500_000, 1_600_000),
        name="spread",
    )(near, pair, chip_coefs, base, *incoming)
    other_in = to_mate(other_out)
    tiles = [tile[0]] + [
        send(array, lambda z, y: (z, targets[y])) for array, targets in zip(tile, rounds)
    ]
    partial, plain = pl.pallas_call(
        finish_kernel,
        out_shape=[shape(*velocity.shape), profile],
        in_specs=[vmem] * 5,
        out_specs=[anywhere, vmem],
        scratch_shapes=[
            pltpu.VMEM((components - 1, cells) + plane, f32),
            pltpu.SemaphoreType.DMA((row_tiles, components - 1)),
        ],
        compiler_params=options(16),
        cost_estimate=cost(3_000_000, 6_000_000),
        name="finish",
    )(own_in, other_in, base, left, right)
    return pl.pallas_call(
        functools.partial(correct_kernel, len(tiles)),
        out_shape=shape(*velocity.shape),
        in_specs=[vmem] * (3 + len(tiles)) + [anywhere],
        out_specs=anywhere,
        scratch_shapes=[
            pltpu.VMEM((cells,) + plane, f32),
            pltpu.SemaphoreType.DMA((row_tiles,)),
        ],
        input_output_aliases={3 + len(tiles): 0},
        compiler_params=options(16),
        cost_estimate=cost(500_000, 1_600_000),
        name="correct",
    )(goal, unit, *tiles, plain, partial)


def solution(mesh):
    return jax.shard_map(
        shards,
        mesh=mesh,
        in_specs=(P(None, "gz", "gy", None), P("gy", None), P("gy", None), P(), P()),
        out_specs=P(None, "gz", "gy", None),
        check_vma=False,
    )
```

```python
import functools

import jax
import jax.numpy as jnp
from jax import lax
from jax.experimental import pallas as pl
from jax.experimental.pallas import tpu as pltpu
from jax.sharding import PartitionSpec as P

SUB = 8
STRETCHES = 7
LANES = 128
MIB = 1024 * 1024


def plane_rounds(columns):
    if columns == 4:
        return [(2, 3, 1, 0), (3, 2, 0, 1), (1, 0, 3, 2)]
    return [[(y + shift) % columns for y in range(columns)] for shift in range(1, columns)]


def row_tile(t):
    return pl.ds(pl.multiple_of(t * SUB, SUB), SUB)


def inverted(array):
    guess = pl.reciprocal(array, approx=True)
    return guess * (2.0 - array * guess)


def put(ref, at, sheet):
    count = sheet.shape[1] // LANES
    for i in range(count):
        ref[at * count + i] = sheet[:, i * LANES:(i + 1) * LANES]


def get(ref, at, count):
    return jnp.concatenate([ref[at * count + i] for i in range(count)], axis=1)


def height(index_ref, k):
    return 0.5 + 0.25 * index_ref[k].astype(jnp.float32)


def half_sum(index_ref, k):
    return 0.5 * (height(index_ref, k) + height(index_ref, k + 1))


def ladder_kernel(
    cells, blocks, chips, lines,
    index_hbm, diffusion_hbm, walls_hbm, velocity_hbm,
    mine_ref, away_ref, pair_ref, through_ref, held_ref, left_ref, right_ref, left_h_ref, right_h_ref,
    ends_ref, volume_ref, velocity_ref,
    index_ref, diffusion_ref, walls_ref, table_ref, sems,
):
    total = cells * blocks
    components = velocity_ref.shape[0]
    row_tiles = diffusion_ref.shape[0] // SUB
    small = [
        pltpu.make_async_copy(index_hbm, index_ref, sems.at[0]),
        pltpu.make_async_copy(diffusion_hbm, diffusion_ref, sems.at[1]),
        pltpu.make_async_copy(walls_hbm, walls_ref, sems.at[2]),
    ]
    large = [
        pltpu.make_async_copy(velocity_hbm.at[c], velocity_ref.at[c], sems.at[3 + c])
        for c in range(components)
    ]
    for copy in small + large:
        copy.start()
    me = lax.axis_index("gz")
    chip = me // 2
    first = chip * 2
    for copy in small:
        copy.wait()
    diffusion = diffusion_ref[...]
    inverse = inverted(diffusion)
    for i in range(STRETCHES):
        table_ref[i] = (0.5 + 0.25 * i) * inverse
    walls = walls_ref[...]

    def wall(bits, k):
        face = 1.0 / jnp.full((SUB, diffusion.shape[1]), 0.5 * height(index_ref, k))
        return bits.astype(jnp.float32) * jnp.concatenate([face] * row_tiles, axis=0)

    lower = wall(walls & 1, 0)
    upper = wall(walls >> 1, total - 1)

    def forward(block, kappa, keep=None):
        start = block * cells
        flux = table_ref[index_ref[start]] + kappa
        value = jnp.ones_like(flux)
        for j in range(cells):
            if keep is not None:
                keep(j, flux, value)
            k = start + j
            if j < cells - 1:
                value = value + half_sum(index_ref, k) * flux
                flux = flux + table_ref[index_ref[k + 1]] * value
        k = jnp.minimum(start + cells - 1, total - 2)
        after = inverted(value + half_sum(index_ref, k) * flux)
        return flux * after, after

    def backward(block, kappa, scale=None, keep=None):
        start = block * cells
        flux = table_ref[index_ref[start + cells - 1]] + kappa
        value = jnp.ones_like(flux)
        if scale is not None:
            flux, value = flux * scale, scale
        for j in reversed(range(cells)):
            if keep is not None:
                keep(j, flux, value)
            k = start + j
            if j > 0:
                value = value + half_sum(index_ref, k - 1) * flux
                flux = flux + table_ref[index_ref[k - 1]] * value
        k = jnp.maximum(start - 1, 0)
        after = inverted(value + half_sum(index_ref, k) * flux)
        return flux * after, after

    def thickness(block):
        parts = [height(index_ref, block * cells + j) for j in range(cells)]
        return functools.reduce(jnp.add, parts)

    def sweep_forward(block, state):
        kappa, product, extent = state
        kappa, after = forward(block, kappa)
        through_ref[block] = after
        return kappa, product * after, extent + thickness(block)

    def sweep_backward(step, state):
        block = blocks - 1 - step
        kappa, product, extent = state
        kappa, after = backward(block, kappa)
        through_ref[block] = after
        return kappa, product * after, extent + thickness(block)

    ones = jnp.ones_like(diffusion)
    kappa_left, product, extent = lax.fori_loop(
        0, me, sweep_forward, (lower, ones, thickness(me))
    )
    ends_ref[0] = diffusion * lower * product
    state = {}

    def keep_left(j, flux, value):
        left_ref[j] = value
        left_h_ref[j] = height(index_ref, me * cells + j) * value
        state["flux"], state["value"] = flux, value

    _, own_forward = forward(me, kappa_left, keep_left)
    held_ref[1] = own_forward
    held_ref[3] = state["flux"]
    held_ref[4] = state["value"]
    held_ref[5] = state["flux"] - kappa_left

    kappa_right, product, extent = lax.fori_loop(
        0, blocks - 1 - me, sweep_backward, (upper, ones, extent)
    )
    ends_ref[1] = diffusion_ref[...] * upper * product
    scale = inverted(diffusion_ref[...] * (held_ref[3] + kappa_right * held_ref[4]))
    held_ref[0] = scale

    def keep_right(j, flux, value):
        right_ref[j] = value
        right_h_ref[j] = height(index_ref, me * cells + j) * value
        state["flux"] = flux

    _, own_backward = backward(me, kappa_right, scale, keep_right)
    held_ref[2] = own_backward
    held_ref[6] = state["flux"] - kappa_right * scale

    is_first = me == first
    forth, back = held_ref[1], own_backward * held_ref[0]
    pair_ref[0] = jnp.where(is_first, back, forth)
    pair_ref[1] = jnp.where(is_first, forth, through_ref[first])
    pair_ref[2] = jnp.where(is_first, through_ref[first + 1], back)

    def fold(array):
        parts = [array[:, i * LANES:(i + 1) * LANES] for i in range(array.shape[1] // LANES)]
        return functools.reduce(jnp.add, parts)

    for copy in large:
        copy.wait()
    volume_ref[...] = jnp.full(volume_ref.shape, extent * lines)
    half = row_tiles // 2
    own_extent = thickness(me)
    heights = [height(index_ref, me * cells + j) for j in range(cells)]

    def sums(ref, whose, parts):
        def of_tile(i, state):
            flow, weight = state
            rows = row_tile(whose * half + i)
            from_left = [0.0] * parts
            from_right = [0.0] * parts
            plain = 0.0
            for j in range(cells):
                left = left_h_ref[j, rows]
                right = right_h_ref[j, rows]
                for c in range(parts):
                    v = velocity_ref[c, j, rows]
                    from_left[c] = from_left[c] + left * v
                    from_right[c] = from_right[c] + right * v
                    if c == 0:
                        plain = plain + heights[j] * v
            for c in range(parts):
                at = i * 2 * parts + c
                put(ref, at, from_left[c] * held_ref[1, rows])
                put(ref, at + parts, from_right[c] * held_ref[2, rows])
            low_part = ends_ref[0, rows]
            high_part = ends_ref[1, rows] * held_ref[0, rows]
            totals = low_part * held_ref[6, rows] + high_part * held_ref[5, rows]
            return (
                flow + fold(plain - low_part * from_right[0] - high_part * from_left[0]),
                weight + fold(own_extent - diffusion_ref[rows] * totals),
            )

        return of_tile

    state = (jnp.zeros((SUB, LANES), jnp.float32),) * 2
    mates = 1 - (me - first)
    for of_tile in (sums(away_ref, mates, components), sums(mine_ref, me - first, 1)):
        for i in range(half):
            state = of_tile(i, state)
    flow, weight = state
    for i in range(half):
        put(away_ref, half * 2 * components + i, pair_ref[0, row_tile(mates * half + i)])
    slot, middle = away_ref.shape[0] - 1, SUB // 2
    away_ref[slot, 0:middle] = flow[0:middle] + flow[middle:]
    away_ref[slot, middle:] = weight[0:middle] + weight[middle:]


def rest_kernel(
    chips, velocity_ref, left_h_ref, right_h_ref, held_ref, through_ref, sums_ref, chip_ref
):
    components, cells, _, lines_x = velocity_ref.shape
    me = lax.axis_index("gz")
    chip = me // 2
    half = sums_ref.shape[0] // (2 * (components - 1) * (lines_x // LANES))
    ones = jnp.ones(chip_ref.shape[1:], jnp.float32)
    for m in range(1, chips):
        other = chip ^ m
        low = jnp.minimum(chip, other)
        high = jnp.maximum(chip, other)
        chip_ref[m - 1] = lax.fori_loop(
            low + 1,
            high,
            lambda r, product: product * (through_ref[2 * r] * through_ref[2 * r + 1]),
            ones,
        )

    def of_tile(i, _):
        rows = row_tile((me - chip * 2) * half + i)
        from_left = [0.0] * (components - 1)
        from_right = [0.0] * (components - 1)
        for j in range(cells):
            left = left_h_ref[j, rows]
            right = right_h_ref[j, rows]
            for c in range(components - 1):
                v = velocity_ref[c + 1, j, rows]
                from_left[c] = from_left[c] + left * v
                from_right[c] = from_right[c] + right * v
        for c in range(components - 1):
            at = i * 2 * (components - 1) + c
            put(sums_ref, at, from_left[c] * held_ref[1, rows])
            put(sums_ref, at + components - 1, from_right[c] * held_ref[2, rows])
        return 0

    lax.fori_loop(0, half, of_tile, 0)


def merge_kernel(chips, components, mine_ref, sums_ref, away_ref, mate_ref, pair_ref, *rest):
    send_refs, near_ref = rest[:-1], rest[-1]
    me = lax.axis_index("gz")
    chip = me // 2
    is_first = me == chip * 2
    count = pair_ref.shape[2] // LANES
    half = mine_ref.shape[0] // (2 * count)
    slot = away_ref.shape[0] - 1
    tile = away_ref[slot] + mate_ref[slot]
    near_ref[near_ref.shape[0] - 1] = tile
    for ref in send_refs:
        for at in range(half * components * count, ref.shape[0]):
            ref[at] = tile
    for i in range(half):
        rows = row_tile((me - chip * 2) * half + i)
        mine, mate = pair_ref[0, rows], get(mate_ref, half * 2 * components + i, count)
        forth = jnp.where(is_first, mate, mine)
        back = jnp.where(is_first, mine, mate)
        for c in range(components):
            at = i * 2 * components + c
            if c == 0:
                own = [get(mine_ref, i * 2 + k, count) for k in range(2)]
            else:
                others = components - 1
                own = [
                    get(sums_ref, i * 2 * others + k * others + c - 1, count) for k in range(2)
                ]
            mine, mate = own[0], get(mate_ref, at, count)
            first = jnp.where(is_first, mine, mate)
            second = jnp.where(is_first, mate, mine)
            put(near_ref, at, first)
            to_right = second + forth * first
            at = at + components
            mine, mate = own[1], get(mate_ref, at, count)
            first = jnp.where(is_first, mine, mate)
            second = jnp.where(is_first, mate, mine)
            put(near_ref, at, second)
            to_left = first + back * second
            for m in range(1, chips):
                goes_right = (chip ^ m) > chip
                sheet = jnp.where(goes_right, to_right, to_left)
                put(send_refs[m - 1], i * components + c, sheet)


def spread_kernel(order, components, near_ref, pair_ref, chip_ref, *rest):
    recv_refs = rest[1:len(order) + 1]
    own_ref, other_ref, *tile_refs = rest[len(order) + 1:]
    me = lax.axis_index("gz")
    chip = me // 2
    is_first = me == chip * 2
    count = pair_ref.shape[2] // LANES
    half = near_ref.shape[0] // (2 * components * count)
    tiles = [ref[ref.shape[0] - 1] for ref in (near_ref, *recv_refs)]
    tile = functools.reduce(jnp.add, tiles)
    for ref in tile_refs:
        for i in range(ref.shape[0]):
            ref[i] = tile
    for i in range(half):
        rows = row_tile((me - chip * 2) * half + i)
        coefs = [chip_ref[m - 1, rows] for m in order]
        for c in range(components):
            left_in = jnp.zeros(own_ref.shape[1:], jnp.float32)
            right_in = jnp.zeros(own_ref.shape[1:], jnp.float32)
            for m, coef, ref in zip(order, coefs, recv_refs):
                term = coef * get(ref, i * components + c, count)
                from_left = (chip ^ m) < chip
                left_in = left_in + jnp.where(from_left, term, 0.0)
                right_in = right_in + jnp.where(from_left, 0.0, term)
            at = i * 2 * components + c
            left_second = get(near_ref, at, count) + pair_ref[1, rows] * left_in
            right_first = get(near_ref, at + components, count) + pair_ref[2, rows] * right_in
            own_ref[at] = jnp.where(is_first, left_in, left_second)
            other_ref[at] = jnp.where(is_first, left_second, left_in)
            at = at + components
            own_ref[at] = jnp.where(is_first, right_first, right_in)
            other_ref[at] = jnp.where(is_first, right_in, right_first)


def inner_kernel(
    velocity_ref, left_ref, right_ref, left_h_ref, right_h_ref, ends_ref, volume_ref, target_ref,
    _, base_ref, unit_ref, goal_ref,
):
    components, cells, lines_y, lines_x = velocity_ref.shape
    goal_ref[...] = target_ref[...] * volume_ref[...]

    def of_tile(t, _):
        rows = row_tile(t)
        gathered = [jnp.zeros((SUB, lines_x), jnp.float32)] * components
        for j in reversed(range(cells)):
            left = left_ref[j, rows]
            right = right_h_ref[j, rows]
            for c in range(components):
                base_ref[c, j, rows] = left * gathered[c]
                if j > 0:
                    gathered[c] = gathered[c] + right * velocity_ref[c, j, rows]
        gathered = [jnp.zeros((SUB, lines_x), jnp.float32)] * components
        low_part = ends_ref[0, rows]
        high_part = ends_ref[1, rows] * right_ref[cells - 1, rows]
        for j in range(cells):
            left = left_h_ref[j, rows]
            right = right_ref[j, rows]
            unit_ref[j, rows] = 1.0 - (low_part * right + high_part * left_ref[j, rows])
            for c in range(components):
                gathered[c] = gathered[c] + left * velocity_ref[c, j, rows]
                base_ref[c, j, rows] = base_ref[c, j, rows] + right * gathered[c]
        return 0

    lax.fori_loop(0, lines_y // SUB, of_tile, 0)


def finish_kernel(
    own_ref, other_ref, base_ref, left_ref, right_ref, out_hbm, plain_ref, result_ref, sems
):
    components, cells, lines_y, _ = base_ref.shape
    half = own_ref.shape[0] // (2 * components)
    me = lax.axis_index("gz")

    def copies(t):
        rows = row_tile(t)
        return [
            pltpu.make_async_copy(
                result_ref.at[c - 1, :, rows], out_hbm.at[c, :, rows], sems.at[t, c - 1])
            for c in range(1, components)
        ]

    def half_of(incoming_ref, side):
        def of_tile(i, _):
            t = lax.rem(me + side, 2) * half + i
            rows = row_tile(t)
            scale = right_ref[cells - 1, rows]
            at = i * 2 * components
            lefts = [incoming_ref[at + c] for c in range(components)]
            rights = [incoming_ref[at + components + c] * scale for c in range(components)]
            for j in range(cells):
                left = left_ref[j, rows]
                right = right_ref[j, rows]
                for c in range(components):
                    value = base_ref[c, j, rows] + (right * lefts[c] + left * rights[c])
                    if c == 0:
                        plain_ref[j, rows] = value
                    else:
                        result_ref[c - 1, j, rows] = value
            for copy in copies(t):
                copy.start()
            return 0

        lax.fori_loop(0, half, of_tile, 0)

    half_of(own_ref, 0)
    half_of(other_ref, 1)
    for t in range(lines_y // SUB):
        for copy in copies(t):
            copy.wait()


def correct_kernel(count, goal_ref, unit_ref, *rest):
    tile_refs = rest[:count]
    plain_ref, _, out_hbm, result_ref, sems = rest[count:]
    totals = functools.reduce(jnp.add, [ref[0] for ref in tile_refs])
    lanes = jnp.sum(totals, axis=1, keepdims=True)
    flow = jnp.sum(lanes[0:SUB // 2], axis=0, keepdims=True)
    weight = jnp.sum(lanes[SUB // 2:], axis=0, keepdims=True)
    alpha = (goal_ref[0:1, 0:1] - flow) / weight
    cells, lines_y, _ = plain_ref.shape

    def copy(t):
        rows = row_tile(t)
        return pltpu.make_async_copy(result_ref.at[:, rows], out_hbm.at[0, :, rows], sems.at[t])

    for t in range(lines_y // SUB):
        rows = row_tile(t)
        for j in range(cells):
            result_ref[j, rows] = plain_ref[j, rows] + alpha * unit_ref[j, rows]
        copy(t).start()
    for t in range(lines_y // SUB):
        copy(t).wait()


def shards(velocity, diffusion, wall_types, stretch_index, bulk_target):
    blocks = lax.axis_size("gz")
    columns = lax.axis_size("gy")
    components, cells, lines_y, lines_x = velocity.shape
    chips = blocks // 2
    row_tiles = lines_y // SUB
    half = row_tiles // 2
    f32 = jnp.float32
    vmem = pl.BlockSpec(memory_space=pltpu.VMEM)
    anywhere = pl.BlockSpec(memory_space=pl.ANY)
    plane = (lines_y, lines_x)
    sheet = (SUB, lines_x)

    def shape(*dims):
        return jax.ShapeDtypeStruct(dims, f32)

    def in_hbm(array):
        return pltpu.with_memory_space_constraint(array, pltpu.HBM)

    def options(mib):
        return pltpu.CompilerParams(vmem_limit_bytes=mib * MIB)

    def cost(flops, transferred):
        return pl.CostEstimate(flops=flops, bytes_accessed=transferred, transcendentals=0)

    def send(array, partner):
        pairs = [((z, y), partner(z, y)) for z in range(blocks) for y in range(columns)]
        route = [(a * columns + b, c * columns + d) for (a, b), (c, d) in pairs]
        return lax.ppermute(array, ("gz", "gy"), route)

    def to_mate(array):
        return send(array, lambda z, y: (z ^ 1, y))

    count = lines_x // LANES
    lines = float(lines_y * columns * lines_x)
    (mine, away, pair, through, held, left, right, left_h, right_h, ends, volume,
     near_velocity) = pl.pallas_call(
        functools.partial(ladder_kernel, cells, blocks, chips, lines),
        out_shape=[
            shape(half * 2 * count, SUB, LANES),
            shape(half * (2 * components + 1) * count + 1, SUB, LANES),
            shape(3, *plane),
            shape(blocks, *plane),
            shape(7, *plane),
            shape(cells, *plane),
            shape(cells, *plane),
            shape(cells, *plane),
            shape(cells, *plane),
            shape(2, *plane),
            shape(SUB, LANES),
            shape(*velocity.shape),
        ],
        in_specs=[anywhere] * 4,
        out_specs=[vmem] * 12,
        scratch_shapes=[
            pltpu.SMEM(stretch_index.shape, jnp.int32),
            pltpu.VMEM(plane, f32),
            pltpu.VMEM(plane, jnp.int32),
            pltpu.VMEM((STRETCHES,) + plane, f32),
            pltpu.SemaphoreType.DMA((3 + components,)),
        ],
        compiler_params=options(24),
        cost_estimate=cost(40_000_000, 6_000_000),
        name="ladder",
    )(in_hbm(stretch_index), in_hbm(diffusion), in_hbm(wall_types), in_hbm(velocity))

    mate = to_mate(away)
    sums, chip_coefs = pl.pallas_call(
        functools.partial(rest_kernel, chips),
        out_shape=[
            shape(half * 2 * (components - 1) * count, SUB, LANES),
            shape(chips - 1, *plane),
        ],
        in_specs=[vmem] * 5,
        out_specs=[vmem] * 2,
        compiler_params=options(16),
        cost_estimate=cost(2_000_000, 2_000_000),
        name="rest",
    )(near_velocity, left_h, right_h, held, through)
    *outgoing, near = pl.pallas_call(
        functools.partial(merge_kernel, chips, components),
        out_shape=[
            shape(half * components * count + m.bit_count(), SUB, LANES) for m in range(1, chips)
        ] + [shape(half * 2 * components * count + 1, SUB, LANES)],
        in_specs=[vmem] * 5,
        out_specs=[vmem] * chips,
        compiler_params=options(16),
        cost_estimate=cost(500_000, 1_600_000),
        name="merge",
    )(mine, sums, away, mate, pair)
    order = sorted(range(1, chips), key=lambda m: -m.bit_count())
    incoming = [send(outgoing[m - 1], lambda z, y: (z ^ (2 * m), y)) for m in order]
    profile = shape(cells, *plane)
    base, unit, goal = pl.pallas_call(
        inner_kernel,
        out_shape=[shape(*velocity.shape), profile, shape(SUB, LANES)],
        in_specs=[vmem] * 8 + [anywhere],
        out_specs=[vmem] * 3,
        compiler_params=options(16),
        cost_estimate=cost(8_000_000, 8_000_000),
        name="inner",
    )(near_velocity, left, right, left_h, right_h, ends, volume, bulk_target.reshape(1, 1),
      outgoing[0])
    rounds = plane_rounds(columns)
    own_in, other_out, *tile = pl.pallas_call(
        functools.partial(spread_kernel, order, components),
        out_shape=[shape(half * 2 * components, *sheet)] * 2
        + [shape(len(rounds) - i, SUB, LANES) for i in range(len(rounds))],
        in_specs=[vmem] * 3 + [anywhere] + [vmem] * (chips - 1),
        out_specs=[vmem] * (2 + len(rounds)),
        compiler_params=options(16),
        cost_estimate=cost(500_000, 1_600_000),
        name="spread",
    )(near, pair, chip_coefs, base, *incoming)
    other_in = to_mate(other_out)
    tiles = [tile[0]] + [
        send(array, lambda z, y: (z, targets[y])) for array, targets in zip(tile, rounds)
    ]
    partial, plain = pl.pallas_call(
        finish_kernel,
        out_shape=[shape(*velocity.shape), profile],
        in_specs=[vmem] * 5,
        out_specs=[anywhere, vmem],
        scratch_shapes=[
            pltpu.VMEM((components - 1, cells) + plane, f32),
            pltpu.SemaphoreType.DMA((row_tiles, components - 1)),
        ],
        compiler_params=options(16),
        cost_estimate=cost(3_000_000, 6_000_000),
        name="finish",
    )(own_in, other_in, base, left, right)
    return pl.pallas_call(
        functools.partial(correct_kernel, len(tiles)),
        out_shape=shape(*velocity.shape),
        in_specs=[vmem] * (3 + len(tiles)) + [anywhere],
        out_specs=anywhere,
        scratch_shapes=[
            pltpu.VMEM((cells,) + plane, f32),
            pltpu.SemaphoreType.DMA((row_tiles,)),
        ],
        input_output_aliases={3 + len(tiles): 0},
        compiler_params=options(16),
        cost_estimate=cost(500_000, 1_600_000),
        name="correct",
    )(goal, unit, *tiles, plain, partial)


def solution(mesh):
    return jax.shard_map(
        shards,
        mesh=mesh,
        in_specs=(P(None, "gz", "gy", None), P("gy", None), P("gy", None), P(), P()),
        out_specs=P(None, "gz", "gy", None),
        check_vma=False,
    )
```
